32 devices in a mesh: row: 4 (over y, core), col: 8 (over z, x).
Axes of the slice: x: 2, y: 2, z: 4, core: 2. Of those that a mesh axis runs over, the one named last changes fastest.
Arguments:
- tokens: bfloat16 [2, 2048, 1024], P(None, 'col', 'row'), may hold values from -6 to 6
- streams: bfloat16 [2, 3, 2048, 1024], P(None, None, 'col', 'row'), may hold values from -6 to 6
- cotangent: bfloat16 [2, 3, 2048, 1024], P(None, None, 'col', 'row'), may hold values from -6 to 6
- block_ids: int32 [2, 4, 512], P(None, 'row'), may hold values from 0 to 3, never falling along the last dimension, each value on 1 to 256 neighbouring positions
- bucket_ids: int32 [1023], replicated, may hold values from 0 to 31
- w_qkv: bfloat16 [1024, 3, 1024], P('row', None, 'col'), may hold values from -0.1875 to 0.1875
- enc_table: float32 [16, 32], P('col'), may hold values from -4 to 4
- w_out: bfloat16 [1024, 1024], P('col', 'row'), may hold values from -1.5 to 1.5
- attention_norm_gain: float32 [1024], P('row'), may hold values from 0.5 to 1.5
- attn_bias: float32 [1024], P('row'), may hold values from -3 to 3
- w_up: bfloat16 [1024, 4096], P('row', 'col'), may hold values from -0.1875 to 0.1875
- w_down: bfloat16 [4096, 1024], P('col', 'row'), may hold values from -0.125 to 0.125
- ffn_gain: float32 [1024], P('row'), may hold values from 0.5 to 1.5
- ffn_bias: float32 [1024], P('row'), may hold values from -3 to 3
- w_query: bfloat16 [1024, 1024], P('row', 'col'), may hold values from -0.1875 to 0.1875
- w_keyval: bfloat16 [1024, 2, 1024], P('row', None, 'col'), may hold values from -0.1875 to 0.1875
- cross_table: float32 [16, 32], P('col'), may hold values from -4 to 4
- w_cross_out: bfloat16 [1024, 1024], P('col', 'row'), may hold values from -1.5 to 1.5
- cross_gain: float32 [1024], P('row'), may hold values from 0.5 to 1.5
- cross_bias: float32 [1024], P('row'), may hold values from -3 to 3
Outputs:
- output: float32 [2, 3, 2048, 1024], P(None, None, 'col', 'row')
- grad_tokens: float32 [2, 2048, 1024], P(None, 'col', 'row')
- grad_streams: float32 [2, 3, 2048, 1024], P(None, None, 'col', 'row')
- gradient_query_key_value_weight: float32 [1024, 3, 1024], P('row', None, 'col')
- grad_enc_table: float32 [16, 32], P('col')
- grad_w_out: float32 [1024, 1024], P('col', 'row')
- grad_attn_gain: float32 [1024], P('row')
- grad_attn_bias: float32 [1024], P('row')
- grad_w_up: float32 [1024, 4096], P('row', 'col')
- grad_w_down: float32 [4096, 1024], P('col', 'row')
- grad_ffn_gain: float32 [1024], P('row')
- grad_ffn_bias: float32 [1024], P('row')
- grad_w_query: float32 [1024, 1024], P('row', 'col')
- grad_w_keyval: float32 [1024, 2, 1024], P('row', None, 'col')
- grad_cross_table: float32 [16, 32], P('col')
- grad_w_cross_out: float32 [1024, 1024], P('col', 'row')
- grad_cross_gain: float32 [1024], P('row')
- grad_cross_bias: float32 [1024], P('row')
The draws below stay inside these ranges and needn't reach their ends.
Inputs may be any that keep to these rules, and one draw needn't show every extreme that they name: `block_ids`: within a sequence the ids never fall, and one id holds 1 to 256 positions.
All inputs are finite; a program needn't handle non-finite values.
Results may differ from the reference program's by a relative error of at most 0.023.
Values may be sent and summed in bfloat16 or wider, within the bound.
A program may use at most 384 MiB of HBM per device.

```python
import math
import jax
import jax.numpy as jnp
import numpy as np
from jax import lax

D = 1024
H = 16
FF = 4096
NB = 32
HD = 64
STREAMS = 3
LEN = 512
BLOCK = 256
MB = 2
NSEQ = 4
TOK = 2048


def place_ends(values, key, least, top_value):
    shape = values.shape
    place = [jax.random.randint(jax.random.fold_in(key, axis), (), 0, shape[axis]) for axis in range(len(shape))]
    values = values.at[tuple(place)].set(least)
    longest = shape.index(max(shape))
    place[longest] = (place[longest] + 1) % shape[longest]
    return values.at[tuple(place)].set(top_value)


def block_levels(key, extent, split, smallest, high):
    gain, own = 1.0, jax.random.fold_in(key, 6)
    for dim, shards_of in split:
        heights = jnp.exp(jax.random.uniform(jax.random.fold_in(own, dim), (shards_of,), jnp.float32, smallest / len(split), high / len(split)))
        gain = gain * jnp.repeat(heights, extent[dim] // shards_of).reshape([-1 if axis == dim else 1 for axis in range(len(extent))])
    return gain


def profile(count, total, limit, skew):
    loads = [(1 << 20) // math.isqrt(grade ** skew) + 1 for grade in range(2, count + 1)]
    rest, given = total - limit - (count - 1), [1] * (count - 1)
    while rest > 0:
        free = [i for i in range(count - 1) if given[i] < limit]
        pool, left = sum([loads[i] for i in free]), rest
        for i in free:
            addition = min(limit - given[i], max(1, left * loads[i] // pool), rest)
            given[i] = given[i] + addition
            rest = rest - addition
    return np.array([limit] + given)


def uneven_parts(own_key, amount, total, bound, skew):
    if amount == 2:
        one = jax.random.randint(own_key, (), max(1, total - bound), min(bound, total - 1) + 1)
        return jnp.stack([one, total - one])
    lengths = jnp.asarray(profile(amount, total, bound, skew), jnp.int32)
    twos = (amount - 1) // 2
    donor, taker = lengths[1:1 + 2 * twos:2], lengths[2:2 + 2 * twos:2]
    room = jnp.minimum(donor - 1, bound - taker)
    moved = jax.random.randint(jax.random.fold_in(own_key, 1), (twos,), 0, 1 << 20) % (room + 1)
    lengths = lengths.at[1:1 + 2 * twos:2].set(donor - moved).at[2:2 + 2 * twos:2].set(taker + moved)
    return lengths[jax.random.permutation(jax.random.fold_in(own_key, 2), amount)]


def noise(stream_key, dims, deviation, reach, shards=(), kind=jnp.bfloat16):
    array = deviation * jax.random.normal(stream_key, dims, jnp.float32)
    if shards:
        array = array * block_levels(stream_key, dims, shards, -0.22, 0.18)
    return jnp.clip(array, -reach, reach).astype(kind)


def setup_inputs(seed: int = 0) -> dict:
    streams_of = jax.random.split(jax.random.key(seed), 21)
    return {
        "tokens": noise(streams_of[0], (MB, TOK, D), 1.0, 6.0, ((1, 8), (2, 4))),
        "streams": noise(streams_of[1], (MB, STREAMS, TOK, D), 1.0, 6.0, ((2, 8), (3, 4))),
        "cotangent": noise(streams_of[2], (MB, STREAMS, TOK, D), 1.0, 6.0, ((2, 8), (3, 4))),
        "block_ids": jax.vmap(lambda own: jnp.searchsorted(jnp.cumsum(uneven_parts(own, 2 * LEN // BLOCK, LEN, BLOCK, 0)), jnp.arange(LEN), side="right"))(jax.random.split(streams_of[3], MB * NSEQ)).reshape((MB, NSEQ, LEN)).astype(jnp.int32),
        "bucket_ids": place_ends(jax.random.randint(streams_of[4], (2 * LEN - 1,), 0, NB), jax.random.fold_in(streams_of[4], 1), 0, NB - 1).astype(jnp.int32),
        "w_qkv": noise(streams_of[5], (D, 3, D), D ** -0.5, 0.1875, ((0, 4), (2, 8))),
        "enc_table": noise(streams_of[6], (H, NB), 1.0, 4.0, ((0, 8),), jnp.float32),
        "w_out": noise(streams_of[7], (D, D), (D // 64) ** -0.5, 1.5, ((0, 8), (1, 4))),
        "attention_norm_gain": jnp.clip(1.0 + 0.1 * jax.random.normal(streams_of[8], (D,), jnp.float32), 0.5, 1.5),
        "attn_bias": noise(streams_of[9], (D,), 0.5, 3.0, ((0, 4),), jnp.float32),
        "w_up": noise(streams_of[10], (D, FF), D ** -0.5, 0.1875, ((0, 4), (1, 8))),
        "w_down": noise(streams_of[11], (FF, D), (FF // 2) ** -0.5, 0.125, ((0, 8), (1, 4))),
        "ffn_gain": jnp.clip(1.0 + 0.1 * jax.random.normal(streams_of[12], (D,), jnp.float32), 0.5, 1.5),
        "ffn_bias": noise(streams_of[13], (D,), 0.5, 3.0, ((0, 4),), jnp.float32),
        "w_query": noise(streams_of[14], (D, D), D ** -0.5, 0.1875, ((0, 4), (1, 8))),
        "w_keyval": noise(streams_of[15], (D, 2, D), D ** -0.5, 0.1875, ((0, 4), (2, 8))),
        "cross_table": noise(streams_of[16], (H, NB), 1.0, 4.0, ((0, 8),), jnp.float32),
        "w_cross_out": noise(streams_of[17], (D, D), (D // 64) ** -0.5, 1.5, ((0, 8), (1, 4))),
        "cross_gain": jnp.clip(1.0 + 0.1 * jax.random.normal(streams_of[18], (D,), jnp.float32), 0.5, 1.5),
        "cross_bias": noise(streams_of[19], (D,), 0.5, 3.0, ((0, 4),), jnp.float32),
    }


@jax.custom_vjp
def low(v):
    return lax.optimization_barrier(v.astype(jnp.bfloat16)).astype(jnp.float32)

@jax.custom_vjp
def low_back(v):
    return v

def low_keep(v):
    return (low(v), None)

def low_pass(kept, grad):
    return (grad,)

def back_keep(v):
    return (v, None)

def back_low(kept, grad):
    return (low(grad),)
low.defvjp(low_keep, low_pass)
low_back.defvjp(back_keep, back_low)
highest = lax.Precision.HIGHEST
epsilon = 1e-05
neg_fill = -1e+30

def layer_norm(residual, gain_vec, bias_vec):
    average = lax.optimization_barrier(jnp.mean(residual, axis=-1, keepdims=True))
    centered = residual - average
    spread = lax.optimization_barrier(jnp.mean(centered * centered, axis=-1, keepdims=True))
    return centered * lax.rsqrt(spread + epsilon) * gain_vec + bias_vec

def attend_sequence(queries, key_rows, value_rows, segment, table, bucket_ids):
    length = key_rows.shape[0]
    score_scale = queries.shape[-1] ** (-0.5)
    raw_scores = low_back(jnp.einsum('sqhd,khd->shqk', queries, key_rows, precision=highest))
    places = jnp.arange(length, dtype=jnp.int32)
    offset_index = places[None, :] - places[:, None] + (length - 1)
    per_offset = jnp.take(table, bucket_ids, axis=1)
    pos_bias = jnp.take(per_offset, offset_index, axis=1)
    visible = segment[None, :] <= segment[:, None]
    score_logits = jnp.where(visible[None, None], raw_scores * score_scale + pos_bias[None], neg_fill)
    row_max = lax.optimization_barrier(jnp.max(score_logits, axis=-1, keepdims=True))
    log_total = row_max + jnp.log(lax.optimization_barrier(jnp.sum(jnp.exp(score_logits - row_max), axis=-1, keepdims=True)))
    probability = low(jnp.exp(score_logits - log_total))
    mixed = jnp.einsum('shqk,khd->sqhd', probability, value_rows, precision=highest)
    return low_back(low(mixed))

def attend_all(queries, key_rows, value_rows, segment, table, bucket_ids):

    def one_sequence(q_seq, k_seq, v_seq, s_seq):
        return attend_sequence(q_seq, k_seq, v_seq, s_seq, table, bucket_ids)
    checked = jax.checkpoint(one_sequence)
    return lax.map(lambda packed: checked(packed[0], packed[1], packed[2], packed[3]), (queries, key_rows, value_rows, segment))

def forward(x_mb, y_mb, segment, bucket_ids, w_qkv, enc_table, w_out, attention_norm_gain, attn_bias, w_up, w_down, ffn_gain, ffn_bias, w_query, w_keyval, cross_table, w_cross_out, cross_gain, cross_bias):
    token_count = x_mb.shape[0]
    seq_count = segment.shape[0]
    length = segment.shape[1]
    qkv = low_back(low(jnp.dot(x_mb, w_qkv.reshape(D, 3 * D), precision=highest)))
    qkv = qkv.reshape(seq_count, length, 3, H, HD)
    enc_mix = attend_all(qkv[:, :, 0][:, None], qkv[:, :, 1], qkv[:, :, 2], segment, enc_table, bucket_ids)
    enc_mix = enc_mix[:, 0].reshape(token_count, D)
    attn_branch = low_back(jnp.dot(enc_mix, w_out, precision=highest))
    hidden = layer_norm(x_mb + attn_branch, attention_norm_gain, attn_bias)
    pre_act = low_back(jnp.dot(low(hidden), w_up, precision=highest))
    act_value = low(jax.nn.gelu(pre_act, approximate=False))
    ffn_branch = low_back(jnp.dot(act_value, w_down, precision=highest))
    encoded = layer_norm(hidden + ffn_branch, ffn_gain, ffn_bias)
    keyval = low_back(low(jnp.dot(low(encoded), w_keyval.reshape(D, 2 * D), precision=highest)))
    keyval = keyval.reshape(seq_count, length, 2, H, HD)
    cross_query = low_back(low(jnp.einsum('std,de->ste', y_mb, w_query, precision=highest)))
    cross_query = cross_query.reshape(STREAMS, seq_count, length, H, HD).transpose(1, 0, 2, 3, 4)
    cross_mix = attend_all(cross_query, keyval[:, :, 0], keyval[:, :, 1], segment, cross_table, bucket_ids)
    cross_mix = cross_mix.transpose(1, 0, 2, 3, 4).reshape(STREAMS, token_count, D)
    cross_branch = low_back(jnp.einsum('std,de->ste', cross_mix, w_cross_out, precision=highest))
    return layer_norm(y_mb + cross_branch, cross_gain, cross_bias)

def reference(tokens, streams, cotangent, block_ids, bucket_ids, w_qkv, enc_table, w_out, attention_norm_gain, attn_bias, w_up, w_down, ffn_gain, ffn_bias, w_query, w_keyval, cross_table, w_cross_out, cross_gain, cross_bias):
    params = tuple((weight_arg.astype(jnp.float32) for weight_arg in (w_qkv, enc_table, w_out, attention_norm_gain, attn_bias, w_up, w_down, ffn_gain, ffn_bias, w_query, w_keyval, cross_table, w_cross_out, cross_gain, cross_bias)))
    totals = tuple((jnp.zeros(weight_arg.shape, jnp.float32) for weight_arg in params))
    outputs = []
    token_grads = []
    stream_grads = []
    for micro in range(tokens.shape[0]):
        segment = block_ids[micro]

        def forward_micro(x_mb, y_mb, *weights):
            return forward(x_mb, y_mb, segment, bucket_ids, *weights)
        result, pullback = jax.vjp(forward_micro, tokens[micro].astype(jnp.float32), streams[micro].astype(jnp.float32), *params)
        gradients = pullback(cotangent[micro].astype(jnp.float32))
        outputs.append(result)
        token_grads.append(gradients[0])
        stream_grads.append(gradients[1])
        totals = tuple((running + addend for running, addend in zip(totals, gradients[2:])))
    return (jnp.stack(outputs), jnp.stack(token_grads), jnp.stack(stream_grads), totals[0], totals[1], totals[2], totals[3], totals[4], totals[5], totals[6], totals[7], totals[8], totals[9], totals[10], totals[11], totals[12], totals[13], totals[14])
```

```python
import functools
import jax
import jax.numpy as jnp
from jax import lax
from jax.experimental import pallas as pl
from jax.experimental.pallas import tpu as pltpu
from jax.sharding import PartitionSpec as P

D = 1024
F32 = jnp.float32
BF = jnp.bfloat16


epsilon = 1e-05
neg_fill = -1e30
highest = lax.Precision.HIGHEST


def gather_cols(local_rows):
    return lax.all_gather(local_rows, "col", axis=1, tiled=True)


def gather_rows(local_rows):
    return lax.all_gather(local_rows, "row", axis=1, tiled=True)


def product(matmul_operand, weight_matrix):
    return jnp.einsum(
        "ray,yw->raw", matmul_operand, weight_matrix, preferred_element_type=jnp.float32
    )


def rows_product(operand_full, matrix):
    return lax.psum_scatter(product(operand_full, matrix), "row", scatter_dimension=1, tiled=True)


def cols_product(operand_full, matrix):
    return lax.psum_scatter(product(operand_full, matrix), "col", scatter_dimension=1, tiled=True)


def weight_grad(matmul_operand, upstream_gradient):
    return jnp.einsum(
        "bpt,bpr->tr", matmul_operand, upstream_gradient, preferred_element_type=jnp.float32
    )


def gelu_exact(argument):
    return jax.nn.gelu(argument, approximate=False)


def norm_forward(residual, gain_vec, bias_vec):
    local_sum = jnp.sum(residual, axis=-1)
    average = lax.psum(local_sum, "row") / D
    centered = residual - average[..., None]
    spread = lax.psum(jnp.sum(centered * centered, axis=-1), "row") / D
    inv_std = lax.rsqrt(spread + epsilon)
    normed = centered * inv_std[..., None]
    return (normed * gain_vec + bias_vec, normed, inv_std)


def norm_back(out_grad, normed, inv_std, gain_vec):
    scaled_grad = out_grad * gain_vec
    first_moment, second_moment = lax.psum(
        (jnp.sum(scaled_grad, axis=-1), jnp.sum(scaled_grad * normed, axis=-1)), "row"
    )
    resid_grad = inv_std[..., None] * (
        scaled_grad - first_moment[..., None] / D - normed * (second_moment[..., None] / D)
    )
    return (resid_grad, jnp.sum(out_grad * normed, axis=(0, 1)), jnp.sum(out_grad, axis=(0, 1)))


def bucket_onehot(bucket_ids, bucket_count):
    return (bucket_ids[None, :] == jnp.arange(bucket_count, dtype=jnp.int32)[:, None]).astype(
        jnp.float32
    )


def block_logits(query_blk, key_rows, offsets, segment, first_row):
    row_count = query_blk.shape[2]
    length = key_rows.shape[1]
    score_scale = query_blk.shape[-1] ** (-0.5)
    raw_scores = jnp.einsum(
        "snqhd,nkhd->snhqk", query_blk, key_rows, preferred_element_type=jnp.float32
    )
    places = jnp.arange(length, dtype=jnp.int32)
    query_pos = first_row + jnp.arange(row_count, dtype=jnp.int32)
    offset_index = places[None, :] - query_pos[:, None] + (length - 1)
    pos_bias = jnp.take(offsets, offset_index, axis=1)
    visible = segment[:, first_row : first_row + row_count, None] >= segment[:, None, :]
    return jnp.where(
        visible[None, :, None], raw_scores * score_scale + pos_bias[None, None], neg_fill
    )


def attend(queries, key_rows, value_rows, segment, offsets):
    score_logits = block_logits(queries, key_rows, offsets, segment, 0)
    row_max = jnp.max(score_logits, axis=-1, keepdims=True)
    log_total = row_max + jnp.log(jnp.sum(jnp.exp(score_logits - row_max), axis=-1, keepdims=True))
    weights = jnp.exp(score_logits - log_total).astype(jnp.bfloat16)
    mixed_parts = jnp.einsum(
        "snhqk,nkhd->snqhd", weights, value_rows, preferred_element_type=jnp.float32
    )
    lse_parts = log_total[..., 0]
    return (mixed_parts, lse_parts)


def diagonal_sums(summand):
    head_count, row_count, length = summand.shape
    flipped = summand[:, ::-1, :]
    padded = jnp.concatenate(
        [flipped, jnp.zeros((head_count, row_count, row_count), summand.dtype)], axis=2
    )
    flattened = padded.reshape(head_count, row_count * (length + row_count))[
        :, : row_count * (length + row_count - 1)
    ]
    return jnp.sum(flattened.reshape(head_count, row_count, length + row_count - 1), axis=1)


def attend_back(queries, key_rows, value_rows, segment, offsets, onehot, log_totals, mix_grad):
    length = key_rows.shape[1]
    block_rows = min(512, length)
    score_scale = queries.shape[-1] ** (-0.5)
    offset_grad = jnp.zeros(offsets.shape, jnp.float32)
    score_logits = block_logits(queries, key_rows, offsets, segment, 0)
    probability = jnp.exp(score_logits - log_totals[:, :, :, 0:block_rows, None])
    prob_grad = jnp.einsum(
        "snqhd,nkhd->snhqk", mix_grad, value_rows, preferred_element_type=jnp.float32
    )
    logit_grad = probability * (
        prob_grad - jnp.sum(probability * prob_grad, axis=-1, keepdims=True)
    )
    scaled = (logit_grad * score_scale).astype(jnp.bfloat16)
    query_parts = jnp.einsum(
        "snhqk,nkhd->snqhd", scaled, key_rows, preferred_element_type=jnp.float32
    )
    key_grad = jnp.einsum("snhqk,snqhd->nkhd", scaled, queries, preferred_element_type=jnp.float32)
    value_grad = jnp.einsum(
        "snhqk,snqhd->nkhd",
        probability.astype(jnp.bfloat16),
        mix_grad,
        preferred_element_type=jnp.float32,
    )
    low_end = length - block_rows
    offset_grad = offset_grad.at[:, low_end : low_end + length + block_rows - 1].add(
        diagonal_sums(jnp.sum(logit_grad, axis=(0, 1)))
    )
    table_grad = jnp.dot(offset_grad, onehot.T, precision=highest)
    return (query_parts, key_grad, value_grad, table_grad)


def on_device_general(
    tokens,
    streams,
    cotangent,
    block_ids,
    bucket_ids,
    w_qkv,
    enc_table,
    w_out,
    attention_norm_gain,
    attn_bias,
    w_up,
    w_down,
    ffn_gain,
    ffn_bias,
    w_query,
    w_keyval,
    cross_table,
    w_cross_out,
    cross_gain,
    cross_bias,
):
    micro_count = tokens.shape[0]
    stream_count = streams.shape[1]
    seq_rows = block_ids.shape[1]
    length = block_ids.shape[2]
    head_count = enc_table.shape[0]
    bucket_count = enc_table.shape[1]
    row_width = w_qkv.shape[0]
    col_width = w_qkv.shape[2]
    head_dim = col_width // head_count
    row_tokens = seq_rows * length
    qkv_matrix = w_qkv.reshape(row_width, 3 * col_width)
    keyval_matrix = w_keyval.reshape(row_width, 2 * col_width)
    onehot = bucket_onehot(bucket_ids, bucket_count)
    enc_offsets = jnp.dot(enc_table, onehot, precision=highest)
    cross_offsets = jnp.dot(cross_table, onehot, precision=highest)
    qkv_acc = jnp.zeros((row_width, 3 * col_width), jnp.float32)
    out_acc = jnp.zeros(w_out.shape, jnp.float32)
    up_acc = jnp.zeros(w_up.shape, jnp.float32)
    down_acc = jnp.zeros(w_down.shape, jnp.float32)
    query_acc = jnp.zeros(w_query.shape, jnp.float32)
    keyval_acc = jnp.zeros((row_width, 2 * col_width), jnp.float32)
    cross_out_acc = jnp.zeros(w_cross_out.shape, jnp.float32)
    enc_table_acc = jnp.zeros(enc_table.shape, jnp.float32)
    cross_table_acc = jnp.zeros(cross_table.shape, jnp.float32)
    norm_accs = [jnp.zeros((row_width,), jnp.float32) for place_holder in range(6)]
    outputs = []
    token_grads = []
    stream_grads = []
    for micro in range(micro_count):
        segment = block_ids[micro]
        x_in = tokens[micro][None]
        y_in = streams[micro]
        x_full = gather_cols(x_in)
        qkv = (
            rows_product(x_full, qkv_matrix)
            .astype(jnp.bfloat16)
            .reshape(seq_rows, length, 3, head_count, head_dim)
        )
        enc_query = qkv[:, :, 0][None]
        enc_key = qkv[:, :, 1]
        encoder_value_rows = qkv[:, :, 2]
        enc_mixed, enc_lse = attend(enc_query, enc_key, encoder_value_rows, segment, enc_offsets)
        enc_mix = enc_mixed.reshape(1, row_tokens, col_width).astype(jnp.bfloat16)
        mix_full = gather_rows(enc_mix)
        attn_branch = cols_product(mix_full, w_out)
        hidden, normed_one, inv_one = norm_forward(
            x_in.astype(jnp.float32) + attn_branch, attention_norm_gain, attn_bias
        )
        hidden_low = hidden.astype(jnp.bfloat16)
        hidden_full = gather_cols(hidden_low)
        pre_act = rows_product(hidden_full, w_up)
        act_value, gelu_pull = jax.vjp(gelu_exact, pre_act)
        act_low = act_value.astype(jnp.bfloat16)
        act_full = gather_rows(act_low)
        ffn_branch = cols_product(act_full, w_down)
        encoded, normed_two, inv_two = norm_forward(hidden + ffn_branch, ffn_gain, ffn_bias)
        encoded_low = encoded.astype(jnp.bfloat16)
        enc_full = gather_cols(encoded_low)
        keyval = (
            rows_product(enc_full, keyval_matrix)
            .astype(jnp.bfloat16)
            .reshape(seq_rows, length, 2, head_count, head_dim)
        )
        cross_key = keyval[:, :, 0]
        cross_value = keyval[:, :, 1]
        stream_full = gather_cols(y_in)
        cross_query = (
            rows_product(stream_full, w_query)
            .astype(jnp.bfloat16)
            .reshape(stream_count, seq_rows, length, head_count, head_dim)
        )
        cross_mixed, cross_lse = attend(cross_query, cross_key, cross_value, segment, cross_offsets)
        cross_mix = cross_mixed.reshape(stream_count, row_tokens, col_width).astype(jnp.bfloat16)
        cross_full = gather_rows(cross_mix)
        cross_branch = cols_product(cross_full, w_cross_out)
        result, normed_three, inv_three = norm_forward(
            y_in.astype(jnp.float32) + cross_branch, cross_gain, cross_bias
        )
        outputs.append(result)
        grad_three, gain_part, bias_part = norm_back(
            cotangent[micro].astype(jnp.float32), normed_three, inv_three, cross_gain
        )
        norm_accs[4] = norm_accs[4] + gain_part
        norm_accs[5] = norm_accs[5] + bias_part
        branch_full = gather_cols(grad_three.astype(jnp.bfloat16))
        cross_out_acc = cross_out_acc + weight_grad(cross_full, branch_full)
        cross_mix_grad = (
            rows_product(branch_full, w_cross_out.T)
            .astype(jnp.bfloat16)
            .reshape(stream_count, seq_rows, length, head_count, head_dim)
        )
        query_grad, key_grad, value_grad, table_grad = attend_back(
            cross_query,
            cross_key,
            cross_value,
            segment,
            cross_offsets,
            onehot,
            cross_lse,
            cross_mix_grad,
        )
        cross_table_acc = cross_table_acc + table_grad
        query_low = query_grad.reshape(stream_count, row_tokens, col_width).astype(jnp.bfloat16)
        keyval_low = (
            jnp.stack(
                [
                    key_grad.reshape(row_tokens, col_width),
                    value_grad.reshape(row_tokens, col_width),
                ],
                axis=1,
            )
            .reshape(1, row_tokens, 2 * col_width)
            .astype(jnp.bfloat16)
        )
        query_full = gather_rows(query_low)
        query_acc = query_acc + weight_grad(stream_full, query_full)
        stream_grads.append(grad_three + cols_product(query_full, w_query.T))
        keyval_full = gather_rows(keyval_low)
        keyval_acc = keyval_acc + weight_grad(enc_full, keyval_full)
        encoded_grad = cols_product(keyval_full, keyval_matrix.T)
        grad_two, gain_part, bias_part = norm_back(encoded_grad, normed_two, inv_two, ffn_gain)
        norm_accs[2] = norm_accs[2] + gain_part
        norm_accs[3] = norm_accs[3] + bias_part
        feedforward_full_output = gather_cols(grad_two.astype(jnp.bfloat16))
        down_acc = down_acc + weight_grad(act_full, feedforward_full_output)
        act_grad = rows_product(feedforward_full_output, w_down.T)
        pre_low = gelu_pull(act_grad)[0].astype(jnp.bfloat16)
        pre_full = gather_rows(pre_low)
        up_acc = up_acc + weight_grad(hidden_full, pre_full)
        hidden_grad = grad_two + cols_product(pre_full, w_up.T)
        grad_one, gain_part, bias_part = norm_back(
            hidden_grad, normed_one, inv_one, attention_norm_gain
        )
        norm_accs[0] = norm_accs[0] + gain_part
        norm_accs[1] = norm_accs[1] + bias_part
        attn_full = gather_cols(grad_one.astype(jnp.bfloat16))
        out_acc = out_acc + weight_grad(mix_full, attn_full)
        enc_mix_grad = (
            rows_product(attn_full, w_out.T)
            .astype(jnp.bfloat16)
            .reshape(1, seq_rows, length, head_count, head_dim)
        )
        enc_qgrad, enc_kgrad, enc_vgrad, table_grad = attend_back(
            enc_query,
            enc_key,
            encoder_value_rows,
            segment,
            enc_offsets,
            onehot,
            enc_lse,
            enc_mix_grad,
        )
        enc_table_acc = enc_table_acc + table_grad
        qkv_low = (
            jnp.stack(
                [
                    enc_qgrad.reshape(row_tokens, col_width),
                    enc_kgrad.reshape(row_tokens, col_width),
                    enc_vgrad.reshape(row_tokens, col_width),
                ],
                axis=1,
            )
            .reshape(1, row_tokens, 3 * col_width)
            .astype(jnp.bfloat16)
        )
        qkv_full = gather_rows(qkv_low)
        qkv_acc = qkv_acc + weight_grad(x_full, qkv_full)
        token_grads.append((grad_one + cols_product(qkv_full, qkv_matrix.T))[0])
    norm_stack = jnp.stack(norm_accs)
    table_stack = jnp.stack([enc_table_acc, cross_table_acc])
    norm_sums = lax.psum(norm_stack, "col")
    table_sums = lax.psum(table_stack, "row")
    return (
        jnp.stack(outputs),
        jnp.stack(token_grads),
        jnp.stack(stream_grads),
        qkv_acc.reshape(row_width, 3, col_width),
        table_sums[0],
        out_acc,
        norm_sums[0],
        norm_sums[1],
        up_acc,
        down_acc,
        norm_sums[2],
        norm_sums[3],
        query_acc,
        keyval_acc.reshape(row_width, 2, col_width),
        table_sums[1],
        cross_out_acc,
        norm_sums[4],
        norm_sums[5],
    )


def mm(a,b):
    return jnp.dot(a,b,preferred_element_type=F32)
def mm_nt(a,b):
    return lax.dot_general(a,b,(((1,),(1,)),((),())),preferred_element_type=F32)

def fwd_kernel(streams, length, width, off_ref, segq_ref, segk_ref, q_ref, k_ref, v_ref, mix_ref, lse_ref, t_ref):
    chunks = 2*length//width - 1
    top = length - width
    for c in range(chunks):
        lo = (chunks-1-c)*width
        w = off_ref[0, :, lo:lo+2*width]
        rolled = pltpu.roll(jnp.broadcast_to(w,(width,2*width)), 0, 1, stride=1, stride_axis=0)
        t_ref[0, c*width:(c+1)*width, :] = rolled[:, width:]
    keys = k_ref[0].T
    values = v_ref[0]
    scale = k_ref.shape[1]**-0.5
    panels = length//width
    for p in range(panels):
        bias = t_ref[0, top-p*width:top-p*width+length, :]
        shown = segk_ref[...] <= segq_ref[:, p*width:(p+1)*width]
        for s in range(streams):
            lo = s*length+p*width
            logits = mm(keys, q_ref[0, :, lo:lo+width])*scale + bias
            logits = jnp.where(shown, logits, neg_fill)
            m = jnp.max(logits, axis=0, keepdims=True)
            e = jnp.exp(logits-m)
            total = jnp.sum(e, axis=0, keepdims=True)
            lse_ref[0, :, lo:lo+width] = m + jnp.log(total)
            prob = (e*(1.0/total)).astype(BF)
            mix_ref[0, :, lo:lo+width] = mm(values, prob).astype(BF)

def bwd_kernel(streams, length, width, t_ref, segq_ref, segk_ref, q_ref, k_ref, v_ref, lse_ref, dmix_ref, dq_ref, dk_ref, dv_ref, doff_ref, g_scr, dk_scr, dv_scr):
    chunks = 2*length//width - 1
    top = length - width
    keysT = k_ref[0]
    keys = keysT.T
    values = v_ref[0].T
    scale = k_ref.shape[1]**-0.5
    panels = length//width
    g_scr[...] = jnp.zeros_like(g_scr)
    dk_scr[...] = jnp.zeros_like(dk_scr)
    dv_scr[...] = jnp.zeros_like(dv_scr)
    for p in range(panels):
        rows = slice(top-p*width, top-p*width+length)
        shown = segk_ref[...] <= segq_ref[:, p*width:(p+1)*width]
        for s in range(streams):
            lo = s*length+p*width
            qs = q_ref[0, :, lo:lo+width]
            dm = dmix_ref[0, :, lo:lo+width]
            logits = mm(keys, qs)*scale + t_ref[0, rows, :]
            prob = jnp.where(shown, jnp.exp(logits - lse_ref[0, :, lo:lo+width]), 0.0)
            dprob = mm(values, dm)
            delta = jnp.sum(prob*dprob, axis=0, keepdims=True)
            dlog = prob*(dprob-delta)
            g_scr[rows, :] += dlog
            g = (dlog*scale).astype(BF)
            dq_ref[0, :, lo:lo+width] = mm(keysT, g).astype(BF)
            dk_scr[...] += mm_nt(qs, g)
            dv_scr[...] += mm_nt(dm, prob.astype(BF))
    dk_ref[0] = dk_scr[...].astype(BF)
    dv_ref[0] = dv_scr[...].astype(BF)
    doff_ref[...] = jnp.zeros_like(doff_ref)
    sub = lax.broadcasted_iota(jnp.int32, (8, 2*width), 0)
    for c in range(chunks):
        acc = jnp.zeros((8, 2*width), F32)
        for i in range(width//8):
            piece = g_scr[c*width+8*i:c*width+8*i+8, :]
            padded = jnp.concatenate([jnp.zeros((8,width),F32), piece], axis=1)
            if i: padded = pltpu.roll(padded, 2*width-8*i, 1)
            acc = acc + padded
        for b in (1,2,4):
            acc = jnp.where((sub//b)%2==1, pltpu.roll(acc, 2*width-b, 1), acc)
        lo = (chunks-1-c)*width
        doff_ref[0, :, lo:lo+2*width] += jnp.sum(acc, axis=0, keepdims=True)

def attention(off_rev, segq, segk, q, k, v, parts, streams):
    heads, length = k.shape[0], k.shape[2]
    hd = 64; width=128
    blk = lambda part,n: pl.BlockSpec((1,hd,n), lambda h: (h,part,0))
    return pl.pallas_call(
        functools.partial(fwd_kernel, streams, length, width),
        grid=(heads,),
        in_specs=[pl.BlockSpec((1,1,2*length),lambda h:(h,0,0)), pl.BlockSpec((1,length),lambda h:(0,0)), pl.BlockSpec((length,width),lambda h:(0,0)),
                  blk(parts[0],streams*length), blk(parts[1],length), blk(parts[2],length)],
        out_specs=[blk(0,streams*length), pl.BlockSpec((1,1,streams*length),lambda h:(h,0,0)), pl.BlockSpec((1,2*length-width,width),lambda h:(h,0,0))],
        out_shape=[jax.ShapeDtypeStruct((heads,hd,streams*length),BF), jax.ShapeDtypeStruct((heads,1,streams*length),F32), jax.ShapeDtypeStruct((heads,2*length-width,width),F32)],
        compiler_params=pltpu.CompilerParams(vmem_limit_bytes=48<<20),
        name="attend",
    )(off_rev, segq, segk, q, k, v)

def attention_back(tiles, segq, segk, q, k, v, parts, lse, dmix, streams):
    heads, length = k.shape[0], k.shape[2]
    hd = 64; width=128
    blk = lambda part,n: pl.BlockSpec((1,hd,n), lambda h: (h,part,0))
    return pl.pallas_call(
        functools.partial(bwd_kernel, streams, length, width),
        grid=(heads,),
        in_specs=[pl.BlockSpec((1,2*length-width,width),lambda h:(h,0,0)), pl.BlockSpec((1,length),lambda h:(0,0)), pl.BlockSpec((length,width),lambda h:(0,0)),
                  blk(parts[0],streams*length), blk(parts[1],length), blk(parts[2],length),
                  pl.BlockSpec((1,1,streams*length),lambda h:(h,0,0)), blk(0,streams*length)],
        out_specs=[blk(0,streams*length), blk(0,length), blk(0,length), pl.BlockSpec((1,1,2*length),lambda h:(h,0,0))],
        out_shape=[jax.ShapeDtypeStruct((heads,hd,streams*length),BF), jax.ShapeDtypeStruct((heads,hd,length),BF), jax.ShapeDtypeStruct((heads,hd,length),BF), jax.ShapeDtypeStruct((heads,1,2*length),F32)],
        scratch_shapes=[pltpu.VMEM((2*length-width,width),F32), pltpu.VMEM((hd,length),F32), pltpu.VMEM((hd,length),F32)],
        compiler_params=pltpu.CompilerParams(vmem_limit_bytes=48<<20),
        name="attend_back",
    )(tiles, segq, segk, q, k, v, lse, dmix)


def send(value, pairs):
    return lax.ppermute(value, ("row", "col"), pairs)


def device_pairs(rows, cols):
    seqs = cols // 2
    place = lambda y, k, s, h: (2 * (y % (rows // 2)) + k % 2) * cols + 2 * (s % seqs) + h % 2
    spots = [(y, k, s, h) for y in range(rows // 2) for k in range(2) for s in range(seqs) for h in range(2)]
    move = lambda dy, dk, ds, dh: [(place(y, k, s, h), place(y + dy, k + dk, s + ds, h + dh)) for y, k, s, h in spots]
    return {
        "core": move(0, 1, 0, 0),
        "half": move(0, 0, 0, 1),
        "micro": move(1, 0, 0, 0),
        "seq": [move(0, 0, d, 0) for d in range(seqs)],
    }


def pick(array, index, axis):
    return lax.dynamic_index_in_dim(array, index, axis, keepdims=False)


def in_order(first, mine, other, axis, join=jnp.concatenate):
    return jnp.where(first, join([mine, other], axis=axis), join([other, mine], axis=axis))


def layer_norm(residual, gain_vec, bias_vec):
    centered = residual - jnp.mean(residual, axis=-1, keepdims=True)
    inv_std = lax.rsqrt(jnp.mean(centered * centered, axis=-1, keepdims=True) + epsilon)
    normed = centered * inv_std
    return (normed * gain_vec + bias_vec, normed, inv_std)


def layer_norm_back(out_grad, normed, inv_std, gain_vec):
    scaled = out_grad * gain_vec
    first = jnp.mean(scaled, axis=-1, keepdims=True)
    second = jnp.mean(scaled * normed, axis=-1, keepdims=True)
    lead = tuple(range(out_grad.ndim - 1))
    return (
        inv_std * (scaled - first - normed * second),
        jnp.sum(out_grad * normed, axis=lead),
        jnp.sum(out_grad, axis=lead),
    )


def dot_f32(spec, left, right):
    return jnp.einsum(spec, left, right, preferred_element_type=F32)


def on_device(
    rows,
    cols,
    tokens,
    streams,
    cotangent,
    block_ids,
    bucket_ids,
    w_qkv,
    enc_table,
    w_out,
    attention_norm_gain,
    attn_bias,
    w_up,
    w_down,
    ffn_gain,
    ffn_bias,
    w_query,
    w_keyval,
    cross_table,
    w_cross_out,
    cross_gain,
    cross_bias,
):
    pairs = device_pairs(rows, cols)
    seqs = cols // 2
    row, col = lax.axis_index("row"), lax.axis_index("col")
    y, k, seq, half = row // 2, row % 2, col // 2, col % 2
    low_core, low_half, low_y = k == 0, half == 0, y == 0
    stream_count = streams.shape[1]
    tok = tokens.shape[1]
    own = tok // 2
    feat = tokens.shape[2]
    length = block_ids.shape[2]
    head_dim = w_qkv.shape[2] // 2
    ff = w_up.shape[1] // 2
    table_heads, bucket_count = enc_table.shape

    norm_params = jnp.stack([attention_norm_gain, attn_bias, ffn_gain, ffn_bias, cross_gain, cross_bias])
    norm_params = lax.all_gather(norm_params, "row", axis=1, tiled=True)
    norm_params = jnp.where(low_y, norm_params, jnp.roll(norm_params, D // 2, axis=1))
    gain1, bias1, gain2, bias2, gain3, bias3 = norm_params
    segment = pick(pick(lax.all_gather(block_ids, "row", axis=1, tiled=True), y, 0), seq, 0)
    segq = segment[None]
    segk = jnp.broadcast_to(segment[:, None], (length, 128))
    tables = lax.all_gather(jnp.stack([enc_table, cross_table]), "col", axis=0)
    slot_col = 2 * ((seq - jnp.arange(seqs)) % seqs) + half
    own_tables = pick(jnp.take(tables, slot_col, axis=0), k, 2)
    reversed_ids = jnp.concatenate([jnp.full((1,), -1, jnp.int32), bucket_ids[::-1]])
    onehot = bucket_onehot(reversed_ids, bucket_count)
    offsets = jnp.einsum("htb,bo->tho", own_tables, onehot, precision=highest)[:, :, None, :]

    def relayout(array):
        count = array.shape[1]
        both = jnp.concatenate([pick(array, y, 0), send(pick(array, 1 - y, 0), pairs["micro"])], axis=-1)
        blocks = both.reshape(count, 2, own, 2, 1, feat)
        other = send(pick(blocks, 1 - k, 1), pairs["core"])
        return in_order(low_core, pick(blocks, k, 1), other, 3).reshape(count, own, D)

    def relayout_back(array, link_type):
        count = array.shape[0]
        blocks = array.reshape(count, own, 2, 2, feat)
        other = send(pick(blocks, 1 - k, 3), pairs["core"])
        both = in_order(low_core, pick(blocks, k, 3), other, 1).reshape(count, tok, 2, feat)
        other = send(both[:, :, 1].astype(link_type), pairs["micro"]).astype(F32)
        return in_order(low_y, both[:, :, 0], other, 0, jnp.stack)

    def gather_tokens(array):
        count = array.shape[0]
        pair = in_order(low_half, array, send(array, pairs["half"]), 1, jnp.stack)
        return in_order(low_core, pair, send(pair, pairs["core"]), 2, jnp.stack).reshape(count, 2 * tok, D)

    def scatter_tokens(partial):
        count = partial.shape[0]
        blocks = partial.reshape(count, 2, 2, own, D)
        other = send(pick(blocks, 1 - k, 2).astype(BF), pairs["core"])
        blocks = pick(blocks, k, 2) + other.astype(F32)
        other = send(pick(blocks, 1 - half, 1).astype(BF), pairs["half"])
        return pick(blocks, half, 1) + other.astype(F32)

    def gather_weights(shards):
        base = in_order(low_core, pick(shards, k, 0), send(pick(shards, 1 - k, 0), pairs["core"]), 1)
        slots = jnp.stack([base] + [send(base, pairs["seq"][d]) for d in range(1, seqs)])
        return jnp.concatenate([slots, send(slots, pairs["micro"])], axis=2)

    def scatter_weights(grad):
        part = grad[:, :, : D // 2] + send(grad[:, :, D // 2 :].astype(BF), pairs["micro"]).astype(F32)
        low = part.astype(BF)
        total = part[0]
        for d in range(1, seqs):
            total = total + send(low[d], pairs["seq"][seqs - d]).astype(F32)
        blocks = total.reshape(-1, 2, feat)
        other = send(pick(blocks, 1 - k, 1), pairs["core"])
        return in_order(low_core, pick(blocks, k, 1), other, 0, jnp.stack)

    def columns(weight, parts):
        return weight.reshape(feat, parts, 2, -1).transpose(2, 1, 3, 0).reshape(2, -1, feat)

    def columns_back(array, parts):
        return array.reshape(2, parts, -1, feat).transpose(3, 1, 0, 2).reshape(feat, parts, -1)

    halves = lambda weight: weight.reshape(2, -1, feat)
    hd3, hd2 = 3 * head_dim, 2 * head_dim
    first = gather_weights(jnp.concatenate([columns(w_qkv, 3), halves(w_out)], axis=1))
    x_own = relayout(tokens[:, None])
    x_full = gather_tokens(x_own)[0]
    up = gather_weights(columns(w_up, 1))
    down = gather_weights(halves(w_down))
    last = gather_weights(jnp.concatenate([columns(w_keyval, 2), columns(w_query, 1), halves(w_cross_out)], axis=1))
    y_own = relayout(streams)
    y_full = gather_tokens(y_own).reshape(stream_count * length, D)
    c_own = relayout(cotangent)
    m_qkv, m_out = first[:, :hd3], first[:, hd3:].reshape(-1, D)
    m_kv, m_q, m_co = last[:, :hd2], last[:, hd2:hd3], last[:, hd3:].reshape(-1, D)
    up, down = up.reshape(-1, D), down.reshape(-1, D)

    qkv = dot_f32("snr,tr->snt", m_qkv, x_full).astype(BF)
    mix, lse, tiles = attention(offsets[0], segq, segk, qkv, qkv, qkv, (0, 1, 2), 1)
    mix_flat = mix.reshape(-1, length)
    branch = scatter_tokens(dot_f32("et,er->tr", mix_flat, m_out)[None])[0]
    hidden, normed1, inv1 = layer_norm(x_own[0].astype(F32) + branch, gain1, bias1)
    hidden_full = gather_tokens(hidden.astype(BF)[None])[0]
    pre = dot_f32("fr,tr->ft", up, hidden_full)
    act, gelu_pull = jax.vjp(gelu_exact, pre)
    act = act.astype(BF)
    branch = scatter_tokens(dot_f32("ft,fr->tr", act, down)[None])[0]
    encoded, normed2, inv2 = layer_norm(hidden + branch, gain2, bias2)
    enc_full = gather_tokens(encoded.astype(BF)[None])[0]
    kv = dot_f32("snr,tr->snt", m_kv, enc_full).astype(BF)
    query = dot_f32("snr,tr->snt", m_q, y_full).astype(BF)
    cmix, clse, ctiles = attention(offsets[1], segq, segk, query, kv, kv, (0, 0, 1), stream_count)
    cmix_flat = cmix.reshape(-1, stream_count * length)
    branch = scatter_tokens(dot_f32("et,er->tr", cmix_flat, m_co).reshape(stream_count, length, D))
    result, normed3, inv3 = layer_norm(y_own.astype(F32) + branch, gain3, bias3)
    output = relayout_back(result, BF)

    d3, gain3_grad, bias3_grad = layer_norm_back(c_own.astype(F32), normed3, inv3, gain3)
    d3_full = gather_tokens(d3.astype(BF)).reshape(stream_count * length, D)
    dcmix = dot_f32("er,tr->et", m_co, d3_full).astype(BF).reshape(cmix.shape)
    g_co = dot_f32("et,tr->er", cmix_flat, d3_full)
    dquery, dkc, dvc, doff_cross = attention_back(
        ctiles, segq, segk, query, kv, kv, (0, 0, 1), clse, dcmix, stream_count
    )
    dkv = jnp.concatenate([dkc, dvc], axis=1)
    d_enc = scatter_tokens(dot_f32("snt,snr->tr", dkv, m_kv)[None])[0]
    d2, gain2_grad, bias2_grad = layer_norm_back(d_enc, normed2, inv2, gain2)
    d2_full = gather_tokens(d2.astype(BF)[None])[0]
    g_q = dot_f32("snt,tr->snr", dquery, y_full)
    g_kv = dot_f32("snt,tr->snr", dkv, enc_full)
    g_last = scatter_weights(
        jnp.concatenate([g_kv, g_q, g_co.reshape(seqs, head_dim, D)], axis=1)
    )
    dy = scatter_tokens(dot_f32("snt,snr->tr", dquery, m_q).reshape(stream_count, length, D))
    grad_streams = relayout_back(d3 + dy, BF)
    dact = dot_f32("fr,tr->ft", down, d2_full)
    dpre = gelu_pull(dact)[0].astype(BF)
    g_down = scatter_weights(dot_f32("ft,tr->fr", act, d2_full).reshape(seqs, ff, D))
    d_hid = d2 + scatter_tokens(dot_f32("ft,fr->tr", dpre, up)[None])[0]
    d1, gain1_grad, bias1_grad = layer_norm_back(d_hid, normed1, inv1, gain1)
    d1_full = gather_tokens(d1.astype(BF)[None])[0]
    g_up = scatter_weights(dot_f32("ft,tr->fr", dpre, hidden_full).reshape(seqs, ff, D))
    dmix = dot_f32("er,tr->et", m_out, d1_full).astype(BF).reshape(mix.shape)
    g_out = dot_f32("et,tr->er", mix_flat, d1_full)
    dq, dk, dv, doff_enc = attention_back(tiles, segq, segk, qkv, qkv, qkv, (0, 1, 2), lse, dmix, 1)
    dqkv = jnp.concatenate([dq, dk, dv], axis=1)
    g_qkv = dot_f32("snt,tr->snr", dqkv, x_full)
    g_first = scatter_weights(jnp.concatenate([g_qkv, g_out.reshape(seqs, head_dim, D)], axis=1))
    dx = scatter_tokens(dot_f32("snt,snr->tr", dqkv, m_qkv)[None])[0]
    grad_tokens = relayout_back((d1 + dx)[None], BF)[:, 0]

    norm_grads = jnp.stack([gain1_grad, bias1_grad, gain2_grad, bias2_grad, gain3_grad, bias3_grad])
    norm_grads = jnp.where(low_y, norm_grads, jnp.roll(norm_grads, D // 2, axis=1))
    table_grads = jnp.einsum(
        "tho,bo->thb", jnp.stack([doff_enc[:, 0], doff_cross[:, 0]]), onehot, precision=highest
    )
    heads = 2 * slot_col + k
    spread = (heads[:, None] == jnp.arange(table_heads * cols)[None, :]).astype(F32)
    table_grads = jnp.einsum("thb,hg->tgb", table_grads, spread, precision=highest)
    small = jnp.concatenate([norm_grads.reshape(-1, 128), table_grads.reshape(-1, 128)])
    small = lax.psum(small, ("row", "col"))
    count = norm_grads.size // 128
    norm_sums = lax.dynamic_slice_in_dim(small[:count].reshape(6, D), row * feat, feat, axis=1)
    table_sums = small[count:].reshape(2, table_heads * cols, bucket_count)
    table_sums = lax.dynamic_slice_in_dim(table_sums, col * table_heads, table_heads, axis=1)
    return (
        output,
        grad_tokens,
        grad_streams,
        columns_back(g_first[:, :hd3], 3),
        table_sums[0],
        g_first[:, hd3:].reshape(w_out.shape),
        norm_sums[0],
        norm_sums[1],
        columns_back(g_up, 1).reshape(w_up.shape),
        g_down.reshape(w_down.shape),
        norm_sums[2],
        norm_sums[3],
        columns_back(g_last[:, hd2:hd3], 1).reshape(w_query.shape),
        columns_back(g_last[:, :hd2], 2),
        table_sums[1],
        g_last[:, hd3:].reshape(w_cross_out.shape),
        norm_sums[4],
        norm_sums[5],
    )


def solution(mesh):
    whole_row, half_col = mesh.shape["row"], mesh.shape["col"]
    weights = (P("row", None, "col"), P("col", None), P("col", "row"), P("row"), P("row"), P("row", "col"), P("col", "row"), P("row"), P("row"), P("row", "col"), P("row", None, "col"), P("col", None), P("col", "row"), P("row"), P("row"))

    def run(tokens, *rest):
        micro_count = tokens.shape[0]
        if whole_row == 2 * micro_count:
            device_fn = functools.partial(on_device, whole_row, half_col)
        else:
            device_fn = on_device_general
        return jax.shard_map(
            device_fn,
            mesh=mesh,
            in_specs=(P(None, "col", "row"), P(None, None, "col", "row"), P(None, None, "col", "row"), P(None, "row", None), P()) + weights,
            out_specs=(P(None, None, "col", "row"), P(None, "col", "row"), P(None, None, "col", "row")) + weights,
            check_vma=False,
        )(tokens, *rest)

    return run
```

```python
import functools
import jax
import jax.numpy as jnp
from jax import lax
from jax.experimental import pallas as pl
from jax.experimental.pallas import tpu as pltpu
from jax.sharding import PartitionSpec as P

D = 1024
F32 = jnp.float32
BF = jnp.bfloat16


epsilon = 1e-05
neg_fill = -1e30
highest = lax.Precision.HIGHEST


def gather_cols(local_rows):
    return lax.all_gather(local_rows, "col", axis=1, tiled=True)


def gather_rows(local_rows):
    return lax.all_gather(local_rows, "row", axis=1, tiled=True)


def product(matmul_operand, weight_matrix):
    return jnp.einsum(
        "ray,yw->raw", matmul_operand, weight_matrix, preferred_element_type=jnp.float32
    )


def rows_product(operand_full, matrix):
    return lax.psum_scatter(product(operand_full, matrix), "row", scatter_dimension=1, tiled=True)


def cols_product(operand_full, matrix):
    return lax.psum_scatter(product(operand_full, matrix), "col", scatter_dimension=1, tiled=True)


def weight_grad(matmul_operand, upstream_gradient):
    return jnp.einsum(
        "bpt,bpr->tr", matmul_operand, upstream_gradient, preferred_element_type=jnp.float32
    )


def gelu_exact(argument):
    return jax.nn.gelu(argument, approximate=False)


def norm_forward(residual, gain_vec, bias_vec):
    local_sum = jnp.sum(residual, axis=-1)
    average = lax.psum(local_sum, "row") / D
    centered = residual - average[..., None]
    spread = lax.psum(jnp.sum(centered * centered, axis=-1), "row") / D
    inv_std = lax.rsqrt(spread + epsilon)
    normed = centered * inv_std[..., None]
    return (normed * gain_vec + bias_vec, normed, inv_std)


def norm_back(out_grad, normed, inv_std, gain_vec):
    scaled_grad = out_grad * gain_vec
    first_moment, second_moment = lax.psum(
        (jnp.sum(scaled_grad, axis=-1), jnp.sum(scaled_grad * normed, axis=-1)), "row"
    )
    resid_grad = inv_std[..., None] * (
        scaled_grad - first_moment[..., None] / D - normed * (second_moment[..., None] / D)
    )
    return (resid_grad, jnp.sum(out_grad * normed, axis=(0, 1)), jnp.sum(out_grad, axis=(0, 1)))


def bucket_onehot(bucket_ids, bucket_count):
    return (bucket_ids[None, :] == jnp.arange(bucket_count, dtype=jnp.int32)[:, None]).astype(
        jnp.float32
    )


def block_logits(query_blk, key_rows, offsets, segment, first_row):
    row_count = query_blk.shape[2]
    length = key_rows.shape[1]
    score_scale = query_blk.shape[-1] ** (-0.5)
    raw_scores = jnp.einsum(
        "snqhd,nkhd->snhqk", query_blk, key_rows, preferred_element_type=jnp.float32
    )
    places = jnp.arange(length, dtype=jnp.int32)
    query_pos = first_row + jnp.arange(row_count, dtype=jnp.int32)
    offset_index = places[None, :] - query_pos[:, None] + (length - 1)
    pos_bias = jnp.take(offsets, offset_index, axis=1)
    visible = segment[:, first_row : first_row + row_count, None] >= segment[:, None, :]
    return jnp.where(
        visible[None, :, None], raw_scores * score_scale + pos_bias[None, None], neg_fill
    )


def attend(queries, key_rows, value_rows, segment, offsets):
    score_logits = block_logits(queries, key_rows, offsets, segment, 0)
    row_max = jnp.max(score_logits, axis=-1, keepdims=True)
    log_total = row_max + jnp.log(jnp.sum(jnp.exp(score_logits - row_max), axis=-1, keepdims=True))
    weights = jnp.exp(score_logits - log_total).astype(jnp.bfloat16)
    mixed_parts = jnp.einsum(
        "snhqk,nkhd->snqhd", weights, value_rows, preferred_element_type=jnp.float32
    )
    lse_parts = log_total[..., 0]
    return (mixed_parts, lse_parts)


def diagonal_sums(summand):
    head_count, row_count, length = summand.shape
    flipped = summand[:, ::-1, :]
    padded = jnp.concatenate(
        [flipped, jnp.zeros((head_count, row_count, row_count), summand.dtype)], axis=2
    )
    flattened = padded.reshape(head_count, row_count * (length + row_count))[
        :, : row_count * (length + row_count - 1)
    ]
    return jnp.sum(flattened.reshape(head_count, row_count, length + row_count - 1), axis=1)


def attend_back(queries, key_rows, value_rows, segment, offsets, onehot, log_totals, mix_grad):
    length = key_rows.shape[1]
    block_rows = min(512, length)
    score_scale = queries.shape[-1] ** (-0.5)
    offset_grad = jnp.zeros(offsets.shape, jnp.float32)
    score_logits = block_logits(queries, key_rows, offsets, segment, 0)
    probability = jnp.exp(score_logits - log_totals[:, :, :, 0:block_rows, None])
    prob_grad = jnp.einsum(
        "snqhd,nkhd->snhqk", mix_grad, value_rows, preferred_element_type=jnp.float32
    )
    logit_grad = probability * (
        prob_grad - jnp.sum(probability * prob_grad, axis=-1, keepdims=True)
    )
    scaled = (logit_grad * score_scale).astype(jnp.bfloat16)
    query_parts = jnp.einsum(
        "snhqk,nkhd->snqhd", scaled, key_rows, preferred_element_type=jnp.float32
    )
    key_grad = jnp.einsum("snhqk,snqhd->nkhd", scaled, queries, preferred_element_type=jnp.float32)
    value_grad = jnp.einsum(
        "snhqk,snqhd->nkhd",
        probability.astype(jnp.bfloat16),
        mix_grad,
        preferred_element_type=jnp.float32,
    )
    low_end = length - block_rows
    offset_grad = offset_grad.at[:, low_end : low_end + length + block_rows - 1].add(
        diagonal_sums(jnp.sum(logit_grad, axis=(0, 1)))
    )
    table_grad = jnp.dot(offset_grad, onehot.T, precision=highest)
    return (query_parts, key_grad, value_grad, table_grad)


def on_device_general(
    tokens,
    streams,
    cotangent,
    block_ids,
    bucket_ids,
    w_qkv,
    enc_table,
    w_out,
    attention_norm_gain,
    attn_bias,
    w_up,
    w_down,
    ffn_gain,
    ffn_bias,
    w_query,
    w_keyval,
    cross_table,
    w_cross_out,
    cross_gain,
    cross_bias,
):
    micro_count = tokens.shape[0]
    stream_count = streams.shape[1]
    seq_rows = block_ids.shape[1]
    length = block_ids.shape[2]
    head_count = enc_table.shape[0]
    bucket_count = enc_table.shape[1]
    row_width = w_qkv.shape[0]
    col_width = w_qkv.shape[2]
    head_dim = col_width // head_count
    row_tokens = seq_rows * length
    qkv_matrix = w_qkv.reshape(row_width, 3 * col_width)
    keyval_matrix = w_keyval.reshape(row_width, 2 * col_width)
    onehot = bucket_onehot(bucket_ids, bucket_count)
    enc_offsets = jnp.dot(enc_table, onehot, precision=highest)
    cross_offsets = jnp.dot(cross_table, onehot, precision=highest)
    qkv_acc = jnp.zeros((row_width, 3 * col_width), jnp.float32)
    out_acc = jnp.zeros(w_out.shape, jnp.float32)
    up_acc = jnp.zeros(w_up.shape, jnp.float32)
    down_acc = jnp.zeros(w_down.shape, jnp.float32)
    query_acc = jnp.zeros(w_query.shape, jnp.float32)
    keyval_acc = jnp.zeros((row_width, 2 * col_width), jnp.float32)
    cross_out_acc = jnp.zeros(w_cross_out.shape, jnp.float32)
    enc_table_acc = jnp.zeros(enc_table.shape, jnp.float32)
    cross_table_acc = jnp.zeros(cross_table.shape, jnp.float32)
    norm_accs = [jnp.zeros((row_width,), jnp.float32) for place_holder in range(6)]
    outputs = []
    token_grads = []
    stream_grads = []
    for micro in range(micro_count):
        segment = block_ids[micro]
        x_in = tokens[micro][None]
        y_in = streams[micro]
        x_full = gather_cols(x_in)
        qkv = (
            rows_product(x_full, qkv_matrix)
            .astype(jnp.bfloat16)
            .reshape(seq_rows, length, 3, head_count, head_dim)
        )
        enc_query = qkv[:, :, 0][None]
        enc_key = qkv[:, :, 1]
        encoder_value_rows = qkv[:, :, 2]
        enc_mixed, enc_lse = attend(enc_query, enc_key, encoder_value_rows, segment, enc_offsets)
        enc_mix = enc_mixed.reshape(1, row_tokens, col_width).astype(jnp.bfloat16)
        mix_full = gather_rows(enc_mix)
        attn_branch = cols_product(mix_full, w_out)
        hidden, normed_one, inv_one = norm_forward(
            x_in.astype(jnp.float32) + attn_branch, attention_norm_gain, attn_bias
        )
        hidden_low = hidden.astype(jnp.bfloat16)
        hidden_full = gather_cols(hidden_low)
        pre_act = rows_product(hidden_full, w_up)
        act_value, gelu_pull = jax.vjp(gelu_exact, pre_act)
        act_low = act_value.astype(jnp.bfloat16)
        act_full = gather_rows(act_low)
        ffn_branch = cols_product(act_full, w_down)
        encoded, normed_two, inv_two = norm_forward(hidden + ffn_branch, ffn_gain, ffn_bias)
        encoded_low = encoded.astype(jnp.bfloat16)
        enc_full = gather_cols(encoded_low)
        keyval = (
            rows_product(enc_full, keyval_matrix)
            .astype(jnp.bfloat16)
            .reshape(seq_rows, length, 2, head_count, head_dim)
        )
        cross_key = keyval[:, :, 0]
        cross_value = keyval[:, :, 1]
        stream_full = gather_cols(y_in)
        cross_query = (
            rows_product(stream_full, w_query)
            .astype(jnp.bfloat16)
            .reshape(stream_count, seq_rows, length, head_count, head_dim)
        )
        cross_mixed, cross_lse = attend(cross_query, cross_key, cross_value, segment, cross_offsets)
        cross_mix = cross_mixed.reshape(stream_count, row_tokens, col_width).astype(jnp.bfloat16)
        cross_full = gather_rows(cross_mix)
        cross_branch = cols_product(cross_full, w_cross_out)
        result, normed_three, inv_three = norm_forward(
            y_in.astype(jnp.float32) + cross_branch, cross_gain, cross_bias
        )
        outputs.append(result)
        grad_three, gain_part, bias_part = norm_back(
            cotangent[micro].astype(jnp.float32), normed_three, inv_three, cross_gain
        )
        norm_accs[4] = norm_accs[4] + gain_part
        norm_accs[5] = norm_accs[5] + bias_part
        branch_full = gather_cols(grad_three.astype(jnp.bfloat16))
        cross_out_acc = cross_out_acc + weight_grad(cross_full, branch_full)
        cross_mix_grad = (
            rows_product(branch_full, w_cross_out.T)
            .astype(jnp.bfloat16)
            .reshape(stream_count, seq_rows, length, head_count, head_dim)
        )
        query_grad, key_grad, value_grad, table_grad = attend_back(
            cross_query,
            cross_key,
            cross_value,
            segment,
            cross_offsets,
            onehot,
            cross_lse,
            cross_mix_grad,
        )
        cross_table_acc = cross_table_acc + table_grad
        query_low = query_grad.reshape(stream_count, row_tokens, col_width).astype(jnp.bfloat16)
        keyval_low = (
            jnp.stack(
                [
                    key_grad.reshape(row_tokens, col_width),
                    value_grad.reshape(row_tokens, col_width),
                ],
                axis=1,
            )
            .reshape(1, row_tokens, 2 * col_width)
            .astype(jnp.bfloat16)
        )
        query_full = gather_rows(query_low)
        query_acc = query_acc + weight_grad(stream_full, query_full)
        stream_grads.append(grad_three + cols_product(query_full, w_query.T))
        keyval_full = gather_rows(keyval_low)
        keyval_acc = keyval_acc + weight_grad(enc_full, keyval_full)
        encoded_grad = cols_product(keyval_full, keyval_matrix.T)
        grad_two, gain_part, bias_part = norm_back(encoded_grad, normed_two, inv_two, ffn_gain)
        norm_accs[2] = norm_accs[2] + gain_part
        norm_accs[3] = norm_accs[3] + bias_part
        feedforward_full_output = gather_cols(grad_two.astype(jnp.bfloat16))
        down_acc = down_acc + weight_grad(act_full, feedforward_full_output)
        act_grad = rows_product(feedforward_full_output, w_down.T)
        pre_low = gelu_pull(act_grad)[0].astype(jnp.bfloat16)
        pre_full = gather_rows(pre_low)
        up_acc = up_acc + weight_grad(hidden_full, pre_full)
        hidden_grad = grad_two + cols_product(pre_full, w_up.T)
        grad_one, gain_part, bias_part = norm_back(
            hidden_grad, normed_one, inv_one, attention_norm_gain
        )
        norm_accs[0] = norm_accs[0] + gain_part
        norm_accs[1] = norm_accs[1] + bias_part
        attn_full = gather_cols(grad_one.astype(jnp.bfloat16))
        out_acc = out_acc + weight_grad(mix_full, attn_full)
        enc_mix_grad = (
            rows_product(attn_full, w_out.T)
            .astype(jnp.bfloat16)
            .reshape(1, seq_rows, length, head_count, head_dim)
        )
        enc_qgrad, enc_kgrad, enc_vgrad, table_grad = attend_back(
            enc_query,
            enc_key,
            encoder_value_rows,
            segment,
            enc_offsets,
            onehot,
            enc_lse,
            enc_mix_grad,
        )
        enc_table_acc = enc_table_acc + table_grad
        qkv_low = (
            jnp.stack(
                [
                    enc_qgrad.reshape(row_tokens, col_width),
                    enc_kgrad.reshape(row_tokens, col_width),
                    enc_vgrad.reshape(row_tokens, col_width),
                ],
                axis=1,
            )
            .reshape(1, row_tokens, 3 * col_width)
            .astype(jnp.bfloat16)
        )
        qkv_full = gather_rows(qkv_low)
        qkv_acc = qkv_acc + weight_grad(x_full, qkv_full)
        token_grads.append((grad_one + cols_product(qkv_full, qkv_matrix.T))[0])
    norm_stack = jnp.stack(norm_accs)
    table_stack = jnp.stack([enc_table_acc, cross_table_acc])
    norm_sums = lax.psum(norm_stack, "col")
    table_sums = lax.psum(table_stack, "row")
    return (
        jnp.stack(outputs),
        jnp.stack(token_grads),
        jnp.stack(stream_grads),
        qkv_acc.reshape(row_width, 3, col_width),
        table_sums[0],
        out_acc,
        norm_sums[0],
        norm_sums[1],
        up_acc,
        down_acc,
        norm_sums[2],
        norm_sums[3],
        query_acc,
        keyval_acc.reshape(row_width, 2, col_width),
        table_sums[1],
        cross_out_acc,
        norm_sums[4],
        norm_sums[5],
    )


def mm(a,b):
    return jnp.dot(a,b,preferred_element_type=F32)
def mm_nt(a,b):
    return lax.dot_general(a,b,(((1,),(1,)),((),())),preferred_element_type=F32)

def fwd_kernel(streams, length, width, off_ref, segq_ref, segk_ref, q_ref, k_ref, v_ref, mix_ref, lse_ref, t_ref):
    chunks = 2*length//width - 1
    top = length - width
    for c in range(chunks):
        lo = (chunks-1-c)*width
        w = off_ref[0, :, lo:lo+2*width]
        rolled = pltpu.roll(jnp.broadcast_to(w,(width,2*width)), 0, 1, stride=1, stride_axis=0)
        t_ref[0, c*width:(c+1)*width, :] = rolled[:, width:]
    keys = k_ref[0].T
    values = v_ref[0]
    scale = k_ref.shape[1]**-0.5
    panels = length//width
    for p in range(panels):
        bias = t_ref[0, top-p*width:top-p*width+length, :]
        shown = segk_ref[...] <= segq_ref[:, p*width:(p+1)*width]
        for s in range(streams):
            lo = s*length+p*width
            logits = mm(keys, q_ref[0, :, lo:lo+width])*scale + bias
            logits = jnp.where(shown, logits, neg_fill)
            m = jnp.max(logits, axis=0, keepdims=True)
            e = jnp.exp(logits-m)
            total = jnp.sum(e, axis=0, keepdims=True)
            lse_ref[0, :, lo:lo+width] = m + jnp.log(total)
            prob = (e*(1.0/total)).astype(BF)
            mix_ref[0, :, lo:lo+width] = mm(values, prob).astype(BF)

def bwd_kernel(streams, length, width, t_ref, segq_ref, segk_ref, q_ref, k_ref, v_ref, lse_ref, dmix_ref, dq_ref, dk_ref, dv_ref, doff_ref, g_scr, dk_scr, dv_scr):
    chunks = 2*length//width - 1
    top = length - width
    keysT = k_ref[0]
    keys = keysT.T
    values = v_ref[0].T
    scale = k_ref.shape[1]**-0.5
    panels = length//width
    g_scr[...] = jnp.zeros_like(g_scr)
    dk_scr[...] = jnp.zeros_like(dk_scr)
    dv_scr[...] = jnp.zeros_like(dv_scr)
    for p in range(panels):
        rows = slice(top-p*width, top-p*width+length)
        shown = segk_ref[...] <= segq_ref[:, p*width:(p+1)*width]
        for s in range(streams):
            lo = s*length+p*width
            qs = q_ref[0, :, lo:lo+width]
            dm = dmix_ref[0, :, lo:lo+width]
            logits = mm(keys, qs)*scale + t_ref[0, rows, :]
            prob = jnp.where(shown, jnp.exp(logits - lse_ref[0, :, lo:lo+width]), 0.0)
            dprob = mm(values, dm)
            delta = jnp.sum(prob*dprob, axis=0, keepdims=True)
            dlog = prob*(dprob-delta)
            g_scr[rows, :] += dlog
            g = (dlog*scale).astype(BF)
            dq_ref[0, :, lo:lo+width] = mm(keysT, g).astype(BF)
            dk_scr[...] += mm_nt(qs, g)
            dv_scr[...] += mm_nt(dm, prob.astype(BF))
    dk_ref[0] = dk_scr[...].astype(BF)
    dv_ref[0] = dv_scr[...].astype(BF)
    doff_ref[...] = jnp.zeros_like(doff_ref)
    sub = lax.broadcasted_iota(jnp.int32, (8, 2*width), 0)
    for c in range(chunks):
        acc = jnp.zeros((8, 2*width), F32)
        for i in range(width//8):
            piece = g_scr[c*width+8*i:c*width+8*i+8, :]
            padded = jnp.concatenate([jnp.zeros((8,width),F32), piece], axis=1)
            if i: padded = pltpu.roll(padded, 2*width-8*i, 1)
            acc = acc + padded
        for b in (1,2,4):
            acc = jnp.where((sub//b)%2==1, pltpu.roll(acc, 2*width-b, 1), acc)
        lo = (chunks-1-c)*width
        doff_ref[0, :, lo:lo+2*width] += jnp.sum(acc, axis=0, keepdims=True)

def attention(off_rev, segq, segk, q, k, v, parts, streams):
    heads, length = k.shape[0], k.shape[2]
    hd = 64; width=128
    blk = lambda part,n: pl.BlockSpec((1,hd,n), lambda h: (h,part,0))
    return pl.pallas_call(
        functools.partial(fwd_kernel, streams, length, width),
        grid=(heads,),
        in_specs=[pl.BlockSpec((1,1,2*length),lambda h:(h,0,0)), pl.BlockSpec((1,length),lambda h:(0,0)), pl.BlockSpec((length,width),lambda h:(0,0)),
                  blk(parts[0],streams*length), blk(parts[1],length), blk(parts[2],length)],
        out_specs=[blk(0,streams*length), pl.BlockSpec((1,1,streams*length),lambda h:(h,0,0)), pl.BlockSpec((1,2*length-width,width),lambda h:(h,0,0))],
        out_shape=[jax.ShapeDtypeStruct((heads,hd,streams*length),BF), jax.ShapeDtypeStruct((heads,1,streams*length),F32), jax.ShapeDtypeStruct((heads,2*length-width,width),F32)],
        compiler_params=pltpu.CompilerParams(vmem_limit_bytes=48<<20),
        name="attend",
    )(off_rev, segq, segk, q, k, v)

def attention_back(tiles, segq, segk, q, k, v, parts, lse, dmix, streams):
    heads, length = k.shape[0], k.shape[2]
    hd = 64; width=128
    blk = lambda part,n: pl.BlockSpec((1,hd,n), lambda h: (h,part,0))
    return pl.pallas_call(
        functools.partial(bwd_kernel, streams, length, width),
        grid=(heads,),
        in_specs=[pl.BlockSpec((1,2*length-width,width),lambda h:(h,0,0)), pl.BlockSpec((1,length),lambda h:(0,0)), pl.BlockSpec((length,width),lambda h:(0,0)),
                  blk(parts[0],streams*length), blk(parts[1],length), blk(parts[2],length),
                  pl.BlockSpec((1,1,streams*length),lambda h:(h,0,0)), blk(0,streams*length)],
        out_specs=[blk(0,streams*length), blk(0,length), blk(0,length), pl.BlockSpec((1,1,2*length),lambda h:(h,0,0))],
        out_shape=[jax.ShapeDtypeStruct((heads,hd,streams*length),BF), jax.ShapeDtypeStruct((heads,hd,length),BF), jax.ShapeDtypeStruct((heads,hd,length),BF), jax.ShapeDtypeStruct((heads,1,2*length),F32)],
        scratch_shapes=[pltpu.VMEM((2*length-width,width),F32), pltpu.VMEM((hd,length),F32), pltpu.VMEM((hd,length),F32)],
        compiler_params=pltpu.CompilerParams(vmem_limit_bytes=48<<20),
        name="attend_back",
    )(tiles, segq, segk, q, k, v, lse, dmix)


MESH = pl.DeviceIdType.MESH


def spot():
    row, col = lax.axis_index("row"), lax.axis_index("col")
    return row // 2, row % 2, col // 2, col % 2


def device(y, k, seq, half):
    return (2 * y + k, 2 * seq + half)


def greet(devices):
    barrier = pltpu.get_barrier_semaphore()
    for target in devices:
        pl.semaphore_signal(barrier, inc=1, device_id=target, device_id_type=MESH)
    pl.semaphore_wait(barrier, len(devices))


def remote(source, target, send_sem, recv_sem, device_id):
    copy = pltpu.make_async_remote_copy(
        src_ref=source, dst_ref=target, send_sem=send_sem, recv_sem=recv_sem, device_id=device_id, device_id_type=MESH
    )
    copy.start()
    return copy


def lanes(start, size):
    return pl.ds(pl.multiple_of(start, size), size)


def rows_of(place):
    y, k, seq, half = place
    return [(dy, dk, (1 - y if dy else y), (1 - k if dk else k)) for dy, dk in ((0, 1), (1, 0), (1, 1))]


class Spread:
    def __init__(self, full_ref, half_sems, core_sems, place, rows):
        self.full, self.place, self.rows = full_ref, place, rows
        self.half_sems, self.core_sems = half_sems, core_sems
        self.first, self.second = {}, {}

    def block(self, n, piece, half, k):
        return self.full.at[n, half, k, pl.ds(piece * self.rows, self.rows)]

    def start(self, unit, n, piece):
        y, k, seq, half = self.place
        mine = self.block(n, piece, half, k)
        hs, cs = self.half_sems, self.core_sems
        self.first[unit] = (
            remote(mine, mine, hs.at[0, unit], hs.at[1, unit], device(y, k, seq, 1 - half)),
            remote(mine, mine, cs.at[0, unit, 0], cs.at[1, unit, 0], device(y, 1 - k, seq, half)),
        )

    def forward(self, unit, n, piece):
        y, k, seq, half = self.place
        self.first[unit][0].wait_recv()
        theirs = self.block(n, piece, 1 - half, k)
        cs = self.core_sems
        self.second[unit] = remote(theirs, theirs, cs.at[0, unit, 1], cs.at[1, unit, 1], device(y, 1 - k, seq, half))

    def finish(self, unit):
        self.first[unit][0].wait_send()
        self.first[unit][1].wait()
        self.second[unit].wait()


class Reduce:
    def __init__(self, partial_ref, core_buf, half_send, half_buf, core_sems, half_sems, place, rows):
        self.partial, self.core_buf, self.half_send, self.half_buf = partial_ref, core_buf, half_send, half_buf
        self.core_sems, self.half_sems, self.place, self.rows = core_sems, half_sems, place, rows
        self.first, self.second = {}, {}

    def part(self, n, piece, half, k):
        return (n, half, k, pl.ds(piece * self.rows, self.rows))

    def start(self, unit, n, piece, away):
        y, k, seq, half = self.place
        side = 1 - half if away else half
        cs = self.core_sems
        lane = 0 if away else 1
        self.first[unit, lane] = remote(
            self.partial.at[self.part(n, piece, side, 1 - k)],
            self.core_buf.at[unit, lane],
            cs.at[0, unit, lane],
            cs.at[1, unit, lane],
            device(y, 1 - k, seq, half),
        )

    def pass_on(self, unit, n, piece):
        y, k, seq, half = self.place
        self.first[unit, 0].wait_recv()
        away = self.partial[self.part(n, piece, 1 - half, k)].astype(F32) + self.core_buf[unit, 0].astype(F32)
        self.half_send[unit] = away.astype(BF)
        hs = self.half_sems
        self.second[unit] = remote(
            self.half_send.at[unit], self.half_buf.at[unit], hs.at[0, unit], hs.at[1, unit], device(y, k, seq, 1 - half)
        )

    def result(self, unit, n, piece):
        y, k, seq, half = self.place
        self.first[unit, 1].wait_recv()
        mine = self.partial[self.part(n, piece, half, k)].astype(F32) + self.core_buf[unit, 1].astype(F32)
        self.second[unit].wait_recv()
        return mine + self.half_buf[unit].astype(F32)

    def finish(self, unit):
        self.first[unit, 0].wait_send()
        self.first[unit, 1].wait_send()
        self.second[unit].wait_send()


class Return:
    def __init__(self, own_ref, landing, sems, place, feat):
        self.own, self.landing, self.sems, self.place, self.feat = own_ref, landing, sems, place, feat
        self.copies = []

    def start(self, unit, n, value):
        y, k, seq, half = self.place
        feat = self.feat
        self.own[unit] = value
        self.landing[y, n, k] = jnp.where(k == 0, value[:, :feat], value[:, feat : 2 * feat])
        for i, (dy, dk, ty, tk) in enumerate(rows_of(self.place)):
            self.copies.append(
                remote(
                    self.own.at[unit, :, lanes(tk * feat + 2 * dy * feat, feat)],
                    self.landing.at[y, n, k],
                    self.sems.at[0, unit, i],
                    self.sems.at[1, unit, i],
                    device(ty, tk, seq, half),
                )
            )

    def finish(self):
        for copy in self.copies:
            copy.wait()


def normalize(residual):
    centered = residual - jnp.mean(residual, axis=-1, keepdims=True)
    inv_std = lax.rsqrt(jnp.mean(centered * centered, axis=-1, keepdims=True) + epsilon)
    return centered * inv_std, inv_std


def normalize_back(out_grad, normed, inv_std, gain):
    scaled = out_grad * gain
    first = jnp.mean(scaled, axis=-1, keepdims=True)
    second = jnp.mean(scaled * normed, axis=-1, keepdims=True)
    return inv_std * (scaled - first - normed * second)


def column_sum(value):
    return jnp.sum(value, axis=0, keepdims=True)


def exchange_kernel(kind, count, pieces, *refs):
    place = spot()
    y, k, seq, half = place
    names = {
        "forward": ("resid", "norm", "full", "out", "normed", "inv"),
        "turn": ("resid", "norm", "cot", "full", "output", "grad", "sums", "own", "landing", "return_sems"),
        "backward": ("resid", "norm", "normed", "inv", "full", "grad", "sums"),
    }[kind]
    partial, refs = refs[0], refs[1:]
    r = dict(zip(names, refs))
    core_buf, half_send, half_buf, rc, rh, gh, gc = refs[len(names) :]
    rows = partial.shape[3] // pieces
    peers = [device(y, 1 - k, seq, half), device(y, k, seq, 1 - half)]
    if kind == "turn":
        peers += [device(ty, tk, seq, half) for dy, dk, ty, tk in rows_of(place) if dy]
    greet(peers)
    units = [(n * pieces + p, n, p) for n in range(count) for p in range(pieces)]
    reduce = Reduce(partial, core_buf, half_send, half_buf, rc, rh, place, rows)
    spread = Spread(r["full"], gh, gc, place, rows)
    for unit, n, p in units:
        reduce.start(unit, n, p, True)
    for unit, n, p in units:
        reduce.start(unit, n, p, False)
    if kind != "forward":
        r["sums"][...] = jnp.zeros_like(r["sums"])
    if kind == "turn":
        back = Return(r["own"], r["landing"], r["return_sems"], place, partial.shape[4] // 4)
    gain, bias = r["norm"][0:1], r["norm"][1:2]
    for unit, n, p in units:
        reduce.pass_on(unit, n, p)
    for unit, n, p in units:
        here = pl.ds(p * rows, rows)
        branch = reduce.result(unit, n, p)
        if kind == "forward":
            normed, inv = normalize(r["resid"][n, here].astype(F32) + branch)
            value = normed * gain + bias
            r["out"][n, here] = value
            r["normed"][n, here] = normed
            r["inv"][n, here] = inv
        elif kind == "turn":
            normed, inv = normalize(r["resid"][n, here].astype(F32) + branch)
            upstream = r["cot"][n, here].astype(F32)
            value = normalize_back(upstream, normed, inv, gain)
            r["grad"][n, here] = value
        else:
            upstream = r["resid"][n, here] + branch if r["resid"].shape[1] == partial.shape[3] else branch
            normed = r["normed"][n, here]
            value = normalize_back(upstream, normed, r["inv"][n, here], gain)
            r["grad"][n, here] = value
        r["full"][n, half, k, here] = value.astype(BF)
        spread.start(unit, n, p)
        if kind != "forward":
            r["sums"][0:1] += column_sum(upstream * normed)
            r["sums"][1:2] += column_sum(upstream)
        if kind == "turn":
            back.start(unit, n, (normed * gain + bias).astype(BF))
    for unit, n, p in units:
        spread.forward(unit, n, p)
    for unit, n, p in units:
        spread.finish(unit)
        reduce.finish(unit)
    if kind == "turn":
        back.finish()
        r["output"][...] = r["landing"][...].astype(F32)


def exchange(kind, collective_id, partial, resid, norm, cot=None, normed=None, inv=None):
    count, _, _, own, depth = partial.shape
    pieces = 2 if count == 1 else 1
    units, rows = count * pieces, own // pieces
    dma = pltpu.SemaphoreType.DMA
    shape = jax.ShapeDtypeStruct
    full = shape((count, 2, 2, own, depth), BF)
    grad, sums = shape((count, own, depth), F32), shape((8, depth), F32)
    scratch = []
    if kind == "forward":
        args = (partial, resid, norm)
        outs = (full, grad, grad, shape((count, own, 1), F32))
    elif kind == "turn":
        args = (partial, resid, norm, cot)
        outs = (full, shape((2, count, 2, own, depth // 4), F32), grad, sums)
        scratch = [pltpu.VMEM((units, rows, depth), BF), pltpu.VMEM((2, count, 2, own, depth // 4), BF), dma((2, units, 3))]
    else:
        args = (partial, resid, norm, normed, inv)
        outs = (full, grad, sums)
    scratch += [
        pltpu.VMEM((units, 2, rows, depth), BF),
        pltpu.VMEM((units, rows, depth), BF),
        pltpu.VMEM((units, rows, depth), BF),
        dma((2, units, 2)),
        dma((2, units)),
        dma((2, units)),
        dma((2, units, 2)),
    ]
    return pl.pallas_call(
        functools.partial(exchange_kernel, kind, count, pieces),
        out_shape=outs,
        in_specs=[pl.BlockSpec(memory_space=pltpu.VMEM)] * len(args),
        out_specs=tuple(pl.BlockSpec(memory_space=pltpu.VMEM) for _ in outs),
        scratch_shapes=scratch,
        compiler_params=pltpu.CompilerParams(collective_id=collective_id, has_side_effects=True, vmem_limit_bytes=50 << 20),
        name="exchange_" + kind,
    )(*args)


def inputs_kernel(seqs, tok_ref, str_ref, cot_ref, norm_ref, ids_ref, tab_ref, x_own, x_full, y_own, y_full, c_own, norm_all, ids_all, tab_all, in_send, in_recv, self_sems, xh, xc, yh, yc, small_sems, tab_sems, small_self):
    place = spot()
    y, k, seq, half = place
    feat = tok_ref.shape[-1]
    own = tok_ref.shape[-2]
    row_peers = rows_of(place)
    rest = [lax.rem(seq + d, seqs) for d in range(1, seqs)]
    greet(
        [device(ty, tk, seq, half) for dy, dk, ty, tk in row_peers]
        + [device(y, k, seq, 1 - half)]
        + [device(y, k, s, half) for s in rest]
    )

    def shuffle(source, target, n, index):
        copies = [pltpu.make_async_copy(source.at[y, n, k], target.at[n, :, lanes(k * feat, feat)], self_sems.at[index])]
        copies[0].start()
        for i, (dy, dk, ty, tk) in enumerate(row_peers):
            copies.append(
                remote(
                    source.at[ty, n, tk],
                    target.at[n, :, lanes(k * feat + 2 * dy * feat, feat)],
                    in_send.at[index, i],
                    in_recv.at[index, i],
                    device(ty, tk, seq, half),
                )
            )
        return copies

    count = str_ref.shape[1]
    x_copies = shuffle(tok_ref, x_own, 0, 0)
    small = []
    for j, (source, target) in enumerate(((norm_ref, norm_all), (ids_ref, ids_all))):
        slot = (lambda dy: (slice(None), lanes(k * feat + 2 * dy * feat, feat))) if j == 0 else (lambda dy: (2 * y + k,))
        copy = pltpu.make_async_copy(source, target.at[slot(0)], small_self.at[j])
        copy.start()
        small.append(copy)
        for i, (dy, dk, ty, tk) in enumerate(row_peers):
            small.append(
                remote(source, target.at[slot(dy)], small_sems.at[0, j, i], small_sems.at[1, j, i], device(ty, tk, seq, half))
            )
    copy = pltpu.make_async_copy(tab_ref, tab_all.at[0], small_self.at[2])
    copy.start()
    small.append(copy)
    for d in range(1, seqs):
        small.append(
            remote(tab_ref, tab_all.at[d], tab_sems.at[0, d - 1], tab_sems.at[1, d - 1], device(y, k, rest[d - 1], half))
        )
    for copy in x_copies:
        copy.wait()
    x_full[0, half, k] = x_own[0]
    x_spread = Spread(x_full, xh, xc, place, own)
    x_spread.start(0, 0, 0)
    y_copies = [shuffle(str_ref, y_own, n, 1 + n) for n in range(count)]
    y_spread = Spread(y_full, yh, yc, place, own)
    x_spread.forward(0, 0, 0)
    for n in range(count):
        for copy in y_copies[n]:
            copy.wait()
        y_full[n, half, k] = y_own[n]
        y_spread.start(n, n, 0)
    c_copies = [shuffle(cot_ref, c_own, n, 1 + count + n) for n in range(count)]
    for n in range(count):
        y_spread.forward(n, n, 0)
    x_spread.finish(0)
    for n in range(count):
        y_spread.finish(n)
        for copy in c_copies[n]:
            copy.wait()
    for copy in small:
        copy.wait()


def gather_inputs(seqs, tokens, streams, cotangent, norm, ids, table):
    count, own, feat = streams.shape[1], streams.shape[-2], streams.shape[-1]
    depth = 4 * feat
    dma = pltpu.SemaphoreType.DMA
    shape = jax.ShapeDtypeStruct
    outs = (
        shape((1, own, depth), BF),
        shape((1, 2, 2, own, depth), BF),
        shape((count, own, depth), BF),
        shape((count, 2, 2, own, depth), BF),
        shape((count, own, depth), BF),
        shape((norm.shape[0], depth), F32),
        shape((4,) + ids.shape, jnp.int32),
        shape((seqs,) + table.shape, F32),
    )
    moves = 1 + 2 * count
    return pl.pallas_call(
        functools.partial(inputs_kernel, seqs),
        out_shape=outs,
        in_specs=[pl.BlockSpec(memory_space=pltpu.VMEM)] * 6,
        out_specs=tuple(pl.BlockSpec(memory_space=pltpu.VMEM) for _ in outs),
        scratch_shapes=[
            dma((moves, 3)),
            dma((moves, 3)),
            dma((moves,)),
            dma((2, 1)),
            dma((2, 1, 2)),
            dma((2, count)),
            dma((2, count, 2)),
            dma((2, 2, 3)),
            dma((2, seqs - 1)),
            dma((3,)),
        ],
        compiler_params=pltpu.CompilerParams(collective_id=0, has_side_effects=True, vmem_limit_bytes=50 << 20),
        name="gather_inputs",
    )(tokens, streams, cotangent, norm, ids, table)


def outputs_kernel(seqs, count, part_x, part_y, d1, d3, small, tok_out, str_out, small_out, core_buf, half_send, half_buf, own, land_x, land_y, rc, rh, rs, small_buf, ss):
    place = spot()
    y, k, seq, half = place
    rows = part_x.shape[3]
    feat = part_x.shape[4] // 4
    bits = []
    while 1 << len(bits) < seqs:
        bits.append(1 << len(bits))
    flips = [device(y, k, seq + b - 2 * b * ((seq // b) % 2), half) for b in bits]
    partners = [device(y, 1 - k, seq, half), device(y, k, seq, 1 - half), device(1 - y, k, seq, half)] + flips
    greet(partners + [device(1 - y, 1 - k, seq, half)])
    small_out[...] = small[...]

    def add_small(stage):
        copy = remote(small_out, small_buf.at[stage], ss.at[0, stage], ss.at[1, stage], partners[stage])
        copy.wait()
        small_out[...] += small_buf[stage]

    class Both:
        def __getitem__(self, index):
            return part_x[(0,) + index[1:]] if index[0] == 0 else part_y[(index[0] - 1,) + index[1:]]

        @property
        def at(self):
            return View()

    class View:
        def __getitem__(self, index):
            return part_x.at[(0,) + index[1:]] if index[0] == 0 else part_y.at[(index[0] - 1,) + index[1:]]

    reduce = Reduce(Both(), core_buf, half_send, half_buf, rc, rh, place, rows)
    units = range(count + 1)
    for unit in units:
        reduce.start(unit, unit, 0, True)
        reduce.start(unit, unit, 0, False)
    for unit in units:
        reduce.pass_on(unit, unit, 0)
    for stage in range(len(partners)):
        add_small(stage)
    x_back = Return(own, land_x, rs, place, feat)
    y_back = Return(own, land_y, rs, place, feat)
    for unit in units:
        branch = reduce.result(unit, unit, 0)
        if unit == 0:
            x_back.start(unit, 0, (d1[0] + branch).astype(BF))
        else:
            y_back.start(unit, unit - 1, (d3[unit - 1] + branch).astype(BF))
    for unit in units:
        reduce.finish(unit)
    x_back.finish()
    tok_out[...] = land_x[:, 0].astype(F32)
    y_back.finish()
    str_out[...] = land_y[...].astype(F32)


def scatter_outputs(seqs, collective_id, part_x, part_y, d1, d3, small):
    count, _, _, own, depth = part_y.shape
    feat = depth // 4
    units = count + 1
    dma = pltpu.SemaphoreType.DMA
    shape = jax.ShapeDtypeStruct
    stages = 3 + (seqs - 1).bit_length()
    outs = (shape((2, 2, own, feat), F32), shape((2, count, 2, own, feat), F32), shape(small.shape, F32))
    return pl.pallas_call(
        functools.partial(outputs_kernel, seqs, count),
        out_shape=outs,
        in_specs=[pl.BlockSpec(memory_space=pltpu.VMEM)] * 5,
        out_specs=tuple(pl.BlockSpec(memory_space=pltpu.VMEM) for _ in outs),
        scratch_shapes=[
            pltpu.VMEM((units, 2, own, depth), BF),
            pltpu.VMEM((units, own, depth), BF),
            pltpu.VMEM((units, own, depth), BF),
            pltpu.VMEM((units, own, depth), BF),
            pltpu.VMEM((2, 1, 2, own, feat), BF),
            pltpu.VMEM((2, count, 2, own, feat), BF),
            dma((2, units, 2)),
            dma((2, units)),
            dma((2, units, 3)),
            pltpu.VMEM((stages,) + small.shape, F32),
            dma((2, stages)),
        ],
        compiler_params=pltpu.CompilerParams(collective_id=collective_id, has_side_effects=True, vmem_limit_bytes=50 << 20),
        name="scatter_outputs",
    )(part_x, part_y, d1, d3, small)


def send(value, pairs):
    return lax.ppermute(value, ("row", "col"), pairs)


def device_pairs(rows, cols):
    seqs = cols // 2
    place = lambda y, k, s, h: (2 * (y % (rows // 2)) + k % 2) * cols + 2 * (s % seqs) + h % 2
    spots = [(y, k, s, h) for y in range(rows // 2) for k in range(2) for s in range(seqs) for h in range(2)]
    move = lambda dy, dk, ds, dh: [(place(y, k, s, h), place(y + dy, k + dk, s + ds, h + dh)) for y, k, s, h in spots]
    return {
        "core": move(0, 1, 0, 0),
        "half": move(0, 0, 0, 1),
        "micro": move(1, 0, 0, 0),
        "seq": [move(0, 0, d, 0) for d in range(seqs)],
    }


def pick(array, index, axis):
    return lax.dynamic_index_in_dim(array, index, axis, keepdims=False)


def in_order(first, mine, other, axis, join=jnp.concatenate):
    return jnp.where(first, join([mine, other], axis=axis), join([other, mine], axis=axis))


def dot_f32(spec, left, right):
    return jnp.einsum(spec, left, right, preferred_element_type=F32)


def on_device(
    rows,
    cols,
    tokens,
    streams,
    cotangent,
    block_ids,
    bucket_ids,
    w_qkv,
    enc_table,
    w_out,
    attention_norm_gain,
    attn_bias,
    w_up,
    w_down,
    ffn_gain,
    ffn_bias,
    w_query,
    w_keyval,
    cross_table,
    w_cross_out,
    cross_gain,
    cross_bias,
):
    pairs = device_pairs(rows, cols)
    seqs = cols // 2
    row, col = lax.axis_index("row"), lax.axis_index("col")
    y, k, seq, half = row // 2, row % 2, col // 2, col % 2
    low_core, low_y = k == 0, y == 0
    stream_count = streams.shape[1]
    tok = tokens.shape[1]
    own = tok // 2
    feat = tokens.shape[2]
    length = block_ids.shape[2]
    head_dim = w_qkv.shape[2] // 2
    ff = w_up.shape[1] // 2
    table_heads, bucket_count = enc_table.shape

    norm_params = jnp.stack([attention_norm_gain, attn_bias, ffn_gain, ffn_bias, cross_gain, cross_bias] + [cross_bias] * 2)
    table_pack = jnp.zeros((8, 128), F32).at[0].set(jnp.stack([enc_table, cross_table]).reshape(-1))
    micro_count = tokens.shape[0]
    x_own, x_full, y_own, y_full, c_own, norm_params, all_ids, all_tables = gather_inputs(
        seqs,
        tokens.reshape(micro_count, 1, 2, own, feat),
        streams.reshape(micro_count, stream_count, 2, own, feat),
        cotangent.reshape(micro_count, stream_count, 2, own, feat),
        norm_params,
        block_ids.reshape(8, -1),
        table_pack,
    )
    x_full, y_full = x_full.reshape(length, D), y_full.reshape(stream_count * length, D)
    segment = pick(pick(all_ids.reshape(rows, micro_count, length), seq, 0), y, 0)
    segq = segment[None]
    segk = jnp.broadcast_to(segment[:, None], (length, 128))
    own_tables = pick(all_tables[:, 0].reshape(seqs, 2, table_heads, bucket_count), k, 2)
    slot_col = 2 * ((seq - jnp.arange(seqs)) % seqs) + half
    reversed_ids = jnp.concatenate([jnp.full((1,), -1, jnp.int32), bucket_ids[::-1]])
    onehot = bucket_onehot(reversed_ids, bucket_count)
    offsets = jnp.einsum("htb,bo->tho", own_tables, onehot, precision=highest)[:, :, None, :]

    def gather_weights(shards):
        base = in_order(low_core, pick(shards, k, 0), send(pick(shards, 1 - k, 0), pairs["core"]), 1)
        slots = jnp.stack([base] + [send(base, pairs["seq"][d]) for d in range(1, seqs)])
        return jnp.concatenate([slots, send(slots, pairs["micro"])], axis=2)

    def scatter_weights(grad):
        part = grad[:, :, : D // 2] + send(grad[:, :, D // 2 :].astype(BF), pairs["micro"]).astype(F32)
        low = part.astype(BF)
        total = part[0]
        for d in range(1, seqs):
            total = total + send(low[d], pairs["seq"][seqs - d]).astype(F32)
        blocks = total.reshape(-1, 2, feat)
        other = send(pick(blocks, 1 - k, 1), pairs["core"])
        return in_order(low_core, pick(blocks, k, 1), other, 0, jnp.stack)

    def columns(weight, parts):
        return weight.reshape(feat, parts, 2, -1).transpose(2, 1, 3, 0).reshape(2, -1, feat)

    def columns_back(array, parts):
        return array.reshape(2, parts, -1, feat).transpose(3, 1, 0, 2).reshape(feat, parts, -1)

    halves = lambda weight: weight.reshape(2, -1, feat)
    hd3, hd2 = 3 * head_dim, 2 * head_dim
    first = gather_weights(jnp.concatenate([columns(w_qkv, 3), halves(w_out)], axis=1))
    up = gather_weights(columns(w_up, 1))
    down = gather_weights(halves(w_down))
    last = gather_weights(jnp.concatenate([columns(w_keyval, 2), columns(w_query, 1), halves(w_cross_out)], axis=1))
    m_qkv, m_out = first[:, :hd3], first[:, hd3:].reshape(-1, D)
    m_kv, m_q, m_co = last[:, :hd2], last[:, hd2:hd3], last[:, hd3:].reshape(-1, D)
    up, down = up.reshape(-1, D), down.reshape(-1, D)
    blocked = lambda product: product.astype(BF).reshape(-1, 2, 2, own, D)

    qkv = dot_f32("snr,tr->snt", m_qkv, x_full).astype(BF)
    mix, lse, tiles = attention(offsets[0], segq, segk, qkv, qkv, qkv, (0, 1, 2), 1)
    mix_flat = mix.reshape(-1, length)
    hidden_full, hidden, normed1, inv1 = exchange(
        "forward", 1, blocked(dot_f32("et,er->tr", mix_flat, m_out)), x_own, norm_params[0:2]
    )
    hidden_full = hidden_full.reshape(length, D)
    pre = dot_f32("fr,tr->ft", up, hidden_full)
    act, gelu_pull = jax.vjp(gelu_exact, pre)
    act = act.astype(BF)
    enc_full, _, normed2, inv2 = exchange(
        "forward", 2, blocked(dot_f32("ft,fr->tr", act, down)), hidden, norm_params[2:4]
    )
    enc_full = enc_full.reshape(length, D)
    kv = dot_f32("snr,tr->snt", m_kv, enc_full).astype(BF)
    query = dot_f32("snr,tr->snt", m_q, y_full).astype(BF)
    cmix, clse, ctiles = attention(offsets[1], segq, segk, query, kv, kv, (0, 0, 1), stream_count)
    cmix_flat = cmix.reshape(-1, stream_count * length)
    d3_full, output, d3, sums3 = exchange(
        "turn", 3, blocked(dot_f32("et,er->tr", cmix_flat, m_co)), y_own, norm_params[4:6], cot=c_own
    )
    d3_full = d3_full.reshape(stream_count * length, D)

    dcmix = dot_f32("er,tr->et", m_co, d3_full).astype(BF).reshape(cmix.shape)
    g_co = dot_f32("et,tr->er", cmix_flat, d3_full)
    dquery, dkc, dvc, doff_cross = attention_back(
        ctiles, segq, segk, query, kv, kv, (0, 0, 1), clse, dcmix, stream_count
    )
    dkv = jnp.concatenate([dkc, dvc], axis=1)
    d2_full, d2, sums2 = exchange(
        "backward", 4, blocked(dot_f32("snt,snr->tr", dkv, m_kv)), norm_params[2:4][None], norm_params[2:4], normed=normed2, inv=inv2
    )
    d2_full = d2_full.reshape(length, D)
    g_q = dot_f32("snt,tr->snr", dquery, y_full)
    g_kv = dot_f32("snt,tr->snr", dkv, enc_full)
    g_last = scatter_weights(jnp.concatenate([g_kv, g_q, g_co.reshape(seqs, head_dim, D)], axis=1))
    part_y = blocked(dot_f32("snt,snr->tr", dquery, m_q))
    dact = dot_f32("fr,tr->ft", down, d2_full)
    dpre = gelu_pull(dact)[0].astype(BF)
    g_down = scatter_weights(dot_f32("ft,tr->fr", act, d2_full).reshape(seqs, ff, D))
    d1_full, d1, sums1 = exchange(
        "backward", 5, blocked(dot_f32("ft,fr->tr", dpre, up)), d2, norm_params[0:2], normed=normed1, inv=inv1
    )
    d1_full = d1_full.reshape(length, D)
    g_up = scatter_weights(dot_f32("ft,tr->fr", dpre, hidden_full).reshape(seqs, ff, D))
    dmix = dot_f32("er,tr->et", m_out, d1_full).astype(BF).reshape(mix.shape)
    g_out = dot_f32("et,tr->er", mix_flat, d1_full)
    dq, dk, dv, doff_enc = attention_back(tiles, segq, segk, qkv, qkv, qkv, (0, 1, 2), lse, dmix, 1)
    dqkv = jnp.concatenate([dq, dk, dv], axis=1)
    g_qkv = dot_f32("snt,tr->snr", dqkv, x_full)
    g_first = scatter_weights(jnp.concatenate([g_qkv, g_out.reshape(seqs, head_dim, D)], axis=1))
    part_x = blocked(dot_f32("snt,snr->tr", dqkv, m_qkv))

    norm_grads = jnp.concatenate([sums1[:2], sums2[:2], sums3[:2]])
    norm_grads = jnp.where(low_y, norm_grads, jnp.roll(norm_grads, D // 2, axis=1))
    table_grads = jnp.einsum(
        "tho,bo->thb", jnp.stack([doff_enc[:, 0], doff_cross[:, 0]]), onehot, precision=highest
    )
    heads = 2 * slot_col + k
    spread = (heads[:, None] == jnp.arange(table_heads * cols)[None, :]).astype(F32)
    table_grads = jnp.einsum("thb,hg->tgb", table_grads, spread, precision=highest)
    small = jnp.concatenate([norm_grads.reshape(-1, 128), table_grads.reshape(-1, 128)])
    grad_tokens, grad_streams, small = scatter_outputs(seqs, 6, part_x, part_y, d1, d3, small)
    output, grad_streams = output.reshape(streams.shape), grad_streams.reshape(streams.shape)
    grad_tokens = grad_tokens.reshape(tokens.shape)
    count = norm_grads.size // 128
    norm_sums = lax.dynamic_slice_in_dim(small[:count].reshape(6, D), row * feat, feat, axis=1)
    table_sums = small[count:].reshape(2, table_heads * cols, bucket_count)
    table_sums = lax.dynamic_slice_in_dim(table_sums, col * table_heads, table_heads, axis=1)
    return (
        output,
        grad_tokens,
        grad_streams,
        columns_back(g_first[:, :hd3], 3),
        table_sums[0],
        g_first[:, hd3:].reshape(w_out.shape),
        norm_sums[0],
        norm_sums[1],
        columns_back(g_up, 1).reshape(w_up.shape),
        g_down.reshape(w_down.shape),
        norm_sums[2],
        norm_sums[3],
        columns_back(g_last[:, hd2:hd3], 1).reshape(w_query.shape),
        columns_back(g_last[:, :hd2], 2),
        table_sums[1],
        g_last[:, hd3:].reshape(w_cross_out.shape),
        norm_sums[4],
        norm_sums[5],
    )


def solution(mesh):
    whole_row, half_col = mesh.shape["row"], mesh.shape["col"]
    weights = (P("row", None, "col"), P("col", None), P("col", "row"), P("row"), P("row"), P("row", "col"), P("col", "row"), P("row"), P("row"), P("row", "col"), P("row", None, "col"), P("col", None), P("col", "row"), P("row"), P("row"))

    def run(tokens, *rest):
        micro_count = tokens.shape[0]
        if whole_row == 4 and micro_count == 2 and half_col % 2 == 0:
            device_fn = functools.partial(on_device, whole_row, half_col)
        else:
            device_fn = on_device_general
        return jax.shard_map(
            device_fn,
            mesh=mesh,
            in_specs=(P(None, "col", "row"), P(None, None, "col", "row"), P(None, None, "col", "row"), P(None, "row", None), P()) + weights,
            out_specs=(P(None, None, "col", "row"), P(None, "col", "row"), P(None, None, "col", "row")) + weights,
            check_vma=False,
        )(tokens, *rest)

    return run
```

```python
import functools
import types
import jax
import jax.numpy as jnp
from jax import lax
from jax.experimental import pallas as pl
from jax.experimental.pallas import tpu as pltpu
from jax.sharding import PartitionSpec as P

D = 1024
F32 = jnp.float32
BF = jnp.bfloat16
ROW, COL = "row", "col"


epsilon = 1e-05
neg_fill = -1e30
highest = lax.Precision.HIGHEST


def gather_cols(local_rows):
    return lax.all_gather(local_rows, COL, axis=1, tiled=True)


def gather_rows(local_rows):
    return lax.all_gather(local_rows, ROW, axis=1, tiled=True)


def product(matmul_operand, weight_matrix):
    return jnp.einsum(
        "ray,yw->raw", matmul_operand, weight_matrix, preferred_element_type=jnp.float32
    )


def rows_product(operand_full, matrix):
    return lax.psum_scatter(product(operand_full, matrix), ROW, scatter_dimension=1, tiled=True)


def cols_product(operand_full, matrix):
    return lax.psum_scatter(product(operand_full, matrix), COL, scatter_dimension=1, tiled=True)


def weight_grad(matmul_operand, upstream_gradient):
    return jnp.einsum(
        "bpt,bpr->tr", matmul_operand, upstream_gradient, preferred_element_type=jnp.float32
    )


def gelu_exact(argument):
    return jax.nn.gelu(argument, approximate=False)


def norm_forward(residual, gain_vec, bias_vec):
    local_sum = jnp.sum(residual, axis=-1)
    average = lax.psum(local_sum, ROW) / D
    centered = residual - average[..., None]
    spread = lax.psum(jnp.sum(centered * centered, axis=-1), ROW) / D
    inv_std = lax.rsqrt(spread + epsilon)
    normed = centered * inv_std[..., None]
    return (normed * gain_vec + bias_vec, normed, inv_std)


def norm_back(out_grad, normed, inv_std, gain_vec):
    scaled_grad = out_grad * gain_vec
    first_moment, second_moment = lax.psum(
        (jnp.sum(scaled_grad, axis=-1), jnp.sum(scaled_grad * normed, axis=-1)), ROW
    )
    resid_grad = inv_std[..., None] * (
        scaled_grad - first_moment[..., None] / D - normed * (second_moment[..., None] / D)
    )
    return (resid_grad, jnp.sum(out_grad * normed, axis=(0, 1)), jnp.sum(out_grad, axis=(0, 1)))


def bucket_onehot(bucket_ids, bucket_count):
    return (bucket_ids[None, :] == jnp.arange(bucket_count, dtype=jnp.int32)[:, None]).astype(
        jnp.float32
    )


def block_logits(query_blk, key_rows, offsets, segment, first_row):
    row_count = query_blk.shape[2]
    length = key_rows.shape[1]
    score_scale = query_blk.shape[-1] ** (-0.5)
    raw_scores = jnp.einsum(
        "snqhd,nkhd->snhqk", query_blk, key_rows, preferred_element_type=jnp.float32
    )
    places = jnp.arange(length, dtype=jnp.int32)
    query_pos = first_row + jnp.arange(row_count, dtype=jnp.int32)
    offset_index = places[None, :] - query_pos[:, None] + (length - 1)
    pos_bias = jnp.take(offsets, offset_index, axis=1)
    visible = segment[:, first_row : first_row + row_count, None] >= segment[:, None, :]
    return jnp.where(
        visible[None, :, None], raw_scores * score_scale + pos_bias[None, None], neg_fill
    )


def attend(queries, key_rows, value_rows, segment, offsets):
    score_logits = block_logits(queries, key_rows, offsets, segment, 0)
    row_max = jnp.max(score_logits, axis=-1, keepdims=True)
    log_total = row_max + jnp.log(jnp.sum(jnp.exp(score_logits - row_max), axis=-1, keepdims=True))
    weights = jnp.exp(score_logits - log_total).astype(jnp.bfloat16)
    mixed_parts = jnp.einsum(
        "snhqk,nkhd->snqhd", weights, value_rows, preferred_element_type=jnp.float32
    )
    lse_parts = log_total[..., 0]
    return (mixed_parts, lse_parts)


def diagonal_sums(summand):
    head_count, row_count, length = summand.shape
    flipped = summand[:, ::-1, :]
    padded = jnp.concatenate(
        [flipped, jnp.zeros((head_count, row_count, row_count), summand.dtype)], axis=2
    )
    flattened = padded.reshape(head_count, row_count * (length + row_count))[
        :, : row_count * (length + row_count - 1)
    ]
    return jnp.sum(flattened.reshape(head_count, row_count, length + row_count - 1), axis=1)


def attend_back(queries, key_rows, value_rows, segment, offsets, onehot, log_totals, mix_grad):
    length = key_rows.shape[1]
    block_rows = min(512, length)
    score_scale = queries.shape[-1] ** (-0.5)
    offset_grad = jnp.zeros(offsets.shape, jnp.float32)
    score_logits = block_logits(queries, key_rows, offsets, segment, 0)
    probability = jnp.exp(score_logits - log_totals[:, :, :, 0:block_rows, None])
    prob_grad = jnp.einsum(
        "snqhd,nkhd->snhqk", mix_grad, value_rows, preferred_element_type=jnp.float32
    )
    logit_grad = probability * (
        prob_grad - jnp.sum(probability * prob_grad, axis=-1, keepdims=True)
    )
    scaled = (logit_grad * score_scale).astype(jnp.bfloat16)
    query_parts = jnp.einsum(
        "snhqk,nkhd->snqhd", scaled, key_rows, preferred_element_type=jnp.float32
    )
    key_grad = jnp.einsum("snhqk,snqhd->nkhd", scaled, queries, preferred_element_type=jnp.float32)
    value_grad = jnp.einsum(
        "snhqk,snqhd->nkhd",
        probability.astype(jnp.bfloat16),
        mix_grad,
        preferred_element_type=jnp.float32,
    )
    low_end = length - block_rows
    offset_grad = offset_grad.at[:, low_end : low_end + length + block_rows - 1].add(
        diagonal_sums(jnp.sum(logit_grad, axis=(0, 1)))
    )
    table_grad = jnp.dot(offset_grad, onehot.T, precision=highest)
    return (query_parts, key_grad, value_grad, table_grad)


def on_device_general(
    tokens,
    streams,
    cotangent,
    block_ids,
    bucket_ids,
    w_qkv,
    enc_table,
    w_out,
    attention_norm_gain,
    attn_bias,
    w_up,
    w_down,
    ffn_gain,
    ffn_bias,
    w_query,
    w_keyval,
    cross_table,
    w_cross_out,
    cross_gain,
    cross_bias,
):
    micro_count = tokens.shape[0]
    stream_count = streams.shape[1]
    seq_rows = block_ids.shape[1]
    length = block_ids.shape[2]
    head_count = enc_table.shape[0]
    bucket_count = enc_table.shape[1]
    row_width = w_qkv.shape[0]
    col_width = w_qkv.shape[2]
    head_dim = col_width // head_count
    row_tokens = seq_rows * length
    qkv_matrix = w_qkv.reshape(row_width, 3 * col_width)
    keyval_matrix = w_keyval.reshape(row_width, 2 * col_width)
    onehot = bucket_onehot(bucket_ids, bucket_count)
    enc_offsets = jnp.dot(enc_table, onehot, precision=highest)
    cross_offsets = jnp.dot(cross_table, onehot, precision=highest)
    qkv_acc = jnp.zeros((row_width, 3 * col_width), jnp.float32)
    out_acc = jnp.zeros(w_out.shape, jnp.float32)
    up_acc = jnp.zeros(w_up.shape, jnp.float32)
    down_acc = jnp.zeros(w_down.shape, jnp.float32)
    query_acc = jnp.zeros(w_query.shape, jnp.float32)
    keyval_acc = jnp.zeros((row_width, 2 * col_width), jnp.float32)
    cross_out_acc = jnp.zeros(w_cross_out.shape, jnp.float32)
    enc_table_acc = jnp.zeros(enc_table.shape, jnp.float32)
    cross_table_acc = jnp.zeros(cross_table.shape, jnp.float32)
    norm_accs = [jnp.zeros((row_width,), jnp.float32) for place_holder in range(6)]
    outputs = []
    token_grads = []
    stream_grads = []
    for micro in range(micro_count):
        segment = block_ids[micro]
        x_in = tokens[micro][None]
        y_in = streams[micro]
        x_full = gather_cols(x_in)
        qkv = (
            rows_product(x_full, qkv_matrix)
            .astype(jnp.bfloat16)
            .reshape(seq_rows, length, 3, head_count, head_dim)
        )
        enc_query = qkv[:, :, 0][None]
        enc_key = qkv[:, :, 1]
        encoder_value_rows = qkv[:, :, 2]
        enc_mixed, enc_lse = attend(enc_query, enc_key, encoder_value_rows, segment, enc_offsets)
        enc_mix = enc_mixed.reshape(1, row_tokens, col_width).astype(jnp.bfloat16)
        mix_full = gather_rows(enc_mix)
        attn_branch = cols_product(mix_full, w_out)
        hidden, normed_one, inv_one = norm_forward(
            x_in.astype(jnp.float32) + attn_branch, attention_norm_gain, attn_bias
        )
        hidden_low = hidden.astype(jnp.bfloat16)
        hidden_full = gather_cols(hidden_low)
        pre_act = rows_product(hidden_full, w_up)
        act_value, gelu_pull = jax.vjp(gelu_exact, pre_act)
        act_low = act_value.astype(jnp.bfloat16)
        act_full = gather_rows(act_low)
        ffn_branch = cols_product(act_full, w_down)
        encoded, normed_two, inv_two = norm_forward(hidden + ffn_branch, ffn_gain, ffn_bias)
        encoded_low = encoded.astype(jnp.bfloat16)
        enc_full = gather_cols(encoded_low)
        keyval = (
            rows_product(enc_full, keyval_matrix)
            .astype(jnp.bfloat16)
            .reshape(seq_rows, length, 2, head_count, head_dim)
        )
        cross_key = keyval[:, :, 0]
        cross_value = keyval[:, :, 1]
        stream_full = gather_cols(y_in)
        cross_query = (
            rows_product(stream_full, w_query)
            .astype(jnp.bfloat16)
            .reshape(stream_count, seq_rows, length, head_count, head_dim)
        )
        cross_mixed, cross_lse = attend(cross_query, cross_key, cross_value, segment, cross_offsets)
        cross_mix = cross_mixed.reshape(stream_count, row_tokens, col_width).astype(jnp.bfloat16)
        cross_full = gather_rows(cross_mix)
        cross_branch = cols_product(cross_full, w_cross_out)
        result, normed_three, inv_three = norm_forward(
            y_in.astype(jnp.float32) + cross_branch, cross_gain, cross_bias
        )
        outputs.append(result)
        grad_three, gain_part, bias_part = norm_back(
            cotangent[micro].astype(jnp.float32), normed_three, inv_three, cross_gain
        )
        norm_accs[4] = norm_accs[4] + gain_part
        norm_accs[5] = norm_accs[5] + bias_part
        branch_full = gather_cols(grad_three.astype(jnp.bfloat16))
        cross_out_acc = cross_out_acc + weight_grad(cross_full, branch_full)
        cross_mix_grad = (
            rows_product(branch_full, w_cross_out.T)
            .astype(jnp.bfloat16)
            .reshape(stream_count, seq_rows, length, head_count, head_dim)
        )
        query_grad, key_grad, value_grad, table_grad = attend_back(
            cross_query,
            cross_key,
            cross_value,
            segment,
            cross_offsets,
            onehot,
            cross_lse,
            cross_mix_grad,
        )
        cross_table_acc = cross_table_acc + table_grad
        query_low = query_grad.reshape(stream_count, row_tokens, col_width).astype(jnp.bfloat16)
        keyval_low = (
            jnp.stack(
                [
                    key_grad.reshape(row_tokens, col_width),
                    value_grad.reshape(row_tokens, col_width),
                ],
                axis=1,
            )
            .reshape(1, row_tokens, 2 * col_width)
            .astype(jnp.bfloat16)
        )
        query_full = gather_rows(query_low)
        query_acc = query_acc + weight_grad(stream_full, query_full)
        stream_grads.append(grad_three + cols_product(query_full, w_query.T))
        keyval_full = gather_rows(keyval_low)
        keyval_acc = keyval_acc + weight_grad(enc_full, keyval_full)
        encoded_grad = cols_product(keyval_full, keyval_matrix.T)
        grad_two, gain_part, bias_part = norm_back(encoded_grad, normed_two, inv_two, ffn_gain)
        norm_accs[2] = norm_accs[2] + gain_part
        norm_accs[3] = norm_accs[3] + bias_part
        feedforward_full_output = gather_cols(grad_two.astype(jnp.bfloat16))
        down_acc = down_acc + weight_grad(act_full, feedforward_full_output)
        act_grad = rows_product(feedforward_full_output, w_down.T)
        pre_low = gelu_pull(act_grad)[0].astype(jnp.bfloat16)
        pre_full = gather_rows(pre_low)
        up_acc = up_acc + weight_grad(hidden_full, pre_full)
        hidden_grad = grad_two + cols_product(pre_full, w_up.T)
        grad_one, gain_part, bias_part = norm_back(
            hidden_grad, normed_one, inv_one, attention_norm_gain
        )
        norm_accs[0] = norm_accs[0] + gain_part
        norm_accs[1] = norm_accs[1] + bias_part
        attn_full = gather_cols(grad_one.astype(jnp.bfloat16))
        out_acc = out_acc + weight_grad(mix_full, attn_full)
        enc_mix_grad = (
            rows_product(attn_full, w_out.T)
            .astype(jnp.bfloat16)
            .reshape(1, seq_rows, length, head_count, head_dim)
        )
        enc_qgrad, enc_kgrad, enc_vgrad, table_grad = attend_back(
            enc_query,
            enc_key,
            encoder_value_rows,
            segment,
            enc_offsets,
            onehot,
            enc_lse,
            enc_mix_grad,
        )
        enc_table_acc = enc_table_acc + table_grad
        qkv_low = (
            jnp.stack(
                [
                    enc_qgrad.reshape(row_tokens, col_width),
                    enc_kgrad.reshape(row_tokens, col_width),
                    enc_vgrad.reshape(row_tokens, col_width),
                ],
                axis=1,
            )
            .reshape(1, row_tokens, 3 * col_width)
            .astype(jnp.bfloat16)
        )
        qkv_full = gather_rows(qkv_low)
        qkv_acc = qkv_acc + weight_grad(x_full, qkv_full)
        token_grads.append((grad_one + cols_product(qkv_full, qkv_matrix.T))[0])
    norm_stack = jnp.stack(norm_accs)
    table_stack = jnp.stack([enc_table_acc, cross_table_acc])
    norm_sums = lax.psum(norm_stack, COL)
    table_sums = lax.psum(table_stack, ROW)
    return (
        jnp.stack(outputs),
        jnp.stack(token_grads),
        jnp.stack(stream_grads),
        qkv_acc.reshape(row_width, 3, col_width),
        table_sums[0],
        out_acc,
        norm_sums[0],
        norm_sums[1],
        up_acc,
        down_acc,
        norm_sums[2],
        norm_sums[3],
        query_acc,
        keyval_acc.reshape(row_width, 2, col_width),
        table_sums[1],
        cross_out_acc,
        norm_sums[4],
        norm_sums[5],
    )


def mm(a,b):
    return jnp.dot(a,b,preferred_element_type=F32)
def mm_nt(a,b):
    return lax.dot_general(a,b,(((1,),(1,)),((),())),preferred_element_type=F32)

def fwd_kernel(streams, length, width, off_ref, segq_ref, segk_ref, q_ref, k_ref, v_ref, mix_ref, lse_ref, t_ref):
    chunks = 2*length//width - 1
    top = length - width
    for c in range(chunks):
        lo = (chunks-1-c)*width
        w = off_ref[0, :, lo:lo+2*width]
        rolled = pltpu.roll(jnp.broadcast_to(w,(width,2*width)), 0, 1, stride=1, stride_axis=0)
        t_ref[0, c*width:(c+1)*width, :] = rolled[:, width:]
    keys = k_ref[0].T
    values = v_ref[0]
    scale = k_ref.shape[1]**-0.5
    panels = length//width
    for p in range(panels):
        bias = t_ref[0, top-p*width:top-p*width+length, :]
        shown = segk_ref[...] <= segq_ref[:, p*width:(p+1)*width]
        for s in range(streams):
            lo = s*length+p*width
            logits = mm(keys, q_ref[0, :, lo:lo+width])*scale + bias
            logits = jnp.where(shown, logits, neg_fill)
            m = jnp.max(logits, axis=0, keepdims=True)
            e = jnp.exp(logits-m)
            total = jnp.sum(e, axis=0, keepdims=True)
            lse_ref[0, :, lo:lo+width] = m + jnp.log(total)
            prob = (e*(1.0/total)).astype(BF)
            mix_ref[0, :, lo:lo+width] = mm(values, prob).astype(BF)

def bwd_kernel(streams, length, width, t_ref, segq_ref, segk_ref, q_ref, k_ref, v_ref, lse_ref, dmix_ref, dq_ref, dk_ref, dv_ref, doff_ref, g_scr, dk_scr, dv_scr):
    chunks = 2*length//width - 1
    top = length - width
    keysT = k_ref[0]
    keys = keysT.T
    values = v_ref[0].T
    scale = k_ref.shape[1]**-0.5
    panels = length//width
    g_scr[...] = jnp.zeros_like(g_scr)
    dk_scr[...] = jnp.zeros_like(dk_scr)
    dv_scr[...] = jnp.zeros_like(dv_scr)
    for p in range(panels):
        rows = slice(top-p*width, top-p*width+length)
        shown = segk_ref[...] <= segq_ref[:, p*width:(p+1)*width]
        for s in range(streams):
            lo = s*length+p*width
            qs = q_ref[0, :, lo:lo+width]
            dm = dmix_ref[0, :, lo:lo+width]
            logits = mm(keys, qs)*scale + t_ref[0, rows, :]
            prob = jnp.where(shown, jnp.exp(logits - lse_ref[0, :, lo:lo+width]), 0.0)
            dprob = mm(values, dm)
            delta = jnp.sum(prob*dprob, axis=0, keepdims=True)
            dlog = prob*(dprob-delta)
            g_scr[rows, :] += dlog
            g = (dlog*scale).astype(BF)
            dq_ref[0, :, lo:lo+width] = mm(keysT, g).astype(BF)
            dk_scr[...] += mm_nt(qs, g)
            dv_scr[...] += mm_nt(dm, prob.astype(BF))
    dk_ref[0] = dk_scr[...].astype(BF)
    dv_ref[0] = dv_scr[...].astype(BF)
    doff_ref[...] = jnp.zeros_like(doff_ref)
    sub = lax.broadcasted_iota(jnp.int32, (8, 2*width), 0)
    for c in range(chunks):
        acc = jnp.zeros((8, 2*width), F32)
        for i in range(width//8):
            piece = g_scr[c*width+8*i:c*width+8*i+8, :]
            padded = jnp.concatenate([jnp.zeros((8,width),F32), piece], axis=1)
            if i: padded = pltpu.roll(padded, 2*width-8*i, 1)
            acc = acc + padded
        for b in (1,2,4):
            acc = jnp.where((sub//b)%2==1, pltpu.roll(acc, 2*width-b, 1), acc)
        lo = (chunks-1-c)*width
        doff_ref[0, :, lo:lo+2*width] += jnp.sum(acc, axis=0, keepdims=True)

def attention(off_rev, segq, segk, q, k, v, parts, streams):
    heads, length = k.shape[0], k.shape[2]
    hd = 64; width=128
    blk = lambda part,n: pl.BlockSpec((1,hd,n), lambda h: (h,part,0))
    return pl.pallas_call(
        functools.partial(fwd_kernel, streams, length, width),
        grid=(heads,),
        in_specs=[pl.BlockSpec((1,1,2*length),lambda h:(h,0,0)), pl.BlockSpec((1,length),lambda h:(0,0)), pl.BlockSpec((length,width),lambda h:(0,0)),
                  blk(parts[0],streams*length), blk(parts[1],length), blk(parts[2],length)],
        out_specs=[blk(0,streams*length), pl.BlockSpec((1,1,streams*length),lambda h:(h,0,0)), pl.BlockSpec((1,2*length-width,width),lambda h:(h,0,0))],
        out_shape=[jax.ShapeDtypeStruct((heads,hd,streams*length),BF), jax.ShapeDtypeStruct((heads,1,streams*length),F32), jax.ShapeDtypeStruct((heads,2*length-width,width),F32)],
        compiler_params=pltpu.CompilerParams(vmem_limit_bytes=48<<20),
        name="attend",
    )(off_rev, segq, segk, q, k, v)

def attention_back(tiles, segq, segk, q, k, v, parts, lse, dmix, streams):
    heads, length = k.shape[0], k.shape[2]
    hd = 64; width=128
    blk = lambda part,n: pl.BlockSpec((1,hd,n), lambda h: (h,part,0))
    return pl.pallas_call(
        functools.partial(bwd_kernel, streams, length, width),
        grid=(heads,),
        in_specs=[pl.BlockSpec((1,2*length-width,width),lambda h:(h,0,0)), pl.BlockSpec((1,length),lambda h:(0,0)), pl.BlockSpec((length,width),lambda h:(0,0)),
                  blk(parts[0],streams*length), blk(parts[1],length), blk(parts[2],length),
                  pl.BlockSpec((1,1,streams*length),lambda h:(h,0,0)), blk(0,streams*length)],
        out_specs=[blk(0,streams*length), blk(0,length), blk(0,length), pl.BlockSpec((1,1,2*length),lambda h:(h,0,0))],
        out_shape=[jax.ShapeDtypeStruct((heads,hd,streams*length),BF), jax.ShapeDtypeStruct((heads,hd,length),BF), jax.ShapeDtypeStruct((heads,hd,length),BF), jax.ShapeDtypeStruct((heads,1,2*length),F32)],
        scratch_shapes=[pltpu.VMEM((2*length-width,width),F32), pltpu.VMEM((hd,length),F32), pltpu.VMEM((hd,length),F32)],
        compiler_params=pltpu.CompilerParams(vmem_limit_bytes=48<<20),
        name="attend_back",
    )(tiles, segq, segk, q, k, v, lse, dmix)


MESH = pl.DeviceIdType.MESH
FORWARD, TURN, BACKWARD = range(3)
ACROSS, THROUGH, ALONG, SUM_ACROSS, SUM_ALONG = range(5)


def spot():
    row, col = lax.axis_index(ROW), lax.axis_index(COL)
    return row // 2, row % 2, col // 2, col % 2


def device(y, k, seq, half):
    return (2 * y + k, 2 * seq + half)


def greet(devices):
    barrier = pltpu.get_barrier_semaphore()
    for target in devices:
        pl.semaphore_signal(barrier, inc=1, device_id=target, device_id_type=MESH)
    pl.semaphore_wait(barrier, len(devices))


def remote(source, target, send_sem, recv_sem, device_id):
    copy = pltpu.make_async_remote_copy(
        src_ref=source, dst_ref=target, send_sem=send_sem, recv_sem=recv_sem, device_id=device_id, device_id_type=MESH
    )
    copy.start()
    return copy


def lanes(start, size):
    return pl.ds(pl.multiple_of(start, size), size)


def rows_of(place):
    y, k, seq, half = place
    return [(dy, dk, (1 - y if dy else y), (1 - k if dk else k)) for dy, dk in ((0, 1), (1, 0), (1, 1))]


class Spread:
    def __init__(self, full_ref, half_sems, core_sems, place, rows):
        self.full, self.place, self.rows = full_ref, place, rows
        self.half_sems, self.core_sems = half_sems, core_sems
        self.first, self.second = {}, {}

    def block(self, n, piece, half, k):
        return self.full.at[n, half, k, pl.ds(piece * self.rows, self.rows)]

    def start(self, unit, n, piece):
        y, k, seq, half = self.place
        mine = self.block(n, piece, half, k)
        hs, cs = self.half_sems, self.core_sems
        self.first[unit] = (
            remote(mine, mine, hs.at[0, unit], hs.at[1, unit], device(y, k, seq, 1 - half)),
            remote(mine, mine, cs.at[0, unit, 0], cs.at[1, unit, 0], device(y, 1 - k, seq, half)),
        )

    def forward(self, unit, n, piece):
        y, k, seq, half = self.place
        self.first[unit][0].wait_recv()
        theirs = self.block(n, piece, 1 - half, k)
        cs = self.core_sems
        self.second[unit] = remote(theirs, theirs, cs.at[0, unit, 1], cs.at[1, unit, 1], device(y, 1 - k, seq, half))

    def finish(self, unit):
        self.first[unit][0].wait_send()
        self.first[unit][1].wait()
        self.second[unit].wait()


class Reduce:
    def __init__(self, partial_ref, core_buf, half_send, half_buf, core_sems, half_sems, place, rows):
        self.partial, self.core_buf, self.half_send, self.half_buf = partial_ref, core_buf, half_send, half_buf
        self.core_sems, self.half_sems, self.place, self.rows = core_sems, half_sems, place, rows
        self.first, self.second = {}, {}

    def part(self, n, piece, half, k):
        return (n, half, k, pl.ds(piece * self.rows, self.rows))

    def start(self, unit, n, piece, away):
        y, k, seq, half = self.place
        side = 1 - half if away else half
        cs = self.core_sems
        lane = 0 if away else 1
        self.first[unit, lane] = remote(
            self.partial.at[self.part(n, piece, side, 1 - k)],
            self.core_buf.at[unit, lane],
            cs.at[0, unit, lane],
            cs.at[1, unit, lane],
            device(y, 1 - k, seq, half),
        )

    def pass_on(self, unit, n, piece):
        y, k, seq, half = self.place
        self.first[unit, 0].wait_recv()
        away = self.partial[self.part(n, piece, 1 - half, k)].astype(F32) + self.core_buf[unit, 0].astype(F32)
        self.half_send[unit] = away.astype(BF)
        hs = self.half_sems
        self.second[unit] = remote(
            self.half_send.at[unit], self.half_buf.at[unit], hs.at[0, unit], hs.at[1, unit], device(y, k, seq, 1 - half)
        )

    def result(self, unit, n, piece):
        y, k, seq, half = self.place
        self.first[unit, 1].wait_recv()
        mine = self.partial[self.part(n, piece, half, k)].astype(F32) + self.core_buf[unit, 1].astype(F32)
        self.second[unit].wait_recv()
        return mine + self.half_buf[unit].astype(F32)

    def finish(self, unit):
        self.first[unit, 0].wait_send()
        self.first[unit, 1].wait_send()
        self.second[unit].wait_send()


class Return:
    def __init__(self, own_ref, landing, sems, place, feat):
        self.own, self.landing, self.sems, self.place, self.feat = own_ref, landing, sems, place, feat
        self.copies = []

    def start(self, unit, n, value):
        y, k, seq, half = self.place
        feat = self.feat
        self.own[unit] = value
        self.landing[y, n, k] = jnp.where(k == 0, value[:, :feat], value[:, feat : 2 * feat])
        for i, (dy, dk, ty, tk) in enumerate(rows_of(self.place)):
            self.copies.append(
                remote(
                    self.own.at[unit, :, lanes(tk * feat + 2 * dy * feat, feat)],
                    self.landing.at[y, n, k],
                    self.sems.at[0, unit, i],
                    self.sems.at[1, unit, i],
                    device(ty, tk, seq, half),
                )
            )

    def finish(self):
        for copy in self.copies:
            copy.wait()


class Freight:
    def __init__(self, full_ref, z_sems, y_sems, place, seqs):
        self.full, self.place, self.seqs = full_ref, place, seqs
        self.z_sems, self.y_sems = z_sems, y_sems
        self.wide = full_ref.shape[2] // 2
        self.z, self.y = {}, {}
        self.turn = seqs // 2

    def along(self, d):
        y, k, seq, half = self.place
        up = d <= self.turn
        source = d - 1 if up else (d + 1) % self.seqs
        if source:
            self.z[source].wait_recv()
        target = lax.rem(seq + (1 if up else self.seqs - 1), self.seqs)
        self.z[d] = remote(
            self.full.at[source, :, : self.wide],
            self.full.at[d, :, : self.wide],
            self.z_sems.at[0, d - 1],
            self.z_sems.at[1, d - 1],
            device(y, k, target, half),
        )

    def first(self):
        return [d for d in (1, self.seqs - 1) if d <= self.turn or d > self.turn][: min(2, self.seqs - 1)]

    def later(self):
        return list(range(2, self.turn + 1)) + list(range(self.seqs - 2, self.turn, -1))

    def last(self):
        return [d for d in range(1, self.seqs) if d == self.turn or d == self.turn + 1]

    def across(self, d):
        y, k, seq, half = self.place
        self.y[d] = remote(
            self.full.at[d, :, : self.wide],
            self.full.at[d, :, self.wide :],
            self.y_sems.at[0, d],
            self.y_sems.at[1, d],
            device(1 - y, k, seq, half),
        )

    def pass_along(self, cross):
        for d in self.later():
            self.along(d)
            if cross:
                self.across(d - 1 if d <= self.turn else d + 1)
        for d in self.last():
            self.z[d].wait_recv()
            if cross:
                self.across(d)

    def finish(self):
        for copy in self.z.values():
            copy.wait_send()
        for copy in self.y.values():
            copy.wait()


class Collect:
    def __init__(self, source, place, seqs, y_refs=None, z_refs=None):
        self.source, self.place, self.seqs = source, place, seqs
        self.y_refs, self.z_refs = y_refs, z_refs
        self.wide = source.shape[2] // 2 if y_refs else source.shape[2]
        self.turn = seqs // 2
        self.order = list(range(self.turn, seqs)) + list(range(self.turn - 1, -1, -1))
        self.y, self.z, self.core = {}, {}, None

    def across(self):
        y, k, seq, half = self.place
        buf, sems = self.y_refs
        for d in self.order:
            self.y[d] = remote(
                self.source.at[d, :, self.wide :], buf.at[d], sems.at[0, d], sems.at[1, d], device(1 - y, k, seq, half)
            )

    def total(self, d):
        if not self.y_refs:
            return self.source[d].astype(F32)
        self.y[d].wait_recv()
        return self.source[d, :, : self.wide].astype(F32) + self.y_refs[0][d].astype(F32)

    def store(self, out):
        for d in self.order:
            out[d] = self.total(d).astype(BF)

    def along(self, d):
        y, k, seq, half = self.place
        out, z_send, z_buf, c_send, z_sems, c_sems = self.z_refs
        left = d <= self.turn
        before = d + 1 if left else d - 1
        value = self.total(d)
        if before in self.z and before not in (self.turn + 1 if left else self.turn,):
            self.z[before].wait_recv()
            value = value + z_buf[before - 1].astype(F32)
        z_send[d - 1] = value.astype(BF)
        target = lax.rem(seq + (self.seqs - 1 if left else 1), self.seqs)
        self.z[d] = remote(
            z_send.at[d - 1], z_buf.at[d - 1], z_sems.at[0, d - 1], z_sems.at[1, d - 1], device(y, k, target, half)
        )

    def close(self):
        y, k, seq, half = self.place
        out, z_send, z_buf, c_send, z_sems, c_sems = self.z_refs
        total = self.total(0)
        for d in sorted({1, self.seqs - 1}):
            self.z[d].wait_recv()
            total = total + z_buf[d - 1].astype(F32)
        low, high = total[:, : self.wide // 2], total[:, self.wide // 2 :]
        out[k] = jnp.where(k == 0, low, high)
        c_send[...] = jnp.where(k == 0, high, low)
        self.core = remote(c_send, out.at[k], c_sems.at[0], c_sems.at[1], device(y, 1 - k, seq, half))

    def finish(self):
        for copy in self.y.values():
            copy.wait_send()
        for copy in self.z.values():
            copy.wait_send()
        if self.core is not None:
            self.core.wait()


def freight_scratch(seqs):
    dma = pltpu.SemaphoreType.DMA
    return [dma((2, seqs - 1)), dma((2, seqs))]


def across_scratch(seqs, n, wide):
    return [pltpu.VMEM((seqs, n, wide), BF), pltpu.SemaphoreType.DMA((2, seqs))]


def along_scratch(seqs, n, wide):
    dma = pltpu.SemaphoreType.DMA
    return [
        pltpu.VMEM((seqs - 1, n, wide), BF),
        pltpu.VMEM((seqs - 1, n, wide), BF),
        pltpu.VMEM((n, wide // 2), F32),
        dma((2, seqs - 1)),
        dma((2,)),
    ]


def along_devices(place, seqs):
    y, k, seq, half = place
    return [device(y, k, lax.rem(seq + d, seqs), half) for d in sorted({1, seqs - 1})]


def shuffle(source, target, n, index, place, sends, receives, local_sems):
    y, k, seq, half = place
    feat = source.shape[-1]
    copies = [pltpu.make_async_copy(source.at[y, n, k], target.at[n, :, lanes(k * feat, feat)], local_sems.at[index])]
    copies[0].start()
    for i, (dy, dk, ty, tk) in enumerate(rows_of(place)):
        copies.append(
            remote(
                source.at[ty, n, tk],
                target.at[n, :, lanes(k * feat + 2 * dy * feat, feat)],
                sends.at[index, i],
                receives.at[index, i],
                device(ty, tk, seq, half),
            )
        )
    return copies


def normalize(residual):
    centered = residual - jnp.mean(residual, axis=-1, keepdims=True)
    inv_std = lax.rsqrt(jnp.mean(centered * centered, axis=-1, keepdims=True) + epsilon)
    return centered * inv_std, inv_std


def normalize_back(out_grad, normed, inv_std, gain):
    scaled = out_grad * gain
    first = jnp.mean(scaled, axis=-1, keepdims=True)
    second = jnp.mean(scaled * normed, axis=-1, keepdims=True)
    return inv_std * (scaled - first - normed * second)


def column_sum(value):
    return jnp.sum(value, axis=0, keepdims=True)


def exchange_kernel(kind, count, pieces, seqs, rides, *refs):
    place = spot()
    y, k, seq, half = place
    refs = list(refs)
    take = lambda amount: [refs.pop(0) for _ in range(amount)]
    r = types.SimpleNamespace()
    partial, r.resid, r.norm = take(3)
    if kind == TURN:
        (r.cot,) = take(1)
    elif kind == BACKWARD:
        r.normed, r.inv = take(2)
    ride_in = take(len(rides))
    (r.full,) = take(1)
    if kind == FORWARD:
        r.out, r.normed, r.inv = take(3)
    elif kind == TURN:
        r.output, r.grad, r.sums = take(3)
    else:
        r.grad, r.sums = take(2)
    ride_out = take(len(rides))
    if kind == TURN:
        r.own, r.landing, r.return_sems, r.cot_own, r.cot_send, r.cot_recv, r.cot_local = take(7)
    core_buf, half_send, half_buf, rc, rh, gh, gc = take(7)
    rows = partial.shape[3] // pieces
    peers = [device(y, 1 - k, seq, half), device(y, k, seq, 1 - half)]
    if kind == TURN:
        peers += [device(ty, tk, seq, half) for dy, dk, ty, tk in rows_of(place) if dy]
    elif {ACROSS, THROUGH, SUM_ACROSS} & set(rides):
        peers.append(device(1 - y, k, seq, half))
    if {ALONG, THROUGH, SUM_ALONG} & set(rides):
        peers += along_devices(place, seqs)
    greet(peers)
    units = [(n * pieces + p, n, p) for n in range(count) for p in range(pieces)]
    reduce = Reduce(partial, core_buf, half_send, half_buf, rc, rh, place, rows)
    spread = Spread(r.full, gh, gc, place, rows)
    for unit, n, p in units:
        reduce.start(unit, n, p, True)
    for unit, n, p in units:
        reduce.start(unit, n, p, False)
    moves, sums_along, sums_across = [], [], []
    for ride, source, target in zip(rides, ride_in, ride_out):
        if ride == SUM_ACROSS:
            sums_across.append((Collect(source, place, seqs, y_refs=take(2)), target))
            sums_across[-1][0].across()
        elif ride == SUM_ALONG:
            sums_along.append(Collect(source, place, seqs, z_refs=[target] + take(5)))
            for d in sums_along[-1].order[:2]:
                sums_along[-1].along(d)
        else:
            moves.append((ride, Freight(target, *take(2), place, seqs)))
            if ride == ACROSS:
                for d in range(seqs):
                    moves[-1][1].across(d)
            else:
                if ride == THROUGH:
                    moves[-1][1].across(0)
                for d in moves[-1][1].first():
                    moves[-1][1].along(d)
    if kind != FORWARD:
        r.sums[...] = jnp.zeros_like(r.sums)
    if kind == TURN:
        back = Return(r.own, r.landing, r.return_sems, place, partial.shape[4] // 4)
        cots = [
            shuffle(r.cot, r.cot_own, n, n, place, r.cot_send, r.cot_recv, r.cot_local) for n in range(count)
        ]
    gain, bias = r.norm[0:1], r.norm[1:2]
    for unit, n, p in units:
        reduce.pass_on(unit, n, p)
    for unit, n, p in units:
        here = pl.ds(p * rows, rows)
        branch = reduce.result(unit, n, p)
        if kind == FORWARD:
            normed, inv = normalize(r.resid[n, here].astype(F32) + branch)
            value = normed * gain + bias
            r.out[n, here] = value
            r.normed[n, here] = normed
            r.inv[n, here] = inv
        elif kind == TURN:
            normed, inv = normalize(r.resid[n, here].astype(F32) + branch)
            if p == 0:
                for copy in cots[n]:
                    copy.wait()
            upstream = r.cot_own[n, here].astype(F32)
            value = normalize_back(upstream, normed, inv, gain)
            r.grad[n, here] = value
        else:
            upstream = r.resid[n, here] + branch if r.resid.shape[1] == partial.shape[3] else branch
            normed = r.normed[n, here]
            value = normalize_back(upstream, normed, r.inv[n, here], gain)
            r.grad[n, here] = value
        r.full[n, half, k, here] = value.astype(BF)
        spread.start(unit, n, p)
        if kind != FORWARD:
            r.sums[0:1] += column_sum(upstream * normed)
            r.sums[1:2] += column_sum(upstream)
        if kind == TURN:
            back.start(unit, n, (normed * gain + bias).astype(BF))
    for collect in sums_along:
        for d in collect.order[2:-1]:
            collect.along(d)
    for ride, move in moves:
        if ride != ACROSS:
            move.pass_along(ride == THROUGH)
    for unit, n, p in units:
        spread.forward(unit, n, p)
    for collect in sums_along:
        collect.close()
    for unit, n, p in units:
        spread.finish(unit)
        reduce.finish(unit)
    if kind == TURN:
        back.finish()
        r.output[...] = r.landing[...].astype(F32)
    for ride, move in moves:
        move.finish()
    for collect, target in sums_across:
        collect.store(target)
        collect.finish()
    for collect in sums_along:
        collect.finish()


def exchange(kind, collective_id, seqs, partial, resid, norm, cot=None, normed=None, inv=None, rides=()):
    count, _, _, own, depth = partial.shape
    pieces = 2 if count == 1 else 1
    units, rows = count * pieces, own // pieces
    dma = pltpu.SemaphoreType.DMA
    shape = jax.ShapeDtypeStruct
    vmem = pl.BlockSpec(memory_space=pltpu.VMEM)
    anywhere = pl.BlockSpec(memory_space=pl.ANY)
    full = shape((count, 2, 2, own, depth), BF)
    grad, sums = shape((count, own, depth), F32), shape((8, depth), F32)
    scratch = []
    if kind == FORWARD:
        args = (partial, resid, norm)
        outs = (full, grad, grad, shape((count, own, 1), F32))
    elif kind == TURN:
        args = (partial, resid, norm, cot)
        outs = (full, shape((2, count, 2, own, depth // 4), F32), grad, sums)
        scratch = [
            pltpu.VMEM((units, rows, depth), BF),
            pltpu.VMEM((2, count, 2, own, depth // 4), BF),
            dma((2, units, 3)),
            pltpu.VMEM((count, own, depth), BF),
            dma((count, 3)),
            dma((count, 3)),
            dma((count,)),
        ]
    else:
        args = (partial, resid, norm, normed, inv)
        outs = (full, grad, sums)
    scratch += [
        pltpu.VMEM((units, 2, rows, depth), BF),
        pltpu.VMEM((units, rows, depth), BF),
        pltpu.VMEM((units, rows, depth), BF),
        dma((2, units, 2)),
        dma((2, units)),
        dma((2, units)),
        dma((2, units, 2)),
    ]
    in_specs, out_specs = [vmem] * len(args), [vmem] * len(outs)
    aliases = {}
    for ride, array in rides:
        if ride == SUM_ACROSS or ride == SUM_ALONG:
            n, wide = array.shape[1], depth // 2
            scratch += (across_scratch if ride == SUM_ACROSS else along_scratch)(seqs, n, wide)
            in_specs.append(vmem)
            out_specs.append(vmem)
            outs += (shape((seqs, n, wide), BF) if ride == SUM_ACROSS else shape((2, n, wide // 2), F32),)
        else:
            scratch += freight_scratch(seqs)
            aliases[len(args)] = len(outs)
            in_specs.append(anywhere)
            out_specs.append(anywhere)
            outs += (shape(array.shape, array.dtype),)
        args += (array,)
    return pl.pallas_call(
        functools.partial(exchange_kernel, kind, count, pieces, seqs, tuple(ride for ride, _ in rides)),
        out_shape=outs,
        in_specs=in_specs,
        out_specs=tuple(out_specs),
        scratch_shapes=scratch,
        input_output_aliases=aliases,
        compiler_params=pltpu.CompilerParams(collective_id=collective_id, has_side_effects=True, vmem_limit_bytes=50 << 20),
        name="exchange_%d" % collective_id,
    )(*args)


def inputs_kernel(seqs, groups, tok_ref, str_ref, norm_ref, ids_ref, tab_ref, *refs):
    refs = list(refs)
    take = lambda amount: [refs.pop(0) for _ in range(amount)]
    packs = take(groups)
    x_own, x_full, y_own, y_full, norm_all, ids_all, tab_all = take(7)
    fulls = take(groups)
    in_send, in_recv, in_local, xh, xc, yh, yc, small_sems, tab_sems, small_self, pack_sems, pack_self = take(12)
    place = spot()
    y, k, seq, half = place
    feat = tok_ref.shape[-1]
    own = tok_ref.shape[-2]
    row_peers = rows_of(place)
    others = [device(y, k, lax.rem(seq + d, seqs), half) for d in range(1, seqs)]
    greet([device(ty, tk, seq, half) for dy, dk, ty, tk in row_peers] + [device(y, k, seq, 1 - half)] + others)
    count = str_ref.shape[1]
    x_copies = shuffle(tok_ref, x_own, 0, 0, place, in_send, in_recv, in_local)
    loads = []
    for g in range(groups):
        here = fulls[g].at[0, :, lanes(k * feat, feat)]
        copy = pltpu.make_async_copy(packs[g].at[k], here, pack_self.at[g])
        copy.start()
        loads.append(
            (
                copy,
                remote(packs[g].at[1 - k], here, pack_sems.at[0, g], pack_sems.at[1, g], device(y, 1 - k, seq, half)),
            )
        )
    small = []
    for j, (source, target) in enumerate(((norm_ref, norm_all), (ids_ref, ids_all))):
        slot = (lambda dy: (slice(None), lanes(k * feat + 2 * dy * feat, feat))) if j == 0 else (lambda dy: (2 * y + k,))
        copy = pltpu.make_async_copy(source, target.at[slot(0)], small_self.at[j])
        copy.start()
        small.append(copy)
        for i, (dy, dk, ty, tk) in enumerate(row_peers):
            small.append(
                remote(source, target.at[slot(dy)], small_sems.at[0, j, i], small_sems.at[1, j, i], device(ty, tk, seq, half))
            )
    copy = pltpu.make_async_copy(tab_ref, tab_all.at[0], small_self.at[2])
    copy.start()
    small.append(copy)
    for d in range(1, seqs):
        small.append(remote(tab_ref, tab_all.at[d], tab_sems.at[0, d - 1], tab_sems.at[1, d - 1], others[d - 1]))
    freights = [Freight(full, *take(2), place, seqs) for full in fulls]
    for copy in loads[0]:
        copy.wait()
    for d in freights[0].first():
        freights[0].along(d)
    freights[0].across(0)
    for copy in x_copies:
        copy.wait()
    x_full[0, half, k] = x_own[0]
    x_spread = Spread(x_full, xh, xc, place, own)
    x_spread.start(0, 0, 0)
    y_copies = [shuffle(str_ref, y_own, n, 1 + n, place, in_send, in_recv, in_local) for n in range(count)]
    y_spread = Spread(y_full, yh, yc, place, own)
    for g in range(1, groups):
        for copy in loads[g]:
            copy.wait()
    x_spread.forward(0, 0, 0)
    for n in range(count):
        for copy in y_copies[n]:
            copy.wait()
        y_full[n, half, k] = y_own[n]
        y_spread.start(n, n, 0)
    freights[0].pass_along(True)
    for d in freights[1].first():
        freights[1].along(d)
    freights[1].across(0)
    for n in range(count):
        y_spread.forward(n, n, 0)
    for copy in small:
        copy.wait()
    freights[1].pass_along(True)
    for d in freights[2].first():
        freights[2].along(d)
    freights[2].pass_along(False)
    x_spread.finish(0)
    for n in range(count):
        y_spread.finish(n)
    for freight in freights:
        freight.finish()


def gather_inputs(seqs, tokens, streams, norm, ids, table, packs):
    count, own, feat = streams.shape[1], streams.shape[-2], streams.shape[-1]
    depth = 4 * feat
    dma = pltpu.SemaphoreType.DMA
    shape = jax.ShapeDtypeStruct
    vmem = pl.BlockSpec(memory_space=pltpu.VMEM)
    outs = (
        shape((1, own, depth), BF),
        shape((1, 2, 2, own, depth), BF),
        shape((count, own, depth), BF),
        shape((count, 2, 2, own, depth), BF),
        shape((norm.shape[0], depth), F32),
        shape((4,) + ids.shape, jnp.int32),
        shape((seqs,) + table.shape, F32),
    )
    specs = [vmem] * len(outs)
    for pack in packs:
        outs += (shape((seqs, pack.shape[1], depth), BF),)
        specs.append(pl.BlockSpec(memory_space=pl.ANY))
    moves = 1 + count
    scratch = [
        dma((moves, 3)),
        dma((moves, 3)),
        dma((moves,)),
        dma((2, 1)),
        dma((2, 1, 2)),
        dma((2, count)),
        dma((2, count, 2)),
        dma((2, 2, 3)),
        dma((2, seqs - 1)),
        dma((3,)),
        dma((2, len(packs))),
        dma((len(packs),)),
    ]
    for _ in packs:
        scratch += freight_scratch(seqs)
    return pl.pallas_call(
        functools.partial(inputs_kernel, seqs, len(packs)),
        out_shape=outs,
        in_specs=[vmem] * (5 + len(packs)),
        out_specs=tuple(specs),
        scratch_shapes=scratch,
        compiler_params=pltpu.CompilerParams(collective_id=0, has_side_effects=True, vmem_limit_bytes=50 << 20),
        name="gather_inputs",
    )(tokens, streams, norm, ids, table, *packs)


def outputs_kernel(seqs, count, part_x, part_y, d1, d3, small, down, up, first, tok_out, str_out, small_out, down_out, up_out, first_out, core_buf, half_send, half_buf, own, land_x, land_y, rc, rh, rs, small_buf, ss, *refs):
    refs = list(refs)
    take = lambda amount: [refs.pop(0) for _ in range(amount)]
    place = spot()
    y, k, seq, half = place
    rows = part_x.shape[3]
    feat = part_x.shape[4] // 4
    bits = [1 << b for b in range((seqs - 1).bit_length())]
    flips = [device(y, k, seq + b - 2 * b * ((seq // b) % 2), half) for b in bits]
    others = [device(y, k, lax.rem(seq + d, seqs), half) for d in range(1, seqs)]
    partners = [device(y, 1 - k, seq, half), device(y, k, seq, 1 - half), device(1 - y, k, seq, half)]
    greet(partners + [device(1 - y, 1 - k, seq, half)] + others)
    partners += flips
    small_out[...] = small[...]

    def add_small(stage):
        copy = remote(small_out, small_buf.at[stage], ss.at[0, stage], ss.at[1, stage], partners[stage])
        copy.wait()
        small_out[...] += small_buf[stage]

    class Both:
        def __getitem__(self, index):
            return part_x[(0,) + index[1:]] if index[0] == 0 else part_y[(index[0] - 1,) + index[1:]]

        @property
        def at(self):
            return View()

    class View:
        def __getitem__(self, index):
            return part_x.at[(0,) + index[1:]] if index[0] == 0 else part_y.at[(index[0] - 1,) + index[1:]]

    reduce = Reduce(Both(), core_buf, half_send, half_buf, rc, rh, place, rows)
    units = range(count + 1)
    down = Collect(down, place, seqs, z_refs=[down_out] + take(5))
    up = Collect(up, place, seqs, y_refs=take(2), z_refs=[up_out] + take(5))
    first = Collect(first, place, seqs, y_refs=take(2), z_refs=[first_out] + take(5))
    reduce.start(0, 0, 0, True)
    reduce.start(0, 0, 0, False)
    add_small(2)
    up.across()
    add_small(1)
    reduce.pass_on(0, 0, 0)
    for stage in range(3, len(partners)):
        add_small(stage)
    for d in down.order[:2]:
        down.along(d)
    add_small(0)
    for unit in units[1:]:
        reduce.start(unit, unit, 0, True)
        reduce.start(unit, unit, 0, False)
    x_back = Return(own, land_x, rs, place, feat)
    y_back = Return(own, land_y, rs, place, feat)
    x_back.start(0, 0, (d1[0] + reduce.result(0, 0, 0)).astype(BF))
    first.across()
    for unit in units[1:]:
        reduce.pass_on(unit, unit, 0)
    for d in down.order[2:-1]:
        down.along(d)
    for d in up.order[:1]:
        up.along(d)
    down.close()
    for d in up.order[1:-1]:
        up.along(d)
    for unit in units[1:]:
        y_back.start(unit, unit - 1, (d3[unit - 1] + reduce.result(unit, unit, 0)).astype(BF))
    for unit in units:
        reduce.finish(unit)
    x_back.finish()
    tok_out[...] = land_x[:, 0].astype(F32)
    up.close()
    for d in first.order[:-1]:
        first.along(d)
    y_back.finish()
    str_out[...] = land_y[...].astype(F32)
    first.close()
    for collect in (down, up, first):
        collect.finish()


def scatter_outputs(seqs, collective_id, part_x, part_y, d1, d3, small, down, up, first):
    count, _, _, own, depth = part_y.shape
    feat, wide = depth // 4, depth // 2
    units = count + 1
    dma = pltpu.SemaphoreType.DMA
    shape = jax.ShapeDtypeStruct
    stages = 3 + (seqs - 1).bit_length()
    outs = (shape((2, 2, own, feat), F32), shape((2, count, 2, own, feat), F32), shape(small.shape, F32))
    outs += tuple(shape((2, group.shape[1], feat), F32) for group in (down, up, first))
    scratch = [
        pltpu.VMEM((units, 2, own, depth), BF),
        pltpu.VMEM((units, own, depth), BF),
        pltpu.VMEM((units, own, depth), BF),
        pltpu.VMEM((units, own, depth), BF),
        pltpu.VMEM((2, 1, 2, own, feat), BF),
        pltpu.VMEM((2, count, 2, own, feat), BF),
        dma((2, units, 2)),
        dma((2, units)),
        dma((2, units, 3)),
        pltpu.VMEM((stages,) + small.shape, F32),
        dma((2, stages)),
    ]
    scratch += along_scratch(seqs, down.shape[1], wide)
    for group in (up, first):
        scratch += across_scratch(seqs, group.shape[1], wide) + along_scratch(seqs, group.shape[1], wide)
    return pl.pallas_call(
        functools.partial(outputs_kernel, seqs, count),
        out_shape=outs,
        in_specs=[pl.BlockSpec(memory_space=pltpu.VMEM)] * 8,
        out_specs=tuple(pl.BlockSpec(memory_space=pltpu.VMEM) for _ in outs),
        scratch_shapes=scratch,
        compiler_params=pltpu.CompilerParams(collective_id=collective_id, has_side_effects=True, vmem_limit_bytes=50 << 20),
        name="scatter_outputs",
    )(part_x, part_y, d1, d3, small, down, up, first)


def pick(array, index, axis):
    return lax.dynamic_index_in_dim(array, index, axis, keepdims=False)


def dot_f32(spec, left, right):
    return jnp.einsum(spec, left, right, preferred_element_type=F32)


def on_device(
    rows,
    cols,
    tokens,
    streams,
    cotangent,
    block_ids,
    bucket_ids,
    w_qkv,
    enc_table,
    w_out,
    attention_norm_gain,
    attn_bias,
    w_up,
    w_down,
    ffn_gain,
    ffn_bias,
    w_query,
    w_keyval,
    cross_table,
    w_cross_out,
    cross_gain,
    cross_bias,
):
    seqs = cols // 2
    row, col = lax.axis_index(ROW), lax.axis_index(COL)
    y, k, seq, half = row // 2, row % 2, col // 2, col % 2
    low_y = y == 0
    stream_count = streams.shape[1]
    tok = tokens.shape[1]
    own = tok // 2
    feat = tokens.shape[2]
    length = block_ids.shape[2]
    head_dim = w_qkv.shape[2] // 2
    ff = w_up.shape[1] // 2
    table_heads, bucket_count = enc_table.shape

    def columns(weight, parts):
        return weight.reshape(feat, parts, 2, -1).transpose(2, 1, 3, 0).reshape(2, -1, feat)

    def columns_back(array, parts):
        return array.reshape(2, parts, -1, feat).transpose(3, 1, 0, 2).reshape(feat, parts, -1)

    halves = lambda weight: weight.reshape(2, -1, feat)
    hd3, hd2 = 3 * head_dim, 2 * head_dim
    packs = (
        jnp.concatenate([columns(w_qkv, 3), halves(w_out)], axis=1),
        columns(w_up, 1),
        halves(w_down),
        jnp.concatenate([columns(w_keyval, 2), columns(w_query, 1), halves(w_cross_out)], axis=1),
    )
    norm_params = jnp.stack([attention_norm_gain, attn_bias, ffn_gain, ffn_bias, cross_gain, cross_bias] + [cross_bias] * 2)
    table_pack = jnp.zeros((8, 128), F32).at[0].set(jnp.stack([enc_table, cross_table]).reshape(-1))
    micro_count = tokens.shape[0]
    x_own, x_full, y_own, y_full, norm_params, all_ids, all_tables, first, up, down, last = gather_inputs(
        seqs,
        tokens.reshape(micro_count, 1, 2, own, feat),
        streams.reshape(micro_count, stream_count, 2, own, feat),
        norm_params,
        block_ids.reshape(8, -1),
        table_pack,
        packs,
    )
    x_full, y_full = x_full.reshape(length, D), y_full.reshape(stream_count * length, D)
    segment = pick(pick(all_ids.reshape(rows, micro_count, length), seq, 0), y, 0)
    segq = segment[None]
    segk = jnp.broadcast_to(segment[:, None], (length, 128))
    own_tables = pick(all_tables[:, 0].reshape(seqs, 2, table_heads, bucket_count), k, 2)
    slot_col = 2 * ((seq - jnp.arange(seqs)) % seqs) + half
    reversed_ids = jnp.concatenate([jnp.full((1,), -1, jnp.int32), bucket_ids[::-1]])
    onehot = bucket_onehot(reversed_ids, bucket_count)
    offsets = jnp.einsum("htb,bo->tho", own_tables, onehot, precision=highest)[:, :, None, :]

    m_qkv, m_out = first[:, :hd3], first[:, hd3:].reshape(-1, D)
    blocked = lambda product: product.astype(BF).reshape(-1, 2, 2, own, D)

    qkv = dot_f32("snr,tr->snt", m_qkv, x_full).astype(BF)
    mix, lse, tiles = attention(offsets[0], segq, segk, qkv, qkv, qkv, (0, 1, 2), 1)
    mix_flat = mix.reshape(-1, length)
    hidden_full, hidden, normed1, inv1, down, last = exchange(
        FORWARD,
        1,
        seqs,
        blocked(dot_f32("et,er->tr", mix_flat, m_out)),
        x_own,
        norm_params[0:2],
        rides=((ACROSS, down), (ALONG, last)),
    )
    up, down = up.reshape(-1, D), down.reshape(-1, D)
    hidden_full = hidden_full.reshape(length, D)
    pre = dot_f32("fr,tr->ft", up, hidden_full)
    act, gelu_pull = jax.vjp(gelu_exact, pre)
    act = act.astype(BF)
    enc_full, _, normed2, inv2, last = exchange(
        FORWARD,
        2,
        seqs,
        blocked(dot_f32("ft,fr->tr", act, down)),
        hidden,
        norm_params[2:4],
        rides=((ACROSS, last),),
    )
    m_kv, m_q, m_co = last[:, :hd2], last[:, hd2:hd3], last[:, hd3:].reshape(-1, D)
    enc_full = enc_full.reshape(length, D)
    kv = dot_f32("snr,tr->snt", m_kv, enc_full).astype(BF)
    query = dot_f32("snr,tr->snt", m_q, y_full).astype(BF)
    cmix, clse, ctiles = attention(offsets[1], segq, segk, query, kv, kv, (0, 0, 1), stream_count)
    cmix_flat = cmix.reshape(-1, stream_count * length)
    d3_full, output, d3, sums3 = exchange(
        TURN, 3, seqs, blocked(dot_f32("et,er->tr", cmix_flat, m_co)), y_own, norm_params[4:6], cot=cotangent.reshape(micro_count, stream_count, 2, own, feat)
    )
    d3_full = d3_full.reshape(stream_count * length, D)

    dcmix = dot_f32("er,tr->et", m_co, d3_full).astype(BF).reshape(cmix.shape)
    g_co = dot_f32("et,tr->er", cmix_flat, d3_full)
    dquery, dkc, dvc, doff_cross = attention_back(
        ctiles, segq, segk, query, kv, kv, (0, 0, 1), clse, dcmix, stream_count
    )
    dkv = jnp.concatenate([dkc, dvc], axis=1)
    g_q = dot_f32("snt,tr->snr", dquery, y_full)
    g_kv = dot_f32("snt,tr->snr", dkv, enc_full)
    g_last = jnp.concatenate([g_kv.astype(BF), g_q.astype(BF), g_co.astype(BF).reshape(seqs, head_dim, D)], axis=1)
    d2_full, d2, sums2, g_last = exchange(
        BACKWARD,
        4,
        seqs,
        blocked(dot_f32("snt,snr->tr", dkv, m_kv)),
        norm_params[2:4][None],
        norm_params[2:4],
        normed=normed2,
        inv=inv2,
        rides=((SUM_ACROSS, g_last),),
    )
    d2_full = d2_full.reshape(length, D)
    part_y = blocked(dot_f32("snt,snr->tr", dquery, m_q))
    dact = dot_f32("fr,tr->ft", down, d2_full)
    dpre = gelu_pull(dact)[0].astype(BF)
    g_down = dot_f32("ft,tr->fr", act, d2_full).astype(BF).reshape(seqs, ff, D)
    d1_full, d1, sums1, g_last, g_down = exchange(
        BACKWARD,
        5,
        seqs,
        blocked(dot_f32("ft,fr->tr", dpre, up)),
        d2,
        norm_params[0:2],
        normed=normed1,
        inv=inv1,
        rides=((SUM_ALONG, g_last), (SUM_ACROSS, g_down)),
    )
    d1_full = d1_full.reshape(length, D)
    g_up = dot_f32("ft,tr->fr", dpre, hidden_full).astype(BF).reshape(seqs, ff, D)
    dmix = dot_f32("er,tr->et", m_out, d1_full).astype(BF).reshape(mix.shape)
    g_out = dot_f32("et,tr->er", mix_flat, d1_full)
    dq, dk, dv, doff_enc = attention_back(tiles, segq, segk, qkv, qkv, qkv, (0, 1, 2), lse, dmix, 1)
    dqkv = jnp.concatenate([dq, dk, dv], axis=1)
    g_qkv = dot_f32("snt,tr->snr", dqkv, x_full)
    g_first = jnp.concatenate([g_qkv.astype(BF), g_out.astype(BF).reshape(seqs, head_dim, D)], axis=1)
    part_x = blocked(dot_f32("snt,snr->tr", dqkv, m_qkv))

    norm_grads = jnp.concatenate([sums1[:2], sums2[:2], sums3[:2]])
    norm_grads = jnp.where(low_y, norm_grads, jnp.roll(norm_grads, D // 2, axis=1))
    table_grads = jnp.einsum(
        "tho,bo->thb", jnp.stack([doff_enc[:, 0], doff_cross[:, 0]]), onehot, precision=highest
    )
    heads = 2 * slot_col + k
    spread = (heads[:, None] == jnp.arange(table_heads * cols)[None, :]).astype(F32)
    table_grads = jnp.einsum("thb,hg->tgb", table_grads, spread, precision=highest)
    small = jnp.concatenate([norm_grads.reshape(-1, 128), table_grads.reshape(-1, 128)])
    grad_tokens, grad_streams, small, g_down, g_up, g_first = scatter_outputs(
        seqs, 6, part_x, part_y, d1, d3, small, g_down, g_up, g_first
    )
    output, grad_streams = output.reshape(streams.shape), grad_streams.reshape(streams.shape)
    grad_tokens = grad_tokens.reshape(tokens.shape)
    count = norm_grads.size // 128
    norm_sums = lax.dynamic_slice_in_dim(small[:count].reshape(6, D), row * feat, feat, axis=1)
    table_sums = small[count:].reshape(2, table_heads * cols, bucket_count)
    table_sums = lax.dynamic_slice_in_dim(table_sums, col * table_heads, table_heads, axis=1)
    return (
        output,
        grad_tokens,
        grad_streams,
        columns_back(g_first[:, :hd3], 3),
        table_sums[0],
        g_first[:, hd3:].reshape(w_out.shape),
        norm_sums[0],
        norm_sums[1],
        columns_back(g_up, 1).reshape(w_up.shape),
        g_down.reshape(w_down.shape),
        norm_sums[2],
        norm_sums[3],
        columns_back(g_last[:, hd2:hd3], 1).reshape(w_query.shape),
        columns_back(g_last[:, :hd2], 2),
        table_sums[1],
        g_last[:, hd3:].reshape(w_cross_out.shape),
        norm_sums[4],
        norm_sums[5],
    )


def solution(mesh):
    whole_row, half_col = mesh.shape[ROW], mesh.shape[COL]
    wide, table, norm = P(ROW, None, COL), P(COL, None), P(ROW)
    up, down = P(ROW, COL), P(COL, ROW)
    weights = (wide, table, down, norm, norm, up, down, norm, norm, up, wide, table, down, norm, norm)

    def run(tokens, *rest):
        micro_count = tokens.shape[0]
        if whole_row == 4 and micro_count == 2 and half_col % 2 == 0:
            device_fn = functools.partial(on_device, whole_row, half_col)
        else:
            device_fn = on_device_general
        return jax.shard_map(
            device_fn,
            mesh=mesh,
            in_specs=(P(None, COL, ROW), P(None, None, COL, ROW), P(None, None, COL, ROW), P(None, ROW, None), P()) + weights,
            out_specs=(P(None, None, COL, ROW), P(None, COL, ROW), P(None, None, COL, ROW)) + weights,
            check_vma=False,
        )(tokens, *rest)

    return run
```

```python
import functools
import types
import jax
import jax.numpy as jnp
from jax import lax
from jax.experimental import pallas as pl
from jax.experimental.pallas import tpu as pltpu
from jax.sharding import PartitionSpec as P

D = 1024
F32 = jnp.float32
BF = jnp.bfloat16
ROW, COL = "row", "col"


epsilon = 1e-05
neg_fill = -1e30
highest = lax.Precision.HIGHEST


def gather_cols(local_rows):
    return lax.all_gather(local_rows, COL, axis=1, tiled=True)


def gather_rows(local_rows):
    return lax.all_gather(local_rows, ROW, axis=1, tiled=True)


def product(matmul_operand, weight_matrix):
    return jnp.einsum(
        "ray,yw->raw", matmul_operand, weight_matrix, preferred_element_type=jnp.float32
    )


def rows_product(operand_full, matrix):
    return lax.psum_scatter(product(operand_full, matrix), ROW, scatter_dimension=1, tiled=True)


def cols_product(operand_full, matrix):
    return lax.psum_scatter(product(operand_full, matrix), COL, scatter_dimension=1, tiled=True)


def weight_grad(matmul_operand, upstream_gradient):
    return jnp.einsum(
        "bpt,bpr->tr", matmul_operand, upstream_gradient, preferred_element_type=jnp.float32
    )


def gelu_exact(argument):
    return jax.nn.gelu(argument, approximate=False)


def norm_forward(residual, gain_vec, bias_vec):
    local_sum = jnp.sum(residual, axis=-1)
    average = lax.psum(local_sum, ROW) / D
    centered = residual - average[..., None]
    spread = lax.psum(jnp.sum(centered * centered, axis=-1), ROW) / D
    inv_std = lax.rsqrt(spread + epsilon)
    normed = centered * inv_std[..., None]
    return (normed * gain_vec + bias_vec, normed, inv_std)


def norm_back(out_grad, normed, inv_std, gain_vec):
    scaled_grad = out_grad * gain_vec
    first_moment, second_moment = lax.psum(
        (jnp.sum(scaled_grad, axis=-1), jnp.sum(scaled_grad * normed, axis=-1)), ROW
    )
    resid_grad = inv_std[..., None] * (
        scaled_grad - first_moment[..., None] / D - normed * (second_moment[..., None] / D)
    )
    return (resid_grad, jnp.sum(out_grad * normed, axis=(0, 1)), jnp.sum(out_grad, axis=(0, 1)))


def bucket_onehot(bucket_ids, bucket_count):
    return (bucket_ids[None, :] == jnp.arange(bucket_count, dtype=jnp.int32)[:, None]).astype(
        jnp.float32
    )


def block_logits(query_blk, key_rows, offsets, segment, first_row):
    row_count = query_blk.shape[2]
    length = key_rows.shape[1]
    score_scale = query_blk.shape[-1] ** (-0.5)
    raw_scores = jnp.einsum(
        "snqhd,nkhd->snhqk", query_blk, key_rows, preferred_element_type=jnp.float32
    )
    places = jnp.arange(length, dtype=jnp.int32)
    query_pos = first_row + jnp.arange(row_count, dtype=jnp.int32)
    offset_index = places[None, :] - query_pos[:, None] + (length - 1)
    pos_bias = jnp.take(offsets, offset_index, axis=1)
    visible = segment[:, first_row : first_row + row_count, None] >= segment[:, None, :]
    return jnp.where(
        visible[None, :, None], raw_scores * score_scale + pos_bias[None, None], neg_fill
    )


def attend(queries, key_rows, value_rows, segment, offsets):
    score_logits = block_logits(queries, key_rows, offsets, segment, 0)
    row_max = jnp.max(score_logits, axis=-1, keepdims=True)
    log_total = row_max + jnp.log(jnp.sum(jnp.exp(score_logits - row_max), axis=-1, keepdims=True))
    weights = jnp.exp(score_logits - log_total).astype(jnp.bfloat16)
    mixed_parts = jnp.einsum(
        "snhqk,nkhd->snqhd", weights, value_rows, preferred_element_type=jnp.float32
    )
    lse_parts = log_total[..., 0]
    return (mixed_parts, lse_parts)


def diagonal_sums(summand):
    head_count, row_count, length = summand.shape
    flipped = summand[:, ::-1, :]
    padded = jnp.concatenate(
        [flipped, jnp.zeros((head_count, row_count, row_count), summand.dtype)], axis=2
    )
    flattened = padded.reshape(head_count, row_count * (length + row_count))[
        :, : row_count * (length + row_count - 1)
    ]
    return jnp.sum(flattened.reshape(head_count, row_count, length + row_count - 1), axis=1)


def attend_back(queries, key_rows, value_rows, segment, offsets, onehot, log_totals, mix_grad):
    length = key_rows.shape[1]
    block_rows = min(512, length)
    score_scale = queries.shape[-1] ** (-0.5)
    offset_grad = jnp.zeros(offsets.shape, jnp.float32)
    score_logits = block_logits(queries, key_rows, offsets, segment, 0)
    probability = jnp.exp(score_logits - log_totals[:, :, :, 0:block_rows, None])
    prob_grad = jnp.einsum(
        "snqhd,nkhd->snhqk", mix_grad, value_rows, preferred_element_type=jnp.float32
    )
    logit_grad = probability * (
        prob_grad - jnp.sum(probability * prob_grad, axis=-1, keepdims=True)
    )
    scaled = (logit_grad * score_scale).astype(jnp.bfloat16)
    query_parts = jnp.einsum(
        "snhqk,nkhd->snqhd", scaled, key_rows, preferred_element_type=jnp.float32
    )
    key_grad = jnp.einsum("snhqk,snqhd->nkhd", scaled, queries, preferred_element_type=jnp.float32)
    value_grad = jnp.einsum(
        "snhqk,snqhd->nkhd",
        probability.astype(jnp.bfloat16),
        mix_grad,
        preferred_element_type=jnp.float32,
    )
    low_end = length - block_rows
    offset_grad = offset_grad.at[:, low_end : low_end + length + block_rows - 1].add(
        diagonal_sums(jnp.sum(logit_grad, axis=(0, 1)))
    )
    table_grad = jnp.dot(offset_grad, onehot.T, precision=highest)
    return (query_parts, key_grad, value_grad, table_grad)


def on_device_general(
    tokens,
    streams,
    cotangent,
    block_ids,
    bucket_ids,
    w_qkv,
    enc_table,
    w_out,
    attention_norm_gain,
    attn_bias,
    w_up,
    w_down,
    ffn_gain,
    ffn_bias,
    w_query,
    w_keyval,
    cross_table,
    w_cross_out,
    cross_gain,
    cross_bias,
):
    micro_count = tokens.shape[0]
    stream_count = streams.shape[1]
    seq_rows = block_ids.shape[1]
    length = block_ids.shape[2]
    head_count = enc_table.shape[0]
    bucket_count = enc_table.shape[1]
    row_width = w_qkv.shape[0]
    col_width = w_qkv.shape[2]
    head_dim = col_width // head_count
    row_tokens = seq_rows * length
    qkv_matrix = w_qkv.reshape(row_width, 3 * col_width)
    keyval_matrix = w_keyval.reshape(row_width, 2 * col_width)
    onehot = bucket_onehot(bucket_ids, bucket_count)
    enc_offsets = jnp.dot(enc_table, onehot, precision=highest)
    cross_offsets = jnp.dot(cross_table, onehot, precision=highest)
    qkv_acc = jnp.zeros((row_width, 3 * col_width), jnp.float32)
    out_acc = jnp.zeros(w_out.shape, jnp.float32)
    up_acc = jnp.zeros(w_up.shape, jnp.float32)
    down_acc = jnp.zeros(w_down.shape, jnp.float32)
    query_acc = jnp.zeros(w_query.shape, jnp.float32)
    keyval_acc = jnp.zeros((row_width, 2 * col_width), jnp.float32)
    cross_out_acc = jnp.zeros(w_cross_out.shape, jnp.float32)
    enc_table_acc = jnp.zeros(enc_table.shape, jnp.float32)
    cross_table_acc = jnp.zeros(cross_table.shape, jnp.float32)
    norm_accs = [jnp.zeros((row_width,), jnp.float32) for place_holder in range(6)]
    outputs = []
    token_grads = []
    stream_grads = []
    for micro in range(micro_count):
        segment = block_ids[micro]
        x_in = tokens[micro][None]
        y_in = streams[micro]
        x_full = gather_cols(x_in)
        qkv = (
            rows_product(x_full, qkv_matrix)
            .astype(jnp.bfloat16)
            .reshape(seq_rows, length, 3, head_count, head_dim)
        )
        enc_query = qkv[:, :, 0][None]
        enc_key = qkv[:, :, 1]
        encoder_value_rows = qkv[:, :, 2]
        enc_mixed, enc_lse = attend(enc_query, enc_key, encoder_value_rows, segment, enc_offsets)
        enc_mix = enc_mixed.reshape(1, row_tokens, col_width).astype(jnp.bfloat16)
        mix_full = gather_rows(enc_mix)
        attn_branch = cols_product(mix_full, w_out)
        hidden, normed_one, inv_one = norm_forward(
            x_in.astype(jnp.float32) + attn_branch, attention_norm_gain, attn_bias
        )
        hidden_low = hidden.astype(jnp.bfloat16)
        hidden_full = gather_cols(hidden_low)
        pre_act = rows_product(hidden_full, w_up)
        act_value, gelu_pull = jax.vjp(gelu_exact, pre_act)
        act_low = act_value.astype(jnp.bfloat16)
        act_full = gather_rows(act_low)
        ffn_branch = cols_product(act_full, w_down)
        encoded, normed_two, inv_two = norm_forward(hidden + ffn_branch, ffn_gain, ffn_bias)
        encoded_low = encoded.astype(jnp.bfloat16)
        enc_full = gather_cols(encoded_low)
        keyval = (
            rows_product(enc_full, keyval_matrix)
            .astype(jnp.bfloat16)
            .reshape(seq_rows, length, 2, head_count, head_dim)
        )
        cross_key = keyval[:, :, 0]
        cross_value = keyval[:, :, 1]
        stream_full = gather_cols(y_in)
        cross_query = (
            rows_product(stream_full, w_query)
            .astype(jnp.bfloat16)
            .reshape(stream_count, seq_rows, length, head_count, head_dim)
        )
        cross_mixed, cross_lse = attend(cross_query, cross_key, cross_value, segment, cross_offsets)
        cross_mix = cross_mixed.reshape(stream_count, row_tokens, col_width).astype(jnp.bfloat16)
        cross_full = gather_rows(cross_mix)
        cross_branch = cols_product(cross_full, w_cross_out)
        result, normed_three, inv_three = norm_forward(
            y_in.astype(jnp.float32) + cross_branch, cross_gain, cross_bias
        )
        outputs.append(result)
        grad_three, gain_part, bias_part = norm_back(
            cotangent[micro].astype(jnp.float32), normed_three, inv_three, cross_gain
        )
        norm_accs[4] = norm_accs[4] + gain_part
        norm_accs[5] = norm_accs[5] + bias_part
        branch_full = gather_cols(grad_three.astype(jnp.bfloat16))
        cross_out_acc = cross_out_acc + weight_grad(cross_full, branch_full)
        cross_mix_grad = (
            rows_product(branch_full, w_cross_out.T)
            .astype(jnp.bfloat16)
            .reshape(stream_count, seq_rows, length, head_count, head_dim)
        )
        query_grad, key_grad, value_grad, table_grad = attend_back(
            cross_query,
            cross_key,
            cross_value,
            segment,
            cross_offsets,
            onehot,
            cross_lse,
            cross_mix_grad,
        )
        cross_table_acc = cross_table_acc + table_grad
        query_low = query_grad.reshape(stream_count, row_tokens, col_width).astype(jnp.bfloat16)
        keyval_low = (
            jnp.stack(
                [
                    key_grad.reshape(row_tokens, col_width),
                    value_grad.reshape(row_tokens, col_width),
                ],
                axis=1,
            )
            .reshape(1, row_tokens, 2 * col_width)
            .astype(jnp.bfloat16)
        )
        query_full = gather_rows(query_low)
        query_acc = query_acc + weight_grad(stream_full, query_full)
        stream_grads.append(grad_three + cols_product(query_full, w_query.T))
        keyval_full = gather_rows(keyval_low)
        keyval_acc = keyval_acc + weight_grad(enc_full, keyval_full)
        encoded_grad = cols_product(keyval_full, keyval_matrix.T)
        grad_two, gain_part, bias_part = norm_back(encoded_grad, normed_two, inv_two, ffn_gain)
        norm_accs[2] = norm_accs[2] + gain_part
        norm_accs[3] = norm_accs[3] + bias_part
        feedforward_full_output = gather_cols(grad_two.astype(jnp.bfloat16))
        down_acc = down_acc + weight_grad(act_full, feedforward_full_output)
        act_grad = rows_product(feedforward_full_output, w_down.T)
        pre_low = gelu_pull(act_grad)[0].astype(jnp.bfloat16)
        pre_full = gather_rows(pre_low)
        up_acc = up_acc + weight_grad(hidden_full, pre_full)
        hidden_grad = grad_two + cols_product(pre_full, w_up.T)
        grad_one, gain_part, bias_part = norm_back(
            hidden_grad, normed_one, inv_one, attention_norm_gain
        )
        norm_accs[0] = norm_accs[0] + gain_part
        norm_accs[1] = norm_accs[1] + bias_part
        attn_full = gather_cols(grad_one.astype(jnp.bfloat16))
        out_acc = out_acc + weight_grad(mix_full, attn_full)
        enc_mix_grad = (
            rows_product(attn_full, w_out.T)
            .astype(jnp.bfloat16)
            .reshape(1, seq_rows, length, head_count, head_dim)
        )
        enc_qgrad, enc_kgrad, enc_vgrad, table_grad = attend_back(
            enc_query,
            enc_key,
            encoder_value_rows,
            segment,
            enc_offsets,
            onehot,
            enc_lse,
            enc_mix_grad,
        )
        enc_table_acc = enc_table_acc + table_grad
        qkv_low = (
            jnp.stack(
                [
                    enc_qgrad.reshape(row_tokens, col_width),
                    enc_kgrad.reshape(row_tokens, col_width),
                    enc_vgrad.reshape(row_tokens, col_width),
                ],
                axis=1,
            )
            .reshape(1, row_tokens, 3 * col_width)
            .astype(jnp.bfloat16)
        )
        qkv_full = gather_rows(qkv_low)
        qkv_acc = qkv_acc + weight_grad(x_full, qkv_full)
        token_grads.append((grad_one + cols_product(qkv_full, qkv_matrix.T))[0])
    norm_stack = jnp.stack(norm_accs)
    table_stack = jnp.stack([enc_table_acc, cross_table_acc])
    norm_sums = lax.psum(norm_stack, COL)
    table_sums = lax.psum(table_stack, ROW)
    return (
        jnp.stack(outputs),
        jnp.stack(token_grads),
        jnp.stack(stream_grads),
        qkv_acc.reshape(row_width, 3, col_width),
        table_sums[0],
        out_acc,
        norm_sums[0],
        norm_sums[1],
        up_acc,
        down_acc,
        norm_sums[2],
        norm_sums[3],
        query_acc,
        keyval_acc.reshape(row_width, 2, col_width),
        table_sums[1],
        cross_out_acc,
        norm_sums[4],
        norm_sums[5],
    )


def mm(a,b):
    return jnp.dot(a,b,preferred_element_type=F32)
def mm_nt(a,b):
    return lax.dot_general(a,b,(((1,),(1,)),((),())),preferred_element_type=F32)

def bias_tiles(off_ref, t_ref, index, length, width):
    chunks = 2 * length // width - 1
    for c in range(chunks):
        lo = (chunks - 1 - c) * width
        row = jnp.broadcast_to(off_ref[index + (slice(None), pl.ds(lo, 2 * width))], (width, 2 * width))
        rolled = pltpu.roll(row, 0, 1, stride=1, stride_axis=0)
        t_ref[index + (pl.ds(c * width, width),)] = rolled[:, width:]


def panel_rows(panel, length, width):
    return slice((length // width - 1 - panel) * width, (2 * length // width - 1 - panel) * width)


def panel_forward(keys, values, query, bias):
    logits = mm(keys, query) + bias
    top = jnp.max(logits, axis=0, keepdims=True)
    weight = jnp.exp(logits - top)
    total = jnp.sum(weight, axis=0, keepdims=True)
    return (mm(values, weight.astype(BF)) * (1.0 / total)).astype(BF), top + jnp.log(total)


def panel_backward(keys, keys_t, values_t, query, grad, lse, bias):
    prob = jnp.exp(mm(keys, query) + (bias - lse))
    dprob = mm(values_t, grad)
    dlogits = prob * (dprob - jnp.sum(prob * dprob, axis=0, keepdims=True))
    low = dlogits.astype(BF)
    return dlogits, mm(keys_t, low).astype(BF), mm_nt(query, low), mm_nt(grad, prob.astype(BF))


def scaled(value, scale):
    return (value.astype(F32) * scale).astype(BF)


def offset_sums(g_ref, doff_ref, g_index, out_index, length, width):
    chunks = 2 * length // width - 1
    doff_ref[out_index] = jnp.zeros((1, 2 * length), F32)
    sub = lax.broadcasted_iota(jnp.int32, (8, 2 * width), 0)
    for c in range(chunks):
        acc = jnp.zeros((8, 2 * width), F32)
        for i in range(width // 8):
            piece = g_ref[g_index + (pl.ds(c * width + 8 * i, 8),)]
            padded = jnp.concatenate([jnp.zeros((8, width), F32), piece], axis=1)
            acc = acc + (pltpu.roll(padded, 2 * width - 8 * i, 1) if i else padded)
        for b in (1, 2, 4):
            acc = jnp.where((sub // b) % 2 == 1, pltpu.roll(acc, 2 * width - b, 1), acc)
        lo = (chunks - 1 - c) * width
        doff_ref[out_index + (slice(None), pl.ds(lo, 2 * width))] += jnp.sum(acc, axis=0, keepdims=True)


def fwd_kernel(length, width, off_ref, segq_ref, segk_ref, q_ref, k_ref, v_ref, mix_ref, lse_ref, t_ref):
    for table in range(off_ref.shape[0]):
        bias_tiles(off_ref, t_ref, (table, 0), length, width)
    keys, values = k_ref[0].T, v_ref[0]
    scale = k_ref.shape[1] ** -0.5
    for p in range(length // width):
        here = slice(p * width, (p + 1) * width)
        bias = jnp.where(segk_ref[...] <= segq_ref[:, here], t_ref[0, 0, panel_rows(p, length, width), :], neg_fill)
        mix_ref[0, :, here], lse_ref[0, :, here] = panel_forward(keys, values, scaled(q_ref[0, :, here], scale), bias)


def bwd_kernel(length, width, t_ref, segq_ref, segk_ref, q_ref, k_ref, v_ref, lse_ref, dmix_ref, dqkv_ref, doff_ref, g_scr, dk_scr, dv_scr):
    keys_t, values_t = k_ref[0], v_ref[0].T
    keys = keys_t.T
    hd = keys_t.shape[0]
    scale = hd**-0.5
    keys_scaled = scaled(keys_t, scale)
    g_scr[...] = jnp.zeros_like(g_scr)
    dk_scr[...] = jnp.zeros_like(dk_scr)
    dv_scr[...] = jnp.zeros_like(dv_scr)
    for p in range(length // width):
        rows = panel_rows(p, length, width)
        here = slice(p * width, (p + 1) * width)
        bias = jnp.where(segk_ref[...] <= segq_ref[:, here], t_ref[0, 0, rows, :], neg_fill)
        query = scaled(q_ref[0, :, here], scale)
        dlogits, dq, dk, dv = panel_backward(
            keys, keys_scaled, values_t, query, dmix_ref[0, :, here], lse_ref[0, :, here], bias
        )
        g_scr[rows, :] += dlogits
        dqkv_ref[0, :hd, here] = dq
        dk_scr[...] += dk
        dv_scr[...] += dv
    dqkv_ref[0, hd : 2 * hd] = dk_scr[...].astype(BF)
    dqkv_ref[0, 2 * hd :] = dv_scr[...].astype(BF)
    offset_sums(g_scr, doff_ref, (), (0,), length, width)


def attention(off_rev, segq, segk, qkv):
    heads, hd, length = qkv.shape[0], qkv.shape[1] // 3, qkv.shape[2]
    width = segk.shape[1]
    blk = lambda part: pl.BlockSpec((1, hd, length), lambda h: (h, part, 0))
    tile = (2, 1, 2 * length - width, width)
    shape = jax.ShapeDtypeStruct
    return pl.pallas_call(
        functools.partial(fwd_kernel, length, width),
        grid=(heads,),
        in_specs=[
            pl.BlockSpec((2, 1, 1, 2 * length), lambda h: (0, h, 0, 0)),
            pl.BlockSpec((1, length), lambda h: (0, 0)),
            pl.BlockSpec((length, width), lambda h: (0, 0)),
            blk(0),
            blk(1),
            blk(2),
        ],
        out_specs=[blk(0), pl.BlockSpec((1, 1, length), lambda h: (h, 0, 0)), pl.BlockSpec(tile, lambda h: (0, h, 0, 0))],
        out_shape=[shape((heads, hd, length), BF), shape((heads, 1, length), F32), shape((2, heads) + tile[2:], F32)],
        compiler_params=pltpu.CompilerParams(vmem_limit_bytes=48 << 20),
        name="attend",
    )(off_rev, segq, segk, qkv, qkv, qkv)


def attention_back(tiles, segq, segk, qkv, lse, dmix):
    heads, hd, length = qkv.shape[0], qkv.shape[1] // 3, qkv.shape[2]
    width = segk.shape[1]
    blk = lambda part: pl.BlockSpec((1, hd, length), lambda h: (h, part, 0))
    line = lambda n: pl.BlockSpec((1, 1, n), lambda h: (h, 0, 0))
    tile = (1, 1, 2 * length - width, width)
    shape = jax.ShapeDtypeStruct
    return pl.pallas_call(
        functools.partial(bwd_kernel, length, width),
        grid=(heads,),
        in_specs=[
            pl.BlockSpec(tile, lambda h: (0, h, 0, 0)),
            pl.BlockSpec((1, length), lambda h: (0, 0)),
            pl.BlockSpec((length, width), lambda h: (0, 0)),
            blk(0),
            blk(1),
            blk(2),
            line(length),
            blk(0),
        ],
        out_specs=[pl.BlockSpec((1, 3 * hd, length), lambda h: (h, 0, 0)), line(2 * length)],
        out_shape=[shape(qkv.shape, BF), shape((heads, 1, 2 * length), F32)],
        scratch_shapes=[pltpu.VMEM(tile[2:], F32), pltpu.VMEM((hd, length), F32), pltpu.VMEM((hd, length), F32)],
        compiler_params=pltpu.CompilerParams(vmem_limit_bytes=48 << 20),
        name="attend_back",
    )(tiles, segq, segk, qkv, qkv, qkv, lse, dmix)


MESH = pl.DeviceIdType.MESH
FORWARD, BACKWARD = range(2)
ACROSS, THROUGH, ALONG, SUM_ACROSS, SUM_ALONG = range(5)


def spot():
    row, col = lax.axis_index(ROW), lax.axis_index(COL)
    return row // 2, row % 2, col // 2, col % 2


def device(y, k, seq, half):
    return (2 * y + k, 2 * seq + half)


def greet(devices):
    barrier = pltpu.get_barrier_semaphore()
    for target in devices:
        pl.semaphore_signal(barrier, inc=1, device_id=target, device_id_type=MESH)
    pl.semaphore_wait(barrier, len(devices))


def remote(source, target, send_sem, recv_sem, device_id):
    copy = pltpu.make_async_remote_copy(
        src_ref=source, dst_ref=target, send_sem=send_sem, recv_sem=recv_sem, device_id=device_id, device_id_type=MESH
    )
    copy.start()
    return copy


def lanes(start, size):
    return pl.ds(pl.multiple_of(start, size), size)


def rows_of(place):
    y, k, seq, half = place
    return [(dy, dk, (1 - y if dy else y), (1 - k if dk else k)) for dy, dk in ((0, 1), (1, 0), (1, 1))]


class Spread:
    def __init__(self, full_ref, half_sems, core_sems, place, rows):
        self.full, self.place, self.rows = full_ref, place, rows
        self.half_sems, self.core_sems = half_sems, core_sems
        self.first, self.second = {}, {}

    def block(self, n, piece, half, k):
        return self.full.at[n, half, k, pl.ds(piece * self.rows, self.rows)]

    def start(self, unit, n, piece):
        y, k, seq, half = self.place
        mine = self.block(n, piece, half, k)
        hs, cs = self.half_sems, self.core_sems
        self.first[unit] = (
            remote(mine, mine, hs.at[0, unit], hs.at[1, unit], device(y, k, seq, 1 - half)),
            remote(mine, mine, cs.at[0, unit, 0], cs.at[1, unit, 0], device(y, 1 - k, seq, half)),
        )

    def forward(self, unit, n, piece):
        y, k, seq, half = self.place
        self.first[unit][0].wait_recv()
        theirs = self.block(n, piece, 1 - half, k)
        cs = self.core_sems
        self.second[unit] = remote(theirs, theirs, cs.at[0, unit, 1], cs.at[1, unit, 1], device(y, 1 - k, seq, half))

    def ready(self, unit):
        self.first[unit][1].wait_recv()
        self.second[unit].wait_recv()

    def sent(self, unit):
        for copy in self.first[unit] + (self.second[unit],):
            copy.wait_send()

    def finish(self, unit):
        self.ready(unit)
        self.sent(unit)


class Reduce:
    def __init__(self, partial_ref, core_buf, half_send, half_buf, core_sems, half_sems, place, rows):
        self.partial, self.core_buf, self.half_send, self.half_buf = partial_ref, core_buf, half_send, half_buf
        self.core_sems, self.half_sems, self.place, self.rows = core_sems, half_sems, place, rows
        self.first, self.second = {}, {}

    def part(self, n, piece, half, k):
        return (n, half, k, pl.ds(piece * self.rows, self.rows))

    def start(self, unit, n, piece, away):
        y, k, seq, half = self.place
        side = 1 - half if away else half
        cs = self.core_sems
        lane = 0 if away else 1
        self.first[unit, lane] = remote(
            self.partial.at[self.part(n, piece, side, 1 - k)],
            self.core_buf.at[unit, lane],
            cs.at[0, unit, lane],
            cs.at[1, unit, lane],
            device(y, 1 - k, seq, half),
        )

    def pass_on(self, unit, n, piece):
        y, k, seq, half = self.place
        self.first[unit, 0].wait_recv()
        away = self.partial[self.part(n, piece, 1 - half, k)].astype(F32) + self.core_buf[unit, 0].astype(F32)
        self.half_send[unit] = away.astype(BF)
        hs = self.half_sems
        self.second[unit] = remote(
            self.half_send.at[unit], self.half_buf.at[unit], hs.at[0, unit], hs.at[1, unit], device(y, k, seq, 1 - half)
        )

    def result(self, unit, n, piece):
        y, k, seq, half = self.place
        self.first[unit, 1].wait_recv()
        mine = self.partial[self.part(n, piece, half, k)].astype(F32) + self.core_buf[unit, 1].astype(F32)
        self.second[unit].wait_recv()
        return mine + self.half_buf[unit].astype(F32)

    def finish(self, unit):
        self.first[unit, 0].wait_send()
        self.first[unit, 1].wait_send()
        self.second[unit].wait_send()


class Return:
    def __init__(self, own_ref, landing, sems, place, feat):
        self.own, self.landing, self.sems, self.place, self.feat = own_ref, landing, sems, place, feat
        self.copies = []

    def start(self, unit, n, value):
        y, k, seq, half = self.place
        feat = self.feat
        self.own[unit] = value
        self.landing[y, n, k] = jnp.where(k == 0, value[:, :feat], value[:, feat : 2 * feat])
        for i, (dy, dk, ty, tk) in enumerate(rows_of(self.place)):
            self.copies.append(
                remote(
                    self.own.at[unit, :, lanes(tk * feat + 2 * dy * feat, feat)],
                    self.landing.at[y, n, k],
                    self.sems.at[0, unit, i],
                    self.sems.at[1, unit, i],
                    device(ty, tk, seq, half),
                )
            )

    def finish(self):
        for copy in self.copies:
            copy.wait()


class Freight:
    def __init__(self, full_ref, z_sems, y_sems, place, seqs):
        self.full, self.place, self.seqs = full_ref, place, seqs
        self.z_sems, self.y_sems = z_sems, y_sems
        self.wide = full_ref.shape[2] // 2
        self.z, self.y = {}, {}
        self.turn = seqs // 2

    def along(self, d):
        y, k, seq, half = self.place
        up = d <= self.turn
        source = d - 1 if up else (d + 1) % self.seqs
        if source:
            self.z[source].wait_recv()
        target = lax.rem(seq + (1 if up else self.seqs - 1), self.seqs)
        self.z[d] = remote(
            self.full.at[source, :, : self.wide],
            self.full.at[d, :, : self.wide],
            self.z_sems.at[0, d - 1],
            self.z_sems.at[1, d - 1],
            device(y, k, target, half),
        )

    def first(self):
        return [d for d in (1, self.seqs - 1) if d <= self.turn or d > self.turn][: min(2, self.seqs - 1)]

    def later(self):
        return list(range(2, self.turn + 1)) + list(range(self.seqs - 2, self.turn, -1))

    def last(self):
        return [d for d in range(1, self.seqs) if d == self.turn or d == self.turn + 1]

    def across(self, d):
        y, k, seq, half = self.place
        self.y[d] = remote(
            self.full.at[d, :, : self.wide],
            self.full.at[d, :, self.wide :],
            self.y_sems.at[0, d],
            self.y_sems.at[1, d],
            device(1 - y, k, seq, half),
        )

    def pass_along(self, cross):
        for d in self.later():
            self.along(d)
            if cross:
                self.across(d - 1 if d <= self.turn else d + 1)
        for d in self.last():
            self.z[d].wait_recv()
            if cross:
                self.across(d)

    def finish(self):
        for copy in self.z.values():
            copy.wait_send()
        for copy in self.y.values():
            copy.wait()


class Collect:
    def __init__(self, source, place, seqs, y_refs=None, z_refs=None):
        self.source, self.place, self.seqs = source, place, seqs
        self.y_refs, self.z_refs = y_refs, z_refs
        self.wide = source.shape[2] // 2 if y_refs else source.shape[2]
        self.turn = seqs // 2
        self.order = list(range(self.turn, seqs)) + list(range(self.turn - 1, -1, -1))
        self.y, self.z, self.core = {}, {}, None

    def across(self):
        y, k, seq, half = self.place
        buf, sems = self.y_refs
        for d in self.order:
            self.y[d] = remote(
                self.source.at[d, :, self.wide :], buf.at[d], sems.at[0, d], sems.at[1, d], device(1 - y, k, seq, half)
            )

    def total(self, d):
        if not self.y_refs:
            return self.source[d].astype(F32)
        self.y[d].wait_recv()
        return self.source[d, :, : self.wide].astype(F32) + self.y_refs[0][d].astype(F32)

    def store(self, out):
        for d in self.order:
            out[d] = self.total(d).astype(BF)

    def along(self, d):
        y, k, seq, half = self.place
        out, z_send, z_buf, c_send, z_sems, c_sems = self.z_refs
        left = d <= self.turn
        before = d + 1 if left else d - 1
        value = self.total(d)
        if before in self.z and before not in (self.turn + 1 if left else self.turn,):
            self.z[before].wait_recv()
            value = value + z_buf[before - 1].astype(F32)
        z_send[d - 1] = value.astype(BF)
        target = lax.rem(seq + (self.seqs - 1 if left else 1), self.seqs)
        self.z[d] = remote(
            z_send.at[d - 1], z_buf.at[d - 1], z_sems.at[0, d - 1], z_sems.at[1, d - 1], device(y, k, target, half)
        )

    def close(self):
        y, k, seq, half = self.place
        out, z_send, z_buf, c_send, z_sems, c_sems = self.z_refs
        total = self.total(0)
        for d in sorted({1, self.seqs - 1}):
            self.z[d].wait_recv()
            total = total + z_buf[d - 1].astype(F32)
        low, high = total[:, : self.wide // 2], total[:, self.wide // 2 :]
        out[k] = jnp.where(k == 0, low, high)
        c_send[...] = jnp.where(k == 0, high, low)
        self.core = remote(c_send, out.at[k], c_sems.at[0], c_sems.at[1], device(y, 1 - k, seq, half))

    def finish(self):
        for copy in self.y.values():
            copy.wait_send()
        for copy in self.z.values():
            copy.wait_send()
        if self.core is not None:
            self.core.wait()


def freight_scratch(seqs):
    dma = pltpu.SemaphoreType.DMA
    return [dma((2, seqs - 1)), dma((2, seqs))]


def across_scratch(seqs, n, wide):
    return [pltpu.VMEM((seqs, n, wide), BF), pltpu.SemaphoreType.DMA((2, seqs))]


def along_scratch(seqs, n, wide):
    dma = pltpu.SemaphoreType.DMA
    return [
        pltpu.VMEM((seqs - 1, n, wide), BF),
        pltpu.VMEM((seqs - 1, n, wide), BF),
        pltpu.VMEM((n, wide // 2), F32),
        dma((2, seqs - 1)),
        dma((2,)),
    ]


def along_devices(place, seqs):
    y, k, seq, half = place
    return [device(y, k, lax.rem(seq + d, seqs), half) for d in sorted({1, seqs - 1})]


def shuffle(source, target, n, index, place, sends, receives, local_sems):
    y, k, seq, half = place
    feat = source.shape[-1]
    copies = [pltpu.make_async_copy(source.at[y, n, k], target.at[n, :, lanes(k * feat, feat)], local_sems.at[index])]
    copies[0].start()
    for i, (dy, dk, ty, tk) in enumerate(rows_of(place)):
        copies.append(
            remote(
                source.at[ty, n, tk],
                target.at[n, :, lanes(k * feat + 2 * dy * feat, feat)],
                sends.at[index, i],
                receives.at[index, i],
                device(ty, tk, seq, half),
            )
        )
    return copies


def normalize(residual):
    centered = residual - jnp.mean(residual, axis=-1, keepdims=True)
    inv_std = lax.rsqrt(jnp.mean(centered * centered, axis=-1, keepdims=True) + epsilon)
    return centered * inv_std, inv_std


def normalize_back(out_grad, normed, inv_std, gain):
    scaled = out_grad * gain
    first = jnp.mean(scaled, axis=-1, keepdims=True)
    second = jnp.mean(scaled * normed, axis=-1, keepdims=True)
    return inv_std * (scaled - first - normed * second)


def column_sum(value):
    return jnp.sum(value, axis=0, keepdims=True)


def exchange_kernel(kind, count, pieces, seqs, rides, *refs):
    place = spot()
    y, k, seq, half = place
    refs = list(refs)
    take = lambda amount: [refs.pop(0) for _ in range(amount)]
    r = types.SimpleNamespace()
    partial, r.resid, r.norm = take(3)
    if kind == BACKWARD:
        r.normed, r.inv = take(2)
    ride_in = take(len(rides))
    (r.full,) = take(1)
    if kind == FORWARD:
        r.out, r.normed, r.inv = take(3)
    else:
        r.grad, r.sums = take(2)
    ride_out = take(len(rides))
    core_buf, half_send, half_buf, rc, rh, gh, gc = take(7)
    rows = partial.shape[3] // pieces
    peers = [device(y, 1 - k, seq, half), device(y, k, seq, 1 - half)]
    if {ACROSS, THROUGH, SUM_ACROSS} & set(rides):
        peers.append(device(1 - y, k, seq, half))
    if {ALONG, THROUGH, SUM_ALONG} & set(rides):
        peers += along_devices(place, seqs)
    greet(peers)
    units = [(n * pieces + p, n, p) for n in range(count) for p in range(pieces)]
    reduce = Reduce(partial, core_buf, half_send, half_buf, rc, rh, place, rows)
    spread = Spread(r.full, gh, gc, place, rows)
    for unit, n, p in units:
        reduce.start(unit, n, p, True)
    for unit, n, p in units:
        reduce.start(unit, n, p, False)
    moves, sums_along, sums_across = [], [], []
    for ride, source, target in zip(rides, ride_in, ride_out):
        if ride == SUM_ACROSS:
            sums_across.append((Collect(source, place, seqs, y_refs=take(2)), target))
            sums_across[-1][0].across()
        elif ride == SUM_ALONG:
            sums_along.append(Collect(source, place, seqs, z_refs=[target] + take(5)))
            for d in sums_along[-1].order[:2]:
                sums_along[-1].along(d)
        else:
            moves.append((ride, Freight(target, *take(2), place, seqs)))
            if ride == ACROSS:
                for d in range(seqs):
                    moves[-1][1].across(d)
            else:
                if ride == THROUGH:
                    moves[-1][1].across(0)
                for d in moves[-1][1].first():
                    moves[-1][1].along(d)
    if kind != FORWARD:
        r.sums[...] = jnp.zeros_like(r.sums)
    gain, bias = r.norm[0:1], r.norm[1:2]
    for unit, n, p in units:
        reduce.pass_on(unit, n, p)
    for unit, n, p in units:
        here = pl.ds(p * rows, rows)
        branch = reduce.result(unit, n, p)
        if kind == FORWARD:
            normed, inv = normalize(r.resid[n, here].astype(F32) + branch)
            value = normed * gain + bias
            r.out[n, here] = value
            r.normed[n, here] = normed
            r.inv[n, here] = inv
        else:
            upstream = r.resid[n, here] + branch if r.resid.shape[1] == partial.shape[3] else branch
            normed = r.normed[n, here]
            value = normalize_back(upstream, normed, r.inv[n, here], gain)
            r.grad[n, here] = value
        r.full[n, half, k, here] = value.astype(BF)
        spread.start(unit, n, p)
        if kind != FORWARD:
            r.sums[0:1] += column_sum(upstream * normed)
            r.sums[1:2] += column_sum(upstream)
    for collect in sums_along:
        for d in collect.order[2:-1]:
            collect.along(d)
    for ride, move in moves:
        if ride != ACROSS:
            move.pass_along(ride == THROUGH)
    for unit, n, p in units:
        spread.forward(unit, n, p)
    for collect in sums_along:
        collect.close()
    for unit, n, p in units:
        spread.finish(unit)
        reduce.finish(unit)
    for ride, move in moves:
        move.finish()
    for collect, target in sums_across:
        collect.store(target)
        collect.finish()
    for collect in sums_along:
        collect.finish()


def exchange(kind, collective_id, seqs, partial, resid, norm, normed=None, inv=None, rides=()):
    count, _, _, own, depth = partial.shape
    pieces = 2 if count == 1 else 1
    units, rows = count * pieces, own // pieces
    dma = pltpu.SemaphoreType.DMA
    shape = jax.ShapeDtypeStruct
    vmem = pl.BlockSpec(memory_space=pltpu.VMEM)
    anywhere = pl.BlockSpec(memory_space=pl.ANY)
    full = shape((count, 2, 2, own, depth), BF)
    grad, sums = shape((count, own, depth), F32), shape((8, depth), F32)
    scratch = []
    if kind == FORWARD:
        args = (partial, resid, norm)
        outs = (full, grad, grad, shape((count, own, 1), F32))
    else:
        args = (partial, resid, norm, normed, inv)
        outs = (full, grad, sums)
    scratch += [
        pltpu.VMEM((units, 2, rows, depth), BF),
        pltpu.VMEM((units, rows, depth), BF),
        pltpu.VMEM((units, rows, depth), BF),
        dma((2, units, 2)),
        dma((2, units)),
        dma((2, units)),
        dma((2, units, 2)),
    ]
    in_specs, out_specs = [vmem] * len(args), [vmem] * len(outs)
    aliases = {}
    for ride, array in rides:
        if ride == SUM_ACROSS or ride == SUM_ALONG:
            n, wide = array.shape[1], depth // 2
            scratch += (across_scratch if ride == SUM_ACROSS else along_scratch)(seqs, n, wide)
            in_specs.append(vmem)
            out_specs.append(vmem)
            outs += (shape((seqs, n, wide), BF) if ride == SUM_ACROSS else shape((2, n, wide // 2), F32),)
        else:
            scratch += freight_scratch(seqs)
            aliases[len(args)] = len(outs)
            in_specs.append(anywhere)
            out_specs.append(anywhere)
            outs += (shape(array.shape, array.dtype),)
        args += (array,)
    return pl.pallas_call(
        functools.partial(exchange_kernel, kind, count, pieces, seqs, tuple(ride for ride, _ in rides)),
        out_shape=outs,
        in_specs=in_specs,
        out_specs=tuple(out_specs),
        scratch_shapes=scratch,
        input_output_aliases=aliases,
        compiler_params=pltpu.CompilerParams(collective_id=collective_id, has_side_effects=True, vmem_limit_bytes=50 << 20),
        name="exchange_%d" % collective_id,
    )(*args)


def cross_kernel(count, query, kv, out_weight, tiles, segq, segk, resid, norm, cot, mix, full, output, grad, sums, dquery, dkv, doff, partial, lse, keys, keys_scaled, values_t, queries, masked, g_scr, dk_scr, dv_scr, dmix, own, landing, return_sems, cot_own, cot_send, cot_recv, cot_local, core_buf, half_send, half_buf, rc, rh, gh, gc):
    place = spot()
    y, k, seq, half = place
    heads, hd, length = query.shape[0], query.shape[1], kv.shape[2]
    width, depth, rows = segk.shape[1], partial.shape[4], partial.shape[3]
    panels, scale = length // width, hd**-0.5
    greet(
        [device(y, 1 - k, seq, half), device(y, k, seq, 1 - half)]
        + [device(ty, tk, seq, half) for dy, dk, ty, tk in rows_of(place) if dy]
    )
    cots = [shuffle(cot, cot_own, n, n, place, cot_send, cot_recv, cot_local) for n in range(count)]
    reduce = Reduce(partial, core_buf, half_send, half_buf, rc, rh, place, rows)
    spread = Spread(full, gh, gc, place, rows)
    back = Return(own, landing, return_sems, place, depth // 4)
    sums[...] = jnp.zeros_like(sums)
    g_scr[...] = jnp.zeros_like(g_scr)
    dk_scr[...] = jnp.zeros_like(dk_scr)
    dv_scr[...] = jnp.zeros_like(dv_scr)

    def prepare(h, carry):
        keys[h] = kv[h, :hd].T
        keys_scaled[h] = scaled(kv[h, :hd], scale)
        values_t[h] = kv[h, hd:].T
        queries[h] = scaled(query[h], scale)
        for p in range(panels):
            here = slice(p * width, (p + 1) * width)
            bias = tiles[0, h, panel_rows(p, length, width), :]
            masked[h, p] = jnp.where(segk[...] <= segq[:, here], bias, neg_fill)
        return carry

    lax.fori_loop(0, heads, prepare, 0)

    def attend_heads(s, low, high):
        def one(h, carry):
            for p in range(panels):
                here = slice(s * length + p * width, s * length + (p + 1) * width)
                mixed, total = panel_forward(keys[h], kv[h, hd:], queries[h, :, here], masked[h, p])
                mix[h, :, here] = mixed
                lse[h, :, here] = total
            return carry

        lax.fori_loop(low, high, one, 0)

    def project(s):
        for a in range(2):
            for b in range(2):
                start = s * length + (2 * a + b) * rows
                mixed = mix[:, :, start : start + rows].reshape(heads * hd, rows)
                partial[s, a, b] = lax.dot_general(
                    mixed, out_weight[...], (((0,), (0,)), ((), ())), preferred_element_type=F32
                ).astype(BF)
        reduce.start(s, s, 0, True)
        reduce.start(s, s, 0, False)

    def turn(s):
        normed, inv = normalize(resid[s].astype(F32) + reduce.result(s, s, 0))
        for copy in cots[s]:
            copy.wait()
        upstream = cot_own[s].astype(F32)
        value = normalize_back(upstream, normed, inv, norm[0:1])
        grad[s] = value
        full[s, half, k] = value.astype(BF)
        spread.start(s, s, 0)
        sums[0:1] += column_sum(upstream * normed)
        sums[1:2] += column_sum(upstream)
        back.start(s, s, (normed * norm[0:1] + norm[1:2]).astype(BF))

    def attend_back(s):
        for a in range(2):
            for b in range(2):
                start = (2 * a + b) * rows
                low = mm_nt(out_weight[...], full[s, a, b]).astype(BF)
                dmix[:, :, start : start + rows] = low.reshape(heads, hd, rows)

        def one(h, carry):
            for p in range(panels):
                here = slice(p * width, (p + 1) * width)
                there = slice(s * length + p * width, s * length + (p + 1) * width)
                around = panel_rows(p, length, width)
                dlogits, dq, dk, dv = panel_backward(
                    keys[h], keys_scaled[h], values_t[h], queries[h, :, there], dmix[h, :, here], lse[h, :, there], masked[h, p]
                )
                g_scr[h, around, :] += dlogits
                dquery[h, :, there] = dq
                dk_scr[h] += dk
                dv_scr[h] += dv
            return carry

        lax.fori_loop(0, heads, one, 0)

    for s in range(count):
        attend_heads(s, 0, heads // 2)
        if s >= 1:
            reduce.pass_on(s - 1, s - 1, 0)
        if s >= 2:
            turn(s - 2)
        attend_heads(s, heads // 2, heads)
        project(s)
    reduce.pass_on(count - 1, count - 1, 0)
    for s in range(max(count - 2, 0), count):
        turn(s)
    for s in range(count):
        spread.forward(s, s, 0)
        spread.ready(s)
        attend_back(s)
    for h in range(heads):
        dkv[h, :hd] = dk_scr[h].astype(BF)
        dkv[h, hd:] = dv_scr[h].astype(BF)

    def offsets_of(h, carry):
        offset_sums(g_scr, doff, (h,), (h,), length, width)
        return carry

    lax.fori_loop(0, heads, offsets_of, 0)
    back.finish()
    output[...] = landing[...].astype(F32)
    for s in range(count):
        spread.sent(s)
        reduce.finish(s)


def cross_attention(collective_id, query, kv, out_weight, tiles, segq, segk, resid, norm, cot):
    count, own, depth = resid.shape
    heads, hd, total = query.shape
    length, width = kv.shape[2], segk.shape[1]
    dma = pltpu.SemaphoreType.DMA
    shape = jax.ShapeDtypeStruct
    tile_rows = tiles.shape[2]
    outs = (
        shape(query.shape, BF),
        shape((count, 2, 2, own, depth), BF),
        shape((2, count, 2, own, depth // 4), F32),
        shape((count, own, depth), F32),
        shape((8, depth), F32),
        shape(query.shape, BF),
        shape(kv.shape, BF),
        shape((heads, 1, 2 * length), F32),
    )
    whole = pl.BlockSpec(memory_space=pltpu.VMEM)
    specs = [whole] * 9
    specs[3] = pl.BlockSpec((1, heads, tile_rows, width), lambda i: (1, 0, 0, 0))
    vmem = pltpu.VMEM
    return pl.pallas_call(
        functools.partial(cross_kernel, count),
        grid=(1,),
        out_shape=outs,
        in_specs=specs,
        out_specs=tuple(whole for _ in outs),
        scratch_shapes=[
            vmem((count, 2, 2, own, depth), BF),
            vmem((heads, 1, total), F32),
            vmem((heads, length, hd), BF),
            vmem((heads, hd, length), BF),
            vmem((heads, length, hd), BF),
            vmem(query.shape, BF),
            vmem((heads, length // width, length, width), F32),
            vmem((heads, tile_rows, width), F32),
            vmem((heads, hd, length), F32),
            vmem((heads, hd, length), F32),
            vmem((heads, hd, length), BF),
            vmem((count, own, depth), BF),
            vmem((2, count, 2, own, depth // 4), BF),
            dma((2, count, 3)),
            vmem((count, own, depth), BF),
            dma((count, 3)),
            dma((count, 3)),
            dma((count,)),
            vmem((count, 2, own, depth), BF),
            vmem((count, own, depth), BF),
            vmem((count, own, depth), BF),
            dma((2, count, 2)),
            dma((2, count)),
            dma((2, count)),
            dma((2, count, 2)),
        ],
        compiler_params=pltpu.CompilerParams(collective_id=collective_id, has_side_effects=True, vmem_limit_bytes=56 << 20),
        name="cross_attention",
    )(query, kv, out_weight, tiles, segq, segk, resid, norm, cot)


def inputs_kernel(seqs, groups, tok_ref, str_ref, norm_ref, ids_ref, tab_ref, *refs):
    refs = list(refs)
    take = lambda amount: [refs.pop(0) for _ in range(amount)]
    packs = take(groups)
    x_own, x_full, y_own, y_full, norm_all, ids_all, tab_all = take(7)
    fulls = take(groups)
    in_send, in_recv, in_local, xh, xc, yh, yc, small_sems, tab_sems, small_self, pack_sems, pack_self = take(12)
    place = spot()
    y, k, seq, half = place
    feat = tok_ref.shape[-1]
    own = tok_ref.shape[-2]
    row_peers = rows_of(place)
    others = [device(y, k, lax.rem(seq + d, seqs), half) for d in range(1, seqs)]
    greet([device(ty, tk, seq, half) for dy, dk, ty, tk in row_peers] + [device(y, k, seq, 1 - half)] + others)
    count = str_ref.shape[1]
    x_copies = shuffle(tok_ref, x_own, 0, 0, place, in_send, in_recv, in_local)
    loads = []
    for g in range(groups):
        here = fulls[g].at[0, :, lanes(k * feat, feat)]
        copy = pltpu.make_async_copy(packs[g].at[k], here, pack_self.at[g])
        copy.start()
        loads.append(
            (
                copy,
                remote(packs[g].at[1 - k], here, pack_sems.at[0, g], pack_sems.at[1, g], device(y, 1 - k, seq, half)),
            )
        )
    small = []
    for j, (source, target) in enumerate(((norm_ref, norm_all), (ids_ref, ids_all))):
        slot = (lambda dy: (slice(None), lanes(k * feat + 2 * dy * feat, feat))) if j == 0 else (lambda dy: (2 * y + k,))
        copy = pltpu.make_async_copy(source, target.at[slot(0)], small_self.at[j])
        copy.start()
        small.append(copy)
        for i, (dy, dk, ty, tk) in enumerate(row_peers):
            small.append(
                remote(source, target.at[slot(dy)], small_sems.at[0, j, i], small_sems.at[1, j, i], device(ty, tk, seq, half))
            )
    copy = pltpu.make_async_copy(tab_ref, tab_all.at[0], small_self.at[2])
    copy.start()
    small.append(copy)
    for d in range(1, seqs):
        small.append(remote(tab_ref, tab_all.at[d], tab_sems.at[0, d - 1], tab_sems.at[1, d - 1], others[d - 1]))
    freights = [Freight(full, *take(2), place, seqs) for full in fulls]
    for copy in loads[0]:
        copy.wait()
    for d in freights[0].first():
        freights[0].along(d)
    freights[0].across(0)
    for copy in x_copies:
        copy.wait()
    x_full[0, half, k] = x_own[0]
    x_spread = Spread(x_full, xh, xc, place, own)
    x_spread.start(0, 0, 0)
    y_copies = [shuffle(str_ref, y_own, n, 1 + n, place, in_send, in_recv, in_local) for n in range(count)]
    y_spread = Spread(y_full, yh, yc, place, own)
    for g in range(1, groups):
        for copy in loads[g]:
            copy.wait()
    x_spread.forward(0, 0, 0)
    for n in range(count):
        for copy in y_copies[n]:
            copy.wait()
        y_full[n, half, k] = y_own[n]
        y_spread.start(n, n, 0)
    freights[0].pass_along(True)
    for d in freights[1].first():
        freights[1].along(d)
    freights[1].across(0)
    for n in range(count):
        y_spread.forward(n, n, 0)
    for copy in small:
        copy.wait()
    freights[1].pass_along(True)
    for d in freights[2].first():
        freights[2].along(d)
    freights[2].pass_along(False)
    x_spread.finish(0)
    for n in range(count):
        y_spread.finish(n)
    for freight in freights:
        freight.finish()


def gather_inputs(seqs, tokens, streams, norm, ids, table, packs):
    count, own, feat = streams.shape[1], streams.shape[-2], streams.shape[-1]
    depth = 4 * feat
    dma = pltpu.SemaphoreType.DMA
    shape = jax.ShapeDtypeStruct
    vmem = pl.BlockSpec(memory_space=pltpu.VMEM)
    outs = (
        shape((1, own, depth), BF),
        shape((1, 2, 2, own, depth), BF),
        shape((count, own, depth), BF),
        shape((count, 2, 2, own, depth), BF),
        shape((norm.shape[0], depth), F32),
        shape((4,) + ids.shape, jnp.int32),
        shape((seqs,) + table.shape, F32),
    )
    specs = [vmem] * len(outs)
    for pack in packs:
        outs += (shape((seqs, pack.shape[1], depth), BF),)
        specs.append(pl.BlockSpec(memory_space=pl.ANY))
    moves = 1 + count
    scratch = [
        dma((moves, 3)),
        dma((moves, 3)),
        dma((moves,)),
        dma((2, 1)),
        dma((2, 1, 2)),
        dma((2, count)),
        dma((2, count, 2)),
        dma((2, 2, 3)),
        dma((2, seqs - 1)),
        dma((3,)),
        dma((2, len(packs))),
        dma((len(packs),)),
    ]
    for _ in packs:
        scratch += freight_scratch(seqs)
    return pl.pallas_call(
        functools.partial(inputs_kernel, seqs, len(packs)),
        out_shape=outs,
        in_specs=[vmem] * (5 + len(packs)),
        out_specs=tuple(specs),
        scratch_shapes=scratch,
        compiler_params=pltpu.CompilerParams(collective_id=0, has_side_effects=True, vmem_limit_bytes=50 << 20),
        name="gather_inputs",
    )(tokens, streams, norm, ids, table, *packs)


def outputs_kernel(seqs, count, part_x, part_y, d1, d3, small, down, up, first, tok_out, str_out, small_out, down_out, up_out, first_out, core_buf, half_send, half_buf, own, land_x, land_y, rc, rh, rs, small_buf, ss, *refs):
    refs = list(refs)
    take = lambda amount: [refs.pop(0) for _ in range(amount)]
    place = spot()
    y, k, seq, half = place
    rows = part_x.shape[3]
    feat = part_x.shape[4] // 4
    bits = [1 << b for b in range((seqs - 1).bit_length())]
    flips = [device(y, k, seq + b - 2 * b * ((seq // b) % 2), half) for b in bits]
    others = [device(y, k, lax.rem(seq + d, seqs), half) for d in range(1, seqs)]
    partners = [device(y, 1 - k, seq, half), device(y, k, seq, 1 - half), device(1 - y, k, seq, half)]
    greet(partners + [device(1 - y, 1 - k, seq, half)] + others)
    partners += flips
    small_out[...] = small[...]

    def add_small(stage):
        copy = remote(small_out, small_buf.at[stage], ss.at[0, stage], ss.at[1, stage], partners[stage])
        copy.wait()
        small_out[...] += small_buf[stage]

    class Both:
        def __getitem__(self, index):
            return part_x[(0,) + index[1:]] if index[0] == 0 else part_y[(index[0] - 1,) + index[1:]]

        @property
        def at(self):
            return View()

    class View:
        def __getitem__(self, index):
            return part_x.at[(0,) + index[1:]] if index[0] == 0 else part_y.at[(index[0] - 1,) + index[1:]]

    reduce = Reduce(Both(), core_buf, half_send, half_buf, rc, rh, place, rows)
    units = range(count + 1)
    down = Collect(down, place, seqs, z_refs=[down_out] + take(5))
    up = Collect(up, place, seqs, y_refs=take(2), z_refs=[up_out] + take(5))
    first = Collect(first, place, seqs, y_refs=take(2), z_refs=[first_out] + take(5))
    reduce.start(0, 0, 0, True)
    reduce.start(0, 0, 0, False)
    add_small(2)
    up.across()
    add_small(1)
    reduce.pass_on(0, 0, 0)
    for stage in range(3, len(partners)):
        add_small(stage)
    for d in down.order[:2]:
        down.along(d)
    add_small(0)
    for unit in units[1:]:
        reduce.start(unit, unit, 0, True)
        reduce.start(unit, unit, 0, False)
    x_back = Return(own, land_x, rs, place, feat)
    y_back = Return(own, land_y, rs, place, feat)
    x_back.start(0, 0, (d1[0] + reduce.result(0, 0, 0)).astype(BF))
    first.across()
    for unit in units[1:]:
        reduce.pass_on(unit, unit, 0)
    for d in down.order[2:-1]:
        down.along(d)
    for d in up.order[:1]:
        up.along(d)
    down.close()
    for d in up.order[1:-1]:
        up.along(d)
    for unit in units[1:]:
        y_back.start(unit, unit - 1, (d3[unit - 1] + reduce.result(unit, unit, 0)).astype(BF))
    for unit in units:
        reduce.finish(unit)
    x_back.finish()
    tok_out[...] = land_x[:, 0].astype(F32)
    up.close()
    for d in first.order[:-1]:
        first.along(d)
    y_back.finish()
    str_out[...] = land_y[...].astype(F32)
    first.close()
    for collect in (down, up, first):
        collect.finish()


def scatter_outputs(seqs, collective_id, part_x, part_y, d1, d3, small, down, up, first):
    count, _, _, own, depth = part_y.shape
    feat, wide = depth // 4, depth // 2
    units = count + 1
    dma = pltpu.SemaphoreType.DMA
    shape = jax.ShapeDtypeStruct
    stages = 3 + (seqs - 1).bit_length()
    outs = (shape((2, 2, own, feat), F32), shape((2, count, 2, own, feat), F32), shape(small.shape, F32))
    outs += tuple(shape((2, group.shape[1], feat), F32) for group in (down, up, first))
    scratch = [
        pltpu.VMEM((units, 2, own, depth), BF),
        pltpu.VMEM((units, own, depth), BF),
        pltpu.VMEM((units, own, depth), BF),
        pltpu.VMEM((units, own, depth), BF),
        pltpu.VMEM((2, 1, 2, own, feat), BF),
        pltpu.VMEM((2, count, 2, own, feat), BF),
        dma((2, units, 2)),
        dma((2, units)),
        dma((2, units, 3)),
        pltpu.VMEM((stages,) + small.shape, F32),
        dma((2, stages)),
    ]
    scratch += along_scratch(seqs, down.shape[1], wide)
    for group in (up, first):
        scratch += across_scratch(seqs, group.shape[1], wide) + along_scratch(seqs, group.shape[1], wide)
    return pl.pallas_call(
        functools.partial(outputs_kernel, seqs, count),
        out_shape=outs,
        in_specs=[pl.BlockSpec(memory_space=pltpu.VMEM)] * 8,
        out_specs=tuple(pl.BlockSpec(memory_space=pltpu.VMEM) for _ in outs),
        scratch_shapes=scratch,
        compiler_params=pltpu.CompilerParams(collective_id=collective_id, has_side_effects=True, vmem_limit_bytes=50 << 20),
        name="scatter_outputs",
    )(part_x, part_y, d1, d3, small, down, up, first)


def pick(array, index, axis):
    return lax.dynamic_index_in_dim(array, index, axis, keepdims=False)


def dot_f32(spec, left, right):
    return jnp.einsum(spec, left, right, preferred_element_type=F32)


def on_device(
    rows,
    cols,
    tokens,
    streams,
    cotangent,
    block_ids,
    bucket_ids,
    w_qkv,
    enc_table,
    w_out,
    attention_norm_gain,
    attn_bias,
    w_up,
    w_down,
    ffn_gain,
    ffn_bias,
    w_query,
    w_keyval,
    cross_table,
    w_cross_out,
    cross_gain,
    cross_bias,
):
    seqs = cols // 2
    row, col = lax.axis_index(ROW), lax.axis_index(COL)
    y, k, seq, half = row // 2, row % 2, col // 2, col % 2
    low_y = y == 0
    stream_count = streams.shape[1]
    tok = tokens.shape[1]
    own = tok // 2
    feat = tokens.shape[2]
    length = block_ids.shape[2]
    head_dim = w_qkv.shape[2] // 2
    ff = w_up.shape[1] // 2
    table_heads, bucket_count = enc_table.shape

    def columns(weight, parts):
        return weight.reshape(feat, parts, 2, -1).transpose(2, 1, 3, 0).reshape(2, -1, feat)

    def columns_back(array, parts):
        return array.reshape(2, parts, -1, feat).transpose(3, 1, 0, 2).reshape(feat, parts, -1)

    halves = lambda weight: weight.reshape(2, -1, feat)
    hd3, hd2 = 3 * head_dim, 2 * head_dim
    packs = (
        jnp.concatenate([columns(w_qkv, 3), halves(w_out)], axis=1),
        columns(w_up, 1),
        halves(w_down),
        jnp.concatenate([columns(w_keyval, 2), columns(w_query, 1), halves(w_cross_out)], axis=1),
    )
    norm_params = jnp.stack([attention_norm_gain, attn_bias, ffn_gain, ffn_bias, cross_gain, cross_bias] + [cross_bias] * 2)
    table_pack = jnp.zeros((8, 128), F32).at[0].set(jnp.stack([enc_table, cross_table]).reshape(-1))
    micro_count = tokens.shape[0]
    x_own, x_full, y_own, y_full, norm_params, all_ids, all_tables, first, up, down, last = gather_inputs(
        seqs,
        tokens.reshape(micro_count, 1, 2, own, feat),
        streams.reshape(micro_count, stream_count, 2, own, feat),
        norm_params,
        block_ids.reshape(8, -1),
        table_pack,
        packs,
    )
    x_full, y_full = x_full.reshape(length, D), y_full.reshape(stream_count * length, D)
    segment = pick(pick(all_ids.reshape(rows, micro_count, length), seq, 0), y, 0)
    segq = segment[None]
    segk = jnp.broadcast_to(segment[:, None], (length, length))
    own_tables = pick(all_tables[:, 0].reshape(seqs, 2, table_heads, bucket_count), k, 2)
    slot_col = 2 * ((seq - jnp.arange(seqs)) % seqs) + half
    reversed_ids = jnp.concatenate([jnp.full((1,), -1, jnp.int32), bucket_ids[::-1]])
    onehot = bucket_onehot(reversed_ids, bucket_count)
    offsets = jnp.einsum("htb,bo->tho", own_tables, onehot, precision=highest)[:, :, None, :]

    m_qkv, m_out = first[:, :hd3], first[:, hd3:].reshape(-1, D)
    blocked = lambda product: product.astype(BF).reshape(-1, 2, 2, own, D)

    qkv = dot_f32("snr,tr->snt", m_qkv, x_full).astype(BF)
    mix, lse, tiles = attention(offsets, segq, segk, qkv)
    mix_flat = mix.reshape(-1, length)
    hidden_full, hidden, normed1, inv1, down, last = exchange(
        FORWARD,
        1,
        seqs,
        blocked(dot_f32("et,er->tr", mix_flat, m_out)),
        x_own,
        norm_params[0:2],
        rides=((ACROSS, down), (ALONG, last)),
    )
    up, down = up.reshape(-1, D), down.reshape(-1, D)
    hidden_full = hidden_full.reshape(length, D)
    pre = dot_f32("fr,tr->ft", up, hidden_full)
    act, gelu_pull = jax.vjp(gelu_exact, pre)
    act = act.astype(BF)
    enc_full, _, normed2, inv2, last = exchange(
        FORWARD,
        2,
        seqs,
        blocked(dot_f32("ft,fr->tr", act, down)),
        hidden,
        norm_params[2:4],
        rides=((ACROSS, last),),
    )
    m_kv, m_q, m_co = last[:, :hd2], last[:, hd2:hd3], last[:, hd3:].reshape(-1, D)
    enc_full = enc_full.reshape(length, D)
    kv = dot_f32("snr,tr->snt", m_kv, enc_full).astype(BF)
    query = dot_f32("snr,tr->snt", m_q, y_full).astype(BF)
    cmix, d3_full, output, d3, sums3, dquery, dkv, doff_cross = cross_attention(
        3,
        query,
        kv,
        m_co,
        tiles,
        segq,
        segk,
        y_own,
        norm_params[4:6],
        cotangent.reshape(micro_count, stream_count, 2, own, feat),
    )
    cmix_flat = cmix.reshape(-1, stream_count * length)
    d3_full = d3_full.reshape(stream_count * length, D)

    g_co = dot_f32("et,tr->er", cmix_flat, d3_full)
    g_q = dot_f32("snt,tr->snr", dquery, y_full)
    g_kv = dot_f32("snt,tr->snr", dkv, enc_full)
    g_last = jnp.concatenate([g_kv.astype(BF), g_q.astype(BF), g_co.astype(BF).reshape(seqs, head_dim, D)], axis=1)
    d2_full, d2, sums2, g_last = exchange(
        BACKWARD,
        4,
        seqs,
        blocked(dot_f32("snt,snr->tr", dkv, m_kv)),
        norm_params[2:4][None],
        norm_params[2:4],
        normed=normed2,
        inv=inv2,
        rides=((SUM_ACROSS, g_last),),
    )
    d2_full = d2_full.reshape(length, D)
    part_y = blocked(dot_f32("snt,snr->tr", dquery, m_q))
    dact = dot_f32("fr,tr->ft", down, d2_full)
    dpre = gelu_pull(dact)[0].astype(BF)
    g_down = dot_f32("ft,tr->fr", act, d2_full).astype(BF).reshape(seqs, ff, D)
    d1_full, d1, sums1, g_last, g_down = exchange(
        BACKWARD,
        5,
        seqs,
        blocked(dot_f32("ft,fr->tr", dpre, up)),
        d2,
        norm_params[0:2],
        normed=normed1,
        inv=inv1,
        rides=((SUM_ALONG, g_last), (SUM_ACROSS, g_down)),
    )
    d1_full = d1_full.reshape(length, D)
    g_up = dot_f32("ft,tr->fr", dpre, hidden_full).astype(BF).reshape(seqs, ff, D)
    dmix = dot_f32("er,tr->et", m_out, d1_full).astype(BF).reshape(mix.shape)
    g_out = dot_f32("et,tr->er", mix_flat, d1_full)
    dqkv, doff_enc = attention_back(tiles, segq, segk, qkv, lse, dmix)
    g_qkv = dot_f32("snt,tr->snr", dqkv, x_full)
    g_first = jnp.concatenate([g_qkv.astype(BF), g_out.astype(BF).reshape(seqs, head_dim, D)], axis=1)
    part_x = blocked(dot_f32("snt,snr->tr", dqkv, m_qkv))

    norm_grads = jnp.concatenate([sums1[:2], sums2[:2], sums3[:2]])
    norm_grads = jnp.where(low_y, norm_grads, jnp.roll(norm_grads, D // 2, axis=1))
    table_grads = jnp.einsum(
        "tho,bo->thb", jnp.stack([doff_enc[:, 0], doff_cross[:, 0]]), onehot, precision=highest
    )
    heads = 2 * slot_col + k
    spread = (heads[:, None] == jnp.arange(table_heads * cols)[None, :]).astype(F32)
    table_grads = jnp.einsum("thb,hg->tgb", table_grads, spread, precision=highest)
    small = jnp.concatenate([norm_grads.reshape(-1, 128), table_grads.reshape(-1, 128)])
    grad_tokens, grad_streams, small, g_down, g_up, g_first = scatter_outputs(
        seqs, 6, part_x, part_y, d1, d3, small, g_down, g_up, g_first
    )
    output, grad_streams = output.reshape(streams.shape), grad_streams.reshape(streams.shape)
    grad_tokens = grad_tokens.reshape(tokens.shape)
    count = norm_grads.size // 128
    norm_sums = lax.dynamic_slice_in_dim(small[:count].reshape(6, D), row * feat, feat, axis=1)
    table_sums = small[count:].reshape(2, table_heads * cols, bucket_count)
    table_sums = lax.dynamic_slice_in_dim(table_sums, col * table_heads, table_heads, axis=1)
    return (
        output,
        grad_tokens,
        grad_streams,
        columns_back(g_first[:, :hd3], 3),
        table_sums[0],
        g_first[:, hd3:].reshape(w_out.shape),
        norm_sums[0],
        norm_sums[1],
        columns_back(g_up, 1).reshape(w_up.shape),
        g_down.reshape(w_down.shape),
        norm_sums[2],
        norm_sums[3],
        columns_back(g_last[:, hd2:hd3], 1).reshape(w_query.shape),
        columns_back(g_last[:, :hd2], 2),
        table_sums[1],
        g_last[:, hd3:].reshape(w_cross_out.shape),
        norm_sums[4],
        norm_sums[5],
    )


def solution(mesh):
    whole_row, half_col = mesh.shape[ROW], mesh.shape[COL]
    wide, table, norm = P(ROW, None, COL), P(COL, None), P(ROW)
    up, down = P(ROW, COL), P(COL, ROW)
    weights = (wide, table, down, norm, norm, up, down, norm, norm, up, wide, table, down, norm, norm)

    def run(tokens, *rest):
        micro_count = tokens.shape[0]
        if whole_row == 4 and micro_count == 2 and half_col % 2 == 0:
            device_fn = functools.partial(on_device, whole_row, half_col)
        else:
            device_fn = on_device_general
        return jax.shard_map(
            device_fn,
            mesh=mesh,
            in_specs=(P(None, COL, ROW), P(None, None, COL, ROW), P(None, None, COL, ROW), P(None, ROW, None), P()) + weights,
            out_specs=(P(None, None, COL, ROW), P(None, COL, ROW), P(None, None, COL, ROW)) + weights,
            check_vma=False,
        )(tokens, *rest)

    return run
```

```python
import functools
import types
import jax
import jax.numpy as jnp
from jax import lax
from jax.experimental import pallas as pl
from jax.experimental.pallas import tpu as pltpu
from jax.sharding import PartitionSpec as P

D = 1024
F32 = jnp.float32
BF = jnp.bfloat16
ROW, COL = "row", "col"


epsilon = 1e-05
neg_fill = -1e30
highest = lax.Precision.HIGHEST


def gather_cols(local_rows):
    return lax.all_gather(local_rows, COL, axis=1, tiled=True)


def gather_rows(local_rows):
    return lax.all_gather(local_rows, ROW, axis=1, tiled=True)


def product(matmul_operand, weight_matrix):
    return jnp.einsum(
        "ray,yw->raw", matmul_operand, weight_matrix, preferred_element_type=jnp.float32
    )


def rows_product(operand_full, matrix):
    return lax.psum_scatter(product(operand_full, matrix), ROW, scatter_dimension=1, tiled=True)


def cols_product(operand_full, matrix):
    return lax.psum_scatter(product(operand_full, matrix), COL, scatter_dimension=1, tiled=True)


def weight_grad(matmul_operand, upstream_gradient):
    return jnp.einsum(
        "bpt,bpr->tr", matmul_operand, upstream_gradient, preferred_element_type=jnp.float32
    )


def gelu_exact(argument):
    return jax.nn.gelu(argument, approximate=False)


def norm_forward(residual, gain_vec, bias_vec):
    local_sum = jnp.sum(residual, axis=-1)
    average = lax.psum(local_sum, ROW) / D
    centered = residual - average[..., None]
    spread = lax.psum(jnp.sum(centered * centered, axis=-1), ROW) / D
    inv_std = lax.rsqrt(spread + epsilon)
    normed = centered * inv_std[..., None]
    return (normed * gain_vec + bias_vec, normed, inv_std)


def norm_back(out_grad, normed, inv_std, gain_vec):
    scaled_grad = out_grad * gain_vec
    first_moment, second_moment = lax.psum(
        (jnp.sum(scaled_grad, axis=-1), jnp.sum(scaled_grad * normed, axis=-1)), ROW
    )
    resid_grad = inv_std[..., None] * (
        scaled_grad - first_moment[..., None] / D - normed * (second_moment[..., None] / D)
    )
    return (resid_grad, jnp.sum(out_grad * normed, axis=(0, 1)), jnp.sum(out_grad, axis=(0, 1)))


def bucket_onehot(bucket_ids, bucket_count):
    return (bucket_ids[None, :] == jnp.arange(bucket_count, dtype=jnp.int32)[:, None]).astype(
        jnp.float32
    )


def block_logits(query_blk, key_rows, offsets, segment, first_row):
    row_count = query_blk.shape[2]
    length = key_rows.shape[1]
    score_scale = query_blk.shape[-1] ** (-0.5)
    raw_scores = jnp.einsum(
        "snqhd,nkhd->snhqk", query_blk, key_rows, preferred_element_type=jnp.float32
    )
    places = jnp.arange(length, dtype=jnp.int32)
    query_pos = first_row + jnp.arange(row_count, dtype=jnp.int32)
    offset_index = places[None, :] - query_pos[:, None] + (length - 1)
    pos_bias = jnp.take(offsets, offset_index, axis=1)
    visible = segment[:, first_row : first_row + row_count, None] >= segment[:, None, :]
    return jnp.where(
        visible[None, :, None], raw_scores * score_scale + pos_bias[None, None], neg_fill
    )


def attend(queries, key_rows, value_rows, segment, offsets):
    score_logits = block_logits(queries, key_rows, offsets, segment, 0)
    row_max = jnp.max(score_logits, axis=-1, keepdims=True)
    log_total = row_max + jnp.log(jnp.sum(jnp.exp(score_logits - row_max), axis=-1, keepdims=True))
    weights = jnp.exp(score_logits - log_total).astype(jnp.bfloat16)
    mixed_parts = jnp.einsum(
        "snhqk,nkhd->snqhd", weights, value_rows, preferred_element_type=jnp.float32
    )
    lse_parts = log_total[..., 0]
    return (mixed_parts, lse_parts)


def diagonal_sums(summand):
    head_count, row_count, length = summand.shape
    flipped = summand[:, ::-1, :]
    padded = jnp.concatenate(
        [flipped, jnp.zeros((head_count, row_count, row_count), summand.dtype)], axis=2
    )
    flattened = padded.reshape(head_count, row_count * (length + row_count))[
        :, : row_count * (length + row_count - 1)
    ]
    return jnp.sum(flattened.reshape(head_count, row_count, length + row_count - 1), axis=1)


def attend_back(queries, key_rows, value_rows, segment, offsets, onehot, log_totals, mix_grad):
    length = key_rows.shape[1]
    block_rows = min(512, length)
    score_scale = queries.shape[-1] ** (-0.5)
    offset_grad = jnp.zeros(offsets.shape, jnp.float32)
    score_logits = block_logits(queries, key_rows, offsets, segment, 0)
    probability = jnp.exp(score_logits - log_totals[:, :, :, 0:block_rows, None])
    prob_grad = jnp.einsum(
        "snqhd,nkhd->snhqk", mix_grad, value_rows, preferred_element_type=jnp.float32
    )
    logit_grad = probability * (
        prob_grad - jnp.sum(probability * prob_grad, axis=-1, keepdims=True)
    )
    scaled = (logit_grad * score_scale).astype(jnp.bfloat16)
    query_parts = jnp.einsum(
        "snhqk,nkhd->snqhd", scaled, key_rows, preferred_element_type=jnp.float32
    )
    key_grad = jnp.einsum("snhqk,snqhd->nkhd", scaled, queries, preferred_element_type=jnp.float32)
    value_grad = jnp.einsum(
        "snhqk,snqhd->nkhd",
        probability.astype(jnp.bfloat16),
        mix_grad,
        preferred_element_type=jnp.float32,
    )
    low_end = length - block_rows
    offset_grad = offset_grad.at[:, low_end : low_end + length + block_rows - 1].add(
        diagonal_sums(jnp.sum(logit_grad, axis=(0, 1)))
    )
    table_grad = jnp.dot(offset_grad, onehot.T, precision=highest)
    return (query_parts, key_grad, value_grad, table_grad)


def on_device_general(
    tokens,
    streams,
    cotangent,
    block_ids,
    bucket_ids,
    w_qkv,
    enc_table,
    w_out,
    attention_norm_gain,
    attn_bias,
    w_up,
    w_down,
    ffn_gain,
    ffn_bias,
    w_query,
    w_keyval,
    cross_table,
    w_cross_out,
    cross_gain,
    cross_bias,
):
    micro_count = tokens.shape[0]
    stream_count = streams.shape[1]
    seq_rows = block_ids.shape[1]
    length = block_ids.shape[2]
    head_count = enc_table.shape[0]
    bucket_count = enc_table.shape[1]
    row_width = w_qkv.shape[0]
    col_width = w_qkv.shape[2]
    head_dim = col_width // head_count
    row_tokens = seq_rows * length
    qkv_matrix = w_qkv.reshape(row_width, 3 * col_width)
    keyval_matrix = w_keyval.reshape(row_width, 2 * col_width)
    onehot = bucket_onehot(bucket_ids, bucket_count)
    enc_offsets = jnp.dot(enc_table, onehot, precision=highest)
    cross_offsets = jnp.dot(cross_table, onehot, precision=highest)
    qkv_acc = jnp.zeros((row_width, 3 * col_width), jnp.float32)
    out_acc = jnp.zeros(w_out.shape, jnp.float32)
    up_acc = jnp.zeros(w_up.shape, jnp.float32)
    down_acc = jnp.zeros(w_down.shape, jnp.float32)
    query_acc = jnp.zeros(w_query.shape, jnp.float32)
    keyval_acc = jnp.zeros((row_width, 2 * col_width), jnp.float32)
    cross_out_acc = jnp.zeros(w_cross_out.shape, jnp.float32)
    enc_table_acc = jnp.zeros(enc_table.shape, jnp.float32)
    cross_table_acc = jnp.zeros(cross_table.shape, jnp.float32)
    norm_accs = [jnp.zeros((row_width,), jnp.float32) for place_holder in range(6)]
    outputs = []
    token_grads = []
    stream_grads = []
    for micro in range(micro_count):
        segment = block_ids[micro]
        x_in = tokens[micro][None]
        y_in = streams[micro]
        x_full = gather_cols(x_in)
        qkv = (
            rows_product(x_full, qkv_matrix)
            .astype(jnp.bfloat16)
            .reshape(seq_rows, length, 3, head_count, head_dim)
        )
        enc_query = qkv[:, :, 0][None]
        enc_key = qkv[:, :, 1]
        encoder_value_rows = qkv[:, :, 2]
        enc_mixed, enc_lse = attend(enc_query, enc_key, encoder_value_rows, segment, enc_offsets)
        enc_mix = enc_mixed.reshape(1, row_tokens, col_width).astype(jnp.bfloat16)
        mix_full = gather_rows(enc_mix)
        attn_branch = cols_product(mix_full, w_out)
        hidden, normed_one, inv_one = norm_forward(
            x_in.astype(jnp.float32) + attn_branch, attention_norm_gain, attn_bias
        )
        hidden_low = hidden.astype(jnp.bfloat16)
        hidden_full = gather_cols(hidden_low)
        pre_act = rows_product(hidden_full, w_up)
        act_value, gelu_pull = jax.vjp(gelu_exact, pre_act)
        act_low = act_value.astype(jnp.bfloat16)
        act_full = gather_rows(act_low)
        ffn_branch = cols_product(act_full, w_down)
        encoded, normed_two, inv_two = norm_forward(hidden + ffn_branch, ffn_gain, ffn_bias)
        encoded_low = encoded.astype(jnp.bfloat16)
        enc_full = gather_cols(encoded_low)
        keyval = (
            rows_product(enc_full, keyval_matrix)
            .astype(jnp.bfloat16)
            .reshape(seq_rows, length, 2, head_count, head_dim)
        )
        cross_key = keyval[:, :, 0]
        cross_value = keyval[:, :, 1]
        stream_full = gather_cols(y_in)
        cross_query = (
            rows_product(stream_full, w_query)
            .astype(jnp.bfloat16)
            .reshape(stream_count, seq_rows, length, head_count, head_dim)
        )
        cross_mixed, cross_lse = attend(cross_query, cross_key, cross_value, segment, cross_offsets)
        cross_mix = cross_mixed.reshape(stream_count, row_tokens, col_width).astype(jnp.bfloat16)
        cross_full = gather_rows(cross_mix)
        cross_branch = cols_product(cross_full, w_cross_out)
        result, normed_three, inv_three = norm_forward(
            y_in.astype(jnp.float32) + cross_branch, cross_gain, cross_bias
        )
        outputs.append(result)
        grad_three, gain_part, bias_part = norm_back(
            cotangent[micro].astype(jnp.float32), normed_three, inv_three, cross_gain
        )
        norm_accs[4] = norm_accs[4] + gain_part
        norm_accs[5] = norm_accs[5] + bias_part
        branch_full = gather_cols(grad_three.astype(jnp.bfloat16))
        cross_out_acc = cross_out_acc + weight_grad(cross_full, branch_full)
        cross_mix_grad = (
            rows_product(branch_full, w_cross_out.T)
            .astype(jnp.bfloat16)
            .reshape(stream_count, seq_rows, length, head_count, head_dim)
        )
        query_grad, key_grad, value_grad, table_grad = attend_back(
            cross_query,
            cross_key,
            cross_value,
            segment,
            cross_offsets,
            onehot,
            cross_lse,
            cross_mix_grad,
        )
        cross_table_acc = cross_table_acc + table_grad
        query_low = query_grad.reshape(stream_count, row_tokens, col_width).astype(jnp.bfloat16)
        keyval_low = (
            jnp.stack(
                [
                    key_grad.reshape(row_tokens, col_width),
                    value_grad.reshape(row_tokens, col_width),
                ],
                axis=1,
            )
            .reshape(1, row_tokens, 2 * col_width)
            .astype(jnp.bfloat16)
        )
        query_full = gather_rows(query_low)
        query_acc = query_acc + weight_grad(stream_full, query_full)
        stream_grads.append(grad_three + cols_product(query_full, w_query.T))
        keyval_full = gather_rows(keyval_low)
        keyval_acc = keyval_acc + weight_grad(enc_full, keyval_full)
        encoded_grad = cols_product(keyval_full, keyval_matrix.T)
        grad_two, gain_part, bias_part = norm_back(encoded_grad, normed_two, inv_two, ffn_gain)
        norm_accs[2] = norm_accs[2] + gain_part
        norm_accs[3] = norm_accs[3] + bias_part
        feedforward_full_output = gather_cols(grad_two.astype(jnp.bfloat16))
        down_acc = down_acc + weight_grad(act_full, feedforward_full_output)
        act_grad = rows_product(feedforward_full_output, w_down.T)
        pre_low = gelu_pull(act_grad)[0].astype(jnp.bfloat16)
        pre_full = gather_rows(pre_low)
        up_acc = up_acc + weight_grad(hidden_full, pre_full)
        hidden_grad = grad_two + cols_product(pre_full, w_up.T)
        grad_one, gain_part, bias_part = norm_back(
            hidden_grad, normed_one, inv_one, attention_norm_gain
        )
        norm_accs[0] = norm_accs[0] + gain_part
        norm_accs[1] = norm_accs[1] + bias_part
        attn_full = gather_cols(grad_one.astype(jnp.bfloat16))
        out_acc = out_acc + weight_grad(mix_full, attn_full)
        enc_mix_grad = (
            rows_product(attn_full, w_out.T)
            .astype(jnp.bfloat16)
            .reshape(1, seq_rows, length, head_count, head_dim)
        )
        enc_qgrad, enc_kgrad, enc_vgrad, table_grad = attend_back(
            enc_query,
            enc_key,
            encoder_value_rows,
            segment,
            enc_offsets,
            onehot,
            enc_lse,
            enc_mix_grad,
        )
        enc_table_acc = enc_table_acc + table_grad
        qkv_low = (
            jnp.stack(
                [
                    enc_qgrad.reshape(row_tokens, col_width),
                    enc_kgrad.reshape(row_tokens, col_width),
                    enc_vgrad.reshape(row_tokens, col_width),
                ],
                axis=1,
            )
            .reshape(1, row_tokens, 3 * col_width)
            .astype(jnp.bfloat16)
        )
        qkv_full = gather_rows(qkv_low)
        qkv_acc = qkv_acc + weight_grad(x_full, qkv_full)
        token_grads.append((grad_one + cols_product(qkv_full, qkv_matrix.T))[0])
    norm_stack = jnp.stack(norm_accs)
    table_stack = jnp.stack([enc_table_acc, cross_table_acc])
    norm_sums = lax.psum(norm_stack, COL)
    table_sums = lax.psum(table_stack, ROW)
    return (
        jnp.stack(outputs),
        jnp.stack(token_grads),
        jnp.stack(stream_grads),
        qkv_acc.reshape(row_width, 3, col_width),
        table_sums[0],
        out_acc,
        norm_sums[0],
        norm_sums[1],
        up_acc,
        down_acc,
        norm_sums[2],
        norm_sums[3],
        query_acc,
        keyval_acc.reshape(row_width, 2, col_width),
        table_sums[1],
        cross_out_acc,
        norm_sums[4],
        norm_sums[5],
    )


def mm(a,b):
    return jnp.dot(a,b,preferred_element_type=F32)
def mm_nt(a,b):
    return lax.dot_general(a,b,(((1,),(1,)),((),())),preferred_element_type=F32)

def masked_bias(off_ref, index, segq, segk):
    length = segk.shape[0]
    row = jnp.broadcast_to(off_ref[index], (length, 2 * length))
    rolled = pltpu.roll(row, 0, 1, stride=1, stride_axis=0)
    return jnp.where(segk[...] <= segq[...], rolled[:, length:], neg_fill)


def head_forward(keys, values, query, bias):
    logits = mm(keys, query) + bias
    top = jnp.max(logits, axis=0, keepdims=True)
    weight = jnp.exp(logits - top)
    total = jnp.sum(weight, axis=0, keepdims=True)
    return (mm(values, weight.astype(BF)) * (1.0 / total)).astype(BF), top + jnp.log(total)


def head_backward(keys, keys_t, values_t, query, grad, lse, bias):
    prob = jnp.exp(mm(keys, query) + (bias - lse))
    dprob = mm(values_t, grad)
    dlogits = prob * (dprob - jnp.sum(prob * dprob, axis=0, keepdims=True))
    low = dlogits.astype(BF)
    return dlogits, mm(keys_t, low).astype(BF), mm_nt(query, low), mm_nt(grad, prob.astype(BF))


def project(mix_ref, weight_ref, start, rows):
    heads, hd = mix_ref.shape[0], mix_ref.shape[1]
    mixed = mix_ref[:, :, start : start + rows].reshape(heads * hd, rows)
    return lax.dot_general(mixed, weight_ref[...], (((0,), (0,)), ((), ())), preferred_element_type=F32).astype(BF)


def project_back(weight_ref, rows_value, dmix_ref, start):
    heads, hd = dmix_ref.shape[0], dmix_ref.shape[1]
    rows = rows_value.shape[0]
    dmix_ref[:, :, start : start + rows] = mm_nt(weight_ref[...], rows_value).astype(BF).reshape(heads, hd, rows)


def scaled(value, scale):
    return (value.astype(F32) * scale).astype(BF)


def offset_sums(g_ref, doff_ref, g_index, out_index, length):
    sub = lax.broadcasted_iota(jnp.int32, (8, 2 * length), 0)
    acc = jnp.zeros((8, 2 * length), F32)
    for i in range(length // 8):
        piece = g_ref[g_index + (pl.ds(8 * i, 8),)]
        padded = jnp.concatenate([jnp.zeros((8, length), F32), piece], axis=1)
        acc = acc + (pltpu.roll(padded, 2 * length - 8 * i, 1) if i else padded)
    for b in (1, 2, 4):
        acc = jnp.where((sub // b) % 2 == 1, pltpu.roll(acc, 2 * length - b, 1), acc)
    doff_ref[out_index] = jnp.sum(acc, axis=0, keepdims=True)


MESH = pl.DeviceIdType.MESH
FORWARD, BACKWARD = range(2)
ACROSS, THROUGH, ALONG, SUM_ACROSS, SUM_ALONG = range(5)


def spot():
    row, col = lax.axis_index(ROW), lax.axis_index(COL)
    return row // 2, row % 2, col // 2, col % 2


def device(y, k, seq, half):
    return (2 * y + k, 2 * seq + half)


def greet(devices):
    barrier = pltpu.get_barrier_semaphore()
    for target in devices:
        pl.semaphore_signal(barrier, inc=1, device_id=target, device_id_type=MESH)
    pl.semaphore_wait(barrier, len(devices))


def remote(source, target, send_sem, recv_sem, device_id):
    copy = pltpu.make_async_remote_copy(
        src_ref=source, dst_ref=target, send_sem=send_sem, recv_sem=recv_sem, device_id=device_id, device_id_type=MESH
    )
    copy.start()
    return copy


def lanes(start, size):
    return pl.ds(pl.multiple_of(start, size), size)


def rows_of(place):
    y, k, seq, half = place
    return [(dy, dk, (1 - y if dy else y), (1 - k if dk else k)) for dy, dk in ((0, 1), (1, 0), (1, 1))]


class Spread:
    def __init__(self, full_ref, half_sems, core_sems, place, rows):
        self.full, self.place, self.rows = full_ref, place, rows
        self.half_sems, self.core_sems = half_sems, core_sems
        self.first, self.second = {}, {}

    def block(self, n, piece, half, k):
        return self.full.at[n, half, k, pl.ds(piece * self.rows, self.rows)]

    def start(self, unit, n, piece):
        y, k, seq, half = self.place
        mine = self.block(n, piece, half, k)
        hs, cs = self.half_sems, self.core_sems
        self.first[unit] = (
            remote(mine, mine, hs.at[0, unit], hs.at[1, unit], device(y, k, seq, 1 - half)),
            remote(mine, mine, cs.at[0, unit, 0], cs.at[1, unit, 0], device(y, 1 - k, seq, half)),
        )

    def forward(self, unit, n, piece):
        y, k, seq, half = self.place
        self.first[unit][0].wait_recv()
        theirs = self.block(n, piece, 1 - half, k)
        cs = self.core_sems
        self.second[unit] = remote(theirs, theirs, cs.at[0, unit, 1], cs.at[1, unit, 1], device(y, 1 - k, seq, half))

    def ready(self, unit):
        self.first[unit][1].wait_recv()
        self.second[unit].wait_recv()

    def sent(self, unit):
        for copy in self.first[unit] + (self.second[unit],):
            copy.wait_send()

    def finish(self, unit):
        self.ready(unit)
        self.sent(unit)


class Reduce:
    def __init__(self, partial_ref, core_buf, half_send, half_buf, core_sems, half_sems, place, rows):
        self.partial, self.core_buf, self.half_send, self.half_buf = partial_ref, core_buf, half_send, half_buf
        self.core_sems, self.half_sems, self.place, self.rows = core_sems, half_sems, place, rows
        self.first, self.second = {}, {}

    def part(self, n, piece, half, k):
        return (n, half, k, pl.ds(piece * self.rows, self.rows))

    def start(self, unit, n, piece, away):
        y, k, seq, half = self.place
        side = 1 - half if away else half
        cs = self.core_sems
        lane = 0 if away else 1
        self.first[unit, lane] = remote(
            self.partial.at[self.part(n, piece, side, 1 - k)],
            self.core_buf.at[unit, lane],
            cs.at[0, unit, lane],
            cs.at[1, unit, lane],
            device(y, 1 - k, seq, half),
        )

    def pass_on(self, unit, n, piece):
        y, k, seq, half = self.place
        self.first[unit, 0].wait_recv()
        away = self.partial[self.part(n, piece, 1 - half, k)].astype(F32) + self.core_buf[unit, 0].astype(F32)
        self.half_send[unit] = away.astype(BF)
        hs = self.half_sems
        self.second[unit] = remote(
            self.half_send.at[unit], self.half_buf.at[unit], hs.at[0, unit], hs.at[1, unit], device(y, k, seq, 1 - half)
        )

    def result(self, unit, n, piece):
        y, k, seq, half = self.place
        self.first[unit, 1].wait_recv()
        mine = self.partial[self.part(n, piece, half, k)].astype(F32) + self.core_buf[unit, 1].astype(F32)
        self.second[unit].wait_recv()
        return mine + self.half_buf[unit].astype(F32)

    def finish(self, unit):
        self.first[unit, 0].wait_send()
        self.first[unit, 1].wait_send()
        self.second[unit].wait_send()


class Return:
    def __init__(self, own_ref, landing, sems, place, feat):
        self.own, self.landing, self.sems, self.place, self.feat = own_ref, landing, sems, place, feat
        self.copies = []

    def start(self, unit, n, value):
        y, k, seq, half = self.place
        feat = self.feat
        self.own[unit] = value
        self.landing[y, n, k] = jnp.where(k == 0, value[:, :feat], value[:, feat : 2 * feat])
        for i, (dy, dk, ty, tk) in enumerate(rows_of(self.place)):
            self.copies.append(
                remote(
                    self.own.at[unit, :, lanes(tk * feat + 2 * dy * feat, feat)],
                    self.landing.at[y, n, k],
                    self.sems.at[0, unit, i],
                    self.sems.at[1, unit, i],
                    device(ty, tk, seq, half),
                )
            )

    def finish(self):
        for copy in self.copies:
            copy.wait()


class Freight:
    def __init__(self, full_ref, z_sems, y_sems, place, seqs):
        self.full, self.place, self.seqs = full_ref, place, seqs
        self.z_sems, self.y_sems = z_sems, y_sems
        self.wide = full_ref.shape[2] // 2
        self.z, self.y = {}, {}
        self.turn = seqs // 2

    def along(self, d):
        y, k, seq, half = self.place
        up = d <= self.turn
        source = d - 1 if up else (d + 1) % self.seqs
        if source:
            self.z[source].wait_recv()
        target = lax.rem(seq + (1 if up else self.seqs - 1), self.seqs)
        self.z[d] = remote(
            self.full.at[source, :, : self.wide],
            self.full.at[d, :, : self.wide],
            self.z_sems.at[0, d - 1],
            self.z_sems.at[1, d - 1],
            device(y, k, target, half),
        )

    def first(self):
        return [d for d in (1, self.seqs - 1) if d <= self.turn or d > self.turn][: min(2, self.seqs - 1)]

    def later(self):
        return list(range(2, self.turn + 1)) + list(range(self.seqs - 2, self.turn, -1))

    def last(self):
        return [d for d in range(1, self.seqs) if d == self.turn or d == self.turn + 1]

    def across(self, d):
        y, k, seq, half = self.place
        self.y[d] = remote(
            self.full.at[d, :, : self.wide],
            self.full.at[d, :, self.wide :],
            self.y_sems.at[0, d],
            self.y_sems.at[1, d],
            device(1 - y, k, seq, half),
        )

    def pass_along(self, cross):
        for d in self.later():
            self.along(d)
            if cross:
                self.across(d - 1 if d <= self.turn else d + 1)

    def arrive(self, cross):
        for d in self.last():
            self.z[d].wait_recv()
            if cross:
                self.across(d)

    def finish(self):
        for copy in self.z.values():
            copy.wait_send()
        for copy in self.y.values():
            copy.wait()


class Collect:
    def __init__(self, source, place, seqs, y_refs=None, z_refs=None):
        self.source, self.place, self.seqs = source, place, seqs
        self.y_refs, self.z_refs = y_refs, z_refs
        self.wide = source.shape[2] // 2 if y_refs else source.shape[2]
        self.turn = seqs // 2
        self.order = list(range(self.turn, seqs)) + list(range(self.turn - 1, -1, -1))
        self.y, self.z, self.core = {}, {}, None

    def across(self):
        y, k, seq, half = self.place
        buf, sems = self.y_refs
        for d in self.order:
            self.y[d] = remote(
                self.source.at[d, :, self.wide :], buf.at[d], sems.at[0, d], sems.at[1, d], device(1 - y, k, seq, half)
            )

    def total(self, d):
        if not self.y_refs:
            return self.source[d].astype(F32)
        self.y[d].wait_recv()
        return self.source[d, :, : self.wide].astype(F32) + self.y_refs[0][d].astype(F32)

    def store(self, out):
        for d in self.order:
            out[d] = self.total(d).astype(BF)

    def along(self, d):
        y, k, seq, half = self.place
        out, z_send, z_buf, c_send, z_sems, c_sems = self.z_refs
        left = d <= self.turn
        before = d + 1 if left else d - 1
        value = self.total(d)
        if before in self.z and before not in (self.turn + 1 if left else self.turn,):
            self.z[before].wait_recv()
            value = value + z_buf[before - 1].astype(F32)
        z_send[d - 1] = value.astype(BF)
        target = lax.rem(seq + (self.seqs - 1 if left else 1), self.seqs)
        self.z[d] = remote(
            z_send.at[d - 1], z_buf.at[d - 1], z_sems.at[0, d - 1], z_sems.at[1, d - 1], device(y, k, target, half)
        )

    def close(self):
        y, k, seq, half = self.place
        out, z_send, z_buf, c_send, z_sems, c_sems = self.z_refs
        total = self.total(0)
        for d in sorted({1, self.seqs - 1}):
            self.z[d].wait_recv()
            total = total + z_buf[d - 1].astype(F32)
        low, high = total[:, : self.wide // 2], total[:, self.wide // 2 :]
        out[k] = jnp.where(k == 0, low, high)
        c_send[...] = jnp.where(k == 0, high, low)
        self.core = remote(c_send, out.at[k], c_sems.at[0], c_sems.at[1], device(y, 1 - k, seq, half))

    def finish(self):
        for copy in self.y.values():
            copy.wait_send()
        for copy in self.z.values():
            copy.wait_send()
        if self.core is not None:
            self.core.wait()


def freight_scratch(seqs):
    dma = pltpu.SemaphoreType.DMA
    return [dma((2, seqs - 1)), dma((2, seqs))]


def across_scratch(seqs, n, wide):
    return [pltpu.VMEM((seqs, n, wide), BF), pltpu.SemaphoreType.DMA((2, seqs))]


def along_scratch(seqs, n, wide):
    dma = pltpu.SemaphoreType.DMA
    return [
        pltpu.VMEM((seqs - 1, n, wide), BF),
        pltpu.VMEM((seqs - 1, n, wide), BF),
        pltpu.VMEM((n, wide // 2), F32),
        dma((2, seqs - 1)),
        dma((2,)),
    ]


def along_devices(place, seqs):
    y, k, seq, half = place
    return [device(y, k, lax.rem(seq + d, seqs), half) for d in sorted({1, seqs - 1})]


def shuffle(source, target, n, index, place, sends, receives, local_sems):
    y, k, seq, half = place
    feat = source.shape[-1]
    copies = [pltpu.make_async_copy(source.at[y, n, k], target.at[n, :, lanes(k * feat, feat)], local_sems.at[index])]
    copies[0].start()
    for i, (dy, dk, ty, tk) in enumerate(rows_of(place)):
        copies.append(
            remote(
                source.at[ty, n, tk],
                target.at[n, :, lanes(k * feat + 2 * dy * feat, feat)],
                sends.at[index, i],
                receives.at[index, i],
                device(ty, tk, seq, half),
            )
        )
    return copies


def normalize(residual):
    centered = residual - jnp.mean(residual, axis=-1, keepdims=True)
    inv_std = lax.rsqrt(jnp.mean(centered * centered, axis=-1, keepdims=True) + epsilon)
    return centered * inv_std, inv_std


def normalize_back(out_grad, normed, inv_std, gain):
    scaled = out_grad * gain
    first = jnp.mean(scaled, axis=-1, keepdims=True)
    second = jnp.mean(scaled * normed, axis=-1, keepdims=True)
    return inv_std * (scaled - first - normed * second)


def column_sum(value):
    return jnp.sum(value, axis=0, keepdims=True)


def start_all(reduce, units):
    for unit, n, p in units:
        reduce.start(unit, n, p, True)
    for unit, n, p in units:
        reduce.start(unit, n, p, False)


def bias_of(r, target, table):
    def one(h, carry):
        target[h] = masked_bias(r.off, (table, h), r.segq, r.segk)
        return carry

    lax.fori_loop(0, r.qkv.shape[0], one, 0)


def attend_all(r):
    heads, hd = r.qkv.shape[0], r.qkv.shape[1] // 3
    bias_of(r, r.masked, 0)

    def one(h, carry):
        query = scaled(r.qkv[h, :hd], hd**-0.5)
        keys, values = r.qkv[h, hd : 2 * hd].T, r.qkv[h, 2 * hd :]
        r.mix[h], r.lse[h] = head_forward(keys, values, query, r.masked[h])
        return carry

    lax.fori_loop(0, heads, one, 0)


def attend_all_back(r):
    heads, hd, length = r.qkv.shape[0], r.qkv.shape[1] // 3, r.qkv.shape[2]
    scale = hd**-0.5

    def one(h, carry):
        query, keys, values = (r.qkv[h, part * hd : (part + 1) * hd] for part in range(3))
        dlogits, dq, dk, dv = head_backward(
            keys.T, scaled(keys, scale), values.T, scaled(query, scale), r.dmix[h], r.lse[h], r.masked[h]
        )
        r.g_scr[...] = dlogits
        r.dqkv[h, :hd] = dq
        r.dqkv[h, hd : 2 * hd] = dk.astype(BF)
        r.dqkv[h, 2 * hd :] = dv.astype(BF)
        offset_sums(r.g_scr, r.doff, (), (h,), length)
        return carry

    lax.fori_loop(0, heads, one, 0)


def exchange_kernel(kind, attend, count, pieces, seqs, rides, *refs):
    place = spot()
    y, k, seq, half = place
    refs = list(refs)
    take = lambda amount: [refs.pop(0) for _ in range(amount)]
    r = types.SimpleNamespace()
    partial, r.resid, r.norm = take(3)
    if kind == BACKWARD:
        r.normed, r.inv = take(2)
    if attend:
        r.qkv, r.weight = take(2)
        if kind == FORWARD:
            r.off, r.segq, r.segk = take(3)
        else:
            r.masked, r.lse = take(2)
    ride_in = take(len(rides))
    (r.full,) = take(1)
    if kind == FORWARD:
        r.out, r.normed, r.inv = take(3)
    else:
        r.grad, r.sums = take(2)
    if attend:
        if kind == FORWARD:
            r.mix, r.lse, r.masked, r.masked_next = take(4)
        else:
            r.dqkv, r.doff = take(2)
    ride_out = take(len(rides))
    if attend:
        if kind == FORWARD:
            (partial,) = take(1)
        else:
            r.g_scr, r.dmix = take(2)
    core_buf, half_send, half_buf, rc, rh, gh, gc = take(7)
    rows = partial.shape[3] // pieces
    peers = [device(y, 1 - k, seq, half), device(y, k, seq, 1 - half)]
    if {ACROSS, THROUGH, SUM_ACROSS} & set(rides):
        peers.append(device(1 - y, k, seq, half))
    if {ALONG, THROUGH, SUM_ALONG} & set(rides):
        peers += along_devices(place, seqs)
    greet(peers)
    units = [(n * pieces + p, n, p) for n in range(count) for p in range(pieces)]
    reduce = Reduce(partial, core_buf, half_send, half_buf, rc, rh, place, rows)
    spread = Spread(r.full, gh, gc, place, rows)
    if not (attend and kind == FORWARD):
        start_all(reduce, units)
    moves, sums_along, sums_across = [], [], []
    for ride, source, target in zip(rides, ride_in, ride_out):
        if ride == SUM_ACROSS:
            sums_across.append((Collect(source, place, seqs, y_refs=take(2)), target))
            sums_across[-1][0].across()
        elif ride == SUM_ALONG:
            sums_along.append(Collect(source, place, seqs, z_refs=[target] + take(5)))
            for d in sums_along[-1].order[:2]:
                sums_along[-1].along(d)
        else:
            moves.append((ride, Freight(target, *take(2), place, seqs)))
            if ride == ACROSS:
                for d in range(seqs):
                    moves[-1][1].across(d)
            else:
                if ride == THROUGH:
                    moves[-1][1].across(0)
                for d in moves[-1][1].first():
                    moves[-1][1].along(d)
    if kind != FORWARD:
        r.sums[...] = jnp.zeros_like(r.sums)
    elif attend:
        attend_all(r)
        for a in range(2):
            for b in range(2):
                own = partial.shape[3]
                partial[0, a, b] = project(r.mix, r.weight, (2 * a + b) * own, own)
        start_all(reduce, units)
    gain, bias = r.norm[0:1], r.norm[1:2]
    for unit, n, p in units:
        reduce.pass_on(unit, n, p)
    for unit, n, p in units:
        here = pl.ds(p * rows, rows)
        branch = reduce.result(unit, n, p)
        if kind == FORWARD:
            normed, inv = normalize(r.resid[n, here].astype(F32) + branch)
            value = normed * gain + bias
            r.out[n, here] = value
            r.normed[n, here] = normed
            r.inv[n, here] = inv
        else:
            upstream = r.resid[n, here] + branch if r.resid.shape[1] == partial.shape[3] else branch
            normed = r.normed[n, here]
            value = normalize_back(upstream, normed, r.inv[n, here], gain)
            r.grad[n, here] = value
        r.full[n, half, k, here] = value.astype(BF)
        spread.start(unit, n, p)
        if kind != FORWARD:
            r.sums[0:1] += column_sum(upstream * normed)
            r.sums[1:2] += column_sum(upstream)
    for collect in sums_along:
        for d in collect.order[2:-1]:
            collect.along(d)
    for ride, move in moves:
        if ride != ACROSS:
            move.pass_along(ride == THROUGH)
            move.arrive(ride == THROUGH)
    if attend and kind == FORWARD:
        bias_of(r, r.masked_next, 1)
    for unit, n, p in units:
        spread.forward(unit, n, p)
    for collect in sums_along:
        collect.close()
    for unit, n, p in units:
        spread.finish(unit)
        reduce.finish(unit)
    if attend and kind == BACKWARD:
        for a in range(2):
            for b in range(2):
                own = partial.shape[3]
                project_back(r.weight, r.full[0, a, b], r.dmix, (2 * a + b) * own)
        attend_all_back(r)
    for ride, move in moves:
        move.finish()
    for collect, target in sums_across:
        collect.store(target)
        collect.finish()
    for collect in sums_along:
        collect.finish()


def exchange(kind, collective_id, seqs, partial, resid, norm, normed=None, inv=None, rides=(), attend=()):
    count, own, depth = 1, resid.shape[1], norm.shape[1]
    if partial is None:
        partial = norm
    else:
        count, _, _, own, depth = partial.shape
    pieces = 2 if count == 1 else 1
    units, rows = count * pieces, own // pieces
    dma = pltpu.SemaphoreType.DMA
    shape = jax.ShapeDtypeStruct
    vmem = pl.BlockSpec(memory_space=pltpu.VMEM)
    anywhere = pl.BlockSpec(memory_space=pl.ANY)
    full = shape((count, 2, 2, own, depth), BF)
    grad, sums = shape((count, own, depth), F32), shape((8, depth), F32)
    scratch = []
    if kind == FORWARD:
        args = (partial, resid, norm)
        outs = (full, grad, grad, shape((count, own, 1), F32))
    else:
        args = (partial, resid, norm, normed, inv)
        outs = (full, grad, sums)
    after = []
    if attend:
        args += tuple(attend)
        qkv = attend[0]
        heads, hd, length = qkv.shape[0], qkv.shape[1] // 3, qkv.shape[2]
        if kind == FORWARD:
            after = [shape((heads, hd, length), BF), shape((heads, 1, length), F32), shape((heads, length, length), F32), shape((heads, length, length), F32)]
            scratch.append(pltpu.VMEM((count, 2, 2, own, depth), BF))
        else:
            after = [shape(qkv.shape, BF), shape((heads, 1, 2 * length), F32)]
            scratch += [pltpu.VMEM((length, length), F32), pltpu.VMEM((heads, hd, length), BF)]
    outs += tuple(after)
    scratch += [
        pltpu.VMEM((units, 2, rows, depth), BF),
        pltpu.VMEM((units, rows, depth), BF),
        pltpu.VMEM((units, rows, depth), BF),
        dma((2, units, 2)),
        dma((2, units)),
        dma((2, units)),
        dma((2, units, 2)),
    ]
    in_specs, out_specs = [vmem] * len(args), [vmem] * len(outs)
    aliases = {}
    for ride, array in rides:
        if ride == SUM_ACROSS or ride == SUM_ALONG:
            n, wide = array.shape[1], depth // 2
            scratch += (across_scratch if ride == SUM_ACROSS else along_scratch)(seqs, n, wide)
            in_specs.append(vmem)
            out_specs.append(vmem)
            outs += (shape((seqs, n, wide), BF) if ride == SUM_ACROSS else shape((2, n, wide // 2), F32),)
        else:
            scratch += freight_scratch(seqs)
            aliases[len(args)] = len(outs)
            in_specs.append(anywhere)
            out_specs.append(anywhere)
            outs += (shape(array.shape, array.dtype),)
        args += (array,)
    return pl.pallas_call(
        functools.partial(exchange_kernel, kind, bool(attend), count, pieces, seqs, tuple(ride for ride, _ in rides)),
        out_shape=outs,
        in_specs=in_specs,
        out_specs=tuple(out_specs),
        scratch_shapes=scratch,
        input_output_aliases=aliases,
        compiler_params=pltpu.CompilerParams(collective_id=collective_id, has_side_effects=True, vmem_limit_bytes=50 << 20),
        name="exchange_%d" % collective_id,
    )(*args)


def cross_kernel(count, query, kv, out_weight, masked, resid, norm, cot, mix, full, output, grad, sums, dquery, dkv, doff, partial, lse, keys, keys_scaled, values_t, queries, g_scr, dk_scr, dv_scr, dmix, own, landing, return_sems, cot_own, cot_send, cot_recv, cot_local, core_buf, half_send, half_buf, rc, rh, gh, gc):
    place = spot()
    y, k, seq, half = place
    heads, hd, length = query.shape[0], query.shape[1], kv.shape[2]
    depth, rows = partial.shape[4], partial.shape[3]
    scale = hd**-0.5
    greet(
        [device(y, 1 - k, seq, half), device(y, k, seq, 1 - half)]
        + [device(ty, tk, seq, half) for dy, dk, ty, tk in rows_of(place) if dy]
    )
    cots = [shuffle(cot, cot_own, n, n, place, cot_send, cot_recv, cot_local) for n in range(count)]
    reduce = Reduce(partial, core_buf, half_send, half_buf, rc, rh, place, rows)
    spread = Spread(full, gh, gc, place, rows)
    back = Return(own, landing, return_sems, place, depth // 4)
    sums[...] = jnp.zeros_like(sums)
    g_scr[...] = jnp.zeros_like(g_scr)
    dk_scr[...] = jnp.zeros_like(dk_scr)
    dv_scr[...] = jnp.zeros_like(dv_scr)

    def prepare(h, carry):
        keys[h] = kv[h, :hd].T
        keys_scaled[h] = scaled(kv[h, :hd], scale)
        values_t[h] = kv[h, hd:].T
        queries[h] = scaled(query[h], scale)
        return carry

    lax.fori_loop(0, heads, prepare, 0)

    def attend_heads(s, low, high):
        def one(h, carry):
            here = slice(s * length, (s + 1) * length)
            mix[h, :, here], lse[h, :, here] = head_forward(keys[h], kv[h, hd:], queries[h, :, here], masked[h])
            return carry

        lax.fori_loop(low, high, one, 0)

    def send_products(s):
        for a in range(2):
            for b in range(2):
                partial[s, a, b] = project(mix, out_weight, s * length + (2 * a + b) * rows, rows)
        reduce.start(s, s, 0, True)
        reduce.start(s, s, 0, False)

    def turn(s):
        normed, inv = normalize(resid[s].astype(F32) + reduce.result(s, s, 0))
        for copy in cots[s]:
            copy.wait()
        upstream = cot_own[s].astype(F32)
        value = normalize_back(upstream, normed, inv, norm[0:1])
        grad[s] = value
        full[s, half, k] = value.astype(BF)
        spread.start(s, s, 0)
        sums[0:1] += column_sum(upstream * normed)
        sums[1:2] += column_sum(upstream)
        back.start(s, s, (normed * norm[0:1] + norm[1:2]).astype(BF))

    def attend_back(s):
        for a in range(2):
            for b in range(2):
                project_back(out_weight, full[s, a, b], dmix, (2 * a + b) * rows)

        def one(h, carry):
            here = slice(s * length, (s + 1) * length)
            dlogits, dq, dk, dv = head_backward(
                keys[h], keys_scaled[h], values_t[h], queries[h, :, here], dmix[h], lse[h, :, here], masked[h]
            )
            g_scr[h] += dlogits
            dquery[h, :, here] = dq
            dk_scr[h] += dk
            dv_scr[h] += dv
            return carry

        lax.fori_loop(0, heads, one, 0)

    for s in range(count):
        attend_heads(s, 0, heads // 2)
        if s >= 1:
            reduce.pass_on(s - 1, s - 1, 0)
        if s >= 2:
            turn(s - 2)
        attend_heads(s, heads // 2, heads)
        send_products(s)
    reduce.pass_on(count - 1, count - 1, 0)
    for s in range(max(count - 2, 0), count):
        turn(s)
    for s in range(count):
        spread.forward(s, s, 0)
        spread.ready(s)
        attend_back(s)
    for h in range(heads):
        dkv[h, :hd] = dk_scr[h].astype(BF)
        dkv[h, hd:] = dv_scr[h].astype(BF)

    def offsets_of(h, carry):
        offset_sums(g_scr, doff, (h,), (h,), length)
        return carry

    lax.fori_loop(0, heads, offsets_of, 0)
    back.finish()
    output[...] = landing[...].astype(F32)
    for s in range(count):
        spread.sent(s)
        reduce.finish(s)


def cross_attention(collective_id, query, kv, out_weight, masked, resid, norm, cot):
    count, own, depth = resid.shape
    heads, hd, total = query.shape
    length = kv.shape[2]
    dma = pltpu.SemaphoreType.DMA
    shape = jax.ShapeDtypeStruct
    outs = (
        shape(query.shape, BF),
        shape((count, 2, 2, own, depth), BF),
        shape((2, count, 2, own, depth // 4), F32),
        shape((count, own, depth), F32),
        shape((8, depth), F32),
        shape(query.shape, BF),
        shape(kv.shape, BF),
        shape((heads, 1, 2 * length), F32),
    )
    whole = pl.BlockSpec(memory_space=pltpu.VMEM)
    specs = [whole] * 7
    vmem = pltpu.VMEM
    return pl.pallas_call(
        functools.partial(cross_kernel, count),
        out_shape=outs,
        in_specs=specs,
        out_specs=tuple(whole for _ in outs),
        scratch_shapes=[
            vmem((count, 2, 2, own, depth), BF),
            vmem((heads, 1, total), F32),
            vmem((heads, length, hd), BF),
            vmem((heads, hd, length), BF),
            vmem((heads, length, hd), BF),
            vmem(query.shape, BF),
            vmem((heads, length, length), F32),
            vmem((heads, hd, length), F32),
            vmem((heads, hd, length), F32),
            vmem((heads, hd, length), BF),
            vmem((count, own, depth), BF),
            vmem((2, count, 2, own, depth // 4), BF),
            dma((2, count, 3)),
            vmem((count, own, depth), BF),
            dma((count, 3)),
            dma((count, 3)),
            dma((count,)),
            vmem((count, 2, own, depth), BF),
            vmem((count, own, depth), BF),
            vmem((count, own, depth), BF),
            dma((2, count, 2)),
            dma((2, count)),
            dma((2, count)),
            dma((2, count, 2)),
        ],
        compiler_params=pltpu.CompilerParams(collective_id=collective_id, has_side_effects=True, vmem_limit_bytes=56 << 20),
        name="cross_attention",
    )(query, kv, out_weight, masked, resid, norm, cot)


def inputs_kernel(seqs, groups, tok_ref, str_ref, norm_ref, ids_ref, tab_ref, *refs):
    refs = list(refs)
    take = lambda amount: [refs.pop(0) for _ in range(amount)]
    packs = take(groups)
    x_own, x_full, y_own, y_full, norm_all, ids_all, tab_all = take(7)
    fulls = take(groups)
    in_send, in_recv, in_local, xh, xc, yh, yc, small_sems, tab_sems, small_self, pack_sems, pack_self = take(12)
    place = spot()
    y, k, seq, half = place
    feat = tok_ref.shape[-1]
    own = tok_ref.shape[-2]
    row_peers = rows_of(place)
    others = [device(y, k, lax.rem(seq + d, seqs), half) for d in range(1, seqs)]
    greet([device(ty, tk, seq, half) for dy, dk, ty, tk in row_peers] + [device(y, k, seq, 1 - half)] + others)
    count = str_ref.shape[1]
    x_copies = shuffle(tok_ref, x_own, 0, 0, place, in_send, in_recv, in_local)
    loads = []
    for g in range(groups):
        here = fulls[g].at[0, :, lanes(k * feat, feat)]
        copy = pltpu.make_async_copy(packs[g].at[k], here, pack_self.at[g])
        copy.start()
        loads.append(
            (
                copy,
                remote(packs[g].at[1 - k], here, pack_sems.at[0, g], pack_sems.at[1, g], device(y, 1 - k, seq, half)),
            )
        )
    small = []
    for j, (source, target) in enumerate(((norm_ref, norm_all), (ids_ref, ids_all))):
        slot = (lambda dy: (slice(None), lanes(k * feat + 2 * dy * feat, feat))) if j == 0 else (lambda dy: (2 * y + k,))
        copy = pltpu.make_async_copy(source, target.at[slot(0)], small_self.at[j])
        copy.start()
        small.append(copy)
        for i, (dy, dk, ty, tk) in enumerate(row_peers):
            small.append(
                remote(source, target.at[slot(dy)], small_sems.at[0, j, i], small_sems.at[1, j, i], device(ty, tk, seq, half))
            )
    copy = pltpu.make_async_copy(tab_ref, tab_all.at[0], small_self.at[2])
    copy.start()
    small.append(copy)
    for d in range(1, seqs):
        small.append(remote(tab_ref, tab_all.at[d], tab_sems.at[0, d - 1], tab_sems.at[1, d - 1], others[d - 1]))
    freights = [Freight(full, *take(2), place, seqs) for full in fulls]
    for copy in loads[0]:
        copy.wait()
    for d in freights[0].first():
        freights[0].along(d)
    freights[0].across(0)
    for copy in x_copies:
        copy.wait()
    x_full[0, half, k] = x_own[0]
    x_spread = Spread(x_full, xh, xc, place, own)
    x_spread.start(0, 0, 0)
    y_copies = [shuffle(str_ref, y_own, n, 1 + n, place, in_send, in_recv, in_local) for n in range(count)]
    y_spread = Spread(y_full, yh, yc, place, own)
    for g in range(1, groups):
        for copy in loads[g]:
            copy.wait()
    x_spread.forward(0, 0, 0)
    for n in range(count):
        for copy in y_copies[n]:
            copy.wait()
        y_full[n, half, k] = y_own[n]
        y_spread.start(n, n, 0)
    freights[0].pass_along(True)
    for d in freights[1].first():
        freights[1].along(d)
    freights[0].arrive(True)
    freights[1].across(0)
    for n in range(count):
        y_spread.forward(n, n, 0)
    for copy in small:
        copy.wait()
    freights[1].pass_along(True)
    for d in freights[2].first():
        freights[2].along(d)
    freights[1].arrive(True)
    freights[2].pass_along(False)
    freights[2].arrive(False)
    x_spread.finish(0)
    for n in range(count):
        y_spread.finish(n)
    for freight in freights:
        freight.finish()


def gather_inputs(seqs, tokens, streams, norm, ids, table, packs):
    count, own, feat = streams.shape[1], streams.shape[-2], streams.shape[-1]
    depth = 4 * feat
    dma = pltpu.SemaphoreType.DMA
    shape = jax.ShapeDtypeStruct
    vmem = pl.BlockSpec(memory_space=pltpu.VMEM)
    outs = (
        shape((1, own, depth), BF),
        shape((1, 2, 2, own, depth), BF),
        shape((count, own, depth), BF),
        shape((count, 2, 2, own, depth), BF),
        shape((norm.shape[0], depth), F32),
        shape((4,) + ids.shape, jnp.int32),
        shape((seqs,) + table.shape, F32),
    )
    specs = [vmem] * len(outs)
    for pack in packs:
        outs += (shape((seqs, pack.shape[1], depth), BF),)
        specs.append(pl.BlockSpec(memory_space=pl.ANY))
    moves = 1 + count
    scratch = [
        dma((moves, 3)),
        dma((moves, 3)),
        dma((moves,)),
        dma((2, 1)),
        dma((2, 1, 2)),
        dma((2, count)),
        dma((2, count, 2)),
        dma((2, 2, 3)),
        dma((2, seqs - 1)),
        dma((3,)),
        dma((2, len(packs))),
        dma((len(packs),)),
    ]
    for _ in packs:
        scratch += freight_scratch(seqs)
    return pl.pallas_call(
        functools.partial(inputs_kernel, seqs, len(packs)),
        out_shape=outs,
        in_specs=[vmem] * (5 + len(packs)),
        out_specs=tuple(specs),
        scratch_shapes=scratch,
        compiler_params=pltpu.CompilerParams(collective_id=0, has_side_effects=True, vmem_limit_bytes=50 << 20),
        name="gather_inputs",
    )(tokens, streams, norm, ids, table, *packs)


def outputs_kernel(seqs, count, part_x, part_y, d1, d3, small, down, up, first, tok_out, str_out, small_out, down_out, up_out, first_out, core_buf, half_send, half_buf, own, land_x, land_y, rc, rh, rs, small_buf, ss, *refs):
    refs = list(refs)
    take = lambda amount: [refs.pop(0) for _ in range(amount)]
    place = spot()
    y, k, seq, half = place
    rows = part_x.shape[3]
    feat = part_x.shape[4] // 4
    bits = [1 << b for b in range((seqs - 1).bit_length())]
    flips = [device(y, k, seq + b - 2 * b * ((seq // b) % 2), half) for b in bits]
    others = [device(y, k, lax.rem(seq + d, seqs), half) for d in range(1, seqs)]
    partners = [device(y, 1 - k, seq, half), device(y, k, seq, 1 - half), device(1 - y, k, seq, half)]
    greet(partners + [device(1 - y, 1 - k, seq, half)] + others)
    partners += flips
    small_out[...] = small[...]

    def add_small(stage):
        copy = remote(small_out, small_buf.at[stage], ss.at[0, stage], ss.at[1, stage], partners[stage])
        copy.wait()
        small_out[...] += small_buf[stage]

    class Both:
        def __getitem__(self, index):
            return part_x[(0,) + index[1:]] if index[0] == 0 else part_y[(index[0] - 1,) + index[1:]]

        @property
        def at(self):
            return View()

    class View:
        def __getitem__(self, index):
            return part_x.at[(0,) + index[1:]] if index[0] == 0 else part_y.at[(index[0] - 1,) + index[1:]]

    reduce = Reduce(Both(), core_buf, half_send, half_buf, rc, rh, place, rows)
    units = range(count + 1)
    down = Collect(down, place, seqs, z_refs=[down_out] + take(5))
    up = Collect(up, place, seqs, y_refs=take(2), z_refs=[up_out] + take(5))
    first = Collect(first, place, seqs, y_refs=take(2), z_refs=[first_out] + take(5))
    reduce.start(0, 0, 0, True)
    reduce.start(0, 0, 0, False)
    add_small(2)
    up.across()
    add_small(1)
    reduce.pass_on(0, 0, 0)
    for stage in range(3, len(partners)):
        add_small(stage)
    for d in down.order[:2]:
        down.along(d)
    add_small(0)
    for unit in units[1:]:
        reduce.start(unit, unit, 0, True)
        reduce.start(unit, unit, 0, False)
    x_back = Return(own, land_x, rs, place, feat)
    y_back = Return(own, land_y, rs, place, feat)
    x_back.start(0, 0, (d1[0] + reduce.result(0, 0, 0)).astype(BF))
    first.across()
    for unit in units[1:]:
        reduce.pass_on(unit, unit, 0)
    for d in down.order[2:-1]:
        down.along(d)
    for d in up.order[:1]:
        up.along(d)
    down.close()
    for d in up.order[1:-1]:
        up.along(d)
    for unit in units[1:]:
        y_back.start(unit, unit - 1, (d3[unit - 1] + reduce.result(unit, unit, 0)).astype(BF))
    for unit in units:
        reduce.finish(unit)
    x_back.finish()
    tok_out[...] = land_x[:, 0].astype(F32)
    up.close()
    for d in first.order[:-1]:
        first.along(d)
    y_back.finish()
    str_out[...] = land_y[...].astype(F32)
    first.close()
    for collect in (down, up, first):
        collect.finish()


def scatter_outputs(seqs, collective_id, part_x, part_y, d1, d3, small, down, up, first):
    count, _, _, own, depth = part_y.shape
    feat, wide = depth // 4, depth // 2
    units = count + 1
    dma = pltpu.SemaphoreType.DMA
    shape = jax.ShapeDtypeStruct
    stages = 3 + (seqs - 1).bit_length()
    outs = (shape((2, 2, own, feat), F32), shape((2, count, 2, own, feat), F32), shape(small.shape, F32))
    outs += tuple(shape((2, group.shape[1], feat), F32) for group in (down, up, first))
    scratch = [
        pltpu.VMEM((units, 2, own, depth), BF),
        pltpu.VMEM((units, own, depth), BF),
        pltpu.VMEM((units, own, depth), BF),
        pltpu.VMEM((units, own, depth), BF),
        pltpu.VMEM((2, 1, 2, own, feat), BF),
        pltpu.VMEM((2, count, 2, own, feat), BF),
        dma((2, units, 2)),
        dma((2, units)),
        dma((2, units, 3)),
        pltpu.VMEM((stages,) + small.shape, F32),
        dma((2, stages)),
    ]
    scratch += along_scratch(seqs, down.shape[1], wide)
    for group in (up, first):
        scratch += across_scratch(seqs, group.shape[1], wide) + along_scratch(seqs, group.shape[1], wide)
    return pl.pallas_call(
        functools.partial(outputs_kernel, seqs, count),
        out_shape=outs,
        in_specs=[pl.BlockSpec(memory_space=pltpu.VMEM)] * 8,
        out_specs=tuple(pl.BlockSpec(memory_space=pltpu.VMEM) for _ in outs),
        scratch_shapes=scratch,
        compiler_params=pltpu.CompilerParams(collective_id=collective_id, has_side_effects=True, vmem_limit_bytes=50 << 20),
        name="scatter_outputs",
    )(part_x, part_y, d1, d3, small, down, up, first)


def pick(array, index, axis):
    return lax.dynamic_index_in_dim(array, index, axis, keepdims=False)


def dot_f32(spec, left, right):
    return jnp.einsum(spec, left, right, preferred_element_type=F32)


def on_device(
    rows,
    cols,
    tokens,
    streams,
    cotangent,
    block_ids,
    bucket_ids,
    w_qkv,
    enc_table,
    w_out,
    attention_norm_gain,
    attn_bias,
    w_up,
    w_down,
    ffn_gain,
    ffn_bias,
    w_query,
    w_keyval,
    cross_table,
    w_cross_out,
    cross_gain,
    cross_bias,
):
    seqs = cols // 2
    row, col = lax.axis_index(ROW), lax.axis_index(COL)
    y, k, seq, half = row // 2, row % 2, col // 2, col % 2
    low_y = y == 0
    stream_count = streams.shape[1]
    tok = tokens.shape[1]
    own = tok // 2
    feat = tokens.shape[2]
    length = block_ids.shape[2]
    head_dim = w_qkv.shape[2] // 2
    ff = w_up.shape[1] // 2
    table_heads, bucket_count = enc_table.shape

    def columns(weight, parts):
        return weight.reshape(feat, parts, 2, -1).transpose(2, 1, 3, 0).reshape(2, -1, feat)

    def columns_back(array, parts):
        return array.reshape(2, parts, -1, feat).transpose(3, 1, 0, 2).reshape(feat, parts, -1)

    halves = lambda weight: weight.reshape(2, -1, feat)
    hd3, hd2 = 3 * head_dim, 2 * head_dim
    packs = (
        jnp.concatenate([columns(w_qkv, 3), halves(w_out)], axis=1),
        columns(w_up, 1),
        halves(w_down),
        jnp.concatenate([columns(w_keyval, 2), columns(w_query, 1), halves(w_cross_out)], axis=1),
    )
    norm_params = jnp.stack([attention_norm_gain, attn_bias, ffn_gain, ffn_bias, cross_gain, cross_bias] + [cross_bias] * 2)
    table_pack = jnp.zeros((8, 128), F32).at[0].set(jnp.stack([enc_table, cross_table]).reshape(-1))
    micro_count = tokens.shape[0]
    x_own, x_full, y_own, y_full, norm_params, all_ids, all_tables, first, up, down, last = gather_inputs(
        seqs,
        tokens.reshape(micro_count, 1, 2, own, feat),
        streams.reshape(micro_count, stream_count, 2, own, feat),
        norm_params,
        block_ids.reshape(8, -1),
        table_pack,
        packs,
    )
    x_full, y_full = x_full.reshape(length, D), y_full.reshape(stream_count * length, D)
    segment = pick(pick(all_ids.reshape(rows, micro_count, length), seq, 0), y, 0)
    segq = segment[None]
    segk = jnp.broadcast_to(segment[:, None], (length, length))
    own_tables = pick(all_tables[:, 0].reshape(seqs, 2, table_heads, bucket_count), k, 2)
    slot_col = 2 * ((seq - jnp.arange(seqs)) % seqs) + half
    reversed_ids = jnp.concatenate([jnp.full((1,), -1, jnp.int32), bucket_ids[::-1]])
    onehot = bucket_onehot(reversed_ids, bucket_count)
    offsets = jnp.einsum("htb,bo->tho", own_tables, onehot, precision=highest)[:, :, None, :]

    m_qkv, m_out = first[:, :hd3], first[:, hd3:].reshape(-1, D)
    blocked = lambda product: product.astype(BF).reshape(-1, 2, 2, own, D)

    qkv = dot_f32("snr,tr->snt", m_qkv, x_full).astype(BF)
    hidden_full, hidden, normed1, inv1, mix, lse, enc_bias, cross_bias_full, down, last = exchange(
        FORWARD,
        1,
        seqs,
        None,
        x_own,
        norm_params[0:2],
        rides=((ACROSS, down), (ALONG, last)),
        attend=(qkv, m_out, offsets, segq, segk),
    )
    mix_flat = mix.reshape(-1, length)
    up, down = up.reshape(-1, D), down.reshape(-1, D)
    hidden_full = hidden_full.reshape(length, D)
    pre = dot_f32("fr,tr->ft", up, hidden_full)
    act, gelu_pull = jax.vjp(gelu_exact, pre)
    act = act.astype(BF)
    enc_full, _, normed2, inv2, last = exchange(
        FORWARD,
        2,
        seqs,
        blocked(dot_f32("ft,fr->tr", act, down)),
        hidden,
        norm_params[2:4],
        rides=((ACROSS, last),),
    )
    m_kv, m_q, m_co = last[:, :hd2], last[:, hd2:hd3], last[:, hd3:].reshape(-1, D)
    enc_full = enc_full.reshape(length, D)
    kv = dot_f32("snr,tr->snt", m_kv, enc_full).astype(BF)
    query = dot_f32("snr,tr->snt", m_q, y_full).astype(BF)
    cmix, d3_full, output, d3, sums3, dquery, dkv, doff_cross = cross_attention(
        3,
        query,
        kv,
        m_co,
        cross_bias_full,
        y_own,
        norm_params[4:6],
        cotangent.reshape(micro_count, stream_count, 2, own, feat),
    )
    cmix_flat = cmix.reshape(-1, stream_count * length)
    d3_full = d3_full.reshape(stream_count * length, D)

    g_co = dot_f32("et,tr->er", cmix_flat, d3_full)
    g_q = dot_f32("snt,tr->snr", dquery, y_full)
    g_kv = dot_f32("snt,tr->snr", dkv, enc_full)
    g_last = jnp.concatenate([g_kv.astype(BF), g_q.astype(BF), g_co.astype(BF).reshape(seqs, head_dim, D)], axis=1)
    d2_full, d2, sums2, g_last = exchange(
        BACKWARD,
        4,
        seqs,
        blocked(dot_f32("snt,snr->tr", dkv, m_kv)),
        norm_params[2:4][None],
        norm_params[2:4],
        normed=normed2,
        inv=inv2,
        rides=((SUM_ACROSS, g_last),),
    )
    d2_full = d2_full.reshape(length, D)
    part_y = blocked(dot_f32("snt,snr->tr", dquery, m_q))
    dact = dot_f32("fr,tr->ft", down, d2_full)
    dpre = gelu_pull(dact)[0].astype(BF)
    g_down = dot_f32("ft,tr->fr", act, d2_full).astype(BF).reshape(seqs, ff, D)
    d1_full, d1, sums1, dqkv, doff_enc, g_last, g_down = exchange(
        BACKWARD,
        5,
        seqs,
        blocked(dot_f32("ft,fr->tr", dpre, up)),
        d2,
        norm_params[0:2],
        normed=normed1,
        inv=inv1,
        rides=((SUM_ALONG, g_last), (SUM_ACROSS, g_down)),
        attend=(qkv, m_out, enc_bias, lse),
    )
    d1_full = d1_full.reshape(length, D)
    g_up = dot_f32("ft,tr->fr", dpre, hidden_full).astype(BF).reshape(seqs, ff, D)
    g_out = dot_f32("et,tr->er", mix_flat, d1_full)
    g_qkv = dot_f32("snt,tr->snr", dqkv, x_full)
    g_first = jnp.concatenate([g_qkv.astype(BF), g_out.astype(BF).reshape(seqs, head_dim, D)], axis=1)
    part_x = blocked(dot_f32("snt,snr->tr", dqkv, m_qkv))

    norm_grads = jnp.concatenate([sums1[:2], sums2[:2], sums3[:2]])
    norm_grads = jnp.where(low_y, norm_grads, jnp.roll(norm_grads, D // 2, axis=1))
    table_grads = jnp.einsum(
        "tho,bo->thb", jnp.stack([doff_enc[:, 0], doff_cross[:, 0]]), onehot, precision=highest
    )
    heads = 2 * slot_col + k
    spread = (heads[:, None] == jnp.arange(table_heads * cols)[None, :]).astype(F32)
    table_grads = jnp.einsum("thb,hg->tgb", table_grads, spread, precision=highest)
    small = jnp.concatenate([norm_grads.reshape(-1, 128), table_grads.reshape(-1, 128)])
    grad_tokens, grad_streams, small, g_down, g_up, g_first = scatter_outputs(
        seqs, 6, part_x, part_y, d1, d3, small, g_down, g_up, g_first
    )
    output, grad_streams = output.reshape(streams.shape), grad_streams.reshape(streams.shape)
    grad_tokens = grad_tokens.reshape(tokens.shape)
    count = norm_grads.size // 128
    norm_sums = lax.dynamic_slice_in_dim(small[:count].reshape(6, D), row * feat, feat, axis=1)
    table_sums = small[count:].reshape(2, table_heads * cols, bucket_count)
    table_sums = lax.dynamic_slice_in_dim(table_sums, col * table_heads, table_heads, axis=1)
    return (
        output,
        grad_tokens,
        grad_streams,
        columns_back(g_first[:, :hd3], 3),
        table_sums[0],
        g_first[:, hd3:].reshape(w_out.shape),
        norm_sums[0],
        norm_sums[1],
        columns_back(g_up, 1).reshape(w_up.shape),
        g_down.reshape(w_down.shape),
        norm_sums[2],
        norm_sums[3],
        columns_back(g_last[:, hd2:hd3], 1).reshape(w_query.shape),
        columns_back(g_last[:, :hd2], 2),
        table_sums[1],
        g_last[:, hd3:].reshape(w_cross_out.shape),
        norm_sums[4],
        norm_sums[5],
    )


def solution(mesh):
    whole_row, half_col = mesh.shape[ROW], mesh.shape[COL]
    wide, table, norm = P(ROW, None, COL), P(COL, None), P(ROW)
    up, down = P(ROW, COL), P(COL, ROW)
    weights = (wide, table, down, norm, norm, up, down, norm, norm, up, wide, table, down, norm, norm)

    def run(tokens, *rest):
        micro_count = tokens.shape[0]
        if whole_row == 4 and micro_count == 2 and half_col % 2 == 0:
            device_fn = functools.partial(on_device, whole_row, half_col)
        else:
            device_fn = on_device_general
        return jax.shard_map(
            device_fn,
            mesh=mesh,
            in_specs=(P(None, COL, ROW), P(None, None, COL, ROW), P(None, None, COL, ROW), P(None, ROW, None), P()) + weights,
            out_specs=(P(None, None, COL, ROW), P(None, COL, ROW), P(None, None, COL, ROW)) + weights,
            check_vma=False,
        )(tokens, *rest)

    return run
```

```python
import functools
import math
import types
import jax
import jax.numpy as jnp
from jax import lax
from jax.experimental import pallas as pl
from jax.experimental.pallas import tpu as pltpu
from jax.sharding import PartitionSpec as P

D = 1024
F32 = jnp.float32
BF = jnp.bfloat16
ROW, COL = "row", "col"


epsilon = 1e-05
neg_fill = -1e30
highest = lax.Precision.HIGHEST


def gather_cols(local_rows):
    return lax.all_gather(local_rows, COL, axis=1, tiled=True)


def gather_rows(local_rows):
    return lax.all_gather(local_rows, ROW, axis=1, tiled=True)


def product(matmul_operand, weight_matrix):
    return jnp.einsum(
        "ray,yw->raw", matmul_operand, weight_matrix, preferred_element_type=jnp.float32
    )


def rows_product(operand_full, matrix):
    return lax.psum_scatter(product(operand_full, matrix), ROW, scatter_dimension=1, tiled=True)


def cols_product(operand_full, matrix):
    return lax.psum_scatter(product(operand_full, matrix), COL, scatter_dimension=1, tiled=True)


def weight_grad(matmul_operand, upstream_gradient):
    return jnp.einsum(
        "bpt,bpr->tr", matmul_operand, upstream_gradient, preferred_element_type=jnp.float32
    )


def gelu_exact(argument):
    return jax.nn.gelu(argument, approximate=False)


def norm_forward(residual, gain_vec, bias_vec):
    local_sum = jnp.sum(residual, axis=-1)
    average = lax.psum(local_sum, ROW) / D
    centered = residual - average[..., None]
    spread = lax.psum(jnp.sum(centered * centered, axis=-1), ROW) / D
    inv_std = lax.rsqrt(spread + epsilon)
    normed = centered * inv_std[..., None]
    return (normed * gain_vec + bias_vec, normed, inv_std)


def norm_back(out_grad, normed, inv_std, gain_vec):
    scaled_grad = out_grad * gain_vec
    first_moment, second_moment = lax.psum(
        (jnp.sum(scaled_grad, axis=-1), jnp.sum(scaled_grad * normed, axis=-1)), ROW
    )
    resid_grad = inv_std[..., None] * (
        scaled_grad - first_moment[..., None] / D - normed * (second_moment[..., None] / D)
    )
    return (resid_grad, jnp.sum(out_grad * normed, axis=(0, 1)), jnp.sum(out_grad, axis=(0, 1)))


def bucket_onehot(bucket_ids, bucket_count):
    return (bucket_ids[None, :] == jnp.arange(bucket_count, dtype=jnp.int32)[:, None]).astype(
        jnp.float32
    )


def block_logits(query_blk, key_rows, offsets, segment, first_row):
    row_count = query_blk.shape[2]
    length = key_rows.shape[1]
    score_scale = query_blk.shape[-1] ** (-0.5)
    raw_scores = jnp.einsum(
        "snqhd,nkhd->snhqk", query_blk, key_rows, preferred_element_type=jnp.float32
    )
    places = jnp.arange(length, dtype=jnp.int32)
    query_pos = first_row + jnp.arange(row_count, dtype=jnp.int32)
    offset_index = places[None, :] - query_pos[:, None] + (length - 1)
    pos_bias = jnp.take(offsets, offset_index, axis=1)
    visible = segment[:, first_row : first_row + row_count, None] >= segment[:, None, :]
    return jnp.where(
        visible[None, :, None], raw_scores * score_scale + pos_bias[None, None], neg_fill
    )


def attend(queries, key_rows, value_rows, segment, offsets):
    score_logits = block_logits(queries, key_rows, offsets, segment, 0)
    row_max = jnp.max(score_logits, axis=-1, keepdims=True)
    log_total = row_max + jnp.log(jnp.sum(jnp.exp(score_logits - row_max), axis=-1, keepdims=True))
    weights = jnp.exp(score_logits - log_total).astype(jnp.bfloat16)
    mixed_parts = jnp.einsum(
        "snhqk,nkhd->snqhd", weights, value_rows, preferred_element_type=jnp.float32
    )
    lse_parts = log_total[..., 0]
    return (mixed_parts, lse_parts)


def diagonal_sums(summand):
    head_count, row_count, length = summand.shape
    flipped = summand[:, ::-1, :]
    padded = jnp.concatenate(
        [flipped, jnp.zeros((head_count, row_count, row_count), summand.dtype)], axis=2
    )
    flattened = padded.reshape(head_count, row_count * (length + row_count))[
        :, : row_count * (length + row_count - 1)
    ]
    return jnp.sum(flattened.reshape(head_count, row_count, length + row_count - 1), axis=1)


def attend_back(queries, key_rows, value_rows, segment, offsets, onehot, log_totals, mix_grad):
    length = key_rows.shape[1]
    block_rows = min(512, length)
    score_scale = queries.shape[-1] ** (-0.5)
    offset_grad = jnp.zeros(offsets.shape, jnp.float32)
    score_logits = block_logits(queries, key_rows, offsets, segment, 0)
    probability = jnp.exp(score_logits - log_totals[:, :, :, 0:block_rows, None])
    prob_grad = jnp.einsum(
        "snqhd,nkhd->snhqk", mix_grad, value_rows, preferred_element_type=jnp.float32
    )
    logit_grad = probability * (
        prob_grad - jnp.sum(probability * prob_grad, axis=-1, keepdims=True)
    )
    scaled = (logit_grad * score_scale).astype(jnp.bfloat16)
    query_parts = jnp.einsum(
        "snhqk,nkhd->snqhd", scaled, key_rows, preferred_element_type=jnp.float32
    )
    key_grad = jnp.einsum("snhqk,snqhd->nkhd", scaled, queries, preferred_element_type=jnp.float32)
    value_grad = jnp.einsum(
        "snhqk,snqhd->nkhd",
        probability.astype(jnp.bfloat16),
        mix_grad,
        preferred_element_type=jnp.float32,
    )
    low_end = length - block_rows
    offset_grad = offset_grad.at[:, low_end : low_end + length + block_rows - 1].add(
        diagonal_sums(jnp.sum(logit_grad, axis=(0, 1)))
    )
    table_grad = jnp.dot(offset_grad, onehot.T, precision=highest)
    return (query_parts, key_grad, value_grad, table_grad)


def on_device_general(
    tokens,
    streams,
    cotangent,
    block_ids,
    bucket_ids,
    w_qkv,
    enc_table,
    w_out,
    attention_norm_gain,
    attn_bias,
    w_up,
    w_down,
    ffn_gain,
    ffn_bias,
    w_query,
    w_keyval,
    cross_table,
    w_cross_out,
    cross_gain,
    cross_bias,
):
    micro_count = tokens.shape[0]
    stream_count = streams.shape[1]
    seq_rows = block_ids.shape[1]
    length = block_ids.shape[2]
    head_count = enc_table.shape[0]
    bucket_count = enc_table.shape[1]
    row_width = w_qkv.shape[0]
    col_width = w_qkv.shape[2]
    head_dim = col_width // head_count
    row_tokens = seq_rows * length
    qkv_matrix = w_qkv.reshape(row_width, 3 * col_width)
    keyval_matrix = w_keyval.reshape(row_width, 2 * col_width)
    onehot = bucket_onehot(bucket_ids, bucket_count)
    enc_offsets = jnp.dot(enc_table, onehot, precision=highest)
    cross_offsets = jnp.dot(cross_table, onehot, precision=highest)
    qkv_acc = jnp.zeros((row_width, 3 * col_width), jnp.float32)
    out_acc = jnp.zeros(w_out.shape, jnp.float32)
    up_acc = jnp.zeros(w_up.shape, jnp.float32)
    down_acc = jnp.zeros(w_down.shape, jnp.float32)
    query_acc = jnp.zeros(w_query.shape, jnp.float32)
    keyval_acc = jnp.zeros((row_width, 2 * col_width), jnp.float32)
    cross_out_acc = jnp.zeros(w_cross_out.shape, jnp.float32)
    enc_table_acc = jnp.zeros(enc_table.shape, jnp.float32)
    cross_table_acc = jnp.zeros(cross_table.shape, jnp.float32)
    norm_accs = [jnp.zeros((row_width,), jnp.float32) for place_holder in range(6)]
    outputs = []
    token_grads = []
    stream_grads = []
    for micro in range(micro_count):
        segment = block_ids[micro]
        x_in = tokens[micro][None]
        y_in = streams[micro]
        x_full = gather_cols(x_in)
        qkv = (
            rows_product(x_full, qkv_matrix)
            .astype(jnp.bfloat16)
            .reshape(seq_rows, length, 3, head_count, head_dim)
        )
        enc_query = qkv[:, :, 0][None]
        enc_key = qkv[:, :, 1]
        encoder_value_rows = qkv[:, :, 2]
        enc_mixed, enc_lse = attend(enc_query, enc_key, encoder_value_rows, segment, enc_offsets)
        enc_mix = enc_mixed.reshape(1, row_tokens, col_width).astype(jnp.bfloat16)
        mix_full = gather_rows(enc_mix)
        attn_branch = cols_product(mix_full, w_out)
        hidden, normed_one, inv_one = norm_forward(
            x_in.astype(jnp.float32) + attn_branch, attention_norm_gain, attn_bias
        )
        hidden_low = hidden.astype(jnp.bfloat16)
        hidden_full = gather_cols(hidden_low)
        pre_act = rows_product(hidden_full, w_up)
        act_value, gelu_pull = jax.vjp(gelu_exact, pre_act)
        act_low = act_value.astype(jnp.bfloat16)
        act_full = gather_rows(act_low)
        ffn_branch = cols_product(act_full, w_down)
        encoded, normed_two, inv_two = norm_forward(hidden + ffn_branch, ffn_gain, ffn_bias)
        encoded_low = encoded.astype(jnp.bfloat16)
        enc_full = gather_cols(encoded_low)
        keyval = (
            rows_product(enc_full, keyval_matrix)
            .astype(jnp.bfloat16)
            .reshape(seq_rows, length, 2, head_count, head_dim)
        )
        cross_key = keyval[:, :, 0]
        cross_value = keyval[:, :, 1]
        stream_full = gather_cols(y_in)
        cross_query = (
            rows_product(stream_full, w_query)
            .astype(jnp.bfloat16)
            .reshape(stream_count, seq_rows, length, head_count, head_dim)
        )
        cross_mixed, cross_lse = attend(cross_query, cross_key, cross_value, segment, cross_offsets)
        cross_mix = cross_mixed.reshape(stream_count, row_tokens, col_width).astype(jnp.bfloat16)
        cross_full = gather_rows(cross_mix)
        cross_branch = cols_product(cross_full, w_cross_out)
        result, normed_three, inv_three = norm_forward(
            y_in.astype(jnp.float32) + cross_branch, cross_gain, cross_bias
        )
        outputs.append(result)
        grad_three, gain_part, bias_part = norm_back(
            cotangent[micro].astype(jnp.float32), normed_three, inv_three, cross_gain
        )
        norm_accs[4] = norm_accs[4] + gain_part
        norm_accs[5] = norm_accs[5] + bias_part
        branch_full = gather_cols(grad_three.astype(jnp.bfloat16))
        cross_out_acc = cross_out_acc + weight_grad(cross_full, branch_full)
        cross_mix_grad = (
            rows_product(branch_full, w_cross_out.T)
            .astype(jnp.bfloat16)
            .reshape(stream_count, seq_rows, length, head_count, head_dim)
        )
        query_grad, key_grad, value_grad, table_grad = attend_back(
            cross_query,
            cross_key,
            cross_value,
            segment,
            cross_offsets,
            onehot,
            cross_lse,
            cross_mix_grad,
        )
        cross_table_acc = cross_table_acc + table_grad
        query_low = query_grad.reshape(stream_count, row_tokens, col_width).astype(jnp.bfloat16)
        keyval_low = (
            jnp.stack(
                [
                    key_grad.reshape(row_tokens, col_width),
                    value_grad.reshape(row_tokens, col_width),
                ],
                axis=1,
            )
            .reshape(1, row_tokens, 2 * col_width)
            .astype(jnp.bfloat16)
        )
        query_full = gather_rows(query_low)
        query_acc = query_acc + weight_grad(stream_full, query_full)
        stream_grads.append(grad_three + cols_product(query_full, w_query.T))
        keyval_full = gather_rows(keyval_low)
        keyval_acc = keyval_acc + weight_grad(enc_full, keyval_full)
        encoded_grad = cols_product(keyval_full, keyval_matrix.T)
        grad_two, gain_part, bias_part = norm_back(encoded_grad, normed_two, inv_two, ffn_gain)
        norm_accs[2] = norm_accs[2] + gain_part
        norm_accs[3] = norm_accs[3] + bias_part
        feedforward_full_output = gather_cols(grad_two.astype(jnp.bfloat16))
        down_acc = down_acc + weight_grad(act_full, feedforward_full_output)
        act_grad = rows_product(feedforward_full_output, w_down.T)
        pre_low = gelu_pull(act_grad)[0].astype(jnp.bfloat16)
        pre_full = gather_rows(pre_low)
        up_acc = up_acc + weight_grad(hidden_full, pre_full)
        hidden_grad = grad_two + cols_product(pre_full, w_up.T)
        grad_one, gain_part, bias_part = norm_back(
            hidden_grad, normed_one, inv_one, attention_norm_gain
        )
        norm_accs[0] = norm_accs[0] + gain_part
        norm_accs[1] = norm_accs[1] + bias_part
        attn_full = gather_cols(grad_one.astype(jnp.bfloat16))
        out_acc = out_acc + weight_grad(mix_full, attn_full)
        enc_mix_grad = (
            rows_product(attn_full, w_out.T)
            .astype(jnp.bfloat16)
            .reshape(1, seq_rows, length, head_count, head_dim)
        )
        enc_qgrad, enc_kgrad, enc_vgrad, table_grad = attend_back(
            enc_query,
            enc_key,
            encoder_value_rows,
            segment,
            enc_offsets,
            onehot,
            enc_lse,
            enc_mix_grad,
        )
        enc_table_acc = enc_table_acc + table_grad
        qkv_low = (
            jnp.stack(
                [
                    enc_qgrad.reshape(row_tokens, col_width),
                    enc_kgrad.reshape(row_tokens, col_width),
                    enc_vgrad.reshape(row_tokens, col_width),
                ],
                axis=1,
            )
            .reshape(1, row_tokens, 3 * col_width)
            .astype(jnp.bfloat16)
        )
        qkv_full = gather_rows(qkv_low)
        qkv_acc = qkv_acc + weight_grad(x_full, qkv_full)
        token_grads.append((grad_one + cols_product(qkv_full, qkv_matrix.T))[0])
    norm_stack = jnp.stack(norm_accs)
    table_stack = jnp.stack([enc_table_acc, cross_table_acc])
    norm_sums = lax.psum(norm_stack, COL)
    table_sums = lax.psum(table_stack, ROW)
    return (
        jnp.stack(outputs),
        jnp.stack(token_grads),
        jnp.stack(stream_grads),
        qkv_acc.reshape(row_width, 3, col_width),
        table_sums[0],
        out_acc,
        norm_sums[0],
        norm_sums[1],
        up_acc,
        down_acc,
        norm_sums[2],
        norm_sums[3],
        query_acc,
        keyval_acc.reshape(row_width, 2, col_width),
        table_sums[1],
        cross_out_acc,
        norm_sums[4],
        norm_sums[5],
    )


def mm(a,b):
    return jnp.dot(a,b,preferred_element_type=F32)
def mm_nt(a,b):
    return lax.dot_general(a,b,(((1,),(1,)),((),())),preferred_element_type=F32)

def mm_tn(a, b):
    return lax.dot_general(a, b, (((0,), (0,)), ((), ())), preferred_element_type=F32)


def masked_bias(off_ref, index, segq, segk):
    length = segk.shape[0]
    row = jnp.broadcast_to(off_ref[index], (length, 2 * length))
    rolled = pltpu.roll(row, 0, 1, stride=1, stride_axis=0)
    return jnp.where(segk[...] <= segq[...], rolled[:, length:], neg_fill)


def head_forward(keys, values, query, bias):
    logits = mm(keys, query) + bias
    top = jnp.max(logits, axis=0, keepdims=True)
    weight = jnp.exp(logits - top)
    total = jnp.sum(weight, axis=0, keepdims=True)
    return (mm(values, weight.astype(BF)) * (1.0 / total)).astype(BF), top + jnp.log(total)


def head_backward(keys, keys_t, values_t, query, grad, lse, bias):
    prob = jnp.exp(mm(keys, query) + (bias - lse))
    dprob = mm(values_t, grad)
    dlogits = prob * (dprob - jnp.sum(prob * dprob, axis=0, keepdims=True))
    low = dlogits.astype(BF)
    return dlogits, mm(keys_t, low).astype(BF), mm_nt(query, low), mm_nt(grad, prob.astype(BF))


def project(mix_ref, weight, start, rows):
    heads, hd = mix_ref.shape[0], mix_ref.shape[1]
    mixed = mix_ref[:, :, start : start + rows].reshape(heads * hd, rows)
    return mm_tn(mixed, weight).astype(BF)


def project_back(weight, rows_value, dmix_ref, start):
    heads, hd = dmix_ref.shape[0], dmix_ref.shape[1]
    rows = rows_value.shape[0]
    dmix_ref[:, :, start : start + rows] = mm_nt(weight, rows_value).astype(BF).reshape(heads, hd, rows)


def scaled(value, scale):
    return (value.astype(F32) * scale).astype(BF)


def offset_sums(g_ref, doff_ref, g_index, out_index, length):
    sub = lax.broadcasted_iota(jnp.int32, (8, 2 * length), 0)
    acc = jnp.zeros((8, 2 * length), F32)
    for i in range(length // 8):
        piece = g_ref[g_index + (pl.ds(8 * i, 8),)]
        padded = jnp.concatenate([jnp.zeros((8, length), F32), piece], axis=1)
        acc = acc + (pltpu.roll(padded, 2 * length - 8 * i, 1) if i else padded)
    for b in (1, 2, 4):
        acc = jnp.where((sub // b) % 2 == 1, pltpu.roll(acc, 2 * length - b, 1), acc)
    doff_ref[out_index] = jnp.sum(acc, axis=0, keepdims=True)


MESH = pl.DeviceIdType.MESH
FORWARD, BACKWARD = range(2)
ACROSS, THROUGH, ALONG, SUM_ALONG = range(4)


def spot():
    row, col = lax.axis_index(ROW), lax.axis_index(COL)
    return row // 2, row % 2, col // 2, col % 2


def device(y, k, seq, half):
    return (2 * y + k, 2 * seq + half)


def greet(devices):
    barrier = pltpu.get_barrier_semaphore()
    for target in devices:
        pl.semaphore_signal(barrier, inc=1, device_id=target, device_id_type=MESH)
    pl.semaphore_wait(barrier, len(devices))


def remote(source, target, send_sem, recv_sem, device_id):
    copy = pltpu.make_async_remote_copy(
        src_ref=source, dst_ref=target, send_sem=send_sem, recv_sem=recv_sem, device_id=device_id, device_id_type=MESH
    )
    copy.start()
    return copy


def lanes(start, size):
    return pl.ds(pl.multiple_of(start, size), size)


def rows_of(place):
    y, k, seq, half = place
    return [(dy, dk, (1 - y if dy else y), (1 - k if dk else k)) for dy, dk in ((0, 1), (1, 0), (1, 1))]


class Spread:
    def __init__(self, full_ref, half_sems, core_sems, place, rows):
        self.full, self.place, self.rows = full_ref, place, rows
        self.half_sems, self.core_sems = half_sems, core_sems
        self.first, self.second = {}, {}

    def block(self, n, piece, half, k):
        return self.full.at[n, half, k, pl.ds(piece * self.rows, self.rows)]

    def start(self, unit, n, piece):
        y, k, seq, half = self.place
        mine = self.block(n, piece, half, k)
        hs, cs = self.half_sems, self.core_sems
        self.first[unit] = (
            remote(mine, mine, hs.at[0, unit], hs.at[1, unit], device(y, k, seq, 1 - half)),
            remote(mine, mine, cs.at[0, unit, 0], cs.at[1, unit, 0], device(y, 1 - k, seq, half)),
        )

    def forward(self, unit, n, piece):
        y, k, seq, half = self.place
        self.first[unit][0].wait_recv()
        theirs = self.block(n, piece, 1 - half, k)
        cs = self.core_sems
        self.second[unit] = remote(theirs, theirs, cs.at[0, unit, 1], cs.at[1, unit, 1], device(y, 1 - k, seq, half))

    def ready(self, unit):
        self.first[unit][1].wait_recv()
        self.second[unit].wait_recv()

    def sent(self, unit):
        for copy in self.first[unit] + (self.second[unit],):
            copy.wait_send()

    def finish(self, unit):
        self.ready(unit)
        self.sent(unit)


class Reduce:
    def __init__(self, partial_ref, core_buf, half_send, half_buf, core_sems, half_sems, place, rows):
        self.partial, self.core_buf, self.half_send, self.half_buf = partial_ref, core_buf, half_send, half_buf
        self.core_sems, self.half_sems, self.place, self.rows = core_sems, half_sems, place, rows
        self.first, self.second = {}, {}

    def part(self, n, piece, half, k):
        return (n, half, k, pl.ds(piece * self.rows, self.rows))

    def start(self, unit, n, piece, away):
        y, k, seq, half = self.place
        side = 1 - half if away else half
        cs = self.core_sems
        lane = 0 if away else 1
        self.first[unit, lane] = remote(
            self.partial.at[self.part(n, piece, side, 1 - k)],
            self.core_buf.at[unit, lane],
            cs.at[0, unit, lane],
            cs.at[1, unit, lane],
            device(y, 1 - k, seq, half),
        )

    def pass_on(self, unit, n, piece):
        y, k, seq, half = self.place
        self.first[unit, 0].wait_recv()
        away = self.partial[self.part(n, piece, 1 - half, k)].astype(F32) + self.core_buf[unit, 0].astype(F32)
        self.half_send[unit] = away.astype(BF)
        hs = self.half_sems
        self.second[unit] = remote(
            self.half_send.at[unit], self.half_buf.at[unit], hs.at[0, unit], hs.at[1, unit], device(y, k, seq, 1 - half)
        )

    def result(self, unit, n, piece):
        y, k, seq, half = self.place
        self.first[unit, 1].wait_recv()
        mine = self.partial[self.part(n, piece, half, k)].astype(F32) + self.core_buf[unit, 1].astype(F32)
        self.second[unit].wait_recv()
        return mine + self.half_buf[unit].astype(F32)

    def finish(self, unit):
        self.first[unit, 0].wait_send()
        self.first[unit, 1].wait_send()
        self.second[unit].wait_send()


class Return:
    def __init__(self, own_ref, landing, sems, place, feat):
        self.own, self.landing, self.sems, self.place, self.feat = own_ref, landing, sems, place, feat
        self.copies = []

    def start(self, unit, n, value):
        y, k, seq, half = self.place
        feat = self.feat
        self.own[unit] = value
        self.landing[y, n, k] = jnp.where(k == 0, value[:, :feat], value[:, feat : 2 * feat])
        for i, (dy, dk, ty, tk) in enumerate(rows_of(self.place)):
            self.copies.append(
                remote(
                    self.own.at[unit, :, lanes(tk * feat + 2 * dy * feat, feat)],
                    self.landing.at[y, n, k],
                    self.sems.at[0, unit, i],
                    self.sems.at[1, unit, i],
                    device(ty, tk, seq, half),
                )
            )

    def finish(self):
        for copy in self.copies:
            copy.wait()


class Freight:
    def __init__(self, full_ref, z_sems, y_sems, place, seqs):
        self.full, self.place, self.seqs = full_ref, place, seqs
        self.z_sems, self.y_sems = z_sems, y_sems
        self.wide = full_ref.shape[2] // 2
        self.z, self.y = {}, {}
        self.turn = seqs // 2

    def along(self, d):
        y, k, seq, half = self.place
        up = d <= self.turn
        source = d - 1 if up else (d + 1) % self.seqs
        if source:
            self.z[source].wait_recv()
        target = lax.rem(seq + (1 if up else self.seqs - 1), self.seqs)
        self.z[d] = remote(
            self.full.at[source, :, : self.wide],
            self.full.at[d, :, : self.wide],
            self.z_sems.at[0, d - 1],
            self.z_sems.at[1, d - 1],
            device(y, k, target, half),
        )

    def first(self):
        return [d for d in (1, self.seqs - 1) if d <= self.turn or d > self.turn][: min(2, self.seqs - 1)]

    def later(self):
        return list(range(2, self.turn + 1)) + list(range(self.seqs - 2, self.turn, -1))

    def last(self):
        return [d for d in range(1, self.seqs) if d == self.turn or d == self.turn + 1]

    def across(self, d):
        y, k, seq, half = self.place
        self.y[d] = remote(
            self.full.at[d, :, : self.wide],
            self.full.at[d, :, self.wide :],
            self.y_sems.at[0, d],
            self.y_sems.at[1, d],
            device(1 - y, k, seq, half),
        )

    def pass_along(self, cross):
        for d in self.later():
            self.along(d)
            if cross:
                self.across(d - 1 if d <= self.turn else d + 1)

    def arrive(self, cross):
        for d in self.last():
            self.z[d].wait_recv()
            if cross:
                self.across(d)

    def finish(self):
        for copy in self.z.values():
            copy.wait_send()
        for copy in self.y.values():
            copy.wait()


class Collect:
    def __init__(self, source, place, seqs, y_refs=None, z_refs=None):
        self.source, self.place, self.seqs = source, place, seqs
        self.y_refs, self.z_refs = y_refs, z_refs
        self.wide = source.shape[2] // 2 if y_refs else source.shape[2]
        self.turn = seqs // 2
        self.order = list(range(self.turn, seqs)) + list(range(self.turn - 1, -1, -1))
        self.y, self.z, self.core = {}, {}, None

    def across(self, d):
        y, k, seq, half = self.place
        buf, sems = self.y_refs
        self.y[d] = remote(
            self.source.at[d, :, self.wide :], buf.at[d], sems.at[0, d], sems.at[1, d], device(1 - y, k, seq, half)
        )

    def total(self, d):
        if not self.y_refs:
            return self.source[d].astype(F32)
        self.y[d].wait_recv()
        return self.source[d, :, : self.wide].astype(F32) + self.y_refs[0][d].astype(F32)

    def store(self, out):
        for d in self.order:
            out[d] = self.total(d).astype(BF)

    def along(self, d):
        y, k, seq, half = self.place
        out, z_send, z_buf, c_send, z_sems, c_sems = self.z_refs
        left = d <= self.turn
        before = d + 1 if left else d - 1
        value = self.total(d)
        if before in self.z and before not in (self.turn + 1 if left else self.turn,):
            self.z[before].wait_recv()
            value = value + z_buf[before - 1].astype(F32)
        z_send[d - 1] = value.astype(BF)
        target = lax.rem(seq + (self.seqs - 1 if left else 1), self.seqs)
        self.z[d] = remote(
            z_send.at[d - 1], z_buf.at[d - 1], z_sems.at[0, d - 1], z_sems.at[1, d - 1], device(y, k, target, half)
        )

    def close(self):
        y, k, seq, half = self.place
        out, z_send, z_buf, c_send, z_sems, c_sems = self.z_refs
        total = self.total(0)
        for d in sorted({1, self.seqs - 1}):
            self.z[d].wait_recv()
            total = total + z_buf[d - 1].astype(F32)
        low, high = total[:, : self.wide // 2], total[:, self.wide // 2 :]
        out[k] = jnp.where(k == 0, low, high)
        c_send[...] = jnp.where(k == 0, high, low)
        self.core = remote(c_send, out.at[k], c_sems.at[0], c_sems.at[1], device(y, 1 - k, seq, half))

    def finish(self):
        for copy in self.y.values():
            copy.wait_send()
        for copy in self.z.values():
            copy.wait_send()
        if self.core is not None:
            self.core.wait()


def freight_scratch(seqs):
    dma = pltpu.SemaphoreType.DMA
    return [dma((2, seqs - 1)), dma((2, seqs))]


def across_scratch(seqs, n, wide):
    return [pltpu.VMEM((seqs, n, wide), BF), pltpu.SemaphoreType.DMA((2, seqs))]


def along_scratch(seqs, n, wide):
    dma = pltpu.SemaphoreType.DMA
    return [
        pltpu.VMEM((seqs - 1, n, wide), BF),
        pltpu.VMEM((seqs - 1, n, wide), BF),
        pltpu.VMEM((n, wide // 2), F32),
        dma((2, seqs - 1)),
        dma((2,)),
    ]


def along_devices(place, seqs):
    y, k, seq, half = place
    return [device(y, k, lax.rem(seq + d, seqs), half) for d in sorted({1, seqs - 1})]


def shuffle(source, target, n, index, place, sends, receives, local_sems):
    y, k, seq, half = place
    feat = source.shape[-1]
    copies = [pltpu.make_async_copy(source.at[y, n, k], target.at[n, :, lanes(k * feat, feat)], local_sems.at[index])]
    copies[0].start()
    for i, (dy, dk, ty, tk) in enumerate(rows_of(place)):
        copies.append(
            remote(
                source.at[ty, n, tk],
                target.at[n, :, lanes(k * feat + 2 * dy * feat, feat)],
                sends.at[index, i],
                receives.at[index, i],
                device(ty, tk, seq, half),
            )
        )
    return copies


def normalize(residual):
    centered = residual - jnp.mean(residual, axis=-1, keepdims=True)
    inv_std = lax.rsqrt(jnp.mean(centered * centered, axis=-1, keepdims=True) + epsilon)
    return centered * inv_std, inv_std


def normalize_back(out_grad, normed, inv_std, gain):
    scaled = out_grad * gain
    first = jnp.mean(scaled, axis=-1, keepdims=True)
    second = jnp.mean(scaled * normed, axis=-1, keepdims=True)
    return inv_std * (scaled - first - normed * second)


def column_sum(value):
    return jnp.sum(value, axis=0, keepdims=True)


def start_all(reduce, units):
    for unit, n, p in units:
        reduce.start(unit, n, p, True)
    for unit, n, p in units:
        reduce.start(unit, n, p, False)


def bias_of(r, target, table):
    def one(h, carry):
        target[h] = masked_bias(r.off, (table, h), r.segq, r.segk)
        return carry

    lax.fori_loop(0, r.qkv.shape[0], one, 0)


def out_part(r):
    heads, width, depth = r.weight.shape
    return r.weight[:, 3 * width // 4 :].reshape(heads * (width // 4), depth)


def feed_forward(r):
    block = r.act.shape[0] // 4
    for b in range(4):
        here = slice(b * block, (b + 1) * block)
        pre = mm_nt(r.up[here], r.row[...])
        share = 0.5 + 0.5 * lax.erf(pre * (0.5**0.5))
        r.act[here] = (pre * share).astype(BF)
        r.slope[here] = share + pre * jnp.exp(-0.5 * pre * pre) * ((2.0 * math.pi) ** -0.5)


def attend_all(r):
    heads, hd = r.qkv.shape[0], r.qkv.shape[1] // 3
    bias_of(r, r.masked, 0)

    def one(h, carry):
        r.qkv[h] = mm_nt(r.weight[h, : 3 * hd], r.row[...]).astype(BF)
        query = scaled(r.qkv[h, :hd], hd**-0.5)
        keys, values = r.qkv[h, hd : 2 * hd].T, r.qkv[h, 2 * hd :]
        r.mix[h], r.lse[h] = head_forward(keys, values, query, r.masked[h])
        return carry

    lax.fori_loop(0, heads, one, 0)


def attend_all_back(r):
    heads, hd, length = r.qkv.shape[0], r.qkv.shape[1] // 3, r.qkv.shape[2]
    scale = hd**-0.5

    def one(h, carry):
        query, keys, values = (r.qkv[h, part * hd : (part + 1) * hd] for part in range(3))
        dlogits, dq, dk, dv = head_backward(
            keys.T, scaled(keys, scale), values.T, scaled(query, scale), r.dmix[h], r.lse[h], r.masked[h]
        )
        r.g_scr[...] = dlogits
        r.dqkv[h, :hd] = dq
        r.dqkv[h, hd : 2 * hd] = dk.astype(BF)
        r.dqkv[h, 2 * hd :] = dv.astype(BF)
        offset_sums(r.g_scr, r.doff, (), (h,), length)
        return carry

    lax.fori_loop(0, heads, one, 0)


def exchange_kernel(kind, attend, feed, count, pieces, seqs, rides, *refs):
    place = spot()
    y, k, seq, half = place
    refs = list(refs)
    take = lambda amount: [refs.pop(0) for _ in range(amount)]
    r = types.SimpleNamespace()
    r.resid, r.norm = take(2)
    if kind == BACKWARD:
        r.normed, r.inv = take(2)
    if attend:
        r.weight, r.row = take(2)
        if kind == FORWARD:
            r.off, r.segq, r.segk = take(3)
        else:
            r.qkv, r.masked, r.lse = r.row, *take(2)
    if feed:
        r.up, r.down, r.row = take(3)
        if kind == BACKWARD:
            r.act, r.slope, r.hidden = take(3)
    elif kind == BACKWARD:
        r.dkv, r.dquery, r.mix, r.weight, r.row, r.stream, r.grad_full = take(7)
    ride_in = take(len(rides))
    (r.full,) = take(1)
    if kind == FORWARD:
        r.out, r.normed, r.inv = take(3)
    else:
        r.grad, r.sums = take(2)
    if attend:
        if kind == FORWARD:
            r.qkv, r.mix, r.lse, r.masked, r.masked_next = take(5)
        else:
            r.dqkv, r.doff = take(2)
    if feed and kind == FORWARD:
        r.act, r.slope = take(2)
    elif feed:
        (r.g_up,) = take(1)
    if kind == BACKWARD:
        (r.summed,) = take(1)
    ride_out = take(len(rides))
    (partial,) = take(1)
    if kind == BACKWARD:
        (r.g,) = take(1)
        inner = Collect(r.g, place, seqs, y_refs=take(2))
        if feed:
            (r.dpre,) = take(1)
    if attend:
        if kind == BACKWARD:
            r.g_scr, r.dmix = take(2)
    core_buf, half_send, half_buf, rc, rh, gh, gc = take(7)
    rows = partial.shape[3] // pieces
    peers = [device(y, 1 - k, seq, half), device(y, k, seq, 1 - half)]
    peers.append(device(1 - y, k, seq, half))
    if {ALONG, THROUGH, SUM_ALONG} & set(rides):
        peers += along_devices(place, seqs)
    greet(peers)
    units = [(n * pieces + p, n, p) for n in range(count) for p in range(pieces)]
    reduce = Reduce(partial, core_buf, half_send, half_buf, rc, rh, place, rows)
    spread = Spread(r.full, gh, gc, place, rows)
    moves, sums_along = [], []
    for ride, source, target in zip(rides, ride_in, ride_out):
        if ride == SUM_ALONG:
            sums_along.append(Collect(source, place, seqs, z_refs=[target] + take(5)))
            for d in sums_along[-1].order[:2]:
                sums_along[-1].along(d)
        else:
            moves.append((ride, Freight(target, *take(2), place, seqs)))
            if ride == ACROSS:
                for d in range(seqs):
                    moves[-1][1].across(d)
            else:
                if ride == THROUGH:
                    moves[-1][1].across(0)
                for d in moves[-1][1].first():
                    moves[-1][1].along(d)
    own = partial.shape[3]
    if kind == FORWARD and attend:
        attend_all(r)
        weight = out_part(r)
        product = lambda start: project(r.mix, weight, start, own)
    elif kind == FORWARD:
        feed_forward(r)
        product = lambda start: mm_tn(r.act[:, start : start + own], r.down[...]).astype(BF)
    elif feed:
        block = r.g.shape[1]
        for d in range(seqs):
            here = slice(d * block, (d + 1) * block)
            r.dpre[here] = (mm_nt(r.down[here], r.row[...]) * r.slope[here]).astype(BF)
        product = lambda start: mm_tn(r.dpre[:, start : start + own], r.up[...]).astype(BF)
    else:
        span = r.dkv.shape[1]
        weight = r.weight[:, :span].reshape(seqs * span, -1)
        product = lambda start: project(r.dkv, weight, start, own)
    for a in range(2):
        for b in range(2):
            partial[0, a, b] = product((2 * a + b) * own)
    start_all(reduce, units)
    if kind == BACKWARD:
        r.sums[...] = jnp.zeros_like(r.sums)
        for d in inner.order:
            if feed:
                here = slice(d * block, (d + 1) * block)
                r.g[d] = mm(r.act[here], r.row[...]).astype(BF)
            else:
                width = r.dquery.shape[1]
                r.g[d, :span] = mm(r.dkv[d], r.row[...]).astype(BF)
                r.g[d, span : span + width] = mm(r.dquery[d], r.stream[...]).astype(BF)
                r.g[d, span + width :] = mm(r.mix[d], r.grad_full[...]).astype(BF)
            inner.across(d)
    gain, bias = r.norm[0:1], r.norm[1:2]
    for unit, n, p in units:
        reduce.pass_on(unit, n, p)
    for unit, n, p in units:
        here = pl.ds(p * rows, rows)
        branch = reduce.result(unit, n, p)
        if kind == FORWARD:
            normed, inv = normalize(r.resid[n, here].astype(F32) + branch)
            value = normed * gain + bias
            r.out[n, here] = value
            r.normed[n, here] = normed
            r.inv[n, here] = inv
        else:
            upstream = r.resid[n, here] + branch if feed else branch
            normed = r.normed[n, here]
            value = normalize_back(upstream, normed, r.inv[n, here], gain)
            r.grad[n, here] = value
        r.full[n, half, k, here] = value.astype(BF)
        spread.start(unit, n, p)
        if kind != FORWARD:
            r.sums[0:1] += column_sum(upstream * normed)
            r.sums[1:2] += column_sum(upstream)
    for collect in sums_along:
        for d in collect.order[2:-1]:
            collect.along(d)
    for ride, move in moves:
        if ride != ACROSS:
            move.pass_along(ride == THROUGH)
            move.arrive(ride == THROUGH)
    if attend and kind == FORWARD:
        bias_of(r, r.masked_next, 1)
    elif attend:
        for d in range(seqs):
            here = slice(d * block, (d + 1) * block)
            r.g_up[d] = mm(r.dpre[here], r.hidden[...]).astype(BF)
    for unit, n, p in units:
        spread.forward(unit, n, p)
    for collect in sums_along:
        collect.close()
    for unit, n, p in units:
        spread.finish(unit)
        reduce.finish(unit)
    if attend and kind == BACKWARD:
        weight = out_part(r)
        for a in range(2):
            for b in range(2):
                project_back(weight, r.full[0, a, b], r.dmix, (2 * a + b) * own)
        attend_all_back(r)
    for ride, move in moves:
        move.finish()
    if kind == BACKWARD:
        inner.store(r.summed)
        inner.finish()
    for collect in sums_along:
        collect.finish()


def exchange(kind, collective_id, seqs, resid, norm, normed=None, inv=None, rides=(), attend=(), feed=(), cross=()):
    count, own, depth = 1, resid.shape[1], norm.shape[1]
    if kind == BACKWARD:
        own = normed.shape[1]
    pieces = 2 if count == 1 else 1
    units, rows = count * pieces, own // pieces
    dma = pltpu.SemaphoreType.DMA
    shape = jax.ShapeDtypeStruct
    vmem = pl.BlockSpec(memory_space=pltpu.VMEM)
    anywhere = pl.BlockSpec(memory_space=pl.ANY)
    full = shape((count, 2, 2, own, depth), BF)
    grad, sums = shape((count, own, depth), F32), shape((8, depth), F32)
    scratch = []
    if kind == FORWARD:
        args = (resid, norm)
        outs = (full, grad, grad, shape((count, own, 1), F32))
    else:
        args = (resid, norm, normed, inv)
        outs = (full, grad, sums)
    args += tuple(attend) + tuple(feed) + tuple(cross)
    scratch.append(pltpu.VMEM((count, 2, 2, own, depth), BF))
    if kind == BACKWARD:
        n = feed[0].shape[0] // seqs if feed else cross[3].shape[1]
        scratch += [pltpu.VMEM((seqs, n, depth), BF)] + across_scratch(seqs, n, depth // 2)
        if feed:
            scratch.append(pltpu.VMEM(feed[3].shape, BF))
    if attend:
        heads, hd = attend[0].shape[0], attend[0].shape[1] // 4
        length = attend[1].shape[0] if kind == FORWARD else attend[1].shape[2]
        qkv = shape((heads, 3 * hd, length), BF)
        if kind == FORWARD:
            bias = shape((heads, length, length), F32)
            outs += (qkv, shape((heads, hd, length), BF), shape((heads, 1, length), F32), bias, bias)
        else:
            outs += (qkv, shape((heads, 1, 2 * length), F32))
            scratch += [pltpu.VMEM((length, length), F32), pltpu.VMEM((heads, hd, length), BF)]
    if feed and kind == FORWARD:
        inner = (feed[0].shape[0], feed[2].shape[0])
        outs += (shape(inner, BF), shape(inner, F32))
    elif feed:
        outs += (shape((seqs, n, depth), BF),)
    if kind == BACKWARD:
        outs += (shape((seqs, n, depth // 2), BF),)
    scratch += [
        pltpu.VMEM((units, 2, rows, depth), BF),
        pltpu.VMEM((units, rows, depth), BF),
        pltpu.VMEM((units, rows, depth), BF),
        dma((2, units, 2)),
        dma((2, units)),
        dma((2, units)),
        dma((2, units, 2)),
    ]
    in_specs, out_specs = [vmem] * len(args), [vmem] * len(outs)
    aliases = {}
    for ride, array in rides:
        if ride == SUM_ALONG:
            n, wide = array.shape[1], depth // 2
            scratch += along_scratch(seqs, n, wide)
            in_specs.append(vmem)
            out_specs.append(vmem)
            outs += (shape((2, n, wide // 2), F32),)
        else:
            scratch += freight_scratch(seqs)
            aliases[len(args)] = len(outs)
            in_specs.append(anywhere)
            out_specs.append(anywhere)
            outs += (shape(array.shape, array.dtype),)
        args += (array,)
    return pl.pallas_call(
        functools.partial(exchange_kernel, kind, bool(attend), bool(feed), count, pieces, seqs, tuple(ride for ride, _ in rides)),
        out_shape=outs,
        in_specs=in_specs,
        out_specs=tuple(out_specs),
        scratch_shapes=scratch,
        input_output_aliases=aliases,
        compiler_params=pltpu.CompilerParams(collective_id=collective_id, has_side_effects=True, vmem_limit_bytes=50 << 20),
        name="exchange_%d" % collective_id,
    )(*args)


def cross_kernel(count, query, kv, out_weight, masked, resid, norm, cot, mix, full, output, grad, sums, dquery, dkv, doff, partial, lse, keys, keys_scaled, values_t, queries, g_scr, dk_scr, dv_scr, dmix, own, landing, return_sems, cot_own, cot_send, cot_recv, cot_local, core_buf, half_send, half_buf, rc, rh, gh, gc):
    place = spot()
    y, k, seq, half = place
    heads, hd, length = query.shape[0], query.shape[1], kv.shape[2]
    depth, rows = partial.shape[4], partial.shape[3]
    scale = hd**-0.5
    greet(
        [device(y, 1 - k, seq, half), device(y, k, seq, 1 - half)]
        + [device(ty, tk, seq, half) for dy, dk, ty, tk in rows_of(place) if dy]
    )
    cots = [shuffle(cot, cot_own, n, n, place, cot_send, cot_recv, cot_local) for n in range(count)]
    reduce = Reduce(partial, core_buf, half_send, half_buf, rc, rh, place, rows)
    spread = Spread(full, gh, gc, place, rows)
    back = Return(own, landing, return_sems, place, depth // 4)
    sums[...] = jnp.zeros_like(sums)
    g_scr[...] = jnp.zeros_like(g_scr)
    dk_scr[...] = jnp.zeros_like(dk_scr)
    dv_scr[...] = jnp.zeros_like(dv_scr)

    def prepare(h, carry):
        keys[h] = kv[h, :hd].T
        keys_scaled[h] = scaled(kv[h, :hd], scale)
        values_t[h] = kv[h, hd:].T
        queries[h] = scaled(query[h], scale)
        return carry

    lax.fori_loop(0, heads, prepare, 0)

    def attend_heads(s, low, high):
        def one(h, carry):
            here = slice(s * length, (s + 1) * length)
            mix[h, :, here], lse[h, :, here] = head_forward(keys[h], kv[h, hd:], queries[h, :, here], masked[h])
            return carry

        lax.fori_loop(low, high, one, 0)

    def send_products(s):
        for a in range(2):
            for b in range(2):
                partial[s, a, b] = project(mix, out_weight[...], s * length + (2 * a + b) * rows, rows)
        reduce.start(s, s, 0, True)
        reduce.start(s, s, 0, False)

    def turn(s):
        normed, inv = normalize(resid[s].astype(F32) + reduce.result(s, s, 0))
        for copy in cots[s]:
            copy.wait()
        upstream = cot_own[s].astype(F32)
        value = normalize_back(upstream, normed, inv, norm[0:1])
        grad[s] = value
        full[s, half, k] = value.astype(BF)
        spread.start(s, s, 0)
        sums[0:1] += column_sum(upstream * normed)
        sums[1:2] += column_sum(upstream)
        back.start(s, s, (normed * norm[0:1] + norm[1:2]).astype(BF))

    def attend_back(s):
        for a in range(2):
            for b in range(2):
                project_back(out_weight[...], full[s, a, b], dmix, (2 * a + b) * rows)

        def one(h, carry):
            here = slice(s * length, (s + 1) * length)
            dlogits, dq, dk, dv = head_backward(
                keys[h], keys_scaled[h], values_t[h], queries[h, :, here], dmix[h], lse[h, :, here], masked[h]
            )
            g_scr[h] += dlogits
            dquery[h, :, here] = dq
            dk_scr[h] += dk
            dv_scr[h] += dv
            return carry

        lax.fori_loop(0, heads, one, 0)

    for s in range(count):
        attend_heads(s, 0, heads // 2)
        if s >= 1:
            reduce.pass_on(s - 1, s - 1, 0)
        if s >= 2:
            turn(s - 2)
        attend_heads(s, heads // 2, heads)
        send_products(s)
    reduce.pass_on(count - 1, count - 1, 0)
    for s in range(max(count - 2, 0), count):
        turn(s)
    for s in range(count):
        spread.forward(s, s, 0)
        spread.ready(s)
        attend_back(s)
    for h in range(heads):
        dkv[h, :hd] = dk_scr[h].astype(BF)
        dkv[h, hd:] = dv_scr[h].astype(BF)

    def offsets_of(h, carry):
        offset_sums(g_scr, doff, (h,), (h,), length)
        return carry

    lax.fori_loop(0, heads, offsets_of, 0)
    back.finish()
    output[...] = landing[...].astype(F32)
    for s in range(count):
        spread.sent(s)
        reduce.finish(s)


def cross_attention(collective_id, query, kv, out_weight, masked, resid, norm, cot):
    count, own, depth = resid.shape
    heads, hd, total = query.shape
    length = kv.shape[2]
    dma = pltpu.SemaphoreType.DMA
    shape = jax.ShapeDtypeStruct
    outs = (
        shape(query.shape, BF),
        shape((count, 2, 2, own, depth), BF),
        shape((2, count, 2, own, depth // 4), F32),
        shape((count, own, depth), F32),
        shape((8, depth), F32),
        shape(query.shape, BF),
        shape(kv.shape, BF),
        shape((heads, 1, 2 * length), F32),
    )
    whole = pl.BlockSpec(memory_space=pltpu.VMEM)
    specs = [whole] * 7
    vmem = pltpu.VMEM
    return pl.pallas_call(
        functools.partial(cross_kernel, count),
        out_shape=outs,
        in_specs=specs,
        out_specs=tuple(whole for _ in outs),
        scratch_shapes=[
            vmem((count, 2, 2, own, depth), BF),
            vmem((heads, 1, total), F32),
            vmem((heads, length, hd), BF),
            vmem((heads, hd, length), BF),
            vmem((heads, length, hd), BF),
            vmem(query.shape, BF),
            vmem((heads, length, length), F32),
            vmem((heads, hd, length), F32),
            vmem((heads, hd, length), F32),
            vmem((heads, hd, length), BF),
            vmem((count, own, depth), BF),
            vmem((2, count, 2, own, depth // 4), BF),
            dma((2, count, 3)),
            vmem((count, own, depth), BF),
            dma((count, 3)),
            dma((count, 3)),
            dma((count,)),
            vmem((count, 2, own, depth), BF),
            vmem((count, own, depth), BF),
            vmem((count, own, depth), BF),
            dma((2, count, 2)),
            dma((2, count)),
            dma((2, count)),
            dma((2, count, 2)),
        ],
        compiler_params=pltpu.CompilerParams(collective_id=collective_id, has_side_effects=True, vmem_limit_bytes=56 << 20),
        name="cross_attention",
    )(query, kv, out_weight, masked, resid, norm, cot)


def inputs_kernel(seqs, groups, tok_ref, str_ref, norm_ref, ids_ref, tab_ref, *refs):
    refs = list(refs)
    take = lambda amount: [refs.pop(0) for _ in range(amount)]
    packs = take(groups)
    x_own, x_full, y_own, y_full, norm_all, ids_all, tab_all = take(7)
    fulls = take(groups)
    in_send, in_recv, in_local, xh, xc, yh, yc, small_sems, tab_sems, small_self, pack_sems, pack_self = take(12)
    place = spot()
    y, k, seq, half = place
    feat = tok_ref.shape[-1]
    own = tok_ref.shape[-2]
    row_peers = rows_of(place)
    others = [device(y, k, lax.rem(seq + d, seqs), half) for d in range(1, seqs)]
    greet([device(ty, tk, seq, half) for dy, dk, ty, tk in row_peers] + [device(y, k, seq, 1 - half)] + others)
    count = str_ref.shape[1]
    x_copies = shuffle(tok_ref, x_own, 0, 0, place, in_send, in_recv, in_local)
    loads = []
    for g in range(groups):
        here = fulls[g].at[0, :, lanes(k * feat, feat)]
        copy = pltpu.make_async_copy(packs[g].at[k], here, pack_self.at[g])
        copy.start()
        loads.append(
            (
                copy,
                remote(packs[g].at[1 - k], here, pack_sems.at[0, g], pack_sems.at[1, g], device(y, 1 - k, seq, half)),
            )
        )
    small = []
    for j, (source, target) in enumerate(((norm_ref, norm_all), (ids_ref, ids_all))):
        slot = (lambda dy: (slice(None), lanes(k * feat + 2 * dy * feat, feat))) if j == 0 else (lambda dy: (2 * y + k,))
        copy = pltpu.make_async_copy(source, target.at[slot(0)], small_self.at[j])
        copy.start()
        small.append(copy)
        for i, (dy, dk, ty, tk) in enumerate(row_peers):
            small.append(
                remote(source, target.at[slot(dy)], small_sems.at[0, j, i], small_sems.at[1, j, i], device(ty, tk, seq, half))
            )
    copy = pltpu.make_async_copy(tab_ref, tab_all.at[0], small_self.at[2])
    copy.start()
    small.append(copy)
    for d in range(1, seqs):
        small.append(remote(tab_ref, tab_all.at[d], tab_sems.at[0, d - 1], tab_sems.at[1, d - 1], others[d - 1]))
    freights = [Freight(full, *take(2), place, seqs) for full in fulls]
    for copy in loads[0]:
        copy.wait()
    for d in freights[0].first():
        freights[0].along(d)
    freights[0].across(0)
    for copy in x_copies:
        copy.wait()
    x_full[0, half, k] = x_own[0]
    x_spread = Spread(x_full, xh, xc, place, own)
    x_spread.start(0, 0, 0)
    y_copies = [shuffle(str_ref, y_own, n, 1 + n, place, in_send, in_recv, in_local) for n in range(count)]
    y_spread = Spread(y_full, yh, yc, place, own)
    for g in range(1, groups):
        for copy in loads[g]:
            copy.wait()
    x_spread.forward(0, 0, 0)
    for n in range(count):
        for copy in y_copies[n]:
            copy.wait()
        y_full[n, half, k] = y_own[n]
        y_spread.start(n, n, 0)
    freights[0].pass_along(True)
    for d in freights[1].first():
        freights[1].along(d)
    freights[0].arrive(True)
    freights[1].across(0)
    for n in range(count):
        y_spread.forward(n, n, 0)
    for copy in small:
        copy.wait()
    freights[1].pass_along(True)
    for d in freights[2].first():
        freights[2].along(d)
    freights[1].arrive(True)
    freights[2].pass_along(False)
    freights[2].arrive(False)
    x_spread.finish(0)
    for n in range(count):
        y_spread.finish(n)
    for freight in freights:
        freight.finish()


def gather_inputs(seqs, tokens, streams, norm, ids, table, packs):
    count, own, feat = streams.shape[1], streams.shape[-2], streams.shape[-1]
    depth = 4 * feat
    dma = pltpu.SemaphoreType.DMA
    shape = jax.ShapeDtypeStruct
    vmem = pl.BlockSpec(memory_space=pltpu.VMEM)
    outs = (
        shape((1, own, depth), BF),
        shape((1, 2, 2, own, depth), BF),
        shape((count, own, depth), BF),
        shape((count, 2, 2, own, depth), BF),
        shape((norm.shape[0], depth), F32),
        shape((4,) + ids.shape, jnp.int32),
        shape((seqs,) + table.shape, F32),
    )
    specs = [vmem] * len(outs)
    for pack in packs:
        outs += (shape((seqs, pack.shape[1], depth), BF),)
        specs.append(pl.BlockSpec(memory_space=pl.ANY))
    moves = 1 + count
    scratch = [
        dma((moves, 3)),
        dma((moves, 3)),
        dma((moves,)),
        dma((2, 1)),
        dma((2, 1, 2)),
        dma((2, count)),
        dma((2, count, 2)),
        dma((2, 2, 3)),
        dma((2, seqs - 1)),
        dma((3,)),
        dma((2, len(packs))),
        dma((len(packs),)),
    ]
    for _ in packs:
        scratch += freight_scratch(seqs)
    return pl.pallas_call(
        functools.partial(inputs_kernel, seqs, len(packs)),
        out_shape=outs,
        in_specs=[vmem] * (5 + len(packs)),
        out_specs=tuple(specs),
        scratch_shapes=scratch,
        compiler_params=pltpu.CompilerParams(collective_id=0, has_side_effects=True, vmem_limit_bytes=50 << 20),
        name="gather_inputs",
    )(tokens, streams, norm, ids, table, *packs)


def outputs_kernel(seqs, count, dqkv, dquery, mix, first_weight, last_weight, x_full, d1_full, d1, d3, small, down, up, tok_out, str_out, small_out, down_out, up_out, first_out, part, first, core_buf, half_send, half_buf, own, land_x, land_y, rc, rh, rs, small_buf, ss, *refs):
    refs = list(refs)
    take = lambda amount: [refs.pop(0) for _ in range(amount)]
    place = spot()
    y, k, seq, half = place
    rows = part.shape[3]
    feat = part.shape[4] // 4
    bits = [1 << b for b in range((seqs - 1).bit_length())]
    flips = [device(y, k, seq + b - 2 * b * ((seq // b) % 2), half) for b in bits]
    others = [device(y, k, lax.rem(seq + d, seqs), half) for d in range(1, seqs)]
    partners = [device(y, 1 - k, seq, half), device(y, k, seq, 1 - half), device(1 - y, k, seq, half)]
    greet(partners + [device(1 - y, 1 - k, seq, half)] + others)
    partners += flips
    small_out[...] = small[...]

    def start_small(stage):
        return stage, remote(small_out, small_buf.at[stage], ss.at[0, stage], ss.at[1, stage], partners[stage])

    def end_small(started):
        stage, copy = started
        copy.wait()
        small_out[...] += small_buf[stage]

    heads, width = mix.shape[0], mix.shape[1]

    def products(unit):
        for a in range(2):
            for b in range(2):
                start = (2 * a + b) * rows
                if unit == 0:
                    weight = first_weight[:, : 3 * width].reshape(heads * 3 * width, -1)
                    part[unit, a, b] = project(dqkv, weight, start, rows)
                else:
                    weight = last_weight[:, 2 * width : 3 * width].reshape(heads * width, -1)
                    part[unit, a, b] = project(dquery, weight, 4 * (unit - 1) * rows + start, rows)
        reduce.start(unit, unit, 0, True)
        reduce.start(unit, unit, 0, False)

    reduce = Reduce(part, core_buf, half_send, half_buf, rc, rh, place, rows)
    units = range(count + 1)
    down = Collect(down, place, seqs, z_refs=[down_out] + take(5))
    up = Collect(up, place, seqs, y_refs=take(2), z_refs=[up_out] + take(5))
    first_ref = first
    first = Collect(first, place, seqs, y_refs=take(2), z_refs=[first_out] + take(5))
    started = start_small(2)
    for d in up.order:
        up.across(d)
    products(0)
    for d in first.order:
        first_ref[d, : 3 * width] = mm(dqkv[d], x_full[...]).astype(BF)
        first_ref[d, 3 * width :] = mm(mix[d], d1_full[...]).astype(BF)
        first.across(d)
    end_small(started)
    started = start_small(3)
    reduce.pass_on(0, 0, 0)
    products(1)
    for stage in range(4, len(partners)):
        end_small(started)
        started = start_small(stage)
    end_small(started)
    for d in down.order[:2]:
        down.along(d)
    started = start_small(0)
    for unit in units[2:]:
        products(unit)
    end_small(started)
    x_back = Return(own, land_x, rs, place, feat)
    y_back = Return(own, land_y, rs, place, feat)
    x_back.start(0, 0, (d1[0] + reduce.result(0, 0, 0)).astype(BF))
    started = start_small(1)
    for unit in units[1:]:
        reduce.pass_on(unit, unit, 0)
    end_small(started)
    for d in down.order[2:-1]:
        down.along(d)
    for d in up.order[:2]:
        up.along(d)
    for unit in units[1:]:
        y_back.start(unit, unit - 1, (d3[unit - 1] + reduce.result(unit, unit, 0)).astype(BF))
    down.close()
    for d in up.order[2:-1]:
        up.along(d)
    for d in first.order[:2]:
        first.along(d)
    up.close()
    for d in first.order[2:-1]:
        first.along(d)
    for unit in units:
        reduce.finish(unit)
    x_back.finish()
    tok_out[...] = land_x[:, 0].astype(F32)
    first.close()
    y_back.finish()
    str_out[...] = land_y[...].astype(F32)
    for collect in (down, up, first):
        collect.finish()


def scatter_outputs(seqs, collective_id, dqkv, dquery, mix, first_weight, last_weight, x_full, d1_full, d1, d3, small, down, up):
    count, own, depth = d3.shape
    feat, wide = depth // 4, depth // 2
    units = count + 1
    dma = pltpu.SemaphoreType.DMA
    shape = jax.ShapeDtypeStruct
    stages = 3 + (seqs - 1).bit_length()
    outs = (shape((2, 2, own, feat), F32), shape((2, count, 2, own, feat), F32), shape(small.shape, F32))
    outs += tuple(shape((2, group.shape[1], feat), F32) for group in (down, up, first_weight))
    scratch = [
        pltpu.VMEM((units, 2, 2, own, depth), BF),
        pltpu.VMEM(first_weight.shape, BF),
        pltpu.VMEM((units, 2, own, depth), BF),
        pltpu.VMEM((units, own, depth), BF),
        pltpu.VMEM((units, own, depth), BF),
        pltpu.VMEM((units, own, depth), BF),
        pltpu.VMEM((2, 1, 2, own, feat), BF),
        pltpu.VMEM((2, count, 2, own, feat), BF),
        dma((2, units, 2)),
        dma((2, units)),
        dma((2, units, 3)),
        pltpu.VMEM((stages,) + small.shape, F32),
        dma((2, stages)),
    ]
    scratch += along_scratch(seqs, down.shape[1], wide)
    for group in (up, first_weight):
        scratch += across_scratch(seqs, group.shape[1], wide) + along_scratch(seqs, group.shape[1], wide)
    return pl.pallas_call(
        functools.partial(outputs_kernel, seqs, count),
        out_shape=outs,
        in_specs=[pl.BlockSpec(memory_space=pltpu.VMEM)] * 12,
        out_specs=tuple(pl.BlockSpec(memory_space=pltpu.VMEM) for _ in outs),
        scratch_shapes=scratch,
        compiler_params=pltpu.CompilerParams(collective_id=collective_id, has_side_effects=True, vmem_limit_bytes=50 << 20),
        name="scatter_outputs",
    )(dqkv, dquery, mix, first_weight, last_weight, x_full, d1_full, d1, d3, small, down, up)


def pick(array, index, axis):
    return lax.dynamic_index_in_dim(array, index, axis, keepdims=False)


def dot_f32(spec, left, right):
    return jnp.einsum(spec, left, right, preferred_element_type=F32)


def on_device(
    rows,
    cols,
    tokens,
    streams,
    cotangent,
    block_ids,
    bucket_ids,
    w_qkv,
    enc_table,
    w_out,
    attention_norm_gain,
    attn_bias,
    w_up,
    w_down,
    ffn_gain,
    ffn_bias,
    w_query,
    w_keyval,
    cross_table,
    w_cross_out,
    cross_gain,
    cross_bias,
):
    seqs = cols // 2
    row, col = lax.axis_index(ROW), lax.axis_index(COL)
    y, k, seq, half = row // 2, row % 2, col // 2, col % 2
    low_y = y == 0
    stream_count = streams.shape[1]
    tok = tokens.shape[1]
    own = tok // 2
    feat = tokens.shape[2]
    length = block_ids.shape[2]
    head_dim = w_qkv.shape[2] // 2
    ff = w_up.shape[1] // 2
    table_heads, bucket_count = enc_table.shape

    def columns(weight, parts):
        return weight.reshape(feat, parts, 2, -1).transpose(2, 1, 3, 0).reshape(2, -1, feat)

    def columns_back(array, parts):
        return array.reshape(2, parts, -1, feat).transpose(3, 1, 0, 2).reshape(feat, parts, -1)

    halves = lambda weight: weight.reshape(2, -1, feat)
    hd3, hd2 = 3 * head_dim, 2 * head_dim
    packs = (
        jnp.concatenate([columns(w_qkv, 3), halves(w_out)], axis=1),
        columns(w_up, 1),
        halves(w_down),
        jnp.concatenate([columns(w_keyval, 2), columns(w_query, 1), halves(w_cross_out)], axis=1),
    )
    norm_params = jnp.stack([attention_norm_gain, attn_bias, ffn_gain, ffn_bias, cross_gain, cross_bias] + [cross_bias] * 2)
    table_pack = jnp.zeros((8, 128), F32).at[0].set(jnp.stack([enc_table, cross_table]).reshape(-1))
    micro_count = tokens.shape[0]
    x_own, x_full, y_own, y_full, norm_params, all_ids, all_tables, first, up, down, last = gather_inputs(
        seqs,
        tokens.reshape(micro_count, 1, 2, own, feat),
        streams.reshape(micro_count, stream_count, 2, own, feat),
        norm_params,
        block_ids.reshape(8, -1),
        table_pack,
        packs,
    )
    x_full, y_full = x_full.reshape(length, D), y_full.reshape(stream_count * length, D)
    segment = pick(pick(all_ids.reshape(rows, micro_count, length), seq, 0), y, 0)
    segq = segment[None]
    segk = segment[:, None]
    own_tables = pick(all_tables[:, 0].reshape(seqs, 2, table_heads, bucket_count), k, 2)
    slot_col = 2 * ((seq - jnp.arange(seqs)) % seqs) + half
    reversed_ids = jnp.concatenate([jnp.full((1,), -1, jnp.int32), bucket_ids[::-1]])
    onehot = bucket_onehot(reversed_ids, bucket_count)
    offsets = jnp.einsum("htb,bo->tho", own_tables, onehot, precision=highest)[:, :, None, :]


    hidden_full, hidden, normed1, inv1, qkv, mix, lse, enc_bias, cross_bias_full, down, last = exchange(
        FORWARD,
        1,
        seqs,
        x_own,
        norm_params[0:2],
        rides=((ACROSS, down), (ALONG, last)),
        attend=(first, x_full, offsets, segq, segk),
    )
    up, down = up.reshape(-1, D), down.reshape(-1, D)
    hidden_full = hidden_full.reshape(length, D)
    enc_full, _, normed2, inv2, act, slope, last = exchange(
        FORWARD,
        2,
        seqs,
        hidden,
        norm_params[2:4],
        rides=((ACROSS, last),),
        feed=(up, down, hidden_full),
    )
    m_kv, m_q, m_co = last[:, :hd2], last[:, hd2:hd3], last[:, hd3:].reshape(-1, D)
    enc_full = enc_full.reshape(length, D)
    kv = dot_f32("snr,tr->snt", m_kv, enc_full).astype(BF)
    query = dot_f32("snr,tr->snt", m_q, y_full).astype(BF)
    cmix, d3_full, output, d3, sums3, dquery, dkv, doff_cross = cross_attention(
        3,
        query,
        kv,
        m_co,
        cross_bias_full,
        y_own,
        norm_params[4:6],
        cotangent.reshape(micro_count, stream_count, 2, own, feat),
    )
    d3_full = d3_full.reshape(stream_count * length, D)

    d2_full, d2, sums2, g_last = exchange(
        BACKWARD,
        4,
        seqs,
        norm_params[2:4][None],
        norm_params[2:4],
        normed=normed2,
        inv=inv2,
        cross=(dkv, dquery, cmix, last, enc_full, y_full, d3_full),
    )
    d2_full = d2_full.reshape(length, D)
    d1_full, d1, sums1, dqkv, doff_enc, g_up, g_down, g_last = exchange(
        BACKWARD,
        5,
        seqs,
        d2,
        norm_params[0:2],
        normed=normed1,
        inv=inv1,
        rides=((SUM_ALONG, g_last),),
        attend=(first, qkv, enc_bias, lse),
        feed=(up, down, d2_full, act, slope, hidden_full),
    )
    d1_full = d1_full.reshape(length, D)

    norm_grads = jnp.concatenate([sums1[:2], sums2[:2], sums3[:2]])
    norm_grads = jnp.where(low_y, norm_grads, jnp.roll(norm_grads, D // 2, axis=1))
    table_grads = jnp.einsum(
        "tho,bo->thb", jnp.stack([doff_enc[:, 0], doff_cross[:, 0]]), onehot, precision=highest
    )
    heads = 2 * slot_col + k
    spread = (heads[:, None] == jnp.arange(table_heads * cols)[None, :]).astype(F32)
    table_grads = jnp.einsum("thb,hg->tgb", table_grads, spread, precision=highest)
    small = jnp.concatenate([norm_grads.reshape(-1, 128), table_grads.reshape(-1, 128)])
    grad_tokens, grad_streams, small, g_down, g_up, g_first = scatter_outputs(
        seqs, 6, dqkv, dquery, mix, first, last, x_full, d1_full, d1, d3, small, g_down, g_up
    )
    output, grad_streams = output.reshape(streams.shape), grad_streams.reshape(streams.shape)
    grad_tokens = grad_tokens.reshape(tokens.shape)
    count = norm_grads.size // 128
    norm_sums = lax.dynamic_slice_in_dim(small[:count].reshape(6, D), row * feat, feat, axis=1)
    table_sums = small[count:].reshape(2, table_heads * cols, bucket_count)
    table_sums = lax.dynamic_slice_in_dim(table_sums, col * table_heads, table_heads, axis=1)
    return (
        output,
        grad_tokens,
        grad_streams,
        columns_back(g_first[:, :hd3], 3),
        table_sums[0],
        g_first[:, hd3:].reshape(w_out.shape),
        norm_sums[0],
        norm_sums[1],
        columns_back(g_up, 1).reshape(w_up.shape),
        g_down.reshape(w_down.shape),
        norm_sums[2],
        norm_sums[3],
        columns_back(g_last[:, hd2:hd3], 1).reshape(w_query.shape),
        columns_back(g_last[:, :hd2], 2),
        table_sums[1],
        g_last[:, hd3:].reshape(w_cross_out.shape),
        norm_sums[4],
        norm_sums[5],
    )


def solution(mesh):
    whole_row, half_col = mesh.shape[ROW], mesh.shape[COL]
    wide, table, norm = P(ROW, None, COL), P(COL, None), P(ROW)
    up, down = P(ROW, COL), P(COL, ROW)
    weights = (wide, table, down, norm, norm, up, down, norm, norm, up, wide, table, down, norm, norm)

    def run(tokens, *rest):
        micro_count = tokens.shape[0]
        if whole_row == 4 and micro_count == 2 and half_col % 2 == 0:
            device_fn = functools.partial(on_device, whole_row, half_col)
        else:
            device_fn = on_device_general
        return jax.shard_map(
            device_fn,
            mesh=mesh,
            in_specs=(P(None, COL, ROW), P(None, None, COL, ROW), P(None, None, COL, ROW), P(None, ROW, None), P()) + weights,
            out_specs=(P(None, None, COL, ROW), P(None, COL, ROW), P(None, None, COL, ROW)) + weights,
            check_vma=False,
        )(tokens, *rest)

    return run
```

```python
import functools
import math
import types
import jax
import jax.numpy as jnp
from jax import lax
from jax.experimental import pallas as pl
from jax.experimental.pallas import tpu as pltpu
from jax.sharding import PartitionSpec as P

D = 1024
F32 = jnp.float32
BF = jnp.bfloat16
ROW, COL = "row", "col"


epsilon = 1e-05
neg_fill = -1e30
highest = lax.Precision.HIGHEST


def gather_cols(local_rows):
    return lax.all_gather(local_rows, COL, axis=1, tiled=True)


def gather_rows(local_rows):
    return lax.all_gather(local_rows, ROW, axis=1, tiled=True)


def product(matmul_operand, weight_matrix):
    return jnp.einsum(
        "ray,yw->raw", matmul_operand, weight_matrix, preferred_element_type=jnp.float32
    )


def rows_product(operand_full, matrix):
    return lax.psum_scatter(product(operand_full, matrix), ROW, scatter_dimension=1, tiled=True)


def cols_product(operand_full, matrix):
    return lax.psum_scatter(product(operand_full, matrix), COL, scatter_dimension=1, tiled=True)


def weight_grad(matmul_operand, upstream_gradient):
    return jnp.einsum(
        "bpt,bpr->tr", matmul_operand, upstream_gradient, preferred_element_type=jnp.float32
    )


def gelu_exact(argument):
    return jax.nn.gelu(argument, approximate=False)


def norm_forward(residual, gain_vec, bias_vec):
    local_sum = jnp.sum(residual, axis=-1)
    average = lax.psum(local_sum, ROW) / D
    centered = residual - average[..., None]
    spread = lax.psum(jnp.sum(centered * centered, axis=-1), ROW) / D
    inv_std = lax.rsqrt(spread + epsilon)
    normed = centered * inv_std[..., None]
    return (normed * gain_vec + bias_vec, normed, inv_std)


def norm_back(out_grad, normed, inv_std, gain_vec):
    scaled_grad = out_grad * gain_vec
    first_moment, second_moment = lax.psum(
        (jnp.sum(scaled_grad, axis=-1), jnp.sum(scaled_grad * normed, axis=-1)), ROW
    )
    resid_grad = inv_std[..., None] * (
        scaled_grad - first_moment[..., None] / D - normed * (second_moment[..., None] / D)
    )
    return (resid_grad, jnp.sum(out_grad * normed, axis=(0, 1)), jnp.sum(out_grad, axis=(0, 1)))


def bucket_onehot(bucket_ids, bucket_count):
    return (bucket_ids[None, :] == jnp.arange(bucket_count, dtype=jnp.int32)[:, None]).astype(
        jnp.float32
    )


def block_logits(query_blk, key_rows, offsets, segment, first_row):
    row_count = query_blk.shape[2]
    length = key_rows.shape[1]
    score_scale = query_blk.shape[-1] ** (-0.5)
    raw_scores = jnp.einsum(
        "snqhd,nkhd->snhqk", query_blk, key_rows, preferred_element_type=jnp.float32
    )
    places = jnp.arange(length, dtype=jnp.int32)
    query_pos = first_row + jnp.arange(row_count, dtype=jnp.int32)
    offset_index = places[None, :] - query_pos[:, None] + (length - 1)
    pos_bias = jnp.take(offsets, offset_index, axis=1)
    visible = segment[:, first_row : first_row + row_count, None] >= segment[:, None, :]
    return jnp.where(
        visible[None, :, None], raw_scores * score_scale + pos_bias[None, None], neg_fill
    )


def attend(queries, key_rows, value_rows, segment, offsets):
    score_logits = block_logits(queries, key_rows, offsets, segment, 0)
    row_max = jnp.max(score_logits, axis=-1, keepdims=True)
    log_total = row_max + jnp.log(jnp.sum(jnp.exp(score_logits - row_max), axis=-1, keepdims=True))
    weights = jnp.exp(score_logits - log_total).astype(jnp.bfloat16)
    mixed_parts = jnp.einsum(
        "snhqk,nkhd->snqhd", weights, value_rows, preferred_element_type=jnp.float32
    )
    lse_parts = log_total[..., 0]
    return (mixed_parts, lse_parts)


def diagonal_sums(summand):
    head_count, row_count, length = summand.shape
    flipped = summand[:, ::-1, :]
    padded = jnp.concatenate(
        [flipped, jnp.zeros((head_count, row_count, row_count), summand.dtype)], axis=2
    )
    flattened = padded.reshape(head_count, row_count * (length + row_count))[
        :, : row_count * (length + row_count - 1)
    ]
    return jnp.sum(flattened.reshape(head_count, row_count, length + row_count - 1), axis=1)


def attend_back(queries, key_rows, value_rows, segment, offsets, onehot, log_totals, mix_grad):
    length = key_rows.shape[1]
    block_rows = min(512, length)
    score_scale = queries.shape[-1] ** (-0.5)
    offset_grad = jnp.zeros(offsets.shape, jnp.float32)
    score_logits = block_logits(queries, key_rows, offsets, segment, 0)
    probability = jnp.exp(score_logits - log_totals[:, :, :, 0:block_rows, None])
    prob_grad = jnp.einsum(
        "snqhd,nkhd->snhqk", mix_grad, value_rows, preferred_element_type=jnp.float32
    )
    logit_grad = probability * (
        prob_grad - jnp.sum(probability * prob_grad, axis=-1, keepdims=True)
    )
    scaled = (logit_grad * score_scale).astype(jnp.bfloat16)
    query_parts = jnp.einsum(
        "snhqk,nkhd->snqhd", scaled, key_rows, preferred_element_type=jnp.float32
    )
    key_grad = jnp.einsum("snhqk,snqhd->nkhd", scaled, queries, preferred_element_type=jnp.float32)
    value_grad = jnp.einsum(
        "snhqk,snqhd->nkhd",
        probability.astype(jnp.bfloat16),
        mix_grad,
        preferred_element_type=jnp.float32,
    )
    low_end = length - block_rows
    offset_grad = offset_grad.at[:, low_end : low_end + length + block_rows - 1].add(
        diagonal_sums(jnp.sum(logit_grad, axis=(0, 1)))
    )
    table_grad = jnp.dot(offset_grad, onehot.T, precision=highest)
    return (query_parts, key_grad, value_grad, table_grad)


def on_device_general(
    tokens,
    streams,
    cotangent,
    block_ids,
    bucket_ids,
    w_qkv,
    enc_table,
    w_out,
    attention_norm_gain,
    attn_bias,
    w_up,
    w_down,
    ffn_gain,
    ffn_bias,
    w_query,
    w_keyval,
    cross_table,
    w_cross_out,
    cross_gain,
    cross_bias,
):
    micro_count = tokens.shape[0]
    stream_count = streams.shape[1]
    seq_rows = block_ids.shape[1]
    length = block_ids.shape[2]
    head_count = enc_table.shape[0]
    bucket_count = enc_table.shape[1]
    row_width = w_qkv.shape[0]
    col_width = w_qkv.shape[2]
    head_dim = col_width // head_count
    row_tokens = seq_rows * length
    qkv_matrix = w_qkv.reshape(row_width, 3 * col_width)
    keyval_matrix = w_keyval.reshape(row_width, 2 * col_width)
    onehot = bucket_onehot(bucket_ids, bucket_count)
    enc_offsets = jnp.dot(enc_table, onehot, precision=highest)
    cross_offsets = jnp.dot(cross_table, onehot, precision=highest)
    qkv_acc = jnp.zeros((row_width, 3 * col_width), jnp.float32)
    out_acc = jnp.zeros(w_out.shape, jnp.float32)
    up_acc = jnp.zeros(w_up.shape, jnp.float32)
    down_acc = jnp.zeros(w_down.shape, jnp.float32)
    query_acc = jnp.zeros(w_query.shape, jnp.float32)
    keyval_acc = jnp.zeros((row_width, 2 * col_width), jnp.float32)
    cross_out_acc = jnp.zeros(w_cross_out.shape, jnp.float32)
    enc_table_acc = jnp.zeros(enc_table.shape, jnp.float32)
    cross_table_acc = jnp.zeros(cross_table.shape, jnp.float32)
    norm_accs = [jnp.zeros((row_width,), jnp.float32) for place_holder in range(6)]
    outputs = []
    token_grads = []
    stream_grads = []
    for micro in range(micro_count):
        segment = block_ids[micro]
        x_in = tokens[micro][None]
        y_in = streams[micro]
        x_full = gather_cols(x_in)
        qkv = (
            rows_product(x_full, qkv_matrix)
            .astype(jnp.bfloat16)
            .reshape(seq_rows, length, 3, head_count, head_dim)
        )
        enc_query = qkv[:, :, 0][None]
        enc_key = qkv[:, :, 1]
        encoder_value_rows = qkv[:, :, 2]
        enc_mixed, enc_lse = attend(enc_query, enc_key, encoder_value_rows, segment, enc_offsets)
        enc_mix = enc_mixed.reshape(1, row_tokens, col_width).astype(jnp.bfloat16)
        mix_full = gather_rows(enc_mix)
        attn_branch = cols_product(mix_full, w_out)
        hidden, normed_one, inv_one = norm_forward(
            x_in.astype(jnp.float32) + attn_branch, attention_norm_gain, attn_bias
        )
        hidden_low = hidden.astype(jnp.bfloat16)
        hidden_full = gather_cols(hidden_low)
        pre_act = rows_product(hidden_full, w_up)
        act_value, gelu_pull = jax.vjp(gelu_exact, pre_act)
        act_low = act_value.astype(jnp.bfloat16)
        act_full = gather_rows(act_low)
        ffn_branch = cols_product(act_full, w_down)
        encoded, normed_two, inv_two = norm_forward(hidden + ffn_branch, ffn_gain, ffn_bias)
        encoded_low = encoded.astype(jnp.bfloat16)
        enc_full = gather_cols(encoded_low)
        keyval = (
            rows_product(enc_full, keyval_matrix)
            .astype(jnp.bfloat16)
            .reshape(seq_rows, length, 2, head_count, head_dim)
        )
        cross_key = keyval[:, :, 0]
        cross_value = keyval[:, :, 1]
        stream_full = gather_cols(y_in)
        cross_query = (
            rows_product(stream_full, w_query)
            .astype(jnp.bfloat16)
            .reshape(stream_count, seq_rows, length, head_count, head_dim)
        )
        cross_mixed, cross_lse = attend(cross_query, cross_key, cross_value, segment, cross_offsets)
        cross_mix = cross_mixed.reshape(stream_count, row_tokens, col_width).astype(jnp.bfloat16)
        cross_full = gather_rows(cross_mix)
        cross_branch = cols_product(cross_full, w_cross_out)
        result, normed_three, inv_three = norm_forward(
            y_in.astype(jnp.float32) + cross_branch, cross_gain, cross_bias
        )
        outputs.append(result)
        grad_three, gain_part, bias_part = norm_back(
            cotangent[micro].astype(jnp.float32), normed_three, inv_three, cross_gain
        )
        norm_accs[4] = norm_accs[4] + gain_part
        norm_accs[5] = norm_accs[5] + bias_part
        branch_full = gather_cols(grad_three.astype(jnp.bfloat16))
        cross_out_acc = cross_out_acc + weight_grad(cross_full, branch_full)
        cross_mix_grad = (
            rows_product(branch_full, w_cross_out.T)
            .astype(jnp.bfloat16)
            .reshape(stream_count, seq_rows, length, head_count, head_dim)
        )
        query_grad, key_grad, value_grad, table_grad = attend_back(
            cross_query,
            cross_key,
            cross_value,
            segment,
            cross_offsets,
            onehot,
            cross_lse,
            cross_mix_grad,
        )
        cross_table_acc = cross_table_acc + table_grad
        query_low = query_grad.reshape(stream_count, row_tokens, col_width).astype(jnp.bfloat16)
        keyval_low = (
            jnp.stack(
                [
                    key_grad.reshape(row_tokens, col_width),
                    value_grad.reshape(row_tokens, col_width),
                ],
                axis=1,
            )
            .reshape(1, row_tokens, 2 * col_width)
            .astype(jnp.bfloat16)
        )
        query_full = gather_rows(query_low)
        query_acc = query_acc + weight_grad(stream_full, query_full)
        stream_grads.append(grad_three + cols_product(query_full, w_query.T))
        keyval_full = gather_rows(keyval_low)
        keyval_acc = keyval_acc + weight_grad(enc_full, keyval_full)
        encoded_grad = cols_product(keyval_full, keyval_matrix.T)
        grad_two, gain_part, bias_part = norm_back(encoded_grad, normed_two, inv_two, ffn_gain)
        norm_accs[2] = norm_accs[2] + gain_part
        norm_accs[3] = norm_accs[3] + bias_part
        feedforward_full_output = gather_cols(grad_two.astype(jnp.bfloat16))
        down_acc = down_acc + weight_grad(act_full, feedforward_full_output)
        act_grad = rows_product(feedforward_full_output, w_down.T)
        pre_low = gelu_pull(act_grad)[0].astype(jnp.bfloat16)
        pre_full = gather_rows(pre_low)
        up_acc = up_acc + weight_grad(hidden_full, pre_full)
        hidden_grad = grad_two + cols_product(pre_full, w_up.T)
        grad_one, gain_part, bias_part = norm_back(
            hidden_grad, normed_one, inv_one, attention_norm_gain
        )
        norm_accs[0] = norm_accs[0] + gain_part
        norm_accs[1] = norm_accs[1] + bias_part
        attn_full = gather_cols(grad_one.astype(jnp.bfloat16))
        out_acc = out_acc + weight_grad(mix_full, attn_full)
        enc_mix_grad = (
            rows_product(attn_full, w_out.T)
            .astype(jnp.bfloat16)
            .reshape(1, seq_rows, length, head_count, head_dim)
        )
        enc_qgrad, enc_kgrad, enc_vgrad, table_grad = attend_back(
            enc_query,
            enc_key,
            encoder_value_rows,
            segment,
            enc_offsets,
            onehot,
            enc_lse,
            enc_mix_grad,
        )
        enc_table_acc = enc_table_acc + table_grad
        qkv_low = (
            jnp.stack(
                [
                    enc_qgrad.reshape(row_tokens, col_width),
                    enc_kgrad.reshape(row_tokens, col_width),
                    enc_vgrad.reshape(row_tokens, col_width),
                ],
                axis=1,
            )
            .reshape(1, row_tokens, 3 * col_width)
            .astype(jnp.bfloat16)
        )
        qkv_full = gather_rows(qkv_low)
        qkv_acc = qkv_acc + weight_grad(x_full, qkv_full)
        token_grads.append((grad_one + cols_product(qkv_full, qkv_matrix.T))[0])
    norm_stack = jnp.stack(norm_accs)
    table_stack = jnp.stack([enc_table_acc, cross_table_acc])
    norm_sums = lax.psum(norm_stack, COL)
    table_sums = lax.psum(table_stack, ROW)
    return (
        jnp.stack(outputs),
        jnp.stack(token_grads),
        jnp.stack(stream_grads),
        qkv_acc.reshape(row_width, 3, col_width),
        table_sums[0],
        out_acc,
        norm_sums[0],
        norm_sums[1],
        up_acc,
        down_acc,
        norm_sums[2],
        norm_sums[3],
        query_acc,
        keyval_acc.reshape(row_width, 2, col_width),
        table_sums[1],
        cross_out_acc,
        norm_sums[4],
        norm_sums[5],
    )


def mm(a,b):
    return jnp.dot(a,b,preferred_element_type=F32)
def mm_nt(a,b):
    return lax.dot_general(a,b,(((1,),(1,)),((),())),preferred_element_type=F32)

def mm_tn(a, b):
    return lax.dot_general(a, b, (((0,), (0,)), ((), ())), preferred_element_type=F32)


def masked_bias(off_ref, index, segq, segk):
    length = segk.shape[0]
    row = jnp.broadcast_to(off_ref[index], (length, 2 * length))
    rolled = pltpu.roll(row, 0, 1, stride=1, stride_axis=0)
    return jnp.where(segk[...] <= segq[...], rolled[:, length:], neg_fill)


def head_forward(keys, values, query, bias):
    logits = mm(keys, query) + bias
    top = jnp.max(logits, axis=0, keepdims=True)
    weight = jnp.exp(logits - top)
    total = jnp.sum(weight, axis=0, keepdims=True)
    return (mm(values, weight.astype(BF)) * (1.0 / total)).astype(BF), top + jnp.log(total)


def head_backward(keys, keys_t, values_t, query, grad, lse, bias):
    prob = jnp.exp(mm(keys, query) + (bias - lse))
    dprob = mm(values_t, grad)
    dlogits = prob * (dprob - jnp.sum(prob * dprob, axis=0, keepdims=True))
    low = dlogits.astype(BF)
    return dlogits, mm(keys_t, low).astype(BF), mm_nt(query, low), mm_nt(grad, prob.astype(BF))


def project(mix_ref, weight, start, rows):
    heads, hd = mix_ref.shape[0], mix_ref.shape[1]
    mixed = mix_ref[:, :, start : start + rows].reshape(heads * hd, rows)
    return mm_tn(mixed, weight).astype(BF)


def project_back(weight, rows_value, dmix_ref, start):
    heads, hd = dmix_ref.shape[0], dmix_ref.shape[1]
    rows = rows_value.shape[0]
    dmix_ref[:, :, start : start + rows] = mm_nt(weight, rows_value).astype(BF).reshape(heads, hd, rows)


def scaled(value, scale):
    return (value.astype(F32) * scale).astype(BF)


def offset_sums(g_ref, doff_ref, g_index, out_index, length):
    sub = lax.broadcasted_iota(jnp.int32, (8, 2 * length), 0)
    acc = jnp.zeros((8, 2 * length), F32)
    for i in range(length // 8):
        piece = g_ref[g_index + (pl.ds(8 * i, 8),)]
        padded = jnp.concatenate([jnp.zeros((8, length), F32), piece], axis=1)
        acc = acc + (pltpu.roll(padded, 2 * length - 8 * i, 1) if i else padded)
    for b in (1, 2, 4):
        acc = jnp.where((sub // b) % 2 == 1, pltpu.roll(acc, 2 * length - b, 1), acc)
    doff_ref[out_index] = jnp.sum(acc, axis=0, keepdims=True)


MESH = pl.DeviceIdType.MESH
FORWARD, BACKWARD = range(2)
ACROSS, THROUGH, ALONG, SUM_ALONG = range(4)


def spot():
    row, col = lax.axis_index(ROW), lax.axis_index(COL)
    return row // 2, row % 2, col // 2, col % 2


def device(y, k, seq, half):
    return (2 * y + k, 2 * seq + half)


def greet(devices):
    barrier = pltpu.get_barrier_semaphore()
    for target in devices:
        pl.semaphore_signal(barrier, inc=1, device_id=target, device_id_type=MESH)
    pl.semaphore_wait(barrier, len(devices))


def remote(source, target, send_sem, recv_sem, device_id):
    copy = pltpu.make_async_remote_copy(
        src_ref=source, dst_ref=target, send_sem=send_sem, recv_sem=recv_sem, device_id=device_id, device_id_type=MESH
    )
    copy.start()
    return copy


def lanes(start, size):
    return pl.ds(pl.multiple_of(start, size), size)


def rows_of(place):
    y, k, seq, half = place
    return [(dy, dk, (1 - y if dy else y), (1 - k if dk else k)) for dy, dk in ((0, 1), (1, 0), (1, 1))]


class Spread:
    def __init__(self, full_ref, half_sems, core_sems, place, rows):
        self.full, self.place, self.rows = full_ref, place, rows
        self.half_sems, self.core_sems = half_sems, core_sems
        self.first, self.second = {}, {}

    def block(self, n, piece, half, k):
        return self.full.at[n, half, k, pl.ds(piece * self.rows, self.rows)]

    def start(self, unit, n, piece):
        y, k, seq, half = self.place
        mine = self.block(n, piece, half, k)
        hs, cs = self.half_sems, self.core_sems
        self.first[unit] = (
            remote(mine, mine, hs.at[0, unit], hs.at[1, unit], device(y, k, seq, 1 - half)),
            remote(mine, mine, cs.at[0, unit, 0], cs.at[1, unit, 0], device(y, 1 - k, seq, half)),
        )

    def forward(self, unit, n, piece):
        y, k, seq, half = self.place
        self.first[unit][0].wait_recv()
        theirs = self.block(n, piece, 1 - half, k)
        cs = self.core_sems
        self.second[unit] = remote(theirs, theirs, cs.at[0, unit, 1], cs.at[1, unit, 1], device(y, 1 - k, seq, half))

    def ready(self, unit):
        self.first[unit][1].wait_recv()
        self.second[unit].wait_recv()

    def sent(self, unit):
        for copy in self.first[unit] + (self.second[unit],):
            copy.wait_send()

    def finish(self, unit):
        self.ready(unit)
        self.sent(unit)


class Reduce:
    def __init__(self, partial_ref, core_buf, half_send, half_buf, core_sems, half_sems, place, rows):
        self.partial, self.core_buf, self.half_send, self.half_buf = partial_ref, core_buf, half_send, half_buf
        self.core_sems, self.half_sems, self.place, self.rows = core_sems, half_sems, place, rows
        self.first, self.second = {}, {}

    def part(self, n, piece, half, k):
        return (n, half, k, pl.ds(piece * self.rows, self.rows))

    def start(self, unit, n, piece, away):
        y, k, seq, half = self.place
        side = 1 - half if away else half
        cs = self.core_sems
        lane = 0 if away else 1
        self.first[unit, lane] = remote(
            self.partial.at[self.part(n, piece, side, 1 - k)],
            self.core_buf.at[unit, lane],
            cs.at[0, unit, lane],
            cs.at[1, unit, lane],
            device(y, 1 - k, seq, half),
        )

    def pass_on(self, unit, n, piece):
        y, k, seq, half = self.place
        self.first[unit, 0].wait_recv()
        away = self.partial[self.part(n, piece, 1 - half, k)].astype(F32) + self.core_buf[unit, 0].astype(F32)
        self.half_send[unit] = away.astype(BF)
        hs = self.half_sems
        self.second[unit] = remote(
            self.half_send.at[unit], self.half_buf.at[unit], hs.at[0, unit], hs.at[1, unit], device(y, k, seq, 1 - half)
        )

    def result(self, unit, n, piece):
        y, k, seq, half = self.place
        self.first[unit, 1].wait_recv()
        mine = self.partial[self.part(n, piece, half, k)].astype(F32) + self.core_buf[unit, 1].astype(F32)
        self.second[unit].wait_recv()
        return mine + self.half_buf[unit].astype(F32)

    def finish(self, unit):
        self.first[unit, 0].wait_send()
        self.first[unit, 1].wait_send()
        self.second[unit].wait_send()


class Return:
    def __init__(self, own_ref, landing, sems, place, feat):
        self.own, self.landing, self.sems, self.place, self.feat = own_ref, landing, sems, place, feat
        self.copies = []

    def start(self, unit, n, value):
        y, k, seq, half = self.place
        feat = self.feat
        self.own[unit] = value
        self.landing[y, n, k] = jnp.where(k == 0, value[:, :feat], value[:, feat : 2 * feat])
        for i, (dy, dk, ty, tk) in enumerate(rows_of(self.place)):
            self.copies.append(
                remote(
                    self.own.at[unit, :, lanes(tk * feat + 2 * dy * feat, feat)],
                    self.landing.at[y, n, k],
                    self.sems.at[0, unit, i],
                    self.sems.at[1, unit, i],
                    device(ty, tk, seq, half),
                )
            )

    def finish(self):
        for copy in self.copies:
            copy.wait()


class Freight:
    def __init__(self, full_ref, z_sems, y_sems, place, seqs):
        self.full, self.place, self.seqs = full_ref, place, seqs
        self.z_sems, self.y_sems = z_sems, y_sems
        self.wide = full_ref.shape[2] // 2
        self.z, self.y = {}, {}
        self.turn = seqs // 2

    def along(self, d):
        y, k, seq, half = self.place
        up = d <= self.turn
        source = d - 1 if up else (d + 1) % self.seqs
        if source:
            self.z[source].wait_recv()
        target = lax.rem(seq + (1 if up else self.seqs - 1), self.seqs)
        self.z[d] = remote(
            self.full.at[source, :, : self.wide],
            self.full.at[d, :, : self.wide],
            self.z_sems.at[0, d - 1],
            self.z_sems.at[1, d - 1],
            device(y, k, target, half),
        )

    def first(self):
        return [d for d in (1, self.seqs - 1) if d <= self.turn or d > self.turn][: min(2, self.seqs - 1)]

    def later(self):
        return list(range(2, self.turn + 1)) + list(range(self.seqs - 2, self.turn, -1))

    def last(self):
        return [d for d in range(self.seqs - 1, 0, -1) if d == self.turn or d == self.turn + 1]

    def across(self, d):
        y, k, seq, half = self.place
        self.y[d] = remote(
            self.full.at[d, :, : self.wide],
            self.full.at[d, :, self.wide :],
            self.y_sems.at[0, d],
            self.y_sems.at[1, d],
            device(1 - y, k, seq, half),
        )

    def pass_along(self, cross):
        for d in self.later():
            self.along(d)
            if cross:
                self.across(d - 1 if d <= self.turn else d + 1)

    def arrive(self, cross):
        for d in self.last():
            self.z[d].wait_recv()
            if cross:
                self.across(d)

    def finish(self):
        for copy in self.z.values():
            copy.wait_send()
        for copy in self.y.values():
            copy.wait()


class Collect:
    def __init__(self, source, place, seqs, y_refs=None, z_refs=None):
        self.source, self.place, self.seqs = source, place, seqs
        self.y_refs, self.z_refs = y_refs, z_refs
        self.wide = source.shape[2] // 2 if y_refs else source.shape[2]
        self.turn = seqs // 2
        self.order = list(range(self.turn, seqs)) + list(range(self.turn - 1, -1, -1))
        self.y, self.z, self.core = {}, {}, None

    def across(self, d):
        y, k, seq, half = self.place
        buf, sems = self.y_refs
        self.y[d] = remote(
            self.source.at[d, :, self.wide :], buf.at[d], sems.at[0, d], sems.at[1, d], device(1 - y, k, seq, half)
        )

    def total(self, d):
        if not self.y_refs:
            return self.source[d].astype(F32)
        self.y[d].wait_recv()
        return self.source[d, :, : self.wide].astype(F32) + self.y_refs[0][d].astype(F32)

    def store(self, out):
        for d in self.order:
            out[d] = self.total(d).astype(BF)

    def along(self, d):
        y, k, seq, half = self.place
        out, z_send, z_buf, c_send, z_sems, c_sems = self.z_refs
        left = d <= self.turn
        before = d + 1 if left else d - 1
        value = self.total(d)
        if before in self.z and before not in (self.turn + 1 if left else self.turn,):
            self.z[before].wait_recv()
            value = value + z_buf[before - 1].astype(F32)
        z_send[d - 1] = value.astype(BF)
        target = lax.rem(seq + (self.seqs - 1 if left else 1), self.seqs)
        self.z[d] = remote(
            z_send.at[d - 1], z_buf.at[d - 1], z_sems.at[0, d - 1], z_sems.at[1, d - 1], device(y, k, target, half)
        )

    def close(self):
        y, k, seq, half = self.place
        out, z_send, z_buf, c_send, z_sems, c_sems = self.z_refs
        total = self.total(0)
        for d in sorted({1, self.seqs - 1}):
            self.z[d].wait_recv()
            total = total + z_buf[d - 1].astype(F32)
        low, high = total[:, : self.wide // 2], total[:, self.wide // 2 :]
        out[k] = jnp.where(k == 0, low, high)
        c_send[...] = jnp.where(k == 0, high, low)
        self.core = remote(c_send, out.at[k], c_sems.at[0], c_sems.at[1], device(y, 1 - k, seq, half))

    def finish(self):
        for copy in self.y.values():
            copy.wait_send()
        for copy in self.z.values():
            copy.wait_send()
        if self.core is not None:
            self.core.wait()


def freight_scratch(seqs):
    dma = pltpu.SemaphoreType.DMA
    return [dma((2, seqs - 1)), dma((2, seqs))]


def across_scratch(seqs, n, wide):
    return [pltpu.VMEM((seqs, n, wide), BF), pltpu.SemaphoreType.DMA((2, seqs))]


def along_scratch(seqs, n, wide):
    dma = pltpu.SemaphoreType.DMA
    return [
        pltpu.VMEM((seqs - 1, n, wide), BF),
        pltpu.VMEM((seqs - 1, n, wide), BF),
        pltpu.VMEM((n, wide // 2), F32),
        dma((2, seqs - 1)),
        dma((2,)),
    ]


def along_devices(place, seqs):
    y, k, seq, half = place
    return [device(y, k, lax.rem(seq + d, seqs), half) for d in sorted({1, seqs - 1})]


def shuffle(source, target, n, index, place, sends, receives, local_sems):
    y, k, seq, half = place
    feat = source.shape[-1]
    copies = [pltpu.make_async_copy(source.at[y, n, k], target.at[n, :, lanes(k * feat, feat)], local_sems.at[index])]
    copies[0].start()
    for i, (dy, dk, ty, tk) in enumerate(rows_of(place)):
        copies.append(
            remote(
                source.at[ty, n, tk],
                target.at[n, :, lanes(k * feat + 2 * dy * feat, feat)],
                sends.at[index, i],
                receives.at[index, i],
                device(ty, tk, seq, half),
            )
        )
    return copies


def normalize(residual):
    centered = residual - jnp.mean(residual, axis=-1, keepdims=True)
    inv_std = lax.rsqrt(jnp.mean(centered * centered, axis=-1, keepdims=True) + epsilon)
    return centered * inv_std, inv_std


def normalize_back(out_grad, normed, inv_std, gain):
    scaled = out_grad * gain
    first = jnp.mean(scaled, axis=-1, keepdims=True)
    second = jnp.mean(scaled * normed, axis=-1, keepdims=True)
    return inv_std * (scaled - first - normed * second)


def column_sum(value):
    return jnp.sum(value, axis=0, keepdims=True)


def start_all(reduce, units):
    for unit, n, p in units:
        reduce.start(unit, n, p, True)
    for unit, n, p in units:
        reduce.start(unit, n, p, False)


def bias_of(r, target, table):
    def one(h, carry):
        target[h] = masked_bias(r.off, (table, h), r.segq, r.segk)
        return carry

    lax.fori_loop(0, r.qkv.shape[0], one, 0)


def out_part(r):
    heads, width, depth = r.weight.shape
    return r.weight[:, 3 * width // 4 :].reshape(heads * (width // 4), depth)


def feed_forward(r):
    block = r.act.shape[0] // 4
    for b in range(4):
        here = slice(b * block, (b + 1) * block)
        pre = mm_nt(r.up[here], r.row[...])
        share = 0.5 + 0.5 * lax.erf(pre * (0.5**0.5))
        r.act[here] = (pre * share).astype(BF)
        r.slope[here] = share + pre * jnp.exp(-0.5 * pre * pre) * ((2.0 * math.pi) ** -0.5)


def attend_all(r):
    heads, hd = r.qkv.shape[0], r.qkv.shape[1] // 3
    bias_of(r, r.masked, 0)
    r.bias_out[0].start()
    weight, row = r.weight.ready(), r.row.ready()

    def one(h, carry):
        r.qkv[h] = mm_nt(weight[h, : 3 * hd], row[...]).astype(BF)
        query = scaled(r.qkv[h, :hd], hd**-0.5)
        keys, values = r.qkv[h, hd : 2 * hd].T, r.qkv[h, 2 * hd :]
        r.mix[h], r.lse[h] = head_forward(keys, values, query, r.masked[h])
        return carry

    lax.fori_loop(0, heads, one, 0)


def cross_slot(r, d):
    span, width = r.dkv.shape[1], r.dquery.shape[1]
    r.g[d, :span] = mm(r.dkv[d], r.row[...]).astype(BF)
    r.g[d, span : span + width] = mm(r.dquery[d], r.stream[...]).astype(BF)
    r.g[d, span + width :] = mm(r.mix[d], r.grad_full[...]).astype(BF)


def attend_all_back(r):
    heads, hd, length = r.qkv.shape[0], r.qkv.shape[1] // 3, r.qkv.shape[2]
    scale = hd**-0.5
    qkv, masked = r.qkv.ready(), r.masked.ready()

    def one(h, carry):
        query, keys, values = (qkv[h, part * hd : (part + 1) * hd] for part in range(3))
        dlogits, dq, dk, dv = head_backward(
            keys.T, scaled(keys, scale), values.T, scaled(query, scale), r.dmix[h], r.lse[h], masked[h]
        )
        r.g_scr[...] = dlogits
        r.dqkv[h, :hd] = dq
        r.dqkv[h, hd : 2 * hd] = dk.astype(BF)
        r.dqkv[h, 2 * hd :] = dv.astype(BF)
        offset_sums(r.g_scr, r.doff, (), (h,), length)
        return carry

    lax.fori_loop(0, heads, one, 0)


def exchange_kernel(kind, attend, feed, extra_count, far, count, pieces, seqs, rides, *refs):
    place = spot()
    y, k, seq, half = place
    refs = list(refs)
    take = lambda amount: [refs.pop(0) for _ in range(amount)]
    r = types.SimpleNamespace()
    r.resid, r.norm = take(2)
    if kind == BACKWARD:
        r.normed, r.inv = take(2)
    extras = take(extra_count)
    ride_in = take(len(rides))
    (r.full,) = take(1)
    if kind == FORWARD:
        r.out, r.normed, r.inv = take(3)
    else:
        r.grad, r.sums = take(2)
    if attend:
        if kind == FORWARD:
            r.qkv, r.mix, r.lse, r.masked, r.masked_next = take(5)
        else:
            r.dqkv, r.doff = take(2)
    if feed and kind == FORWARD:
        r.act, r.slope = take(2)
    elif feed:
        (r.g_up,) = take(1)
    if kind == BACKWARD:
        (r.summed,) = take(1)
    ride_out = take(len(rides))
    if far:
        near, (sems,) = take(len(far)), take(1)
        for i, index in enumerate(far):
            extras[index] = Lazy(extras[index], near[i], sems.at[i])
    if kind == BACKWARD and attend:
        r.up, r.down, r.row, r.act, r.slope, r.hidden, r.weight, r.qkv, r.masked, r.lse = extras
    elif kind == BACKWARD:
        r.dkv, r.dquery, r.weight, r.mix, r.row, r.stream, r.grad_full = extras
    elif attend:
        r.weight, r.row, r.off, r.segq, r.segk = extras
        biases = [(r.masked, 0), (r.masked_next, 1)]
        r.masked, r.masked_next, bias_sems = take(3)
        r.bias_out = [
            pltpu.make_async_copy(source, target, bias_sems.at[i])
            for i, (source, (target, _)) in enumerate(zip((r.masked, r.masked_next), biases))
        ]
    else:
        r.up, r.down, r.row = extras
    (partial,) = take(1)
    if kind == BACKWARD:
        (r.g,) = take(1)
        inner = Collect(r.g, place, seqs, y_refs=take(2))
        if feed:
            (r.dpre,) = take(1)
    if attend:
        if kind == BACKWARD:
            r.g_scr, r.dmix = take(2)
    core_buf, half_send, half_buf, rc, rh, gh, gc = take(7)
    rows = partial.shape[3] // pieces
    peers = [device(y, 1 - k, seq, half), device(y, k, seq, 1 - half)]
    peers.append(device(1 - y, k, seq, half))
    if {ALONG, THROUGH, SUM_ALONG} & set(rides):
        peers += along_devices(place, seqs)
    greet(peers)
    units = [(n * pieces + p, n, p) for n in range(count) for p in range(pieces)]
    reduce = Reduce(partial, core_buf, half_send, half_buf, rc, rh, place, rows)
    spread = Spread(r.full, gh, gc, place, rows)
    moves, sums_along = [], []
    for ride, source, target in zip(rides, ride_in, ride_out):
        if ride == SUM_ALONG:
            sums_along.append(Collect(source, place, seqs, z_refs=[target] + take(5)))
            for d in sums_along[-1].order[:2]:
                sums_along[-1].along(d)
        else:
            moves.append((ride, Freight(target, *take(2), place, seqs)))
            if ride == ACROSS:
                for d in range(seqs):
                    moves[-1][1].across(d)
            else:
                if ride == THROUGH:
                    moves[-1][1].across(0)
                for d in moves[-1][1].first():
                    moves[-1][1].along(d)
    own = partial.shape[3]
    if kind == FORWARD and attend:
        attend_all(r)
        weight = out_part(r)
        product = lambda start: project(r.mix, weight, start, own)
    elif kind == FORWARD:
        feed_forward(r)
        product = lambda start: mm_tn(r.act[:, start : start + own], r.down[...]).astype(BF)
    elif feed:
        block = r.g.shape[1]
        for d in range(seqs):
            here = slice(d * block, (d + 1) * block)
            r.dpre[here] = (mm_nt(r.down[here], r.row[...]) * r.slope[here]).astype(BF)
        product = lambda start: mm_tn(r.dpre[:, start : start + own], r.up[...]).astype(BF)
    else:
        span = r.dkv.shape[1]
        weight = r.weight[:, :span].reshape(seqs * span, -1)
        product = lambda start: project(r.dkv, weight, start, own)
    if kind == BACKWARD and not feed:
        grad_slot = lambda d: cross_slot(r, d)
        grad_slot(inner.order[0])
        inner.across(inner.order[0])
    for a in range(2):
        for b in range(2):
            partial[0, a, b] = product((2 * a + b) * own)
    start_all(reduce, units)
    if kind == BACKWARD:
        r.sums[...] = jnp.zeros_like(r.sums)
        for d in inner.order[0 if feed else 1 :]:
            if feed:
                here = slice(d * block, (d + 1) * block)
                r.g[d] = mm(r.act[here], r.row[...]).astype(BF)
            else:
                grad_slot(d)
            inner.across(d)
    gain, bias = r.norm[0:1], r.norm[1:2]
    for unit, n, p in units:
        reduce.pass_on(unit, n, p)
    for unit, n, p in units:
        here = pl.ds(p * rows, rows)
        branch = reduce.result(unit, n, p)
        if kind == FORWARD:
            normed, inv = normalize(r.resid[n, here].astype(F32) + branch)
            value = normed * gain + bias
            r.out[n, here] = value
            r.normed[n, here] = normed
            r.inv[n, here] = inv
        else:
            upstream = r.resid[n, here] + branch if feed else branch
            normed = r.normed[n, here]
            value = normalize_back(upstream, normed, r.inv[n, here], gain)
            r.grad[n, here] = value
        r.full[n, half, k, here] = value.astype(BF)
        spread.start(unit, n, p)
        if kind != FORWARD:
            r.sums[0:1] += column_sum(upstream * normed)
            r.sums[1:2] += column_sum(upstream)
    for collect in sums_along:
        for d in collect.order[2:-1]:
            collect.along(d)
    for ride, move in moves:
        if ride != ACROSS:
            move.pass_along(ride == THROUGH)
            move.arrive(ride == THROUGH)
    if attend and kind == FORWARD:
        bias_of(r, r.masked_next, 1)
        r.bias_out[1].start()
    elif attend:
        for d in range(seqs):
            here = slice(d * block, (d + 1) * block)
            r.g_up[d] = mm(r.dpre[here], r.hidden[...]).astype(BF)
    for unit, n, p in units:
        spread.forward(unit, n, p)
    for collect in sums_along:
        collect.close()
    for unit, n, p in units:
        spread.finish(unit)
        reduce.finish(unit)
    if attend and kind == BACKWARD:
        weight = out_part(r)
        for a in range(2):
            for b in range(2):
                project_back(weight, r.full[0, a, b], r.dmix, (2 * a + b) * own)
        attend_all_back(r)
    if attend and kind == FORWARD:
        for copy in r.bias_out:
            copy.wait()
    for ride, move in moves:
        move.finish()
    if kind == BACKWARD:
        inner.store(r.summed)
        inner.finish()
    for collect in sums_along:
        collect.finish()


def exchange(kind, collective_id, seqs, resid, norm, normed=None, inv=None, rides=(), attend=(), feed=(), cross=()):
    count, own, depth = 1, resid.shape[1], norm.shape[1]
    if kind == BACKWARD:
        own = normed.shape[1]
    pieces = 2 if count == 1 else 1
    units, rows = count * pieces, own // pieces
    dma = pltpu.SemaphoreType.DMA
    shape = jax.ShapeDtypeStruct
    vmem = pl.BlockSpec(memory_space=pltpu.VMEM)
    anywhere = pl.BlockSpec(memory_space=pl.ANY)
    full = shape((count, 2, 2, own, depth), BF)
    grad, sums = shape((count, own, depth), F32), shape((8, depth), F32)
    scratch = []
    if kind == FORWARD:
        args = (resid, norm)
        outs = (full, grad, grad, shape((count, own, 1), F32))
    else:
        args = (resid, norm, normed, inv)
        outs = (full, grad, sums)
    extras = tuple(feed) + tuple(attend) + tuple(cross)
    far = tuple(i for i, array in enumerate(extras) if array.size >= 1 << 17)
    base = len(args)
    args += extras
    scratch += [pltpu.VMEM(extras[i].shape, extras[i].dtype) for i in far] + [dma((len(far),))]
    if attend and kind == FORWARD:
        bias = (attend[0].shape[0],) + (attend[1].shape[0],) * 2
        scratch += [pltpu.VMEM(bias, F32), pltpu.VMEM(bias, F32), dma((2,))]
    scratch.append(pltpu.VMEM((count, 2, 2, own, depth), BF))
    if kind == BACKWARD:
        n = feed[0].shape[0] // seqs if feed else cross[2].shape[1]
        scratch += [pltpu.VMEM((seqs, n, depth), BF)] + across_scratch(seqs, n, depth // 2)
        if feed:
            scratch.append(pltpu.VMEM(feed[3].shape, BF))
    if attend:
        heads, hd = attend[0].shape[0], attend[0].shape[1] // 4
        length = attend[1].shape[0] if kind == FORWARD else attend[1].shape[2]
        qkv = shape((heads, 3 * hd, length), BF)
        if kind == FORWARD:
            bias = shape((heads, length, length), F32)
            outs += (qkv, shape((heads, hd, length), BF), shape((heads, 1, length), F32), bias, bias)
        else:
            outs += (qkv, shape((heads, 1, 2 * length), F32))
            scratch += [pltpu.VMEM((length, length), F32), pltpu.VMEM((heads, hd, length), BF)]
    if feed and kind == FORWARD:
        inner = (feed[0].shape[0], feed[2].shape[0])
        outs += (shape(inner, BF), shape(inner, F32))
    elif feed:
        outs += (shape((seqs, n, depth), BF),)
    if kind == BACKWARD:
        outs += (shape((seqs, n, depth // 2), BF),)
    scratch += [
        pltpu.VMEM((units, 2, rows, depth), BF),
        pltpu.VMEM((units, rows, depth), BF),
        pltpu.VMEM((units, rows, depth), BF),
        dma((2, units, 2)),
        dma((2, units)),
        dma((2, units)),
        dma((2, units, 2)),
    ]
    in_specs, out_specs = [vmem] * len(args), [vmem] * len(outs)
    for i in far:
        in_specs[base + i] = anywhere
    if attend and kind == FORWARD:
        out_specs[-2:] = [anywhere] * 2
    aliases = {}
    for ride, array in rides:
        if ride == SUM_ALONG:
            n, wide = array.shape[1], depth // 2
            scratch += along_scratch(seqs, n, wide)
            in_specs.append(vmem)
            out_specs.append(vmem)
            outs += (shape((2, n, wide // 2), F32),)
        else:
            scratch += freight_scratch(seqs)
            aliases[len(args)] = len(outs)
            in_specs.append(anywhere)
            out_specs.append(anywhere)
            outs += (shape(array.shape, array.dtype),)
        args += (array,)
    return pl.pallas_call(
        functools.partial(exchange_kernel, kind, bool(attend), bool(feed), len(extras), far, count, pieces, seqs, tuple(ride for ride, _ in rides)),
        out_shape=outs,
        in_specs=in_specs,
        out_specs=tuple(out_specs),
        scratch_shapes=scratch,
        input_output_aliases=aliases,
        compiler_params=pltpu.CompilerParams(collective_id=collective_id, has_side_effects=True, vmem_limit_bytes=60 << 20),
        name="exchange_%d" % collective_id,
    )(*args)


def cross_kernel(count, query, kv, out_weight, bias, resid, norm, cot, mix, full, output, grad, sums, dquery, dkv, doff, partial, lse, keys, keys_scaled, values_t, queries, masked, bias_sem, g_scr, dk_scr, dv_scr, dmix, own, landing, return_sems, cot_own, cot_send, cot_recv, cot_local, core_buf, half_send, half_buf, rc, rh, gh, gc):
    place = spot()
    y, k, seq, half = place
    heads, hd, length = query.shape[0], query.shape[1], kv.shape[2]
    depth, rows = partial.shape[4], partial.shape[3]
    scale = hd**-0.5
    bias_copy = pltpu.make_async_copy(bias, masked, bias_sem)
    bias_copy.start()
    greet(
        [device(y, 1 - k, seq, half), device(y, k, seq, 1 - half)]
        + [device(ty, tk, seq, half) for dy, dk, ty, tk in rows_of(place) if dy]
    )
    cots = [shuffle(cot, cot_own, n, n, place, cot_send, cot_recv, cot_local) for n in range(count)]
    reduce = Reduce(partial, core_buf, half_send, half_buf, rc, rh, place, rows)
    spread = Spread(full, gh, gc, place, rows)
    back = Return(own, landing, return_sems, place, depth // 4)
    sums[...] = jnp.zeros_like(sums)
    g_scr[...] = jnp.zeros_like(g_scr)
    dk_scr[...] = jnp.zeros_like(dk_scr)
    dv_scr[...] = jnp.zeros_like(dv_scr)

    def prepare(h, carry):
        keys[h] = kv[h, :hd].T
        keys_scaled[h] = scaled(kv[h, :hd], scale)
        values_t[h] = kv[h, hd:].T
        queries[h] = scaled(query[h], scale)
        return carry

    lax.fori_loop(0, heads, prepare, 0)
    bias_copy.wait()

    def attend_heads(s, low, high):
        def one(h, carry):
            here = slice(s * length, (s + 1) * length)
            mix[h, :, here], lse[h, :, here] = head_forward(keys[h], kv[h, hd:], queries[h, :, here], masked[h])
            return carry

        lax.fori_loop(low, high, one, 0)

    def send_products(s):
        for a in range(2):
            for b in range(2):
                partial[s, a, b] = project(mix, out_weight[...], s * length + (2 * a + b) * rows, rows)
        reduce.start(s, s, 0, True)
        reduce.start(s, s, 0, False)

    def turn(s):
        normed, inv = normalize(resid[s].astype(F32) + reduce.result(s, s, 0))
        for copy in cots[s]:
            copy.wait()
        upstream = cot_own[s].astype(F32)
        value = normalize_back(upstream, normed, inv, norm[0:1])
        grad[s] = value
        full[s, half, k] = value.astype(BF)
        spread.start(s, s, 0)
        sums[0:1] += column_sum(upstream * normed)
        sums[1:2] += column_sum(upstream)
        back.start(s, s, (normed * norm[0:1] + norm[1:2]).astype(BF))

    def attend_back(s):
        for a in range(2):
            for b in range(2):
                project_back(out_weight[...], full[s, a, b], dmix, (2 * a + b) * rows)

        def one(h, carry):
            here = slice(s * length, (s + 1) * length)
            dlogits, dq, dk, dv = head_backward(
                keys[h], keys_scaled[h], values_t[h], queries[h, :, here], dmix[h], lse[h, :, here], masked[h]
            )
            g_scr[h] += dlogits
            dquery[h, :, here] = dq
            dk_scr[h] += dk
            dv_scr[h] += dv
            return carry

        lax.fori_loop(0, heads, one, 0)

    for s in range(count):
        attend_heads(s, 0, heads // 2)
        if s >= 1:
            reduce.pass_on(s - 1, s - 1, 0)
        if s >= 2:
            turn(s - 2)
        attend_heads(s, heads // 2, heads)
        send_products(s)
    reduce.pass_on(count - 1, count - 1, 0)
    for s in range(max(count - 2, 0), count):
        turn(s)
    for s in range(count):
        spread.forward(s, s, 0)
        spread.ready(s)
        attend_back(s)
    for h in range(heads):
        dkv[h, :hd] = dk_scr[h].astype(BF)
        dkv[h, hd:] = dv_scr[h].astype(BF)

    def offsets_of(h, carry):
        offset_sums(g_scr, doff, (h,), (h,), length)
        return carry

    lax.fori_loop(0, heads, offsets_of, 0)
    back.finish()
    output[...] = landing[...].astype(F32)
    for s in range(count):
        spread.sent(s)
        reduce.finish(s)


def cross_attention(collective_id, query, kv, out_weight, masked, resid, norm, cot):
    count, own, depth = resid.shape
    heads, hd, total = query.shape
    length = kv.shape[2]
    dma = pltpu.SemaphoreType.DMA
    shape = jax.ShapeDtypeStruct
    outs = (
        shape(query.shape, BF),
        shape((count, 2, 2, own, depth), BF),
        shape((2, count, 2, own, depth // 4), F32),
        shape((count, own, depth), F32),
        shape((8, depth), F32),
        shape(query.shape, BF),
        shape(kv.shape, BF),
        shape((heads, 1, 2 * length), F32),
    )
    whole = pl.BlockSpec(memory_space=pltpu.VMEM)
    anywhere = pl.BlockSpec(memory_space=pl.ANY)
    specs = [whole] * 3 + [anywhere] + [whole] * 2 + [anywhere]
    vmem = pltpu.VMEM
    return pl.pallas_call(
        functools.partial(cross_kernel, count),
        out_shape=outs,
        in_specs=specs,
        out_specs=tuple(whole for _ in outs),
        scratch_shapes=[
            vmem((count, 2, 2, own, depth), BF),
            vmem((heads, 1, total), F32),
            vmem((heads, length, hd), BF),
            vmem((heads, hd, length), BF),
            vmem((heads, length, hd), BF),
            vmem(query.shape, BF),
            vmem(masked.shape, F32),
            pltpu.SemaphoreType.DMA,
            vmem((heads, length, length), F32),
            vmem((heads, hd, length), F32),
            vmem((heads, hd, length), F32),
            vmem((heads, hd, length), BF),
            vmem((count, own, depth), BF),
            vmem((2, count, 2, own, depth // 4), BF),
            dma((2, count, 3)),
            vmem((count, own, depth), BF),
            dma((count, 3)),
            dma((count, 3)),
            dma((count,)),
            vmem((count, 2, own, depth), BF),
            vmem((count, own, depth), BF),
            vmem((count, own, depth), BF),
            dma((2, count, 2)),
            dma((2, count)),
            dma((2, count)),
            dma((2, count, 2)),
        ],
        compiler_params=pltpu.CompilerParams(collective_id=collective_id, has_side_effects=True, vmem_limit_bytes=60 << 20),
        name="cross_attention",
    )(query, kv, out_weight, masked, resid, norm, cot)


class Lazy:
    def __init__(self, source, target, sem):
        self.copy, self.ref, self.shape = pltpu.make_async_copy(source, target, sem), target, target.shape
        self.copy.start()

    def ready(self):
        if self.copy is not None:
            self.copy.wait()
            self.copy = None
        return self.ref

    def __getitem__(self, index):
        return self.ready()[index]

    @property
    def at(self):
        return self.ready().at


def fetch(far, near, sems):
    copies = [pltpu.make_async_copy(source, target, sems.at[i]) for i, (source, target) in enumerate(zip(far, near))]
    for copy in copies:
        copy.start()
    return copies


def inputs_kernel(seqs, tok_ref, str_ref, norm_ref, ids_ref, tab_ref, *refs):
    refs = list(refs)
    take = lambda amount: [refs.pop(0) for _ in range(amount)]
    groups = 4
    far = take(7)
    x_own, x_full, y_own, y_full, norm_all, ids_all, tab_all = take(7)
    fulls = take(groups)
    in_send, in_recv, in_local, xh, xc, yh, yc, small_sems, tab_sems, small_self, pack_sems, pack_self = take(12)
    pack_first, pack_up, pack_last = take(3)
    w_qkv, w_out, w_up, w_kv, w_query, w_co = near = take(6)
    (fetch_sems,) = take(1)
    w_down = far.pop(3)
    fetched = fetch(far, near, fetch_sems)
    packs = [pack_first, pack_up, w_down, pack_last]
    place = spot()
    y, k, seq, half = place
    feat = tok_ref.shape[-1]
    own = tok_ref.shape[-2]
    row_peers = rows_of(place)
    others = [device(y, k, lax.rem(seq + d, seqs), half) for d in range(1, seqs)]
    greet([device(ty, tk, seq, half) for dy, dk, ty, tk in row_peers] + [device(y, k, seq, 1 - half)] + others)
    count = str_ref.shape[1]
    x_copies = shuffle(tok_ref, x_own, 0, 0, place, in_send, in_recv, in_local)
    hd = w_out.shape[0] // 2

    def columns_in(pack, start, matrix):
        rows = matrix.T
        half_rows = rows.shape[0] // 2
        for core in range(2):
            pack[core, start : start + half_rows] = rows[core * half_rows : (core + 1) * half_rows]

    def rows_in(pack, start, matrix):
        half_rows = matrix.shape[0] // 2
        for core in range(2):
            pack[core, start : start + half_rows] = matrix[core * half_rows : (core + 1) * half_rows]

    def load(g):
        here = fulls[g].at[0, :, lanes(k * feat, feat)]
        copy = pltpu.make_async_copy(packs[g].at[k], here, pack_self.at[g])
        copy.start()
        return (
            copy,
            remote(packs[g].at[1 - k], here, pack_sems.at[0, g], pack_sems.at[1, g], device(y, 1 - k, seq, half)),
        )

    for copy in fetched[:2]:
        copy.wait()
    for part in range(3):
        columns_in(pack_first, part * hd, w_qkv[part])
    rows_in(pack_first, 3 * hd, w_out)
    loads = [load(0)]
    small = []
    for j, (source, target) in enumerate(((norm_ref, norm_all), (ids_ref, ids_all))):
        slot = (lambda dy: (slice(None), lanes(k * feat + 2 * dy * feat, feat))) if j == 0 else (lambda dy: (2 * y + k,))
        copy = pltpu.make_async_copy(source, target.at[slot(0)], small_self.at[j])
        copy.start()
        small.append(copy)
        for i, (dy, dk, ty, tk) in enumerate(row_peers):
            small.append(
                remote(source, target.at[slot(dy)], small_sems.at[0, j, i], small_sems.at[1, j, i], device(ty, tk, seq, half))
            )
    copy = pltpu.make_async_copy(tab_ref, tab_all.at[0], small_self.at[2])
    copy.start()
    small.append(copy)
    for d in range(1, seqs):
        small.append(remote(tab_ref, tab_all.at[d], tab_sems.at[0, d - 1], tab_sems.at[1, d - 1], others[d - 1]))
    freights = [Freight(full, *take(2), place, seqs) for full in fulls]
    for copy in loads[0]:
        copy.wait()
    for d in freights[0].first():
        freights[0].along(d)
    freights[0].across(0)
    fetched[2].wait()
    columns_in(pack_up, 0, w_up[...])
    loads.append(load(1))
    for copy in x_copies:
        copy.wait()
    x_full[0, half, k] = x_own[0]
    x_spread = Spread(x_full, xh, xc, place, own)
    x_spread.start(0, 0, 0)
    y_copies = [shuffle(str_ref, y_own, n, 1 + n, place, in_send, in_recv, in_local) for n in range(count)]
    y_spread = Spread(y_full, yh, yc, place, own)
    freights[0].pass_along(True)
    for copy in loads[1]:
        copy.wait()
    for d in freights[1].first():
        freights[1].along(d)
    loads.append(load(2))
    for copy in fetched[3:]:
        copy.wait()
    for part in range(2):
        columns_in(pack_last, part * hd, w_kv[part])
    columns_in(pack_last, 2 * hd, w_query[...])
    rows_in(pack_last, 3 * hd, w_co)
    loads.append(load(3))
    x_spread.forward(0, 0, 0)
    freights[0].arrive(True)
    freights[1].across(0)
    for n in range(count):
        for copy in y_copies[n]:
            copy.wait()
        y_full[n, half, k] = y_own[n]
        y_spread.start(n, n, 0)
    freights[1].pass_along(True)
    for g in range(2, groups):
        for copy in loads[g]:
            copy.wait()
    for d in freights[2].first():
        freights[2].along(d)
    freights[1].arrive(True)
    freights[2].pass_along(False)
    for n in range(count):
        y_spread.forward(n, n, 0)
    for copy in small:
        copy.wait()
    freights[2].arrive(False)
    x_spread.finish(0)
    for n in range(count):
        y_spread.finish(n)
    for freight in freights:
        freight.finish()


def gather_inputs(seqs, tokens, streams, norm, ids, table, *weights):
    count, own, feat = streams.shape[1], streams.shape[-2], streams.shape[-1]
    depth = 4 * feat
    dma = pltpu.SemaphoreType.DMA
    shape = jax.ShapeDtypeStruct
    vmem = pl.BlockSpec(memory_space=pltpu.VMEM)
    outs = (
        shape((1, own, depth), BF),
        shape((1, 2, 2, own, depth), BF),
        shape((count, own, depth), BF),
        shape((count, 2, 2, own, depth), BF),
        shape((norm.shape[0], depth), F32),
        shape((4,) + ids.shape, jnp.int32),
        shape((seqs,) + table.shape, F32),
    )
    specs = [vmem] * len(outs)
    hd, ff = weights[1].shape[0] // 2, weights[2].shape[1] // 2
    for n in (4 * hd, ff, ff, 4 * hd):
        outs += (shape((seqs, n, depth), BF),)
        specs.append(pl.BlockSpec(memory_space=pl.ANY))
    moves = 1 + count
    scratch = [
        dma((moves, 3)),
        dma((moves, 3)),
        dma((moves,)),
        dma((2, 1)),
        dma((2, 1, 2)),
        dma((2, count)),
        dma((2, count, 2)),
        dma((2, 2, 3)),
        dma((2, seqs - 1)),
        dma((3,)),
        dma((2, 4)),
        dma((4,)),
    ]
    scratch += [pltpu.VMEM((2, n, feat), BF) for n in (4 * hd, ff, 4 * hd)]
    fetched = weights[:3] + weights[4:]
    scratch += [pltpu.VMEM(weight.shape, BF) for weight in fetched] + [dma((len(fetched),))]
    for _ in range(4):
        scratch += freight_scratch(seqs)
    return pl.pallas_call(
        functools.partial(inputs_kernel, seqs),
        out_shape=outs,
        in_specs=[pl.BlockSpec(memory_space=pl.ANY)] * (5 + len(weights)),
        out_specs=tuple(specs),
        scratch_shapes=scratch,
        compiler_params=pltpu.CompilerParams(collective_id=0, has_side_effects=True, vmem_limit_bytes=60 << 20),
        name="gather_inputs",
    )(tokens, streams, norm, ids, table, *weights)


def outputs_kernel(seqs, count, dqkv, dquery, mix, first_weight, last_weight, x_full, d1_full, d1, d3, small, down, up, tok_out, str_out, small_out, down_out, up_out, first_out, part, first, core_buf, half_send, half_buf, own, land_x, land_y, rc, rh, rs, small_buf, ss, *refs):
    refs = list(refs)
    take = lambda amount: [refs.pop(0) for _ in range(amount)]
    place = spot()
    far = [up, dqkv, first_weight, x_full, mix, d1_full, last_weight, dquery, down, d1, d3]
    near, (sems,) = take(len(far)), take(1)
    lazy = [Lazy(source, target, sems.at[i]) for i, (source, target) in enumerate(zip(far, near))]
    up, dqkv, first_weight, x_full, mix, d1_full, last_weight, dquery, down, d1, d3 = lazy
    y, k, seq, half = place
    rows = part.shape[3]
    feat = part.shape[4] // 4
    bits = [1 << b for b in range((seqs - 1).bit_length())]
    flips = [device(y, k, seq + b - 2 * b * ((seq // b) % 2), half) for b in bits]
    others = [device(y, k, lax.rem(seq + d, seqs), half) for d in range(1, seqs)]
    partners = [device(y, 1 - k, seq, half), device(y, k, seq, 1 - half), device(1 - y, k, seq, half)]
    greet(partners + [device(1 - y, 1 - k, seq, half)] + others)
    partners += flips
    small_out[...] = small[...]

    def start_small(stage):
        return stage, remote(small_out, small_buf.at[stage], ss.at[0, stage], ss.at[1, stage], partners[stage])

    def end_small(started):
        stage, copy = started
        copy.wait()
        small_out[...] += small_buf[stage]

    heads, width = mix.shape[0], mix.shape[1]

    def products(unit):
        for a in range(2):
            for b in range(2):
                start = (2 * a + b) * rows
                if unit == 0:
                    weight = first_weight[:, : 3 * width].reshape(heads * 3 * width, -1)
                    part[unit, a, b] = project(dqkv, weight, start, rows)
                else:
                    weight = last_weight[:, 2 * width : 3 * width].reshape(heads * width, -1)
                    part[unit, a, b] = project(dquery, weight, 4 * (unit - 1) * rows + start, rows)
        reduce.start(unit, unit, 0, True)
        reduce.start(unit, unit, 0, False)

    reduce = Reduce(part, core_buf, half_send, half_buf, rc, rh, place, rows)
    units = range(count + 1)
    down = Collect(down, place, seqs, z_refs=[down_out] + take(5))
    up = Collect(up, place, seqs, y_refs=take(2), z_refs=[up_out] + take(5))
    first_ref = first
    first = Collect(first, place, seqs, y_refs=take(2), z_refs=[first_out] + take(5))
    started = start_small(2)
    for d in up.order:
        up.across(d)
    products(0)
    for d in first.order:
        first_ref[d, : 3 * width] = mm(dqkv[d], x_full[...]).astype(BF)
        first_ref[d, 3 * width :] = mm(mix[d], d1_full[...]).astype(BF)
        first.across(d)
    end_small(started)
    started = start_small(3)
    reduce.pass_on(0, 0, 0)
    products(1)
    for stage in range(4, len(partners)):
        end_small(started)
        started = start_small(stage)
    end_small(started)
    for d in down.order[:2]:
        down.along(d)
    started = start_small(0)
    for unit in units[2:]:
        products(unit)
    end_small(started)
    x_back = Return(own, land_x, rs, place, feat)
    y_back = Return(own, land_y, rs, place, feat)
    x_back.start(0, 0, (d1[0] + reduce.result(0, 0, 0)).astype(BF))
    started = start_small(1)
    for unit in units[1:]:
        reduce.pass_on(unit, unit, 0)
    end_small(started)
    for d in down.order[2:-1]:
        down.along(d)
    for d in up.order[:2]:
        up.along(d)
    for unit in units[1:]:
        y_back.start(unit, unit - 1, (d3[unit - 1] + reduce.result(unit, unit, 0)).astype(BF))
    down.close()
    for d in up.order[2:-1]:
        up.along(d)
    for d in first.order[:2]:
        first.along(d)
    up.close()
    for d in first.order[2:-1]:
        first.along(d)
    for unit in units:
        reduce.finish(unit)
    x_back.finish()
    tok_out[...] = land_x[:, 0].astype(F32)
    first.close()
    y_back.finish()
    str_out[...] = land_y[...].astype(F32)
    for collect in (down, up, first):
        collect.finish()


def scatter_outputs(seqs, collective_id, dqkv, dquery, mix, first_weight, last_weight, x_full, d1_full, d1, d3, small, down, up):
    count, own, depth = d3.shape
    feat, wide = depth // 4, depth // 2
    units = count + 1
    dma = pltpu.SemaphoreType.DMA
    shape = jax.ShapeDtypeStruct
    stages = 3 + (seqs - 1).bit_length()
    outs = (shape((2, 2, own, feat), F32), shape((2, count, 2, own, feat), F32), shape(small.shape, F32))
    outs += tuple(shape((2, group.shape[1], feat), F32) for group in (down, up, first_weight))
    scratch = [
        pltpu.VMEM((units, 2, 2, own, depth), BF),
        pltpu.VMEM(first_weight.shape, BF),
        pltpu.VMEM((units, 2, own, depth), BF),
        pltpu.VMEM((units, own, depth), BF),
        pltpu.VMEM((units, own, depth), BF),
        pltpu.VMEM((units, own, depth), BF),
        pltpu.VMEM((2, 1, 2, own, feat), BF),
        pltpu.VMEM((2, count, 2, own, feat), BF),
        dma((2, units, 2)),
        dma((2, units)),
        dma((2, units, 3)),
        pltpu.VMEM((stages,) + small.shape, F32),
        dma((2, stages)),
    ]
    far = (up, dqkv, first_weight, x_full, mix, d1_full, last_weight, dquery, down, d1, d3)
    scratch += [pltpu.VMEM(array.shape, array.dtype) for array in far] + [dma((len(far),))]
    scratch += along_scratch(seqs, down.shape[1], wide)
    for group in (up, first_weight):
        scratch += across_scratch(seqs, group.shape[1], wide) + along_scratch(seqs, group.shape[1], wide)
    args = (dqkv, dquery, mix, first_weight, last_weight, x_full, d1_full, d1, d3, small, down, up)
    return pl.pallas_call(
        functools.partial(outputs_kernel, seqs, count),
        out_shape=outs,
        in_specs=[pl.BlockSpec(memory_space=pltpu.VMEM if array is small else pl.ANY) for array in args],
        out_specs=tuple(pl.BlockSpec(memory_space=pltpu.VMEM) for _ in outs),
        scratch_shapes=scratch,
        compiler_params=pltpu.CompilerParams(collective_id=collective_id, has_side_effects=True, vmem_limit_bytes=60 << 20),
        name="scatter_outputs",
    )(*args)


def pick(array, index, axis):
    return lax.dynamic_index_in_dim(array, index, axis, keepdims=False)


def dot_f32(spec, left, right):
    return jnp.einsum(spec, left, right, preferred_element_type=F32)


def on_device(
    rows,
    cols,
    tokens,
    streams,
    cotangent,
    block_ids,
    bucket_ids,
    w_qkv,
    enc_table,
    w_out,
    attention_norm_gain,
    attn_bias,
    w_up,
    w_down,
    ffn_gain,
    ffn_bias,
    w_query,
    w_keyval,
    cross_table,
    w_cross_out,
    cross_gain,
    cross_bias,
):
    seqs = cols // 2
    row, col = lax.axis_index(ROW), lax.axis_index(COL)
    y, k, seq, half = row // 2, row % 2, col // 2, col % 2
    low_y = y == 0
    stream_count = streams.shape[1]
    tok = tokens.shape[1]
    own = tok // 2
    feat = tokens.shape[2]
    length = block_ids.shape[2]
    head_dim = w_qkv.shape[2] // 2
    ff = w_up.shape[1] // 2
    table_heads, bucket_count = enc_table.shape

    def columns_back(array, parts):
        return array.reshape(2, parts, -1, feat).transpose(3, 1, 0, 2).reshape(feat, parts, -1)

    hd3, hd2 = 3 * head_dim, 2 * head_dim
    norm_params = jnp.stack([attention_norm_gain, attn_bias, ffn_gain, ffn_bias, cross_gain, cross_bias] + [cross_bias] * 2)
    table_pack = jnp.zeros((8, 128), F32).at[0].set(jnp.stack([enc_table, cross_table]).reshape(-1))
    micro_count = tokens.shape[0]
    x_own, x_full, y_own, y_full, norm_params, all_ids, all_tables, first, up, down, last = gather_inputs(
        seqs,
        tokens.reshape(micro_count, 1, 2, own, feat),
        streams.reshape(micro_count, stream_count, 2, own, feat),
        norm_params,
        block_ids.reshape(8, -1),
        table_pack,
        w_qkv.transpose(1, 0, 2),
        w_out,
        w_up,
        w_down.reshape(2, ff, feat),
        w_keyval.transpose(1, 0, 2),
        w_query,
        w_cross_out,
    )
    x_full, y_full = x_full.reshape(length, D), y_full.reshape(stream_count * length, D)
    segment = pick(pick(all_ids.reshape(rows, micro_count, length), seq, 0), y, 0)
    segq = segment[None]
    segk = segment[:, None]
    own_tables = pick(all_tables[:, 0].reshape(seqs, 2, table_heads, bucket_count), k, 2)
    slot_col = 2 * ((seq - jnp.arange(seqs)) % seqs) + half
    reversed_ids = jnp.concatenate([jnp.full((1,), -1, jnp.int32), bucket_ids[::-1]])
    onehot = bucket_onehot(reversed_ids, bucket_count)
    offsets = jnp.einsum("htb,bo->tho", own_tables, onehot, precision=highest)[:, :, None, :]


    hidden_full, hidden, normed1, inv1, qkv, mix, lse, enc_bias, cross_bias_full, down, last = exchange(
        FORWARD,
        1,
        seqs,
        x_own,
        norm_params[0:2],
        rides=((ACROSS, down), (ALONG, last)),
        attend=(first, x_full, offsets, segq, segk),
    )
    up, down = up.reshape(-1, D), down.reshape(-1, D)
    hidden_full = hidden_full.reshape(length, D)
    enc_full, _, normed2, inv2, act, slope, last = exchange(
        FORWARD,
        2,
        seqs,
        hidden,
        norm_params[2:4],
        rides=((ACROSS, last),),
        feed=(up, down, hidden_full),
    )
    m_kv, m_q, m_co = last[:, :hd2], last[:, hd2:hd3], last[:, hd3:].reshape(-1, D)
    enc_full = enc_full.reshape(length, D)
    kv = dot_f32("snr,tr->snt", m_kv, enc_full).astype(BF)
    query = dot_f32("snr,tr->snt", m_q, y_full).astype(BF)
    cmix, d3_full, output, d3, sums3, dquery, dkv, doff_cross = cross_attention(
        3,
        query,
        kv,
        m_co,
        cross_bias_full,
        y_own,
        norm_params[4:6],
        cotangent.reshape(micro_count, stream_count, 2, own, feat),
    )
    d3_full = d3_full.reshape(stream_count * length, D)

    d2_full, d2, sums2, g_last = exchange(
        BACKWARD,
        4,
        seqs,
        norm_params[2:4][None],
        norm_params[2:4],
        normed=normed2,
        inv=inv2,
        cross=(dkv, dquery, last, cmix, enc_full, y_full, d3_full),
    )
    d2_full = d2_full.reshape(length, D)
    d1_full, d1, sums1, dqkv, doff_enc, g_up, g_down, g_last = exchange(
        BACKWARD,
        5,
        seqs,
        d2,
        norm_params[0:2],
        normed=normed1,
        inv=inv1,
        rides=((SUM_ALONG, g_last),),
        attend=(first, qkv, enc_bias, lse),
        feed=(up, down, d2_full, act, slope, hidden_full),
    )
    d1_full = d1_full.reshape(length, D)

    norm_grads = jnp.concatenate([sums1[:2], sums2[:2], sums3[:2]])
    norm_grads = jnp.where(low_y, norm_grads, jnp.roll(norm_grads, D // 2, axis=1))
    table_grads = jnp.einsum(
        "tho,bo->thb", jnp.stack([doff_enc[:, 0], doff_cross[:, 0]]), onehot, precision=highest
    )
    heads = 2 * slot_col + k
    spread = (heads[:, None] == jnp.arange(table_heads * cols)[None, :]).astype(F32)
    table_grads = jnp.einsum("thb,hg->tgb", table_grads, spread, precision=highest)
    small = jnp.concatenate([norm_grads.reshape(-1, 128), table_grads.reshape(-1, 128)])
    grad_tokens, grad_streams, small, g_down, g_up, g_first = scatter_outputs(
        seqs, 6, dqkv, dquery, mix, first, last, x_full, d1_full, d1, d3, small, g_down, g_up
    )
    output, grad_streams = output.reshape(streams.shape), grad_streams.reshape(streams.shape)
    grad_tokens = grad_tokens.reshape(tokens.shape)
    count = norm_grads.size // 128
    norm_sums = lax.dynamic_slice_in_dim(small[:count].reshape(6, D), row * feat, feat, axis=1)
    table_sums = small[count:].reshape(2, table_heads * cols, bucket_count)
    table_sums = lax.dynamic_slice_in_dim(table_sums, col * table_heads, table_heads, axis=1)
    return (
        output,
        grad_tokens,
        grad_streams,
        columns_back(g_first[:, :hd3], 3),
        table_sums[0],
        g_first[:, hd3:].reshape(w_out.shape),
        norm_sums[0],
        norm_sums[1],
        columns_back(g_up, 1).reshape(w_up.shape),
        g_down.reshape(w_down.shape),
        norm_sums[2],
        norm_sums[3],
        columns_back(g_last[:, hd2:hd3], 1).reshape(w_query.shape),
        columns_back(g_last[:, :hd2], 2),
        table_sums[1],
        g_last[:, hd3:].reshape(w_cross_out.shape),
        norm_sums[4],
        norm_sums[5],
    )


def solution(mesh):
    whole_row, half_col = mesh.shape[ROW], mesh.shape[COL]
    wide, table, norm = P(ROW, None, COL), P(COL, None), P(ROW)
    up, down = P(ROW, COL), P(COL, ROW)
    weights = (wide, table, down, norm, norm, up, down, norm, norm, up, wide, table, down, norm, norm)

    def run(tokens, *rest):
        micro_count = tokens.shape[0]
        if whole_row == 4 and micro_count == 2 and half_col % 2 == 0:
            device_fn = functools.partial(on_device, whole_row, half_col)
        else:
            device_fn = on_device_general
        return jax.shard_map(
            device_fn,
            mesh=mesh,
            in_specs=(P(None, COL, ROW), P(None, None, COL, ROW), P(None, None, COL, ROW), P(None, ROW, None), P()) + weights,
            out_specs=(P(None, None, COL, ROW), P(None, COL, ROW), P(None, None, COL, ROW)) + weights,
            check_vma=False,
        )(tokens, *rest)

    return run
```

```python
import functools
import math
import types
import jax
import jax.numpy as jnp
from jax import lax
from jax.experimental import pallas as pl
from jax.experimental.pallas import tpu as pltpu
from jax.sharding import PartitionSpec as P

D = 1024
F32 = jnp.float32
BF = jnp.bfloat16
ROW, COL = "row", "col"


epsilon = 1e-05
neg_fill = -1e30
highest = lax.Precision.HIGHEST


def gather_cols(local_rows):
    return lax.all_gather(local_rows, COL, axis=1, tiled=True)


def gather_rows(local_rows):
    return lax.all_gather(local_rows, ROW, axis=1, tiled=True)


def product(matmul_operand, weight_matrix):
    return jnp.einsum(
        "ray,yw->raw", matmul_operand, weight_matrix, preferred_element_type=jnp.float32
    )


def rows_product(operand_full, matrix):
    return lax.psum_scatter(product(operand_full, matrix), ROW, scatter_dimension=1, tiled=True)


def cols_product(operand_full, matrix):
    return lax.psum_scatter(product(operand_full, matrix), COL, scatter_dimension=1, tiled=True)


def weight_grad(matmul_operand, upstream_gradient):
    return jnp.einsum(
        "bpt,bpr->tr", matmul_operand, upstream_gradient, preferred_element_type=jnp.float32
    )


def gelu_exact(argument):
    return jax.nn.gelu(argument, approximate=False)


def norm_forward(residual, gain_vec, bias_vec):
    local_sum = jnp.sum(residual, axis=-1)
    average = lax.psum(local_sum, ROW) / D
    centered = residual - average[..., None]
    spread = lax.psum(jnp.sum(centered * centered, axis=-1), ROW) / D
    inv_std = lax.rsqrt(spread + epsilon)
    normed = centered * inv_std[..., None]
    return (normed * gain_vec + bias_vec, normed, inv_std)


def norm_back(out_grad, normed, inv_std, gain_vec):
    scaled_grad = out_grad * gain_vec
    first_moment, second_moment = lax.psum(
        (jnp.sum(scaled_grad, axis=-1), jnp.sum(scaled_grad * normed, axis=-1)), ROW
    )
    resid_grad = inv_std[..., None] * (
        scaled_grad - first_moment[..., None] / D - normed * (second_moment[..., None] / D)
    )
    return (resid_grad, jnp.sum(out_grad * normed, axis=(0, 1)), jnp.sum(out_grad, axis=(0, 1)))


def bucket_onehot(bucket_ids, bucket_count):
    return (bucket_ids[None, :] == jnp.arange(bucket_count, dtype=jnp.int32)[:, None]).astype(
        jnp.float32
    )


def block_logits(query_blk, key_rows, offsets, segment, first_row):
    row_count = query_blk.shape[2]
    length = key_rows.shape[1]
    score_scale = query_blk.shape[-1] ** (-0.5)
    raw_scores = jnp.einsum(
        "snqhd,nkhd->snhqk", query_blk, key_rows, preferred_element_type=jnp.float32
    )
    places = jnp.arange(length, dtype=jnp.int32)
    query_pos = first_row + jnp.arange(row_count, dtype=jnp.int32)
    offset_index = places[None, :] - query_pos[:, None] + (length - 1)
    pos_bias = jnp.take(offsets, offset_index, axis=1)
    visible = segment[:, first_row : first_row + row_count, None] >= segment[:, None, :]
    return jnp.where(
        visible[None, :, None], raw_scores * score_scale + pos_bias[None, None], neg_fill
    )


def attend(queries, key_rows, value_rows, segment, offsets):
    score_logits = block_logits(queries, key_rows, offsets, segment, 0)
    row_max = jnp.max(score_logits, axis=-1, keepdims=True)
    log_total = row_max + jnp.log(jnp.sum(jnp.exp(score_logits - row_max), axis=-1, keepdims=True))
    weights = jnp.exp(score_logits - log_total).astype(jnp.bfloat16)
    mixed_parts = jnp.einsum(
        "snhqk,nkhd->snqhd", weights, value_rows, preferred_element_type=jnp.float32
    )
    lse_parts = log_total[..., 0]
    return (mixed_parts, lse_parts)


def diagonal_sums(summand):
    head_count, row_count, length = summand.shape
    flipped = summand[:, ::-1, :]
    padded = jnp.concatenate(
        [flipped, jnp.zeros((head_count, row_count, row_count), summand.dtype)], axis=2
    )
    flattened = padded.reshape(head_count, row_count * (length + row_count))[
        :, : row_count * (length + row_count - 1)
    ]
    return jnp.sum(flattened.reshape(head_count, row_count, length + row_count - 1), axis=1)


def attend_back(queries, key_rows, value_rows, segment, offsets, onehot, log_totals, mix_grad):
    length = key_rows.shape[1]
    block_rows = min(512, length)
    score_scale = queries.shape[-1] ** (-0.5)
    offset_grad = jnp.zeros(offsets.shape, jnp.float32)
    score_logits = block_logits(queries, key_rows, offsets, segment, 0)
    probability = jnp.exp(score_logits - log_totals[:, :, :, 0:block_rows, None])
    prob_grad = jnp.einsum(
        "snqhd,nkhd->snhqk", mix_grad, value_rows, preferred_element_type=jnp.float32
    )
    logit_grad = probability * (
        prob_grad - jnp.sum(probability * prob_grad, axis=-1, keepdims=True)
    )
    scaled = (logit_grad * score_scale).astype(jnp.bfloat16)
    query_parts = jnp.einsum(
        "snhqk,nkhd->snqhd", scaled, key_rows, preferred_element_type=jnp.float32
    )
    key_grad = jnp.einsum("snhqk,snqhd->nkhd", scaled, queries, preferred_element_type=jnp.float32)
    value_grad = jnp.einsum(
        "snhqk,snqhd->nkhd",
        probability.astype(jnp.bfloat16),
        mix_grad,
        preferred_element_type=jnp.float32,
    )
    low_end = length - block_rows
    offset_grad = offset_grad.at[:, low_end : low_end + length + block_rows - 1].add(
        diagonal_sums(jnp.sum(logit_grad, axis=(0, 1)))
    )
    table_grad = jnp.dot(offset_grad, onehot.T, precision=highest)
    return (query_parts, key_grad, value_grad, table_grad)


def on_device_general(
    tokens,
    streams,
    cotangent,
    block_ids,
    bucket_ids,
    w_qkv,
    enc_table,
    w_out,
    attention_norm_gain,
    attn_bias,
    w_up,
    w_down,
    ffn_gain,
    ffn_bias,
    w_query,
    w_keyval,
    cross_table,
    w_cross_out,
    cross_gain,
    cross_bias,
):
    micro_count = tokens.shape[0]
    stream_count = streams.shape[1]
    seq_rows = block_ids.shape[1]
    length = block_ids.shape[2]
    head_count = enc_table.shape[0]
    bucket_count = enc_table.shape[1]
    row_width = w_qkv.shape[0]
    col_width = w_qkv.shape[2]
    head_dim = col_width // head_count
    row_tokens = seq_rows * length
    qkv_matrix = w_qkv.reshape(row_width, 3 * col_width)
    keyval_matrix = w_keyval.reshape(row_width, 2 * col_width)
    onehot = bucket_onehot(bucket_ids, bucket_count)
    enc_offsets = jnp.dot(enc_table, onehot, precision=highest)
    cross_offsets = jnp.dot(cross_table, onehot, precision=highest)
    qkv_acc = jnp.zeros((row_width, 3 * col_width), jnp.float32)
    out_acc = jnp.zeros(w_out.shape, jnp.float32)
    up_acc = jnp.zeros(w_up.shape, jnp.float32)
    down_acc = jnp.zeros(w_down.shape, jnp.float32)
    query_acc = jnp.zeros(w_query.shape, jnp.float32)
    keyval_acc = jnp.zeros((row_width, 2 * col_width), jnp.float32)
    cross_out_acc = jnp.zeros(w_cross_out.shape, jnp.float32)
    enc_table_acc = jnp.zeros(enc_table.shape, jnp.float32)
    cross_table_acc = jnp.zeros(cross_table.shape, jnp.float32)
    norm_accs = [jnp.zeros((row_width,), jnp.float32) for place_holder in range(6)]
    outputs = []
    token_grads = []
    stream_grads = []
    for micro in range(micro_count):
        segment = block_ids[micro]
        x_in = tokens[micro][None]
        y_in = streams[micro]
        x_full = gather_cols(x_in)
        qkv = (
            rows_product(x_full, qkv_matrix)
            .astype(jnp.bfloat16)
            .reshape(seq_rows, length, 3, head_count, head_dim)
        )
        enc_query = qkv[:, :, 0][None]
        enc_key = qkv[:, :, 1]
        encoder_value_rows = qkv[:, :, 2]
        enc_mixed, enc_lse = attend(enc_query, enc_key, encoder_value_rows, segment, enc_offsets)
        enc_mix = enc_mixed.reshape(1, row_tokens, col_width).astype(jnp.bfloat16)
        mix_full = gather_rows(enc_mix)
        attn_branch = cols_product(mix_full, w_out)
        hidden, normed_one, inv_one = norm_forward(
            x_in.astype(jnp.float32) + attn_branch, attention_norm_gain, attn_bias
        )
        hidden_low = hidden.astype(jnp.bfloat16)
        hidden_full = gather_cols(hidden_low)
        pre_act = rows_product(hidden_full, w_up)
        act_value, gelu_pull = jax.vjp(gelu_exact, pre_act)
        act_low = act_value.astype(jnp.bfloat16)
        act_full = gather_rows(act_low)
        ffn_branch = cols_product(act_full, w_down)
        encoded, normed_two, inv_two = norm_forward(hidden + ffn_branch, ffn_gain, ffn_bias)
        encoded_low = encoded.astype(jnp.bfloat16)
        enc_full = gather_cols(encoded_low)
        keyval = (
            rows_product(enc_full, keyval_matrix)
            .astype(jnp.bfloat16)
            .reshape(seq_rows, length, 2, head_count, head_dim)
        )
        cross_key = keyval[:, :, 0]
        cross_value = keyval[:, :, 1]
        stream_full = gather_cols(y_in)
        cross_query = (
            rows_product(stream_full, w_query)
            .astype(jnp.bfloat16)
            .reshape(stream_count, seq_rows, length, head_count, head_dim)
        )
        cross_mixed, cross_lse = attend(cross_query, cross_key, cross_value, segment, cross_offsets)
        cross_mix = cross_mixed.reshape(stream_count, row_tokens, col_width).astype(jnp.bfloat16)
        cross_full = gather_rows(cross_mix)
        cross_branch = cols_product(cross_full, w_cross_out)
        result, normed_three, inv_three = norm_forward(
            y_in.astype(jnp.float32) + cross_branch, cross_gain, cross_bias
        )
        outputs.append(result)
        grad_three, gain_part, bias_part = norm_back(
            cotangent[micro].astype(jnp.float32), normed_three, inv_three, cross_gain
        )
        norm_accs[4] = norm_accs[4] + gain_part
        norm_accs[5] = norm_accs[5] + bias_part
        branch_full = gather_cols(grad_three.astype(jnp.bfloat16))
        cross_out_acc = cross_out_acc + weight_grad(cross_full, branch_full)
        cross_mix_grad = (
            rows_product(branch_full, w_cross_out.T)
            .astype(jnp.bfloat16)
            .reshape(stream_count, seq_rows, length, head_count, head_dim)
        )
        query_grad, key_grad, value_grad, table_grad = attend_back(
            cross_query,
            cross_key,
            cross_value,
            segment,
            cross_offsets,
            onehot,
            cross_lse,
            cross_mix_grad,
        )
        cross_table_acc = cross_table_acc + table_grad
        query_low = query_grad.reshape(stream_count, row_tokens, col_width).astype(jnp.bfloat16)
        keyval_low = (
            jnp.stack(
                [
                    key_grad.reshape(row_tokens, col_width),
                    value_grad.reshape(row_tokens, col_width),
                ],
                axis=1,
            )
            .reshape(1, row_tokens, 2 * col_width)
            .astype(jnp.bfloat16)
        )
        query_full = gather_rows(query_low)
        query_acc = query_acc + weight_grad(stream_full, query_full)
        stream_grads.append(grad_three + cols_product(query_full, w_query.T))
        keyval_full = gather_rows(keyval_low)
        keyval_acc = keyval_acc + weight_grad(enc_full, keyval_full)
        encoded_grad = cols_product(keyval_full, keyval_matrix.T)
        grad_two, gain_part, bias_part = norm_back(encoded_grad, normed_two, inv_two, ffn_gain)
        norm_accs[2] = norm_accs[2] + gain_part
        norm_accs[3] = norm_accs[3] + bias_part
        feedforward_full_output = gather_cols(grad_two.astype(jnp.bfloat16))
        down_acc = down_acc + weight_grad(act_full, feedforward_full_output)
        act_grad = rows_product(feedforward_full_output, w_down.T)
        pre_low = gelu_pull(act_grad)[0].astype(jnp.bfloat16)
        pre_full = gather_rows(pre_low)
        up_acc = up_acc + weight_grad(hidden_full, pre_full)
        hidden_grad = grad_two + cols_product(pre_full, w_up.T)
        grad_one, gain_part, bias_part = norm_back(
            hidden_grad, normed_one, inv_one, attention_norm_gain
        )
        norm_accs[0] = norm_accs[0] + gain_part
        norm_accs[1] = norm_accs[1] + bias_part
        attn_full = gather_cols(grad_one.astype(jnp.bfloat16))
        out_acc = out_acc + weight_grad(mix_full, attn_full)
        enc_mix_grad = (
            rows_product(attn_full, w_out.T)
            .astype(jnp.bfloat16)
            .reshape(1, seq_rows, length, head_count, head_dim)
        )
        enc_qgrad, enc_kgrad, enc_vgrad, table_grad = attend_back(
            enc_query,
            enc_key,
            encoder_value_rows,
            segment,
            enc_offsets,
            onehot,
            enc_lse,
            enc_mix_grad,
        )
        enc_table_acc = enc_table_acc + table_grad
        qkv_low = (
            jnp.stack(
                [
                    enc_qgrad.reshape(row_tokens, col_width),
                    enc_kgrad.reshape(row_tokens, col_width),
                    enc_vgrad.reshape(row_tokens, col_width),
                ],
                axis=1,
            )
            .reshape(1, row_tokens, 3 * col_width)
            .astype(jnp.bfloat16)
        )
        qkv_full = gather_rows(qkv_low)
        qkv_acc = qkv_acc + weight_grad(x_full, qkv_full)
        token_grads.append((grad_one + cols_product(qkv_full, qkv_matrix.T))[0])
    norm_stack = jnp.stack(norm_accs)
    table_stack = jnp.stack([enc_table_acc, cross_table_acc])
    norm_sums = lax.psum(norm_stack, COL)
    table_sums = lax.psum(table_stack, ROW)
    return (
        jnp.stack(outputs),
        jnp.stack(token_grads),
        jnp.stack(stream_grads),
        qkv_acc.reshape(row_width, 3, col_width),
        table_sums[0],
        out_acc,
        norm_sums[0],
        norm_sums[1],
        up_acc,
        down_acc,
        norm_sums[2],
        norm_sums[3],
        query_acc,
        keyval_acc.reshape(row_width, 2, col_width),
        table_sums[1],
        cross_out_acc,
        norm_sums[4],
        norm_sums[5],
    )


def mm(a,b):
    return jnp.dot(a,b,preferred_element_type=F32)
def mm_nt(a,b):
    return lax.dot_general(a,b,(((1,),(1,)),((),())),preferred_element_type=F32)

def mm_tn(a, b):
    return lax.dot_general(a, b, (((0,), (0,)), ((), ())), preferred_element_type=F32)


def masked_bias(off_ref, index, segq, segk):
    length = segk.shape[0]
    row = jnp.broadcast_to(off_ref[index], (length, 2 * length))
    rolled = pltpu.roll(row, 0, 1, stride=1, stride_axis=0)
    return jnp.where(segk[...] <= segq[...], rolled[:, length:], neg_fill)


def head_forward(keys, values, query, bias):
    logits = mm(keys, query) + bias
    top = jnp.max(logits, axis=0, keepdims=True)
    weight = jnp.exp(logits - top)
    total = jnp.sum(weight, axis=0, keepdims=True)
    return (mm(values, weight.astype(BF)) * (1.0 / total)).astype(BF), top + jnp.log(total)


def head_backward(keys, keys_t, values_t, query, grad, lse, bias):
    prob = jnp.exp(mm(keys, query) + (bias - lse))
    dprob = mm(values_t, grad)
    dlogits = prob * (dprob - jnp.sum(prob * dprob, axis=0, keepdims=True))
    low = dlogits.astype(BF)
    return dlogits, mm(keys_t, low).astype(BF), mm_nt(query, low), mm_nt(grad, prob.astype(BF))


def project(mix_ref, weight, start, rows):
    heads, hd = mix_ref.shape[0], mix_ref.shape[1]
    mixed = mix_ref[:, :, start : start + rows].reshape(heads * hd, rows)
    return mm_tn(mixed, weight).astype(BF)


def project_back(weight, rows_value, dmix_ref, start):
    heads, hd = dmix_ref.shape[0], dmix_ref.shape[1]
    rows = rows_value.shape[0]
    dmix_ref[:, :, start : start + rows] = mm_nt(weight, rows_value).astype(BF).reshape(heads, hd, rows)


def scaled(value, scale):
    return (value.astype(F32) * scale).astype(BF)


def offset_sums(g_ref, doff_ref, g_index, out_index, length):
    sub = lax.broadcasted_iota(jnp.int32, (8, 2 * length), 0)
    acc = jnp.zeros((8, 2 * length), F32)
    for i in range(length // 8):
        piece = g_ref[g_index + (pl.ds(8 * i, 8),)]
        padded = jnp.concatenate([jnp.zeros((8, length), F32), piece], axis=1)
        acc = acc + (pltpu.roll(padded, 2 * length - 8 * i, 1) if i else padded)
    for b in (1, 2, 4):
        acc = jnp.where((sub // b) % 2 == 1, pltpu.roll(acc, 2 * length - b, 1), acc)
    doff_ref[out_index] = jnp.sum(acc, axis=0, keepdims=True)


MESH = pl.DeviceIdType.MESH
FORWARD, BACKWARD = range(2)
ACROSS, THROUGH, ALONG, SUM_ALONG = range(4)


def spot():
    row, col = lax.axis_index(ROW), lax.axis_index(COL)
    return row // 2, row % 2, col // 2, col % 2


def device(y, k, seq, half):
    return (2 * y + k, 2 * seq + half)


def greet(devices):
    barrier = pltpu.get_barrier_semaphore()
    for target in devices:
        pl.semaphore_signal(barrier, inc=1, device_id=target, device_id_type=MESH)
    pl.semaphore_wait(barrier, len(devices))


def remote(source, target, send_sem, recv_sem, device_id):
    copy = pltpu.make_async_remote_copy(
        src_ref=source, dst_ref=target, send_sem=send_sem, recv_sem=recv_sem, device_id=device_id, device_id_type=MESH
    )
    copy.start()
    return copy


def lanes(start, size):
    return pl.ds(pl.multiple_of(start, size), size)


def rows_of(place):
    y, k, seq, half = place
    return [(dy, dk, (1 - y if dy else y), (1 - k if dk else k)) for dy, dk in ((0, 1), (1, 0), (1, 1))]


class Spread:
    def __init__(self, full_ref, half_sems, core_sems, place, rows):
        self.full, self.place, self.rows = full_ref, place, rows
        self.half_sems, self.core_sems = half_sems, core_sems
        self.first, self.second = {}, {}

    def block(self, n, piece, half, k):
        return self.full.at[n, half, k, pl.ds(piece * self.rows, self.rows)]

    def start(self, unit, n, piece):
        y, k, seq, half = self.place
        mine = self.block(n, piece, half, k)
        hs, cs = self.half_sems, self.core_sems
        self.first[unit] = (
            remote(mine, mine, hs.at[0, unit], hs.at[1, unit], device(y, k, seq, 1 - half)),
            remote(mine, mine, cs.at[0, unit, 0], cs.at[1, unit, 0], device(y, 1 - k, seq, half)),
        )

    def forward(self, unit, n, piece):
        y, k, seq, half = self.place
        self.first[unit][0].wait_recv()
        theirs = self.block(n, piece, 1 - half, k)
        cs = self.core_sems
        self.second[unit] = remote(theirs, theirs, cs.at[0, unit, 1], cs.at[1, unit, 1], device(y, 1 - k, seq, half))

    def ready(self, unit):
        self.first[unit][1].wait_recv()
        self.second[unit].wait_recv()

    def sent(self, unit):
        for copy in self.first[unit] + (self.second[unit],):
            copy.wait_send()

    def finish(self, unit):
        self.ready(unit)
        self.sent(unit)


class Reduce:
    def __init__(self, partial_ref, core_buf, half_send, half_buf, core_sems, half_sems, place, rows):
        self.partial, self.core_buf, self.half_send, self.half_buf = partial_ref, core_buf, half_send, half_buf
        self.core_sems, self.half_sems, self.place, self.rows = core_sems, half_sems, place, rows
        self.first, self.second = {}, {}

    def part(self, n, piece, half, k):
        return (n, half, k, pl.ds(piece * self.rows, self.rows))

    def start(self, unit, n, piece, away):
        y, k, seq, half = self.place
        side = 1 - half if away else half
        cs = self.core_sems
        lane = 0 if away else 1
        self.first[unit, lane] = remote(
            self.partial.at[self.part(n, piece, side, 1 - k)],
            self.core_buf.at[unit, lane],
            cs.at[0, unit, lane],
            cs.at[1, unit, lane],
            device(y, 1 - k, seq, half),
        )

    def pass_on(self, unit, n, piece):
        y, k, seq, half = self.place
        self.first[unit, 0].wait_recv()
        away = self.partial[self.part(n, piece, 1 - half, k)].astype(F32) + self.core_buf[unit, 0].astype(F32)
        self.half_send[unit] = away.astype(BF)
        hs = self.half_sems
        self.second[unit] = remote(
            self.half_send.at[unit], self.half_buf.at[unit], hs.at[0, unit], hs.at[1, unit], device(y, k, seq, 1 - half)
        )

    def result(self, unit, n, piece):
        y, k, seq, half = self.place
        self.first[unit, 1].wait_recv()
        mine = self.partial[self.part(n, piece, half, k)].astype(F32) + self.core_buf[unit, 1].astype(F32)
        self.second[unit].wait_recv()
        return mine + self.half_buf[unit].astype(F32)

    def finish(self, unit):
        self.first[unit, 0].wait_send()
        self.first[unit, 1].wait_send()
        self.second[unit].wait_send()


class Return:
    def __init__(self, own_ref, landing, sems, place, feat):
        self.own, self.landing, self.sems, self.place, self.feat = own_ref, landing, sems, place, feat
        self.copies = []

    def start(self, unit, n, value):
        y, k, seq, half = self.place
        feat = self.feat
        self.own[unit] = value
        self.landing[y, n, k] = jnp.where(k == 0, value[:, :feat], value[:, feat : 2 * feat])
        for i, (dy, dk, ty, tk) in enumerate(rows_of(self.place)):
            self.copies.append(
                remote(
                    self.own.at[unit, :, lanes(tk * feat + 2 * dy * feat, feat)],
                    self.landing.at[y, n, k],
                    self.sems.at[0, unit, i],
                    self.sems.at[1, unit, i],
                    device(ty, tk, seq, half),
                )
            )

    def finish(self):
        for copy in self.copies:
            copy.wait()


class Freight:
    def __init__(self, full_ref, z_sems, y_sems, place, seqs):
        self.full, self.place, self.seqs = full_ref, place, seqs
        self.z_sems, self.y_sems = z_sems, y_sems
        self.wide = full_ref.shape[2] // 2
        self.z, self.y = {}, {}
        self.turn = seqs // 2

    def along(self, d):
        y, k, seq, half = self.place
        up = d <= self.turn
        source = d - 1 if up else (d + 1) % self.seqs
        if source:
            self.z[source].wait_recv()
        target = lax.rem(seq + (1 if up else self.seqs - 1), self.seqs)
        self.z[d] = remote(
            self.full.at[source, :, : self.wide],
            self.full.at[d, :, : self.wide],
            self.z_sems.at[0, d - 1],
            self.z_sems.at[1, d - 1],
            device(y, k, target, half),
        )

    def first(self):
        return [d for d in (1, self.seqs - 1) if d <= self.turn or d > self.turn][: min(2, self.seqs - 1)]

    def later(self):
        return list(range(2, self.turn + 1)) + list(range(self.seqs - 2, self.turn, -1))

    def last(self):
        return [d for d in range(self.seqs - 1, 0, -1) if d == self.turn or d == self.turn + 1]

    def across(self, d):
        y, k, seq, half = self.place
        self.y[d] = remote(
            self.full.at[d, :, : self.wide],
            self.full.at[d, :, self.wide :],
            self.y_sems.at[0, d],
            self.y_sems.at[1, d],
            device(1 - y, k, seq, half),
        )

    def pass_along(self, cross):
        for d in self.later():
            self.along(d)
            if cross:
                self.across(d - 1 if d <= self.turn else d + 1)

    def arrive(self, cross):
        for d in self.last():
            self.z[d].wait_recv()
            if cross:
                self.across(d)

    def finish(self):
        for copy in self.z.values():
            copy.wait_send()
        for copy in self.y.values():
            copy.wait()


class Collect:
    def __init__(self, source, place, seqs, y_refs=None, z_refs=None):
        self.source, self.place, self.seqs = source, place, seqs
        self.y_refs, self.z_refs = y_refs, z_refs
        self.wide = source.shape[2] // 2 if y_refs else source.shape[2]
        self.turn = seqs // 2
        self.order = list(range(self.turn, seqs)) + list(range(self.turn - 1, -1, -1))
        self.y, self.z, self.core = {}, {}, None

    def across(self, d):
        y, k, seq, half = self.place
        buf, sems = self.y_refs
        self.y[d] = remote(
            self.source.at[d, :, self.wide :], buf.at[d], sems.at[0, d], sems.at[1, d], device(1 - y, k, seq, half)
        )

    def total(self, d):
        if not self.y_refs:
            return self.source[d].astype(F32)
        self.y[d].wait_recv()
        return self.source[d, :, : self.wide].astype(F32) + self.y_refs[0][d].astype(F32)

    def store(self, out):
        for d in self.order:
            out[d] = self.total(d).astype(BF)

    def along(self, d):
        y, k, seq, half = self.place
        out, z_send, z_buf, c_send, z_sems, c_sems = self.z_refs
        left = d <= self.turn
        before = d + 1 if left else d - 1
        value = self.total(d)
        if before in self.z and before not in (self.turn + 1 if left else self.turn,):
            self.z[before].wait_recv()
            value = value + z_buf[before - 1].astype(F32)
        z_send[d - 1] = value.astype(BF)
        target = lax.rem(seq + (self.seqs - 1 if left else 1), self.seqs)
        self.z[d] = remote(
            z_send.at[d - 1], z_buf.at[d - 1], z_sems.at[0, d - 1], z_sems.at[1, d - 1], device(y, k, target, half)
        )

    def close(self):
        y, k, seq, half = self.place
        out, z_send, z_buf, c_send, z_sems, c_sems = self.z_refs
        total = self.total(0)
        for d in sorted({1, self.seqs - 1}):
            self.z[d].wait_recv()
            total = total + z_buf[d - 1].astype(F32)
        low, high = total[:, : self.wide // 2], total[:, self.wide // 2 :]
        out[k] = jnp.where(k == 0, low, high)
        c_send[...] = jnp.where(k == 0, high, low)
        self.core = remote(c_send, out.at[k], c_sems.at[0], c_sems.at[1], device(y, 1 - k, seq, half))

    def finish(self):
        for copy in self.y.values():
            copy.wait_send()
        for copy in self.z.values():
            copy.wait_send()
        if self.core is not None:
            self.core.wait()


def freight_scratch(seqs):
    dma = pltpu.SemaphoreType.DMA
    return [dma((2, seqs - 1)), dma((2, seqs))]


def across_scratch(seqs, n, wide):
    return [pltpu.VMEM((seqs, n, wide), BF), pltpu.SemaphoreType.DMA((2, seqs))]


def along_scratch(seqs, n, wide):
    dma = pltpu.SemaphoreType.DMA
    return [
        pltpu.VMEM((seqs - 1, n, wide), BF),
        pltpu.VMEM((seqs - 1, n, wide), BF),
        pltpu.VMEM((n, wide // 2), F32),
        dma((2, seqs - 1)),
        dma((2,)),
    ]


def along_devices(place, seqs):
    y, k, seq, half = place
    return [device(y, k, lax.rem(seq + d, seqs), half) for d in sorted({1, seqs - 1})]


def shuffle(source, target, n, index, place, sends, receives, local_sems):
    y, k, seq, half = place
    feat = source.shape[-1]
    copies = [pltpu.make_async_copy(source.at[y, n, k], target.at[n, :, lanes(k * feat, feat)], local_sems.at[index])]
    copies[0].start()
    for i, (dy, dk, ty, tk) in enumerate(rows_of(place)):
        copies.append(
            remote(
                source.at[ty, n, tk],
                target.at[n, :, lanes(k * feat + 2 * dy * feat, feat)],
                sends.at[index, i],
                receives.at[index, i],
                device(ty, tk, seq, half),
            )
        )
    return copies


def normalize(residual):
    centered = residual - jnp.mean(residual, axis=-1, keepdims=True)
    inv_std = lax.rsqrt(jnp.mean(centered * centered, axis=-1, keepdims=True) + epsilon)
    return centered * inv_std, inv_std


def normalize_back(out_grad, normed, inv_std, gain):
    scaled = out_grad * gain
    first = jnp.mean(scaled, axis=-1, keepdims=True)
    second = jnp.mean(scaled * normed, axis=-1, keepdims=True)
    return inv_std * (scaled - first - normed * second)


def column_sum(value):
    return jnp.sum(value, axis=0, keepdims=True)


def start_all(reduce, units):
    for unit, n, p in units:
        reduce.start(unit, n, p, True)
    for unit, n, p in units:
        reduce.start(unit, n, p, False)


def bias_of(r, target, table):
    def one(h, carry):
        target[h] = masked_bias(r.off, (table, h), r.segq, r.segk)
        return carry

    lax.fori_loop(0, r.qkv.shape[0], one, 0)


def out_part(r):
    heads, width, depth = r.weight.shape
    return r.weight[:, 3 * width // 4 :].reshape(heads * (width // 4), depth)


def feed_forward(r):
    block = r.act.shape[0] // 4
    for b in range(4):
        here = slice(b * block, (b + 1) * block)
        pre = mm_nt(r.up[here], r.row[...])
        share = 0.5 + 0.5 * lax.erf(pre * (0.5**0.5))
        r.act[here] = (pre * share).astype(BF)
        r.slope[here] = share + pre * jnp.exp(-0.5 * pre * pre) * ((2.0 * math.pi) ** -0.5)


def attend_all(r):
    heads, hd = r.qkv.shape[0], r.qkv.shape[1] // 3
    bias_of(r, r.masked, 0)
    r.bias_out[0].start()
    weight, row = r.weight.ready(), r.row.ready()

    def one(h, carry):
        r.qkv[h] = mm_nt(weight[h, : 3 * hd], row[...]).astype(BF)
        query = scaled(r.qkv[h, :hd], hd**-0.5)
        keys, values = r.qkv[h, hd : 2 * hd].T, r.qkv[h, 2 * hd :]
        r.mix[h], r.lse[h] = head_forward(keys, values, query, r.masked[h])
        return carry

    lax.fori_loop(0, heads, one, 0)


def cross_slot(r, d):
    span, width = r.dkv.shape[1], r.dquery.shape[1]
    r.g[d, :span] = mm(r.dkv[d], r.row[...]).astype(BF)
    r.g[d, span : span + width] = mm(r.dquery[d], r.stream[...]).astype(BF)
    r.g[d, span + width :] = mm(r.mix[d], r.grad_full[...]).astype(BF)


def attend_all_back(r):
    heads, hd, length = r.qkv.shape[0], r.qkv.shape[1] // 3, r.qkv.shape[2]
    scale = hd**-0.5
    qkv, masked = r.qkv.ready(), r.masked.ready()

    def one(h, carry):
        query, keys, values = (qkv[h, part * hd : (part + 1) * hd] for part in range(3))
        dlogits, dq, dk, dv = head_backward(
            keys.T, scaled(keys, scale), values.T, scaled(query, scale), r.dmix[h], r.lse[h], masked[h]
        )
        r.g_scr[...] = dlogits
        r.dqkv[h, :hd] = dq
        r.dqkv[h, hd : 2 * hd] = dk.astype(BF)
        r.dqkv[h, 2 * hd :] = dv.astype(BF)
        offset_sums(r.g_scr, r.doff, (), (h,), length)
        return carry

    lax.fori_loop(0, heads, one, 0)


def exchange_kernel(kind, attend, feed, extra_count, far, count, pieces, seqs, rides, *refs):
    place = spot()
    y, k, seq, half = place
    refs = list(refs)
    take = lambda amount: [refs.pop(0) for _ in range(amount)]
    r = types.SimpleNamespace()
    r.resid, r.norm = take(2)
    if kind == BACKWARD:
        r.normed, r.inv = take(2)
    extras = take(extra_count)
    ride_in = take(len(rides))
    (r.full,) = take(1)
    if kind == FORWARD:
        r.out, r.normed, r.inv = take(3)
    else:
        r.grad, r.sums = take(2)
    if attend:
        if kind == FORWARD:
            r.qkv, r.mix, r.lse, r.masked, r.masked_next = take(5)
        else:
            r.dqkv, r.doff = take(2)
    leave_out = take(2 if kind == FORWARD else 1) if feed else []
    if kind == BACKWARD:
        (r.summed,) = take(1)
    ride_out = take(len(rides))
    if far:
        near, (sems,) = take(len(far)), take(1)
        for i, index in enumerate(far):
            extras[index] = Lazy(extras[index], near[i], sems.at[i])
    if kind == BACKWARD and attend:
        r.up, r.down, r.row, r.act, r.slope, r.hidden, r.weight, r.qkv, r.masked, r.lse = extras
    elif kind == BACKWARD:
        r.dkv, r.dquery, r.weight, r.mix, r.row, r.stream, r.grad_full = extras
    elif attend:
        r.weight, r.row, r.off, r.segq, r.segk = extras
        biases = [(r.masked, 0), (r.masked_next, 1)]
        r.masked, r.masked_next, bias_sems = take(3)
        r.bias_out = [
            pltpu.make_async_copy(source, target, bias_sems.at[i])
            for i, (source, (target, _)) in enumerate(zip((r.masked, r.masked_next), biases))
        ]
    else:
        r.up, r.down, r.row = extras
    if feed:
        leaving, (sems,) = take(len(leave_out)), take(1)
        if kind == FORWARD:
            r.act, r.slope = leaving
        else:
            (r.g_up,) = leaving
        leaving = [pltpu.make_async_copy(a, b, sems.at[i]) for i, (a, b) in enumerate(zip(leaving, leave_out))]
    (partial,) = take(1)
    if kind == BACKWARD:
        (r.g,) = take(1)
        inner = Collect(r.g, place, seqs, y_refs=take(2))
        if feed:
            (r.dpre,) = take(1)
    if attend:
        if kind == BACKWARD:
            r.g_scr, r.dmix = take(2)
    core_buf, half_send, half_buf, rc, rh, gh, gc = take(7)
    rows = partial.shape[3] // pieces
    peers = [device(y, 1 - k, seq, half), device(y, k, seq, 1 - half)]
    peers.append(device(1 - y, k, seq, half))
    if {ALONG, THROUGH, SUM_ALONG} & set(rides):
        peers += along_devices(place, seqs)
    greet(peers)
    units = [(n * pieces + p, n, p) for n in range(count) for p in range(pieces)]
    reduce = Reduce(partial, core_buf, half_send, half_buf, rc, rh, place, rows)
    spread = Spread(r.full, gh, gc, place, rows)
    moves, sums_along = [], []
    for ride, source, target in zip(rides, ride_in, ride_out):
        if ride == SUM_ALONG:
            sums_along.append(Collect(source, place, seqs, z_refs=[target] + take(5)))
            for d in sums_along[-1].order[:2]:
                sums_along[-1].along(d)
        else:
            moves.append((ride, Freight(target, *take(2), place, seqs)))
            if ride == ACROSS:
                for d in range(seqs):
                    moves[-1][1].across(d)
            else:
                if ride == THROUGH:
                    moves[-1][1].across(0)
                for d in moves[-1][1].first():
                    moves[-1][1].along(d)
    own = partial.shape[3]
    if kind == FORWARD and attend:
        attend_all(r)
        weight = out_part(r)
        product = lambda start: project(r.mix, weight, start, own)
    elif kind == FORWARD:
        feed_forward(r)
        for copy in leaving:
            copy.start()
        product = lambda start: mm_tn(r.act[:, start : start + own], r.down[...]).astype(BF)
    elif feed:
        block = r.g.shape[1]
        for d in range(seqs):
            here = slice(d * block, (d + 1) * block)
            r.dpre[here] = (mm_nt(r.down[here], r.row[...]) * r.slope[here]).astype(BF)
        product = lambda start: mm_tn(r.dpre[:, start : start + own], r.up[...]).astype(BF)
    else:
        span = r.dkv.shape[1]
        weight = r.weight[:, :span].reshape(seqs * span, -1)
        product = lambda start: project(r.dkv, weight, start, own)
    if kind == BACKWARD and not feed:
        grad_slot = lambda d: cross_slot(r, d)
        grad_slot(inner.order[0])
        inner.across(inner.order[0])
    for a in range(2):
        for b in range(2):
            partial[0, a, b] = product((2 * a + b) * own)
    start_all(reduce, units)
    if kind == BACKWARD:
        r.sums[...] = jnp.zeros_like(r.sums)
        for d in inner.order[0 if feed else 1 :]:
            if feed:
                here = slice(d * block, (d + 1) * block)
                r.g[d] = mm(r.act[here], r.row[...]).astype(BF)
            else:
                grad_slot(d)
            inner.across(d)
    gain, bias = r.norm[0:1], r.norm[1:2]
    for unit, n, p in units:
        reduce.pass_on(unit, n, p)
    for unit, n, p in units:
        here = pl.ds(p * rows, rows)
        branch = reduce.result(unit, n, p)
        if kind == FORWARD:
            normed, inv = normalize(r.resid[n, here].astype(F32) + branch)
            value = normed * gain + bias
            r.out[n, here] = value
            r.normed[n, here] = normed
            r.inv[n, here] = inv
        else:
            upstream = r.resid[n, here] + branch if feed else branch
            normed = r.normed[n, here]
            value = normalize_back(upstream, normed, r.inv[n, here], gain)
            r.grad[n, here] = value
        r.full[n, half, k, here] = value.astype(BF)
        spread.start(unit, n, p)
        if kind != FORWARD:
            r.sums[0:1] += column_sum(upstream * normed)
            r.sums[1:2] += column_sum(upstream)
    for collect in sums_along:
        for d in collect.order[2:-1]:
            collect.along(d)
    for ride, move in moves:
        if ride != ACROSS:
            move.pass_along(ride == THROUGH)
            move.arrive(ride == THROUGH)
    if attend and kind == FORWARD:
        bias_of(r, r.masked_next, 1)
        r.bias_out[1].start()
    elif attend:
        for d in range(seqs):
            here = slice(d * block, (d + 1) * block)
            r.g_up[d] = mm(r.dpre[here], r.hidden[...]).astype(BF)
        for copy in leaving:
            copy.start()
    for unit, n, p in units:
        spread.forward(unit, n, p)
    for collect in sums_along:
        collect.close()
    for unit, n, p in units:
        spread.finish(unit)
        reduce.finish(unit)
    if attend and kind == BACKWARD:
        weight = out_part(r)
        for a in range(2):
            for b in range(2):
                project_back(weight, r.full[0, a, b], r.dmix, (2 * a + b) * own)
        attend_all_back(r)
    if attend and kind == FORWARD:
        for copy in r.bias_out:
            copy.wait()
    if feed:
        for copy in leaving:
            copy.wait()
    for ride, move in moves:
        move.finish()
    if kind == BACKWARD:
        inner.store(r.summed)
        inner.finish()
    for collect in sums_along:
        collect.finish()


def exchange(kind, collective_id, seqs, resid, norm, normed=None, inv=None, rides=(), attend=(), feed=(), cross=()):
    count, own, depth = 1, resid.shape[1], norm.shape[1]
    if kind == BACKWARD:
        own = normed.shape[1]
    pieces = 2 if count == 1 else 1
    units, rows = count * pieces, own // pieces
    dma = pltpu.SemaphoreType.DMA
    shape = jax.ShapeDtypeStruct
    vmem = pl.BlockSpec(memory_space=pltpu.VMEM)
    anywhere = pl.BlockSpec(memory_space=pl.ANY)
    full = shape((count, 2, 2, own, depth), BF)
    grad, sums = shape((count, own, depth), F32), shape((8, depth), F32)
    scratch = []
    if kind == FORWARD:
        args = (resid, norm)
        outs = (full, grad, grad, shape((count, own, 1), F32))
    else:
        args = (resid, norm, normed, inv)
        outs = (full, grad, sums)
    extras = tuple(feed) + tuple(attend) + tuple(cross)
    far = tuple(i for i, array in enumerate(extras) if array.size >= 1 << 17)
    base = len(args)
    args += extras
    scratch += [pltpu.VMEM(extras[i].shape, extras[i].dtype) for i in far] + [dma((len(far),))]
    if attend and kind == FORWARD:
        bias = (attend[0].shape[0],) + (attend[1].shape[0],) * 2
        scratch += [pltpu.VMEM(bias, F32), pltpu.VMEM(bias, F32), dma((2,))]
    if feed and kind == FORWARD:
        inner = (feed[0].shape[0], feed[2].shape[0])
        scratch += [pltpu.VMEM(inner, BF), pltpu.VMEM(inner, F32), dma((2,))]
    elif feed:
        scratch += [pltpu.VMEM((seqs, feed[0].shape[0] // seqs, depth), BF), dma((1,))]
    scratch.append(pltpu.VMEM((count, 2, 2, own, depth), BF))
    if kind == BACKWARD:
        n = feed[0].shape[0] // seqs if feed else cross[2].shape[1]
        scratch += [pltpu.VMEM((seqs, n, depth), BF)] + across_scratch(seqs, n, depth // 2)
        if feed:
            scratch.append(pltpu.VMEM(feed[3].shape, BF))
    if attend:
        heads, hd = attend[0].shape[0], attend[0].shape[1] // 4
        length = attend[1].shape[0] if kind == FORWARD else attend[1].shape[2]
        qkv = shape((heads, 3 * hd, length), BF)
        if kind == FORWARD:
            bias = shape((heads, length, length), F32)
            outs += (qkv, shape((heads, hd, length), BF), shape((heads, 1, length), F32), bias, bias)
        else:
            outs += (qkv, shape((heads, 1, 2 * length), F32))
            scratch += [pltpu.VMEM((length, length), F32), pltpu.VMEM((heads, hd, length), BF)]
    if feed and kind == FORWARD:
        inner = (feed[0].shape[0], feed[2].shape[0])
        outs += (shape(inner, BF), shape(inner, F32))
    elif feed:
        outs += (shape((seqs, n, depth), BF),)
    if kind == BACKWARD:
        outs += (shape((seqs, n, depth // 2), BF),)
    scratch += [
        pltpu.VMEM((units, 2, rows, depth), BF),
        pltpu.VMEM((units, rows, depth), BF),
        pltpu.VMEM((units, rows, depth), BF),
        dma((2, units, 2)),
        dma((2, units)),
        dma((2, units)),
        dma((2, units, 2)),
    ]
    in_specs, out_specs = [vmem] * len(args), [vmem] * len(outs)
    for i in far:
        in_specs[base + i] = anywhere
    if kind == FORWARD:
        out_specs[-2:] = [anywhere] * 2
    elif feed:
        out_specs[-2] = anywhere
    aliases = {}
    for ride, array in rides:
        if ride == SUM_ALONG:
            n, wide = array.shape[1], depth // 2
            scratch += along_scratch(seqs, n, wide)
            in_specs.append(vmem)
            out_specs.append(vmem)
            outs += (shape((2, n, wide // 2), F32),)
        else:
            scratch += freight_scratch(seqs)
            aliases[len(args)] = len(outs)
            in_specs.append(anywhere)
            out_specs.append(anywhere)
            outs += (shape(array.shape, array.dtype),)
        args += (array,)
    return pl.pallas_call(
        functools.partial(exchange_kernel, kind, bool(attend), bool(feed), len(extras), far, count, pieces, seqs, tuple(ride for ride, _ in rides)),
        out_shape=outs,
        in_specs=in_specs,
        out_specs=tuple(out_specs),
        scratch_shapes=scratch,
        input_output_aliases=aliases,
        compiler_params=pltpu.CompilerParams(collective_id=collective_id, has_side_effects=True, vmem_limit_bytes=60 << 20),
        name="exchange_%d" % collective_id,
    )(*args)


def cross_kernel(count, query, kv, out_weight, bias, resid, norm, cot, mix, full_out, output, grad_out, sums, dquery, dkv, doff, full, grad, leave_sems, partial, lse, keys, keys_scaled, values_t, queries, masked, bias_sem, g_scr, dk_scr, dv_scr, dmix, own, landing, return_sems, cot_own, cot_send, cot_recv, cot_local, core_buf, half_send, half_buf, rc, rh, gh, gc):
    place = spot()
    y, k, seq, half = place
    heads, hd, length = query.shape[0], query.shape[1], kv.shape[2]
    depth, rows = partial.shape[4], partial.shape[3]
    scale = hd**-0.5
    bias_copy = pltpu.make_async_copy(bias, masked, bias_sem)
    bias_copy.start()
    greet(
        [device(y, 1 - k, seq, half), device(y, k, seq, 1 - half)]
        + [device(ty, tk, seq, half) for dy, dk, ty, tk in rows_of(place) if dy]
    )
    cots = [shuffle(cot, cot_own, n, n, place, cot_send, cot_recv, cot_local) for n in range(count)]
    reduce = Reduce(partial, core_buf, half_send, half_buf, rc, rh, place, rows)
    spread = Spread(full, gh, gc, place, rows)
    back = Return(own, landing, return_sems, place, depth // 4)
    leaving = []
    sums[...] = jnp.zeros_like(sums)
    g_scr[...] = jnp.zeros_like(g_scr)
    dk_scr[...] = jnp.zeros_like(dk_scr)
    dv_scr[...] = jnp.zeros_like(dv_scr)

    def prepare(h, carry):
        keys[h] = kv[h, :hd].T
        keys_scaled[h] = scaled(kv[h, :hd], scale)
        values_t[h] = kv[h, hd:].T
        queries[h] = scaled(query[h], scale)
        return carry

    lax.fori_loop(0, heads, prepare, 0)
    bias_copy.wait()

    def attend_heads(s, low, high):
        def one(h, carry):
            here = slice(s * length, (s + 1) * length)
            mix[h, :, here], lse[h, :, here] = head_forward(keys[h], kv[h, hd:], queries[h, :, here], masked[h])
            return carry

        lax.fori_loop(low, high, one, 0)

    def send_products(s):
        for a in range(2):
            for b in range(2):
                partial[s, a, b] = project(mix, out_weight[...], s * length + (2 * a + b) * rows, rows)
        reduce.start(s, s, 0, True)
        reduce.start(s, s, 0, False)

    def turn(s):
        normed, inv = normalize(resid[s].astype(F32) + reduce.result(s, s, 0))
        for copy in cots[s]:
            copy.wait()
        upstream = cot_own[s].astype(F32)
        value = normalize_back(upstream, normed, inv, norm[0:1])
        grad[s] = value
        leaving.append(pltpu.make_async_copy(grad.at[s], grad_out.at[s], leave_sems.at[0, s]))
        leaving[-1].start()
        full[s, half, k] = value.astype(BF)
        spread.start(s, s, 0)
        sums[0:1] += column_sum(upstream * normed)
        sums[1:2] += column_sum(upstream)
        back.start(s, s, (normed * norm[0:1] + norm[1:2]).astype(BF))

    def attend_back(s):
        for a in range(2):
            for b in range(2):
                project_back(out_weight[...], full[s, a, b], dmix, (2 * a + b) * rows)

        def one(h, carry):
            here = slice(s * length, (s + 1) * length)
            dlogits, dq, dk, dv = head_backward(
                keys[h], keys_scaled[h], values_t[h], queries[h, :, here], dmix[h], lse[h, :, here], masked[h]
            )
            g_scr[h] += dlogits
            dquery[h, :, here] = dq
            dk_scr[h] += dk
            dv_scr[h] += dv
            return carry

        lax.fori_loop(0, heads, one, 0)

    for s in range(count):
        attend_heads(s, 0, heads // 2)
        if s >= 1:
            reduce.pass_on(s - 1, s - 1, 0)
        if s >= 2:
            turn(s - 2)
        attend_heads(s, heads // 2, heads)
        send_products(s)
    reduce.pass_on(count - 1, count - 1, 0)
    for s in range(max(count - 2, 0), count):
        turn(s)
    for s in range(count):
        spread.forward(s, s, 0)
        spread.ready(s)
        leaving.append(pltpu.make_async_copy(full.at[s], full_out.at[s], leave_sems.at[1, s]))
        leaving[-1].start()
        attend_back(s)
    for h in range(heads):
        dkv[h, :hd] = dk_scr[h].astype(BF)
        dkv[h, hd:] = dv_scr[h].astype(BF)

    def offsets_of(h, carry):
        offset_sums(g_scr, doff, (h,), (h,), length)
        return carry

    lax.fori_loop(0, heads, offsets_of, 0)
    back.finish()
    output[...] = landing[...].astype(F32)
    for copy in leaving:
        copy.wait()
    for s in range(count):
        spread.sent(s)
        reduce.finish(s)


def cross_attention(collective_id, query, kv, out_weight, masked, resid, norm, cot):
    count, own, depth = resid.shape
    heads, hd, total = query.shape
    length = kv.shape[2]
    dma = pltpu.SemaphoreType.DMA
    shape = jax.ShapeDtypeStruct
    outs = (
        shape(query.shape, BF),
        shape((count, 2, 2, own, depth), BF),
        shape((2, count, 2, own, depth // 4), F32),
        shape((count, own, depth), F32),
        shape((8, depth), F32),
        shape(query.shape, BF),
        shape(kv.shape, BF),
        shape((heads, 1, 2 * length), F32),
    )
    whole = pl.BlockSpec(memory_space=pltpu.VMEM)
    anywhere = pl.BlockSpec(memory_space=pl.ANY)
    specs = [whole] * 3 + [anywhere] + [whole] * 2 + [anywhere]
    vmem = pltpu.VMEM
    return pl.pallas_call(
        functools.partial(cross_kernel, count),
        out_shape=outs,
        in_specs=specs,
        out_specs=tuple(anywhere if i in (1, 3) else whole for i in range(len(outs))),
        scratch_shapes=[
            vmem((count, 2, 2, own, depth), BF),
            vmem((count, own, depth), F32),
            dma((2, count)),
            vmem((count, 2, 2, own, depth), BF),
            vmem((heads, 1, total), F32),
            vmem((heads, length, hd), BF),
            vmem((heads, hd, length), BF),
            vmem((heads, length, hd), BF),
            vmem(query.shape, BF),
            vmem(masked.shape, F32),
            pltpu.SemaphoreType.DMA,
            vmem((heads, length, length), F32),
            vmem((heads, hd, length), F32),
            vmem((heads, hd, length), F32),
            vmem((heads, hd, length), BF),
            vmem((count, own, depth), BF),
            vmem((2, count, 2, own, depth // 4), BF),
            dma((2, count, 3)),
            vmem((count, own, depth), BF),
            dma((count, 3)),
            dma((count, 3)),
            dma((count,)),
            vmem((count, 2, own, depth), BF),
            vmem((count, own, depth), BF),
            vmem((count, own, depth), BF),
            dma((2, count, 2)),
            dma((2, count)),
            dma((2, count)),
            dma((2, count, 2)),
        ],
        compiler_params=pltpu.CompilerParams(collective_id=collective_id, has_side_effects=True, vmem_limit_bytes=60 << 20),
        name="cross_attention",
    )(query, kv, out_weight, masked, resid, norm, cot)


class Lazy:
    def __init__(self, source, target, sem):
        self.copy, self.ref, self.shape = pltpu.make_async_copy(source, target, sem), target, target.shape
        self.copy.start()

    def ready(self):
        if self.copy is not None:
            self.copy.wait()
            self.copy = None
        return self.ref

    def __getitem__(self, index):
        return self.ready()[index]

    @property
    def at(self):
        return self.ready().at


def fetch(far, near, sems):
    copies = [pltpu.make_async_copy(source, target, sems.at[i]) for i, (source, target) in enumerate(zip(far, near))]
    for copy in copies:
        copy.start()
    return copies


def inputs_kernel(seqs, tok_ref, str_ref, norm_ref, ids_ref, tab_ref, *refs):
    refs = list(refs)
    take = lambda amount: [refs.pop(0) for _ in range(amount)]
    groups = 4
    far = take(7)
    x_own, *leave_out, norm_all, ids_all, tab_all = take(7)
    fulls = take(groups)
    in_send, in_recv, in_local, xh, xc, yh, yc, small_sems, tab_sems, small_self, pack_sems, pack_self = take(12)
    pack_first, pack_up, pack_last = take(3)
    w_qkv, w_out, w_up, w_kv, w_query, w_co = near = take(6)
    (fetch_sems,) = take(1)
    x_full, y_own, y_full = leaving = take(3)
    (leave_sems,) = take(1)
    leaving = [pltpu.make_async_copy(a, b, leave_sems.at[n]) for n, (a, b) in enumerate(zip(leaving, leave_out))]
    w_down = far.pop(3)
    fetched = fetch(far, near, fetch_sems)
    packs = [pack_first, pack_up, w_down, pack_last]
    place = spot()
    y, k, seq, half = place
    feat = tok_ref.shape[-1]
    own = tok_ref.shape[-2]
    row_peers = rows_of(place)
    others = [device(y, k, lax.rem(seq + d, seqs), half) for d in range(1, seqs)]
    greet([device(ty, tk, seq, half) for dy, dk, ty, tk in row_peers] + [device(y, k, seq, 1 - half)] + others)
    count = str_ref.shape[1]
    x_copies = shuffle(tok_ref, x_own, 0, 0, place, in_send, in_recv, in_local)
    hd = w_out.shape[0] // 2

    def columns_in(pack, start, matrix):
        rows = matrix.T
        half_rows = rows.shape[0] // 2
        for core in range(2):
            pack[core, start : start + half_rows] = rows[core * half_rows : (core + 1) * half_rows]

    def rows_in(pack, start, matrix):
        half_rows = matrix.shape[0] // 2
        for core in range(2):
            pack[core, start : start + half_rows] = matrix[core * half_rows : (core + 1) * half_rows]

    def load(g):
        here = fulls[g].at[0, :, lanes(k * feat, feat)]
        copy = pltpu.make_async_copy(packs[g].at[k], here, pack_self.at[g])
        copy.start()
        return (
            copy,
            remote(packs[g].at[1 - k], here, pack_sems.at[0, g], pack_sems.at[1, g], device(y, 1 - k, seq, half)),
        )

    for copy in fetched[:2]:
        copy.wait()
    for part in range(3):
        columns_in(pack_first, part * hd, w_qkv[part])
    rows_in(pack_first, 3 * hd, w_out)
    loads = [load(0)]
    small = []
    for j, (source, target) in enumerate(((norm_ref, norm_all), (ids_ref, ids_all))):
        slot = (lambda dy: (slice(None), lanes(k * feat + 2 * dy * feat, feat))) if j == 0 else (lambda dy: (2 * y + k,))
        copy = pltpu.make_async_copy(source, target.at[slot(0)], small_self.at[j])
        copy.start()
        small.append(copy)
        for i, (dy, dk, ty, tk) in enumerate(row_peers):
            small.append(
                remote(source, target.at[slot(dy)], small_sems.at[0, j, i], small_sems.at[1, j, i], device(ty, tk, seq, half))
            )
    copy = pltpu.make_async_copy(tab_ref, tab_all.at[0], small_self.at[2])
    copy.start()
    small.append(copy)
    for d in range(1, seqs):
        small.append(remote(tab_ref, tab_all.at[d], tab_sems.at[0, d - 1], tab_sems.at[1, d - 1], others[d - 1]))
    freights = [Freight(full, *take(2), place, seqs) for full in fulls]
    for copy in loads[0]:
        copy.wait()
    for d in freights[0].first():
        freights[0].along(d)
    freights[0].across(0)
    fetched[2].wait()
    columns_in(pack_up, 0, w_up[...])
    loads.append(load(1))
    for copy in x_copies:
        copy.wait()
    x_full[0, half, k] = x_own[0]
    x_spread = Spread(x_full, xh, xc, place, own)
    x_spread.start(0, 0, 0)
    y_copies = [shuffle(str_ref, y_own, n, 1 + n, place, in_send, in_recv, in_local) for n in range(count)]
    y_spread = Spread(y_full, yh, yc, place, own)
    freights[0].pass_along(True)
    for copy in loads[1]:
        copy.wait()
    for d in freights[1].first():
        freights[1].along(d)
    loads.append(load(2))
    for copy in fetched[3:]:
        copy.wait()
    for part in range(2):
        columns_in(pack_last, part * hd, w_kv[part])
    columns_in(pack_last, 2 * hd, w_query[...])
    rows_in(pack_last, 3 * hd, w_co)
    loads.append(load(3))
    x_spread.forward(0, 0, 0)
    freights[0].arrive(True)
    freights[1].across(0)
    for n in range(count):
        for copy in y_copies[n]:
            copy.wait()
        y_full[n, half, k] = y_own[n]
        y_spread.start(n, n, 0)
    freights[1].pass_along(True)
    for g in range(2, groups):
        for copy in loads[g]:
            copy.wait()
    for d in freights[2].first():
        freights[2].along(d)
    freights[1].arrive(True)
    freights[2].pass_along(False)
    for n in range(count):
        y_spread.forward(n, n, 0)
    x_spread.finish(0)
    for n in range(count):
        y_spread.finish(n)
    for copy in leaving:
        copy.start()
    for copy in small:
        copy.wait()
    freights[2].arrive(False)
    for freight in freights:
        freight.finish()
    for copy in leaving:
        copy.wait()


def gather_inputs(seqs, tokens, streams, norm, ids, table, *weights):
    count, own, feat = streams.shape[1], streams.shape[-2], streams.shape[-1]
    depth = 4 * feat
    dma = pltpu.SemaphoreType.DMA
    shape = jax.ShapeDtypeStruct
    vmem = pl.BlockSpec(memory_space=pltpu.VMEM)
    outs = (
        shape((1, own, depth), BF),
        shape((1, 2, 2, own, depth), BF),
        shape((count, own, depth), BF),
        shape((count, 2, 2, own, depth), BF),
        shape((norm.shape[0], depth), F32),
        shape((4,) + ids.shape, jnp.int32),
        shape((seqs,) + table.shape, F32),
    )
    specs = [vmem] * len(outs)
    hd, ff = weights[1].shape[0] // 2, weights[2].shape[1] // 2
    for n in (4 * hd, ff, ff, 4 * hd):
        outs += (shape((seqs, n, depth), BF),)
        specs.append(pl.BlockSpec(memory_space=pl.ANY))
    moves = 1 + count
    scratch = [
        dma((moves, 3)),
        dma((moves, 3)),
        dma((moves,)),
        dma((2, 1)),
        dma((2, 1, 2)),
        dma((2, count)),
        dma((2, count, 2)),
        dma((2, 2, 3)),
        dma((2, seqs - 1)),
        dma((3,)),
        dma((2, 4)),
        dma((4,)),
    ]
    scratch += [pltpu.VMEM((2, n, feat), BF) for n in (4 * hd, ff, 4 * hd)]
    fetched = weights[:3] + weights[4:]
    scratch += [pltpu.VMEM(weight.shape, BF) for weight in fetched] + [dma((len(fetched),))]
    scratch += [pltpu.VMEM(out.shape, out.dtype) for out in outs[1:4]] + [dma((3,))]
    specs[1:4] = [pl.BlockSpec(memory_space=pl.ANY)] * 3
    for _ in range(4):
        scratch += freight_scratch(seqs)
    return pl.pallas_call(
        functools.partial(inputs_kernel, seqs),
        out_shape=outs,
        in_specs=[pl.BlockSpec(memory_space=pl.ANY)] * (5 + len(weights)),
        out_specs=tuple(specs),
        scratch_shapes=scratch,
        compiler_params=pltpu.CompilerParams(collective_id=0, has_side_effects=True, vmem_limit_bytes=60 << 20),
        name="gather_inputs",
    )(tokens, streams, norm, ids, table, *weights)


def outputs_kernel(seqs, count, dqkv, dquery, mix, first_weight, last_weight, x_full, d1_full, d1, d3, small, down, up, tok_out, str_out, small_out, down_out, up_out, first_out, part, first, core_buf, half_send, half_buf, own, land_x, land_y, rc, rh, rs, small_buf, ss, *refs):
    refs = list(refs)
    take = lambda amount: [refs.pop(0) for _ in range(amount)]
    place = spot()
    far = [up, dqkv, first_weight, x_full, mix, d1_full, last_weight, dquery, down, d1, d3]
    near, (sems,) = take(len(far)), take(1)
    lazy = [Lazy(source, target, sems.at[i]) for i, (source, target) in enumerate(zip(far, near))]
    up, dqkv, first_weight, x_full, mix, d1_full, last_weight, dquery, down, d1, d3 = lazy
    y, k, seq, half = place
    rows = part.shape[3]
    feat = part.shape[4] // 4
    bits = [1 << b for b in range((seqs - 1).bit_length())]
    flips = [device(y, k, seq + b - 2 * b * ((seq // b) % 2), half) for b in bits]
    others = [device(y, k, lax.rem(seq + d, seqs), half) for d in range(1, seqs)]
    partners = [device(y, 1 - k, seq, half), device(y, k, seq, 1 - half), device(1 - y, k, seq, half)]
    greet(partners + [device(1 - y, 1 - k, seq, half)] + others)
    partners += flips
    small_out[...] = small[...]

    def start_small(stage):
        return stage, remote(small_out, small_buf.at[stage], ss.at[0, stage], ss.at[1, stage], partners[stage])

    def end_small(started):
        stage, copy = started
        copy.wait()
        small_out[...] += small_buf[stage]

    heads, width = mix.shape[0], mix.shape[1]

    def products(unit):
        for a in range(2):
            for b in range(2):
                start = (2 * a + b) * rows
                if unit == 0:
                    weight = first_weight[:, : 3 * width].reshape(heads * 3 * width, -1)
                    part[unit, a, b] = project(dqkv, weight, start, rows)
                else:
                    weight = last_weight[:, 2 * width : 3 * width].reshape(heads * width, -1)
                    part[unit, a, b] = project(dquery, weight, 4 * (unit - 1) * rows + start, rows)
        reduce.start(unit, unit, 0, True)
        reduce.start(unit, unit, 0, False)

    reduce = Reduce(part, core_buf, half_send, half_buf, rc, rh, place, rows)
    units = range(count + 1)
    down = Collect(down, place, seqs, z_refs=[down_out] + take(5))
    up = Collect(up, place, seqs, y_refs=take(2), z_refs=[up_out] + take(5))
    first_ref = first
    first = Collect(first, place, seqs, y_refs=take(2), z_refs=[first_out] + take(5))
    started = start_small(2)
    for d in up.order:
        up.across(d)
    products(0)
    for d in first.order:
        first_ref[d, : 3 * width] = mm(dqkv[d], x_full[...]).astype(BF)
        first_ref[d, 3 * width :] = mm(mix[d], d1_full[...]).astype(BF)
        first.across(d)
    end_small(started)
    started = start_small(3)
    reduce.pass_on(0, 0, 0)
    products(1)
    for stage in range(4, len(partners)):
        end_small(started)
        started = start_small(stage)
    end_small(started)
    for d in down.order[:2]:
        down.along(d)
    started = start_small(0)
    for unit in units[2:]:
        products(unit)
    end_small(started)
    x_back = Return(own, land_x, rs, place, feat)
    y_back = Return(own, land_y, rs, place, feat)
    x_back.start(0, 0, (d1[0] + reduce.result(0, 0, 0)).astype(BF))
    started = start_small(1)
    for unit in units[1:]:
        reduce.pass_on(unit, unit, 0)
    end_small(started)
    for d in down.order[2:-1]:
        down.along(d)
    for d in up.order[:2]:
        up.along(d)
    for unit in units[1:]:
        y_back.start(unit, unit - 1, (d3[unit - 1] + reduce.result(unit, unit, 0)).astype(BF))
    down.close()
    for d in up.order[2:-1]:
        up.along(d)
    for d in first.order[:2]:
        first.along(d)
    up.close()
    for d in first.order[2:-1]:
        first.along(d)
    for unit in units:
        reduce.finish(unit)
    x_back.finish()
    tok_out[...] = land_x[:, 0].astype(F32)
    first.close()
    y_back.finish()
    str_out[...] = land_y[...].astype(F32)
    for collect in (down, up, first):
        collect.finish()


def scatter_outputs(seqs, collective_id, dqkv, dquery, mix, first_weight, last_weight, x_full, d1_full, d1, d3, small, down, up):
    count, own, depth = d3.shape
    feat, wide = depth // 4, depth // 2
    units = count + 1
    dma = pltpu.SemaphoreType.DMA
    shape = jax.ShapeDtypeStruct
    stages = 3 + (seqs - 1).bit_length()
    outs = (shape((2, 2, own, feat), F32), shape((2, count, 2, own, feat), F32), shape(small.shape, F32))
    outs += tuple(shape((2, group.shape[1], feat), F32) for group in (down, up, first_weight))
    scratch = [
        pltpu.VMEM((units, 2, 2, own, depth), BF),
        pltpu.VMEM(first_weight.shape, BF),
        pltpu.VMEM((units, 2, own, depth), BF),
        pltpu.VMEM((units, own, depth), BF),
        pltpu.VMEM((units, own, depth), BF),
        pltpu.VMEM((units, own, depth), BF),
        pltpu.VMEM((2, 1, 2, own, feat), BF),
        pltpu.VMEM((2, count, 2, own, feat), BF),
        dma((2, units, 2)),
        dma((2, units)),
        dma((2, units, 3)),
        pltpu.VMEM((stages,) + small.shape, F32),
        dma((2, stages)),
    ]
    far = (up, dqkv, first_weight, x_full, mix, d1_full, last_weight, dquery, down, d1, d3)
    scratch += [pltpu.VMEM(array.shape, array.dtype) for array in far] + [dma((len(far),))]
    scratch += along_scratch(seqs, down.shape[1], wide)
    for group in (up, first_weight):
        scratch += across_scratch(seqs, group.shape[1], wide) + along_scratch(seqs, group.shape[1], wide)
    args = (dqkv, dquery, mix, first_weight, last_weight, x_full, d1_full, d1, d3, small, down, up)
    return pl.pallas_call(
        functools.partial(outputs_kernel, seqs, count),
        out_shape=outs,
        in_specs=[pl.BlockSpec(memory_space=pltpu.VMEM if array is small else pl.ANY) for array in args],
        out_specs=tuple(pl.BlockSpec(memory_space=pltpu.VMEM) for _ in outs),
        scratch_shapes=scratch,
        compiler_params=pltpu.CompilerParams(collective_id=collective_id, has_side_effects=True, vmem_limit_bytes=60 << 20),
        name="scatter_outputs",
    )(*args)


def pick(array, index, axis):
    return lax.dynamic_index_in_dim(array, index, axis, keepdims=False)


def dot_f32(spec, left, right):
    return jnp.einsum(spec, left, right, preferred_element_type=F32)


def on_device(
    rows,
    cols,
    tokens,
    streams,
    cotangent,
    block_ids,
    bucket_ids,
    w_qkv,
    enc_table,
    w_out,
    attention_norm_gain,
    attn_bias,
    w_up,
    w_down,
    ffn_gain,
    ffn_bias,
    w_query,
    w_keyval,
    cross_table,
    w_cross_out,
    cross_gain,
    cross_bias,
):
    seqs = cols // 2
    row, col = lax.axis_index(ROW), lax.axis_index(COL)
    y, k, seq, half = row // 2, row % 2, col // 2, col % 2
    low_y = y == 0
    stream_count = streams.shape[1]
    tok = tokens.shape[1]
    own = tok // 2
    feat = tokens.shape[2]
    length = block_ids.shape[2]
    head_dim = w_qkv.shape[2] // 2
    ff = w_up.shape[1] // 2
    table_heads, bucket_count = enc_table.shape

    def columns_back(array, parts):
        return array.reshape(2, parts, -1, feat).transpose(3, 1, 0, 2).reshape(feat, parts, -1)

    hd3, hd2 = 3 * head_dim, 2 * head_dim
    norm_params = jnp.stack([attention_norm_gain, attn_bias, ffn_gain, ffn_bias, cross_gain, cross_bias] + [cross_bias] * 2)
    table_pack = jnp.zeros((8, 128), F32).at[0].set(jnp.stack([enc_table, cross_table]).reshape(-1))
    micro_count = tokens.shape[0]
    x_own, x_full, y_own, y_full, norm_params, all_ids, all_tables, first, up, down, last = gather_inputs(
        seqs,
        tokens.reshape(micro_count, 1, 2, own, feat),
        streams.reshape(micro_count, stream_count, 2, own, feat),
        norm_params,
        block_ids.reshape(8, -1),
        table_pack,
        w_qkv.transpose(1, 0, 2),
        w_out,
        w_up,
        w_down.reshape(2, ff, feat),
        w_keyval.transpose(1, 0, 2),
        w_query,
        w_cross_out,
    )
    x_full, y_full = x_full.reshape(length, D), y_full.reshape(stream_count * length, D)
    segment = pick(pick(all_ids.reshape(rows, micro_count, length), seq, 0), y, 0)
    segq = segment[None]
    segk = segment[:, None]
    own_tables = pick(all_tables[:, 0].reshape(seqs, 2, table_heads, bucket_count), k, 2)
    slot_col = 2 * ((seq - jnp.arange(seqs)) % seqs) + half
    reversed_ids = jnp.concatenate([jnp.full((1,), -1, jnp.int32), bucket_ids[::-1]])
    onehot = bucket_onehot(reversed_ids, bucket_count)
    offsets = jnp.einsum("htb,bo->tho", own_tables, onehot, precision=highest)[:, :, None, :]


    hidden_full, hidden, normed1, inv1, qkv, mix, lse, enc_bias, cross_bias_full, down, last = exchange(
        FORWARD,
        1,
        seqs,
        x_own,
        norm_params[0:2],
        rides=((ACROSS, down), (ALONG, last)),
        attend=(first, x_full, offsets, segq, segk),
    )
    up, down = up.reshape(-1, D), down.reshape(-1, D)
    hidden_full = hidden_full.reshape(length, D)
    enc_full, _, normed2, inv2, act, slope, last = exchange(
        FORWARD,
        2,
        seqs,
        hidden,
        norm_params[2:4],
        rides=((ACROSS, last),),
        feed=(up, down, hidden_full),
    )
    m_kv, m_q, m_co = last[:, :hd2], last[:, hd2:hd3], last[:, hd3:].reshape(-1, D)
    enc_full = enc_full.reshape(length, D)
    kv = dot_f32("snr,tr->snt", m_kv, enc_full).astype(BF)
    query = dot_f32("snr,tr->snt", m_q, y_full).astype(BF)
    cmix, d3_full, output, d3, sums3, dquery, dkv, doff_cross = cross_attention(
        3,
        query,
        kv,
        m_co,
        cross_bias_full,
        y_own,
        norm_params[4:6],
        cotangent.reshape(micro_count, stream_count, 2, own, feat),
    )
    d3_full = d3_full.reshape(stream_count * length, D)

    d2_full, d2, sums2, g_last = exchange(
        BACKWARD,
        4,
        seqs,
        norm_params[2:4][None],
        norm_params[2:4],
        normed=normed2,
        inv=inv2,
        cross=(dkv, dquery, last, cmix, enc_full, y_full, d3_full),
    )
    d2_full = d2_full.reshape(length, D)
    d1_full, d1, sums1, dqkv, doff_enc, g_up, g_down, g_last = exchange(
        BACKWARD,
        5,
        seqs,
        d2,
        norm_params[0:2],
        normed=normed1,
        inv=inv1,
        rides=((SUM_ALONG, g_last),),
        attend=(first, qkv, enc_bias, lse),
        feed=(up, down, d2_full, act, slope, hidden_full),
    )
    d1_full = d1_full.reshape(length, D)

    norm_grads = jnp.concatenate([sums1[:2], sums2[:2], sums3[:2]])
    norm_grads = jnp.where(low_y, norm_grads, jnp.roll(norm_grads, D // 2, axis=1))
    table_grads = jnp.einsum(
        "tho,bo->thb", jnp.stack([doff_enc[:, 0], doff_cross[:, 0]]), onehot, precision=highest
    )
    heads = 2 * slot_col + k
    spread = (heads[:, None] == jnp.arange(table_heads * cols)[None, :]).astype(F32)
    table_grads = jnp.einsum("thb,hg->tgb", table_grads, spread, precision=highest)
    small = jnp.concatenate([norm_grads.reshape(-1, 128), table_grads.reshape(-1, 128)])
    grad_tokens, grad_streams, small, g_down, g_up, g_first = scatter_outputs(
        seqs, 6, dqkv, dquery, mix, first, last, x_full, d1_full, d1, d3, small, g_down, g_up
    )
    output, grad_streams = output.reshape(streams.shape), grad_streams.reshape(streams.shape)
    grad_tokens = grad_tokens.reshape(tokens.shape)
    count = norm_grads.size // 128
    norm_sums = lax.dynamic_slice_in_dim(small[:count].reshape(6, D), row * feat, feat, axis=1)
    table_sums = small[count:].reshape(2, table_heads * cols, bucket_count)
    table_sums = lax.dynamic_slice_in_dim(table_sums, col * table_heads, table_heads, axis=1)
    return (
        output,
        grad_tokens,
        grad_streams,
        columns_back(g_first[:, :hd3], 3),
        table_sums[0],
        g_first[:, hd3:].reshape(w_out.shape),
        norm_sums[0],
        norm_sums[1],
        columns_back(g_up, 1).reshape(w_up.shape),
        g_down.reshape(w_down.shape),
        norm_sums[2],
        norm_sums[3],
        columns_back(g_last[:, hd2:hd3], 1).reshape(w_query.shape),
        columns_back(g_last[:, :hd2], 2),
        table_sums[1],
        g_last[:, hd3:].reshape(w_cross_out.shape),
        norm_sums[4],
        norm_sums[5],
    )


def solution(mesh):
    whole_row, half_col = mesh.shape[ROW], mesh.shape[COL]
    wide, table, norm = P(ROW, None, COL), P(COL, None), P(ROW)
    up, down = P(ROW, COL), P(COL, ROW)
    weights = (wide, table, down, norm, norm, up, down, norm, norm, up, wide, table, down, norm, norm)

    def run(tokens, *rest):
        micro_count = tokens.shape[0]
        if whole_row == 4 and micro_count == 2 and half_col % 2 == 0:
            device_fn = functools.partial(on_device, whole_row, half_col)
        else:
            device_fn = on_device_general
        return jax.shard_map(
            device_fn,
            mesh=mesh,
            in_specs=(P(None, COL, ROW), P(None, None, COL, ROW), P(None, None, COL, ROW), P(None, ROW, None), P()) + weights,
            out_specs=(P(None, None, COL, ROW), P(None, COL, ROW), P(None, None, COL, ROW)) + weights,
            check_vma=False,
        )(tokens, *rest)

    return run
```

```python
import functools
import math
import types
import jax
import jax.numpy as jnp
from jax import lax
from jax.experimental import pallas as pl
from jax.experimental.pallas import tpu as pltpu
from jax.sharding import PartitionSpec as P

D = 1024
F32 = jnp.float32
BF = jnp.bfloat16
ROW, COL = "row", "col"


epsilon = 1e-05
neg_fill = -1e30
highest = lax.Precision.HIGHEST


def gather_cols(local_rows):
    return lax.all_gather(local_rows, COL, axis=1, tiled=True)


def gather_rows(local_rows):
    return lax.all_gather(local_rows, ROW, axis=1, tiled=True)


def product(matmul_operand, weight_matrix):
    return jnp.einsum(
        "ray,yw->raw", matmul_operand, weight_matrix, preferred_element_type=jnp.float32
    )


def rows_product(operand_full, matrix):
    return lax.psum_scatter(product(operand_full, matrix), ROW, scatter_dimension=1, tiled=True)


def cols_product(operand_full, matrix):
    return lax.psum_scatter(product(operand_full, matrix), COL, scatter_dimension=1, tiled=True)


def weight_grad(matmul_operand, upstream_gradient):
    return jnp.einsum(
        "bpt,bpr->tr", matmul_operand, upstream_gradient, preferred_element_type=jnp.float32
    )


def gelu_exact(argument):
    return jax.nn.gelu(argument, approximate=False)


def norm_forward(residual, gain_vec, bias_vec):
    local_sum = jnp.sum(residual, axis=-1)
    average = lax.psum(local_sum, ROW) / D
    centered = residual - average[..., None]
    spread = lax.psum(jnp.sum(centered * centered, axis=-1), ROW) / D
    inv_std = lax.rsqrt(spread + epsilon)
    normed = centered * inv_std[..., None]
    return (normed * gain_vec + bias_vec, normed, inv_std)


def norm_back(out_grad, normed, inv_std, gain_vec):
    scaled_grad = out_grad * gain_vec
    first_moment, second_moment = lax.psum(
        (jnp.sum(scaled_grad, axis=-1), jnp.sum(scaled_grad * normed, axis=-1)), ROW
    )
    resid_grad = inv_std[..., None] * (
        scaled_grad - first_moment[..., None] / D - normed * (second_moment[..., None] / D)
    )
    return (resid_grad, jnp.sum(out_grad * normed, axis=(0, 1)), jnp.sum(out_grad, axis=(0, 1)))


def bucket_onehot(bucket_ids, bucket_count):
    return (bucket_ids[None, :] == jnp.arange(bucket_count, dtype=jnp.int32)[:, None]).astype(
        jnp.float32
    )


def block_logits(query_blk, key_rows, offsets, segment, first_row):
    row_count = query_blk.shape[2]
    length = key_rows.shape[1]
    score_scale = query_blk.shape[-1] ** (-0.5)
    raw_scores = jnp.einsum(
        "snqhd,nkhd->snhqk", query_blk, key_rows, preferred_element_type=jnp.float32
    )
    places = jnp.arange(length, dtype=jnp.int32)
    query_pos = first_row + jnp.arange(row_count, dtype=jnp.int32)
    offset_index = places[None, :] - query_pos[:, None] + (length - 1)
    pos_bias = jnp.take(offsets, offset_index, axis=1)
    visible = segment[:, first_row : first_row + row_count, None] >= segment[:, None, :]
    return jnp.where(
        visible[None, :, None], raw_scores * score_scale + pos_bias[None, None], neg_fill
    )


def attend(queries, key_rows, value_rows, segment, offsets):
    score_logits = block_logits(queries, key_rows, offsets, segment, 0)
    row_max = jnp.max(score_logits, axis=-1, keepdims=True)
    log_total = row_max + jnp.log(jnp.sum(jnp.exp(score_logits - row_max), axis=-1, keepdims=True))
    weights = jnp.exp(score_logits - log_total).astype(jnp.bfloat16)
    mixed_parts = jnp.einsum(
        "snhqk,nkhd->snqhd", weights, value_rows, preferred_element_type=jnp.float32
    )
    lse_parts = log_total[..., 0]
    return (mixed_parts, lse_parts)


def diagonal_sums(summand):
    head_count, row_count, length = summand.shape
    flipped = summand[:, ::-1, :]
    padded = jnp.concatenate(
        [flipped, jnp.zeros((head_count, row_count, row_count), summand.dtype)], axis=2
    )
    flattened = padded.reshape(head_count, row_count * (length + row_count))[
        :, : row_count * (length + row_count - 1)
    ]
    return jnp.sum(flattened.reshape(head_count, row_count, length + row_count - 1), axis=1)


def attend_back(queries, key_rows, value_rows, segment, offsets, onehot, log_totals, mix_grad):
    length = key_rows.shape[1]
    block_rows = min(512, length)
    score_scale = queries.shape[-1] ** (-0.5)
    offset_grad = jnp.zeros(offsets.shape, jnp.float32)
    score_logits = block_logits(queries, key_rows, offsets, segment, 0)
    probability = jnp.exp(score_logits - log_totals[:, :, :, 0:block_rows, None])
    prob_grad = jnp.einsum(
        "snqhd,nkhd->snhqk", mix_grad, value_rows, preferred_element_type=jnp.float32
    )
    logit_grad = probability * (
        prob_grad - jnp.sum(probability * prob_grad, axis=-1, keepdims=True)
    )
    scaled = (logit_grad * score_scale).astype(jnp.bfloat16)
    query_parts = jnp.einsum(
        "snhqk,nkhd->snqhd", scaled, key_rows, preferred_element_type=jnp.float32
    )
    key_grad = jnp.einsum("snhqk,snqhd->nkhd", scaled, queries, preferred_element_type=jnp.float32)
    value_grad = jnp.einsum(
        "snhqk,snqhd->nkhd",
        probability.astype(jnp.bfloat16),
        mix_grad,
        preferred_element_type=jnp.float32,
    )
    low_end = length - block_rows
    offset_grad = offset_grad.at[:, low_end : low_end + length + block_rows - 1].add(
        diagonal_sums(jnp.sum(logit_grad, axis=(0, 1)))
    )
    table_grad = jnp.dot(offset_grad, onehot.T, precision=highest)
    return (query_parts, key_grad, value_grad, table_grad)


def on_device_general(
    tokens,
    streams,
    cotangent,
    block_ids,
    bucket_ids,
    w_qkv,
    enc_table,
    w_out,
    attention_norm_gain,
    attn_bias,
    w_up,
    w_down,
    ffn_gain,
    ffn_bias,
    w_query,
    w_keyval,
    cross_table,
    w_cross_out,
    cross_gain,
    cross_bias,
):
    micro_count = tokens.shape[0]
    stream_count = streams.shape[1]
    seq_rows = block_ids.shape[1]
    length = block_ids.shape[2]
    head_count = enc_table.shape[0]
    bucket_count = enc_table.shape[1]
    row_width = w_qkv.shape[0]
    col_width = w_qkv.shape[2]
    head_dim = col_width // head_count
    row_tokens = seq_rows * length
    qkv_matrix = w_qkv.reshape(row_width, 3 * col_width)
    keyval_matrix = w_keyval.reshape(row_width, 2 * col_width)
    onehot = bucket_onehot(bucket_ids, bucket_count)
    enc_offsets = jnp.dot(enc_table, onehot, precision=highest)
    cross_offsets = jnp.dot(cross_table, onehot, precision=highest)
    qkv_acc = jnp.zeros((row_width, 3 * col_width), jnp.float32)
    out_acc = jnp.zeros(w_out.shape, jnp.float32)
    up_acc = jnp.zeros(w_up.shape, jnp.float32)
    down_acc = jnp.zeros(w_down.shape, jnp.float32)
    query_acc = jnp.zeros(w_query.shape, jnp.float32)
    keyval_acc = jnp.zeros((row_width, 2 * col_width), jnp.float32)
    cross_out_acc = jnp.zeros(w_cross_out.shape, jnp.float32)
    enc_table_acc = jnp.zeros(enc_table.shape, jnp.float32)
    cross_table_acc = jnp.zeros(cross_table.shape, jnp.float32)
    norm_accs = [jnp.zeros((row_width,), jnp.float32) for place_holder in range(6)]
    outputs = []
    token_grads = []
    stream_grads = []
    for micro in range(micro_count):
        segment = block_ids[micro]
        x_in = tokens[micro][None]
        y_in = streams[micro]
        x_full = gather_cols(x_in)
        qkv = (
            rows_product(x_full, qkv_matrix)
            .astype(jnp.bfloat16)
            .reshape(seq_rows, length, 3, head_count, head_dim)
        )
        enc_query = qkv[:, :, 0][None]
        enc_key = qkv[:, :, 1]
        encoder_value_rows = qkv[:, :, 2]
        enc_mixed, enc_lse = attend(enc_query, enc_key, encoder_value_rows, segment, enc_offsets)
        enc_mix = enc_mixed.reshape(1, row_tokens, col_width).astype(jnp.bfloat16)
        mix_full = gather_rows(enc_mix)
        attn_branch = cols_product(mix_full, w_out)
        hidden, normed_one, inv_one = norm_forward(
            x_in.astype(jnp.float32) + attn_branch, attention_norm_gain, attn_bias
        )
        hidden_low = hidden.astype(jnp.bfloat16)
        hidden_full = gather_cols(hidden_low)
        pre_act = rows_product(hidden_full, w_up)
        act_value, gelu_pull = jax.vjp(gelu_exact, pre_act)
        act_low = act_value.astype(jnp.bfloat16)
        act_full = gather_rows(act_low)
        ffn_branch = cols_product(act_full, w_down)
        encoded, normed_two, inv_two = norm_forward(hidden + ffn_branch, ffn_gain, ffn_bias)
        encoded_low = encoded.astype(jnp.bfloat16)
        enc_full = gather_cols(encoded_low)
        keyval = (
            rows_product(enc_full, keyval_matrix)
            .astype(jnp.bfloat16)
            .reshape(seq_rows, length, 2, head_count, head_dim)
        )
        cross_key = keyval[:, :, 0]
        cross_value = keyval[:, :, 1]
        stream_full = gather_cols(y_in)
        cross_query = (
            rows_product(stream_full, w_query)
            .astype(jnp.bfloat16)
            .reshape(stream_count, seq_rows, length, head_count, head_dim)
        )
        cross_mixed, cross_lse = attend(cross_query, cross_key, cross_value, segment, cross_offsets)
        cross_mix = cross_mixed.reshape(stream_count, row_tokens, col_width).astype(jnp.bfloat16)
        cross_full = gather_rows(cross_mix)
        cross_branch = cols_product(cross_full, w_cross_out)
        result, normed_three, inv_three = norm_forward(
            y_in.astype(jnp.float32) + cross_branch, cross_gain, cross_bias
        )
        outputs.append(result)
        grad_three, gain_part, bias_part = norm_back(
            cotangent[micro].astype(jnp.float32), normed_three, inv_three, cross_gain
        )
        norm_accs[4] = norm_accs[4] + gain_part
        norm_accs[5] = norm_accs[5] + bias_part
        branch_full = gather_cols(grad_three.astype(jnp.bfloat16))
        cross_out_acc = cross_out_acc + weight_grad(cross_full, branch_full)
        cross_mix_grad = (
            rows_product(branch_full, w_cross_out.T)
            .astype(jnp.bfloat16)
            .reshape(stream_count, seq_rows, length, head_count, head_dim)
        )
        query_grad, key_grad, value_grad, table_grad = attend_back(
            cross_query,
            cross_key,
            cross_value,
            segment,
            cross_offsets,
            onehot,
            cross_lse,
            cross_mix_grad,
        )
        cross_table_acc = cross_table_acc + table_grad
        query_low = query_grad.reshape(stream_count, row_tokens, col_width).astype(jnp.bfloat16)
        keyval_low = (
            jnp.stack(
                [
                    key_grad.reshape(row_tokens, col_width),
                    value_grad.reshape(row_tokens, col_width),
                ],
                axis=1,
            )
            .reshape(1, row_tokens, 2 * col_width)
            .astype(jnp.bfloat16)
        )
        query_full = gather_rows(query_low)
        query_acc = query_acc + weight_grad(stream_full, query_full)
        stream_grads.append(grad_three + cols_product(query_full, w_query.T))
        keyval_full = gather_rows(keyval_low)
        keyval_acc = keyval_acc + weight_grad(enc_full, keyval_full)
        encoded_grad = cols_product(keyval_full, keyval_matrix.T)
        grad_two, gain_part, bias_part = norm_back(encoded_grad, normed_two, inv_two, ffn_gain)
        norm_accs[2] = norm_accs[2] + gain_part
        norm_accs[3] = norm_accs[3] + bias_part
        feedforward_full_output = gather_cols(grad_two.astype(jnp.bfloat16))
        down_acc = down_acc + weight_grad(act_full, feedforward_full_output)
        act_grad = rows_product(feedforward_full_output, w_down.T)
        pre_low = gelu_pull(act_grad)[0].astype(jnp.bfloat16)
        pre_full = gather_rows(pre_low)
        up_acc = up_acc + weight_grad(hidden_full, pre_full)
        hidden_grad = grad_two + cols_product(pre_full, w_up.T)
        grad_one, gain_part, bias_part = norm_back(
            hidden_grad, normed_one, inv_one, attention_norm_gain
        )
        norm_accs[0] = norm_accs[0] + gain_part
        norm_accs[1] = norm_accs[1] + bias_part
        attn_full = gather_cols(grad_one.astype(jnp.bfloat16))
        out_acc = out_acc + weight_grad(mix_full, attn_full)
        enc_mix_grad = (
            rows_product(attn_full, w_out.T)
            .astype(jnp.bfloat16)
            .reshape(1, seq_rows, length, head_count, head_dim)
        )
        enc_qgrad, enc_kgrad, enc_vgrad, table_grad = attend_back(
            enc_query,
            enc_key,
            encoder_value_rows,
            segment,
            enc_offsets,
            onehot,
            enc_lse,
            enc_mix_grad,
        )
        enc_table_acc = enc_table_acc + table_grad
        qkv_low = (
            jnp.stack(
                [
                    enc_qgrad.reshape(row_tokens, col_width),
                    enc_kgrad.reshape(row_tokens, col_width),
                    enc_vgrad.reshape(row_tokens, col_width),
                ],
                axis=1,
            )
            .reshape(1, row_tokens, 3 * col_width)
            .astype(jnp.bfloat16)
        )
        qkv_full = gather_rows(qkv_low)
        qkv_acc = qkv_acc + weight_grad(x_full, qkv_full)
        token_grads.append((grad_one + cols_product(qkv_full, qkv_matrix.T))[0])
    norm_stack = jnp.stack(norm_accs)
    table_stack = jnp.stack([enc_table_acc, cross_table_acc])
    norm_sums = lax.psum(norm_stack, COL)
    table_sums = lax.psum(table_stack, ROW)
    return (
        jnp.stack(outputs),
        jnp.stack(token_grads),
        jnp.stack(stream_grads),
        qkv_acc.reshape(row_width, 3, col_width),
        table_sums[0],
        out_acc,
        norm_sums[0],
        norm_sums[1],
        up_acc,
        down_acc,
        norm_sums[2],
        norm_sums[3],
        query_acc,
        keyval_acc.reshape(row_width, 2, col_width),
        table_sums[1],
        cross_out_acc,
        norm_sums[4],
        norm_sums[5],
    )


def mm(a,b):
    return jnp.dot(a,b,preferred_element_type=F32)
def mm_nt(a,b):
    return lax.dot_general(a,b,(((1,),(1,)),((),())),preferred_element_type=F32)

def mm_tn(a, b):
    return lax.dot_general(a, b, (((0,), (0,)), ((), ())), preferred_element_type=F32)


def masked_bias(off_ref, index, segq, segk):
    length = segk.shape[0]
    row = jnp.broadcast_to(off_ref[index], (length, 2 * length))
    rolled = pltpu.roll(row, 0, 1, stride=1, stride_axis=0)
    return jnp.where(segk <= segq, rolled[:, length:], neg_fill)


def head_forward(keys, values, query, bias):
    logits = mm(keys, query) + bias
    top = jnp.max(logits, axis=0, keepdims=True)
    weight = jnp.exp(logits - top)
    total = jnp.sum(weight, axis=0, keepdims=True)
    return (mm(values, weight.astype(BF)) * (1.0 / total)).astype(BF), top + jnp.log(total)


def head_backward(keys, keys_t, values_t, query, grad, lse, bias):
    prob = jnp.exp(mm(keys, query) + (bias - lse))
    dprob = mm(values_t, grad)
    dlogits = prob * (dprob - jnp.sum(prob * dprob, axis=0, keepdims=True))
    low = dlogits.astype(BF)
    return dlogits, mm(keys_t, low).astype(BF), mm_nt(query, low), mm_nt(grad, prob.astype(BF))


def project(mix_ref, weight, start, rows):
    heads, hd = mix_ref.shape[0], mix_ref.shape[1]
    mixed = mix_ref[:, :, start : start + rows].reshape(heads * hd, rows)
    return mm_tn(mixed, weight).astype(BF)


def project_back(weight, rows_value, dmix_ref, start):
    heads, hd = dmix_ref.shape[0], dmix_ref.shape[1]
    rows = rows_value.shape[0]
    dmix_ref[:, :, start : start + rows] = mm_nt(weight, rows_value).astype(BF).reshape(heads, hd, rows)


def scaled(value, scale):
    return (value.astype(F32) * scale).astype(BF)


def offset_sums(g_ref, doff_ref, g_index, out_index, length):
    sub = lax.broadcasted_iota(jnp.int32, (8, 2 * length), 0)
    acc = jnp.zeros((8, 2 * length), F32)
    for i in range(length // 8):
        piece = g_ref[g_index + (pl.ds(8 * i, 8),)]
        padded = jnp.concatenate([jnp.zeros((8, length), F32), piece], axis=1)
        acc = acc + (pltpu.roll(padded, 2 * length - 8 * i, 1) if i else padded)
    for b in (1, 2, 4):
        acc = jnp.where((sub // b) % 2 == 1, pltpu.roll(acc, 2 * length - b, 1), acc)
    doff_ref[out_index] = jnp.sum(acc, axis=0, keepdims=True)


MESH = pl.DeviceIdType.MESH
FORWARD, BACKWARD = range(2)
ACROSS, THROUGH, ALONG, SUM_ALONG = range(4)


def spot():
    row, col = lax.axis_index(ROW), lax.axis_index(COL)
    return row // 2, row % 2, col // 2, col % 2


def device(y, k, seq, half):
    return (2 * y + k, 2 * seq + half)


def greet(devices):
    barrier = pltpu.get_barrier_semaphore()
    for target in devices:
        pl.semaphore_signal(barrier, inc=1, device_id=target, device_id_type=MESH)
    pl.semaphore_wait(barrier, len(devices))


def remote(source, target, send_sem, recv_sem, device_id):
    copy = pltpu.make_async_remote_copy(
        src_ref=source, dst_ref=target, send_sem=send_sem, recv_sem=recv_sem, device_id=device_id, device_id_type=MESH
    )
    copy.start()
    return copy


def lanes(start, size):
    return pl.ds(pl.multiple_of(start, size), size)


def rows_of(place):
    y, k, seq, half = place
    return [(dy, dk, (1 - y if dy else y), (1 - k if dk else k)) for dy, dk in ((0, 1), (1, 0), (1, 1))]


class Spread:
    def __init__(self, full_ref, half_sems, core_sems, place, rows):
        self.full, self.place, self.rows = full_ref, place, rows
        self.half_sems, self.core_sems = half_sems, core_sems
        self.first, self.second = {}, {}

    def block(self, n, piece, half, k):
        return self.full.at[n, half, k, pl.ds(piece * self.rows, self.rows)]

    def start(self, unit, n, piece):
        y, k, seq, half = self.place
        mine = self.block(n, piece, half, k)
        hs, cs = self.half_sems, self.core_sems
        self.first[unit] = (
            remote(mine, mine, hs.at[0, unit], hs.at[1, unit], device(y, k, seq, 1 - half)),
            remote(mine, mine, cs.at[0, unit, 0], cs.at[1, unit, 0], device(y, 1 - k, seq, half)),
        )

    def forward(self, unit, n, piece):
        y, k, seq, half = self.place
        self.first[unit][0].wait_recv()
        theirs = self.block(n, piece, 1 - half, k)
        cs = self.core_sems
        self.second[unit] = remote(theirs, theirs, cs.at[0, unit, 1], cs.at[1, unit, 1], device(y, 1 - k, seq, half))

    def ready(self, unit):
        self.first[unit][1].wait_recv()
        self.second[unit].wait_recv()

    def sent(self, unit):
        for copy in self.first[unit] + (self.second[unit],):
            copy.wait_send()

    def finish(self, unit):
        self.ready(unit)
        self.sent(unit)


class Reduce:
    def __init__(self, partial_ref, core_buf, half_send, half_buf, core_sems, half_sems, place, rows):
        self.partial, self.core_buf, self.half_send, self.half_buf = partial_ref, core_buf, half_send, half_buf
        self.core_sems, self.half_sems, self.place, self.rows = core_sems, half_sems, place, rows
        self.first, self.second = {}, {}

    def part(self, n, piece, half, k):
        return (n, half, k, pl.ds(piece * self.rows, self.rows))

    def start(self, unit, n, piece, away):
        y, k, seq, half = self.place
        side = 1 - half if away else half
        cs = self.core_sems
        lane = 0 if away else 1
        self.first[unit, lane] = remote(
            self.partial.at[self.part(n, piece, side, 1 - k)],
            self.core_buf.at[unit, lane],
            cs.at[0, unit, lane],
            cs.at[1, unit, lane],
            device(y, 1 - k, seq, half),
        )

    def pass_on(self, unit, n, piece):
        y, k, seq, half = self.place
        self.first[unit, 0].wait_recv()
        away = self.partial[self.part(n, piece, 1 - half, k)].astype(F32) + self.core_buf[unit, 0].astype(F32)
        self.half_send[unit] = away.astype(BF)
        hs = self.half_sems
        self.second[unit] = remote(
            self.half_send.at[unit], self.half_buf.at[unit], hs.at[0, unit], hs.at[1, unit], device(y, k, seq, 1 - half)
        )

    def result(self, unit, n, piece):
        y, k, seq, half = self.place
        self.first[unit, 1].wait_recv()
        mine = self.partial[self.part(n, piece, half, k)].astype(F32) + self.core_buf[unit, 1].astype(F32)
        self.second[unit].wait_recv()
        return mine + self.half_buf[unit].astype(F32)

    def finish(self, unit):
        self.first[unit, 0].wait_send()
        self.first[unit, 1].wait_send()
        self.second[unit].wait_send()


class Return:
    def __init__(self, own_ref, landing, sems, place, feat):
        self.own, self.landing, self.sems, self.place, self.feat = own_ref, landing, sems, place, feat
        self.copies = []

    def start(self, unit, n, value):
        y, k, seq, half = self.place
        feat = self.feat
        self.own[unit] = value
        self.landing[y, n, k] = jnp.where(k == 0, value[:, :feat], value[:, feat : 2 * feat])
        for i, (dy, dk, ty, tk) in enumerate(rows_of(self.place)):
            self.copies.append(
                remote(
                    self.own.at[unit, :, lanes(tk * feat + 2 * dy * feat, feat)],
                    self.landing.at[y, n, k],
                    self.sems.at[0, unit, i],
                    self.sems.at[1, unit, i],
                    device(ty, tk, seq, half),
                )
            )

    def finish(self):
        for copy in self.copies:
            copy.wait()


class Freight:
    def __init__(self, full_ref, z_sems, y_sems, place, seqs):
        self.full, self.place, self.seqs = full_ref, place, seqs
        self.z_sems, self.y_sems = z_sems, y_sems
        self.wide = full_ref.shape[2] // 2
        self.z, self.y = {}, {}
        self.turn = seqs // 2

    def along(self, d):
        y, k, seq, half = self.place
        up = d <= self.turn
        source = d - 1 if up else (d + 1) % self.seqs
        if source:
            self.z[source].wait_recv()
        target = lax.rem(seq + (1 if up else self.seqs - 1), self.seqs)
        self.z[d] = remote(
            self.full.at[source, :, : self.wide],
            self.full.at[d, :, : self.wide],
            self.z_sems.at[0, d - 1],
            self.z_sems.at[1, d - 1],
            device(y, k, target, half),
        )

    def first(self):
        return [d for d in (1, self.seqs - 1) if d <= self.turn or d > self.turn][: min(2, self.seqs - 1)]

    def later(self):
        return list(range(2, self.turn + 1)) + list(range(self.seqs - 2, self.turn, -1))

    def last(self):
        return [d for d in range(self.seqs - 1, 0, -1) if d == self.turn or d == self.turn + 1]

    def across(self, d):
        y, k, seq, half = self.place
        self.y[d] = remote(
            self.full.at[d, :, : self.wide],
            self.full.at[d, :, self.wide :],
            self.y_sems.at[0, d],
            self.y_sems.at[1, d],
            device(1 - y, k, seq, half),
        )

    def pass_along(self, cross):
        for d in self.later():
            self.along(d)
            if cross:
                self.across(d - 1 if d <= self.turn else d + 1)

    def arrive(self, cross):
        for d in self.last():
            self.z[d].wait_recv()
            if cross:
                self.across(d)

    def finish(self):
        for copy in self.z.values():
            copy.wait_send()
        for copy in self.y.values():
            copy.wait()


class Collect:
    def __init__(self, source, place, seqs, y_refs=None, z_refs=None):
        self.source, self.place, self.seqs = source, place, seqs
        self.y_refs, self.z_refs = y_refs, z_refs
        self.wide = source.shape[2] // 2 if y_refs else source.shape[2]
        self.turn = seqs // 2
        self.order = list(range(self.turn, seqs)) + list(range(self.turn - 1, -1, -1))
        self.y, self.z, self.core = {}, {}, None

    def across(self, d):
        y, k, seq, half = self.place
        buf, sems = self.y_refs
        self.y[d] = remote(
            self.source.at[d, :, self.wide :], buf.at[d], sems.at[0, d], sems.at[1, d], device(1 - y, k, seq, half)
        )

    def total(self, d):
        if not self.y_refs:
            return self.source[d].astype(F32)
        self.y[d].wait_recv()
        return self.source[d, :, : self.wide].astype(F32) + self.y_refs[0][d].astype(F32)

    def store(self, out):
        for d in self.order:
            out[d] = self.total(d).astype(BF)

    def along(self, d):
        y, k, seq, half = self.place
        out, z_send, z_buf, c_send, z_sems, c_sems = self.z_refs
        left = d <= self.turn
        before = d + 1 if left else d - 1
        value = self.total(d)
        if before in self.z and before not in (self.turn + 1 if left else self.turn,):
            self.z[before].wait_recv()
            value = value + z_buf[before - 1].astype(F32)
        z_send[d - 1] = value.astype(BF)
        target = lax.rem(seq + (self.seqs - 1 if left else 1), self.seqs)
        self.z[d] = remote(
            z_send.at[d - 1], z_buf.at[d - 1], z_sems.at[0, d - 1], z_sems.at[1, d - 1], device(y, k, target, half)
        )

    def close(self):
        y, k, seq, half = self.place
        out, z_send, z_buf, c_send, z_sems, c_sems = self.z_refs
        total = self.total(0)
        for d in sorted({1, self.seqs - 1}):
            self.z[d].wait_recv()
            total = total + z_buf[d - 1].astype(F32)
        low, high = total[:, : self.wide // 2], total[:, self.wide // 2 :]
        out[k] = jnp.where(k == 0, low, high)
        c_send[...] = jnp.where(k == 0, high, low)
        self.core = remote(c_send, out.at[k], c_sems.at[0], c_sems.at[1], device(y, 1 - k, seq, half))

    def finish(self):
        for copy in self.y.values():
            copy.wait_send()
        for copy in self.z.values():
            copy.wait_send()
        if self.core is not None:
            self.core.wait()


def freight_scratch(seqs):
    dma = pltpu.SemaphoreType.DMA
    return [dma((2, seqs - 1)), dma((2, seqs))]


def across_scratch(seqs, n, wide):
    return [pltpu.VMEM((seqs, n, wide), BF), pltpu.SemaphoreType.DMA((2, seqs))]


def along_scratch(seqs, n, wide):
    dma = pltpu.SemaphoreType.DMA
    return [
        pltpu.VMEM((seqs - 1, n, wide), BF),
        pltpu.VMEM((seqs - 1, n, wide), BF),
        pltpu.VMEM((n, wide // 2), F32),
        dma((2, seqs - 1)),
        dma((2,)),
    ]


def along_devices(place, seqs):
    y, k, seq, half = place
    return [device(y, k, lax.rem(seq + d, seqs), half) for d in sorted({1, seqs - 1})]


def shuffle(source, target, n, index, place, sends, receives, local_sems):
    y, k, seq, half = place
    feat = source.shape[-1]
    copies = [pltpu.make_async_copy(source.at[y, n, k], target.at[n, :, lanes(k * feat, feat)], local_sems.at[index])]
    copies[0].start()
    for i, (dy, dk, ty, tk) in enumerate(rows_of(place)):
        copies.append(
            remote(
                source.at[ty, n, tk],
                target.at[n, :, lanes(k * feat + 2 * dy * feat, feat)],
                sends.at[index, i],
                receives.at[index, i],
                device(ty, tk, seq, half),
            )
        )
    return copies


def normalize(residual):
    centered = residual - jnp.mean(residual, axis=-1, keepdims=True)
    inv_std = lax.rsqrt(jnp.mean(centered * centered, axis=-1, keepdims=True) + epsilon)
    return centered * inv_std, inv_std


def normalize_back(out_grad, normed, inv_std, gain):
    scaled = out_grad * gain
    first = jnp.mean(scaled, axis=-1, keepdims=True)
    second = jnp.mean(scaled * normed, axis=-1, keepdims=True)
    return inv_std * (scaled - first - normed * second)


def column_sum(value):
    return jnp.sum(value, axis=0, keepdims=True)


def start_all(reduce, units):
    for unit, n, p in units:
        reduce.start(unit, n, p, True)
    for unit, n, p in units:
        reduce.start(unit, n, p, False)


def bias_of(r, target, table):
    segq = r.seg[...].astype(F32)
    length = segq.shape[1]
    segk = jnp.broadcast_to(segq, (8, length)).T[:, :1]

    def one(h, carry):
        target[h] = masked_bias(r.off, (table, h), segq, segk)
        return carry

    lax.fori_loop(0, r.qkv.shape[0], one, 0)


def out_part(r):
    heads, width, depth = r.weight.shape
    return r.weight[:, 3 * width // 4 :].reshape(heads * (width // 4), depth)


def feed_forward(r):
    block = r.act.shape[0] // 4
    for b in range(4):
        here = slice(b * block, (b + 1) * block)
        pre = mm_nt(r.up[here], r.row[...])
        share = 0.5 + 0.5 * lax.erf(pre * (0.5**0.5))
        r.act[here] = (pre * share).astype(BF)
        r.slope[here] = share + pre * jnp.exp(-0.5 * pre * pre) * ((2.0 * math.pi) ** -0.5)


def attend_all(r):
    heads, hd = r.qkv.shape[0], r.qkv.shape[1] // 3
    bias_of(r, r.masked, 0)
    r.bias_out[0].start()
    weight, row = r.weight.ready(), r.row.ready()

    def one(h, carry):
        r.qkv[h] = mm_nt(weight[h, : 3 * hd], row[...]).astype(BF)
        query = scaled(r.qkv[h, :hd], hd**-0.5)
        keys, values = r.qkv[h, hd : 2 * hd].T, r.qkv[h, 2 * hd :]
        r.mix[h], r.lse[h] = head_forward(keys, values, query, r.masked[h])
        return carry

    lax.fori_loop(0, heads, one, 0)


def cross_slot(r, d):
    span, width = r.dkv.shape[1], r.dquery.shape[1]
    r.g[d, :span] = mm(r.dkv[d], r.row[...]).astype(BF)
    r.g[d, span : span + width] = mm(r.dquery[d], r.stream[...]).astype(BF)
    r.g[d, span + width :] = mm(r.mix[d], r.grad_full[...]).astype(BF)


def attend_all_back(r):
    heads, hd, length = r.qkv.shape[0], r.qkv.shape[1] // 3, r.qkv.shape[2]
    scale = hd**-0.5
    qkv, masked = r.qkv.ready(), r.masked.ready()

    def one(h, carry):
        query, keys, values = (qkv[h, part * hd : (part + 1) * hd] for part in range(3))
        dlogits, dq, dk, dv = head_backward(
            keys.T, scaled(keys, scale), values.T, scaled(query, scale), r.dmix[h], r.lse[h], masked[h]
        )
        r.g_scr[...] = dlogits
        r.dqkv[h, :hd] = dq
        r.dqkv[h, hd : 2 * hd] = dk.astype(BF)
        r.dqkv[h, 2 * hd :] = dv.astype(BF)
        offset_sums(r.g_scr, r.doff, (), (h,), length)
        return carry

    lax.fori_loop(0, heads, one, 0)


def exchange_kernel(kind, norm_row, attend, feed, extra_count, far, count, pieces, seqs, rides, *refs):
    place = spot()
    y, k, seq, half = place
    refs = list(refs)
    take = lambda amount: [refs.pop(0) for _ in range(amount)]
    r = types.SimpleNamespace()
    r.resid, r.norm = take(2)
    if kind == BACKWARD:
        r.normed, r.inv = take(2)
    extras = take(extra_count)
    ride_in = take(len(rides))
    (r.full,) = take(1)
    if kind == FORWARD:
        r.out, r.normed, r.inv = take(3)
    else:
        r.grad, r.sums = take(2)
    if attend:
        if kind == FORWARD:
            r.qkv, r.mix, r.lse, r.masked, r.masked_next = take(5)
        else:
            r.dqkv, r.doff = take(2)
    leave_out = take(2 if kind == FORWARD else 1) if feed else []
    if kind == BACKWARD:
        (r.summed,) = take(1)
    ride_out = take(len(rides))
    if far:
        near, (sems,) = take(len(far)), take(1)
        for i, index in enumerate(far):
            extras[index] = Lazy(extras[index], near[i], sems.at[i])
    if kind == BACKWARD and attend:
        r.up, r.down, r.row, r.act, r.slope, r.hidden, r.weight, r.qkv, r.masked, r.lse = extras
    elif kind == BACKWARD:
        r.dkv, r.dquery, r.weight, r.mix, r.row, r.stream, r.grad_full = extras
    elif attend:
        r.weight, r.row, r.off, r.seg = extras
        biases = [(r.masked, 0), (r.masked_next, 1)]
        r.masked, r.masked_next, bias_sems = take(3)
        r.bias_out = [
            pltpu.make_async_copy(source, target, bias_sems.at[i])
            for i, (source, (target, _)) in enumerate(zip((r.masked, r.masked_next), biases))
        ]
    else:
        r.up, r.down, r.row = extras
    if feed:
        leaving, (sems,) = take(len(leave_out)), take(1)
        if kind == FORWARD:
            r.act, r.slope = leaving
        else:
            (r.g_up,) = leaving
        leaving = [pltpu.make_async_copy(a, b, sems.at[i]) for i, (a, b) in enumerate(zip(leaving, leave_out))]
    (partial,) = take(1)
    if kind == BACKWARD:
        (r.g,) = take(1)
        inner = Collect(r.g, place, seqs, y_refs=take(2))
        if feed:
            (r.dpre,) = take(1)
    if attend:
        if kind == BACKWARD:
            r.g_scr, r.dmix = take(2)
    core_buf, half_send, half_buf, rc, rh, gh, gc = take(7)
    rows = partial.shape[3] // pieces
    peers = [device(y, 1 - k, seq, half), device(y, k, seq, 1 - half)]
    peers.append(device(1 - y, k, seq, half))
    if {ALONG, THROUGH, SUM_ALONG} & set(rides):
        peers += along_devices(place, seqs)
    greet(peers)
    units = [(n * pieces + p, n, p) for n in range(count) for p in range(pieces)]
    reduce = Reduce(partial, core_buf, half_send, half_buf, rc, rh, place, rows)
    spread = Spread(r.full, gh, gc, place, rows)
    moves, sums_along = [], []
    for ride, source, target in zip(rides, ride_in, ride_out):
        if ride == SUM_ALONG:
            sums_along.append(Collect(source, place, seqs, z_refs=[target] + take(5)))
            for d in sums_along[-1].order[:2]:
                sums_along[-1].along(d)
        else:
            moves.append((ride, Freight(target, *take(2), place, seqs)))
            if ride == ACROSS:
                for d in range(seqs):
                    moves[-1][1].across(d)
            else:
                if ride == THROUGH:
                    moves[-1][1].across(0)
                for d in moves[-1][1].first():
                    moves[-1][1].along(d)
    own = partial.shape[3]
    if kind == FORWARD and attend:
        attend_all(r)
        weight = out_part(r)
        product = lambda start: project(r.mix, weight, start, own)
    elif kind == FORWARD:
        feed_forward(r)
        for copy in leaving:
            copy.start()
        product = lambda start: mm_tn(r.act[:, start : start + own], r.down[...]).astype(BF)
    elif feed:
        block = r.g.shape[1]
        for d in range(seqs):
            here = slice(d * block, (d + 1) * block)
            r.dpre[here] = (mm_nt(r.down[here], r.row[...]) * r.slope[here]).astype(BF)
        product = lambda start: mm_tn(r.dpre[:, start : start + own], r.up[...]).astype(BF)
    else:
        span = r.dkv.shape[1]
        weight = r.weight[:, :span].reshape(seqs * span, -1)
        product = lambda start: project(r.dkv, weight, start, own)
    if kind == BACKWARD and not feed:
        grad_slot = lambda d: cross_slot(r, d)
        grad_slot(inner.order[0])
        inner.across(inner.order[0])
    for a in range(2):
        for b in range(2):
            partial[0, a, b] = product((2 * a + b) * own)
    start_all(reduce, units)
    if kind == BACKWARD:
        r.sums[...] = jnp.zeros_like(r.sums)
        for d in inner.order[0 if feed else 1 :]:
            if feed:
                here = slice(d * block, (d + 1) * block)
                r.g[d] = mm(r.act[here], r.row[...]).astype(BF)
            else:
                grad_slot(d)
            inner.across(d)
    gain, bias = r.norm[norm_row : norm_row + 1], r.norm[norm_row + 1 : norm_row + 2]
    for unit, n, p in units:
        reduce.pass_on(unit, n, p)
    for unit, n, p in units:
        here = pl.ds(p * rows, rows)
        branch = reduce.result(unit, n, p)
        if kind == FORWARD:
            normed, inv = normalize(r.resid[n, here].astype(F32) + branch)
            value = normed * gain + bias
            r.out[n, here] = value
            r.normed[n, here] = normed
            r.inv[n, here] = inv
        else:
            upstream = r.resid[n, here] + branch if feed else branch
            normed = r.normed[n, here]
            value = normalize_back(upstream, normed, r.inv[n, here], gain)
            r.grad[n, here] = value
        r.full[n, half, k, here] = value.astype(BF)
        spread.start(unit, n, p)
        if kind != FORWARD:
            r.sums[0:1] += column_sum(upstream * normed)
            r.sums[1:2] += column_sum(upstream)
    for collect in sums_along:
        for d in collect.order[2:-1]:
            collect.along(d)
    for ride, move in moves:
        if ride != ACROSS:
            move.pass_along(ride == THROUGH)
            move.arrive(ride == THROUGH)
    if attend and kind == FORWARD:
        bias_of(r, r.masked_next, 1)
        r.bias_out[1].start()
    elif attend:
        for d in range(seqs):
            here = slice(d * block, (d + 1) * block)
            r.g_up[d] = mm(r.dpre[here], r.hidden[...]).astype(BF)
        for copy in leaving:
            copy.start()
    for unit, n, p in units:
        spread.forward(unit, n, p)
    for collect in sums_along:
        collect.close()
    for unit, n, p in units:
        spread.finish(unit)
        reduce.finish(unit)
    if attend and kind == BACKWARD:
        weight = out_part(r)
        for a in range(2):
            for b in range(2):
                project_back(weight, r.full[0, a, b], r.dmix, (2 * a + b) * own)
        attend_all_back(r)
    if attend and kind == FORWARD:
        for copy in r.bias_out:
            copy.wait()
    if feed:
        for copy in leaving:
            copy.wait()
    for ride, move in moves:
        move.finish()
    if kind == BACKWARD:
        inner.store(r.summed)
        inner.finish()
    for collect in sums_along:
        collect.finish()


def exchange(kind, collective_id, seqs, resid, norm, norm_row, normed=None, inv=None, rides=(), attend=(), feed=(), cross=()):
    count, own, depth = 1, resid.shape[1], norm.shape[1]
    if kind == BACKWARD:
        own = normed.shape[1]
    pieces = 2 if count == 1 else 1
    units, rows = count * pieces, own // pieces
    dma = pltpu.SemaphoreType.DMA
    shape = jax.ShapeDtypeStruct
    vmem = pl.BlockSpec(memory_space=pltpu.VMEM)
    anywhere = pl.BlockSpec(memory_space=pl.ANY)
    full = shape((count, 2, 2, own, depth), BF)
    grad, sums = shape((count, own, depth), F32), shape((2, depth), F32)
    scratch = []
    if kind == FORWARD:
        args = (resid, norm)
        outs = (full, grad, grad, shape((count, own, 1), F32))
    else:
        args = (resid, norm, normed, inv)
        outs = (full, grad, sums)
    extras = tuple(feed) + tuple(attend) + tuple(cross)
    far = tuple(i for i, array in enumerate(extras) if array.size >= 1 << 17)
    base = len(args)
    args += extras
    scratch += [pltpu.VMEM(extras[i].shape, extras[i].dtype) for i in far] + [dma((len(far),))]
    if attend and kind == FORWARD:
        bias = (attend[0].shape[0],) + (attend[1].shape[0],) * 2
        scratch += [pltpu.VMEM(bias, F32), pltpu.VMEM(bias, F32), dma((2,))]
    if feed and kind == FORWARD:
        inner = (feed[0].shape[0], feed[2].shape[0])
        scratch += [pltpu.VMEM(inner, BF), pltpu.VMEM(inner, F32), dma((2,))]
    elif feed:
        scratch += [pltpu.VMEM((seqs, feed[0].shape[0] // seqs, depth), BF), dma((1,))]
    scratch.append(pltpu.VMEM((count, 2, 2, own, depth), BF))
    if kind == BACKWARD:
        n = feed[0].shape[0] // seqs if feed else cross[2].shape[1]
        scratch += [pltpu.VMEM((seqs, n, depth), BF)] + across_scratch(seqs, n, depth // 2)
        if feed:
            scratch.append(pltpu.VMEM(feed[3].shape, BF))
    if attend:
        heads, hd = attend[0].shape[0], attend[0].shape[1] // 4
        length = attend[1].shape[0] if kind == FORWARD else attend[1].shape[2]
        qkv = shape((heads, 3 * hd, length), BF)
        if kind == FORWARD:
            bias = shape((heads, length, length), F32)
            outs += (qkv, shape((heads, hd, length), BF), shape((heads, 1, length), F32), bias, bias)
        else:
            outs += (qkv, shape((heads, 1, 2 * length), F32))
            scratch += [pltpu.VMEM((length, length), F32), pltpu.VMEM((heads, hd, length), BF)]
    if feed and kind == FORWARD:
        inner = (feed[0].shape[0], feed[2].shape[0])
        outs += (shape(inner, BF), shape(inner, F32))
    elif feed:
        outs += (shape((seqs, n, depth), BF),)
    if kind == BACKWARD:
        outs += (shape((seqs, n, depth // 2), BF),)
    scratch += [
        pltpu.VMEM((units, 2, rows, depth), BF),
        pltpu.VMEM((units, rows, depth), BF),
        pltpu.VMEM((units, rows, depth), BF),
        dma((2, units, 2)),
        dma((2, units)),
        dma((2, units)),
        dma((2, units, 2)),
    ]
    in_specs, out_specs = [vmem] * len(args), [vmem] * len(outs)
    for i in far:
        in_specs[base + i] = anywhere
    if kind == FORWARD:
        out_specs[-2:] = [anywhere] * 2
    elif feed:
        out_specs[-2] = anywhere
    aliases = {}
    for ride, array in rides:
        if ride == SUM_ALONG:
            n, wide = array.shape[1], depth // 2
            scratch += along_scratch(seqs, n, wide)
            in_specs.append(vmem)
            out_specs.append(vmem)
            outs += (shape((2, n, wide // 2), F32),)
        else:
            scratch += freight_scratch(seqs)
            aliases[len(args)] = len(outs)
            in_specs.append(anywhere)
            out_specs.append(anywhere)
            outs += (shape(array.shape, array.dtype),)
        args += (array,)
    return pl.pallas_call(
        functools.partial(exchange_kernel, kind, norm_row, bool(attend), bool(feed), len(extras), far, count, pieces, seqs, tuple(ride for ride, _ in rides)),
        out_shape=outs,
        in_specs=in_specs,
        out_specs=tuple(out_specs),
        scratch_shapes=scratch,
        input_output_aliases=aliases,
        compiler_params=pltpu.CompilerParams(collective_id=collective_id, has_side_effects=True, vmem_limit_bytes=60 << 20),
        name="exchange_%d" % collective_id,
    )(*args)


def cross_kernel(count, norm_row, query, kv, out_weight, bias, resid, norm, cot, mix, full_out, output, grad_out, sums, dquery, dkv, doff, full, grad, leave_sems, partial, lse, keys, keys_scaled, values_t, queries, masked, bias_sem, g_scr, dk_scr, dv_scr, dmix, own, landing, return_sems, cot_own, cot_send, cot_recv, cot_local, core_buf, half_send, half_buf, rc, rh, gh, gc):
    place = spot()
    y, k, seq, half = place
    heads, hd, length = query.shape[0], query.shape[1], kv.shape[2]
    depth, rows = partial.shape[4], partial.shape[3]
    scale = hd**-0.5
    bias_copy = pltpu.make_async_copy(bias, masked, bias_sem)
    bias_copy.start()
    greet(
        [device(y, 1 - k, seq, half), device(y, k, seq, 1 - half)]
        + [device(ty, tk, seq, half) for dy, dk, ty, tk in rows_of(place) if dy]
    )
    cots = [shuffle(cot, cot_own, n, n, place, cot_send, cot_recv, cot_local) for n in range(count)]
    reduce = Reduce(partial, core_buf, half_send, half_buf, rc, rh, place, rows)
    spread = Spread(full, gh, gc, place, rows)
    back = Return(own, landing, return_sems, place, depth // 4)
    leaving = []
    sums[...] = jnp.zeros_like(sums)
    g_scr[...] = jnp.zeros_like(g_scr)
    dk_scr[...] = jnp.zeros_like(dk_scr)
    dv_scr[...] = jnp.zeros_like(dv_scr)

    def prepare(h, carry):
        keys[h] = kv[h, :hd].T
        keys_scaled[h] = scaled(kv[h, :hd], scale)
        values_t[h] = kv[h, hd:].T
        queries[h] = scaled(query[h], scale)
        return carry

    lax.fori_loop(0, heads, prepare, 0)
    bias_copy.wait()

    def attend_heads(s, low, high):
        def one(h, carry):
            here = slice(s * length, (s + 1) * length)
            mix[h, :, here], lse[h, :, here] = head_forward(keys[h], kv[h, hd:], queries[h, :, here], masked[h])
            return carry

        lax.fori_loop(low, high, one, 0)

    def send_products(s):
        for a in range(2):
            for b in range(2):
                partial[s, a, b] = project(mix, out_weight[...], s * length + (2 * a + b) * rows, rows)
        reduce.start(s, s, 0, True)
        reduce.start(s, s, 0, False)

    def turn(s):
        normed, inv = normalize(resid[s].astype(F32) + reduce.result(s, s, 0))
        for copy in cots[s]:
            copy.wait()
        upstream = cot_own[s].astype(F32)
        value = normalize_back(upstream, normed, inv, norm[norm_row : norm_row + 1])
        grad[s] = value
        leaving.append(pltpu.make_async_copy(grad.at[s], grad_out.at[s], leave_sems.at[0, s]))
        leaving[-1].start()
        full[s, half, k] = value.astype(BF)
        spread.start(s, s, 0)
        sums[0:1] += column_sum(upstream * normed)
        sums[1:2] += column_sum(upstream)
        back.start(s, s, (normed * norm[norm_row : norm_row + 1] + norm[norm_row + 1 : norm_row + 2]).astype(BF))

    def attend_back(s):
        for a in range(2):
            for b in range(2):
                project_back(out_weight[...], full[s, a, b], dmix, (2 * a + b) * rows)

        def one(h, carry):
            here = slice(s * length, (s + 1) * length)
            dlogits, dq, dk, dv = head_backward(
                keys[h], keys_scaled[h], values_t[h], queries[h, :, here], dmix[h], lse[h, :, here], masked[h]
            )
            g_scr[h] += dlogits
            dquery[h, :, here] = dq
            dk_scr[h] += dk
            dv_scr[h] += dv
            return carry

        lax.fori_loop(0, heads, one, 0)

    for s in range(count):
        attend_heads(s, 0, heads // 2)
        if s >= 1:
            reduce.pass_on(s - 1, s - 1, 0)
        if s >= 2:
            turn(s - 2)
        attend_heads(s, heads // 2, heads)
        send_products(s)
    reduce.pass_on(count - 1, count - 1, 0)
    for s in range(max(count - 2, 0), count):
        turn(s)
    for s in range(count):
        spread.forward(s, s, 0)
        spread.ready(s)
        leaving.append(pltpu.make_async_copy(full.at[s], full_out.at[s], leave_sems.at[1, s]))
        leaving[-1].start()
        attend_back(s)
    for h in range(heads):
        dkv[h, :hd] = dk_scr[h].astype(BF)
        dkv[h, hd:] = dv_scr[h].astype(BF)

    def offsets_of(h, carry):
        offset_sums(g_scr, doff, (h,), (h,), length)
        return carry

    lax.fori_loop(0, heads, offsets_of, 0)
    back.finish()
    output[...] = landing[...].astype(F32)
    for copy in leaving:
        copy.wait()
    for s in range(count):
        spread.sent(s)
        reduce.finish(s)


def cross_attention(collective_id, query, kv, out_weight, masked, resid, norm, norm_row, cot):
    count, own, depth = resid.shape
    heads, hd, total = query.shape
    length = kv.shape[2]
    dma = pltpu.SemaphoreType.DMA
    shape = jax.ShapeDtypeStruct
    outs = (
        shape(query.shape, BF),
        shape((count, 2, 2, own, depth), BF),
        shape((2, count, 2, own, depth // 4), F32),
        shape((count, own, depth), F32),
        shape((2, depth), F32),
        shape(query.shape, BF),
        shape(kv.shape, BF),
        shape((heads, 1, 2 * length), F32),
    )
    whole = pl.BlockSpec(memory_space=pltpu.VMEM)
    anywhere = pl.BlockSpec(memory_space=pl.ANY)
    specs = [whole] * 3 + [anywhere] + [whole] * 2 + [anywhere]
    vmem = pltpu.VMEM
    return pl.pallas_call(
        functools.partial(cross_kernel, count, norm_row),
        out_shape=outs,
        in_specs=specs,
        out_specs=tuple(anywhere if i in (1, 3) else whole for i in range(len(outs))),
        scratch_shapes=[
            vmem((count, 2, 2, own, depth), BF),
            vmem((count, own, depth), F32),
            dma((2, count)),
            vmem((count, 2, 2, own, depth), BF),
            vmem((heads, 1, total), F32),
            vmem((heads, length, hd), BF),
            vmem((heads, hd, length), BF),
            vmem((heads, length, hd), BF),
            vmem(query.shape, BF),
            vmem(masked.shape, F32),
            pltpu.SemaphoreType.DMA,
            vmem((heads, length, length), F32),
            vmem((heads, hd, length), F32),
            vmem((heads, hd, length), F32),
            vmem((heads, hd, length), BF),
            vmem((count, own, depth), BF),
            vmem((2, count, 2, own, depth // 4), BF),
            dma((2, count, 3)),
            vmem((count, own, depth), BF),
            dma((count, 3)),
            dma((count, 3)),
            dma((count,)),
            vmem((count, 2, own, depth), BF),
            vmem((count, own, depth), BF),
            vmem((count, own, depth), BF),
            dma((2, count, 2)),
            dma((2, count)),
            dma((2, count)),
            dma((2, count, 2)),
        ],
        compiler_params=pltpu.CompilerParams(collective_id=collective_id, has_side_effects=True, vmem_limit_bytes=60 << 20),
        name="cross_attention",
    )(query, kv, out_weight, masked, resid, norm, cot)


class Lazy:
    def __init__(self, source, target, sem):
        self.copy, self.ref, self.shape = pltpu.make_async_copy(source, target, sem), target, target.shape
        self.copy.start()

    def ready(self):
        if self.copy is not None:
            self.copy.wait()
            self.copy = None
        return self.ref

    def __getitem__(self, index):
        return self.ready()[index]

    @property
    def at(self):
        return self.ready().at


def fetch(far, near, sems):
    copies = [pltpu.make_async_copy(source, target, sems.at[i]) for i, (source, target) in enumerate(zip(far, near))]
    for copy in copies:
        copy.start()
    return copies


def inputs_kernel(seqs, tok_ref, str_ref, norm_ref, ids_ref, tab_ref, *refs):
    refs = list(refs)
    take = lambda amount: [refs.pop(0) for _ in range(amount)]
    groups = 4
    far = take(7)
    x_own, *leave_out, norm_all, ids_all, tab_all = take(7)
    fulls = take(groups)
    in_send, in_recv, in_local, xh, xc, yh, yc, small_sems, tab_sems, small_self, pack_sems, pack_self = take(12)
    pack_first, pack_up, pack_last = take(3)
    w_qkv, w_out, w_up, w_kv, w_query, w_co = near = take(6)
    (fetch_sems,) = take(1)
    x_full, y_own, y_full = leaving = take(3)
    (leave_sems,) = take(1)
    leaving = [pltpu.make_async_copy(a, b, leave_sems.at[n]) for n, (a, b) in enumerate(zip(leaving, leave_out))]
    w_down = far.pop(3)
    fetched = fetch(far, near, fetch_sems)
    packs = [pack_first, pack_up, w_down, pack_last]
    place = spot()
    y, k, seq, half = place
    feat = tok_ref.shape[-1]
    own = tok_ref.shape[-2]
    row_peers = rows_of(place)
    others = [device(y, k, lax.rem(seq + d, seqs), half) for d in range(1, seqs)]
    greet([device(ty, tk, seq, half) for dy, dk, ty, tk in row_peers] + [device(y, k, seq, 1 - half)] + others)
    count = str_ref.shape[1]
    x_copies = shuffle(tok_ref, x_own, 0, 0, place, in_send, in_recv, in_local)
    hd = w_out.shape[0] // 2

    def columns_in(pack, start, matrix):
        rows = matrix.T
        half_rows = rows.shape[0] // 2
        for core in range(2):
            pack[core, start : start + half_rows] = rows[core * half_rows : (core + 1) * half_rows]

    def rows_in(pack, start, matrix):
        half_rows = matrix.shape[0] // 2
        for core in range(2):
            pack[core, start : start + half_rows] = matrix[core * half_rows : (core + 1) * half_rows]

    def load(g):
        here = fulls[g].at[0, :, lanes(k * feat, feat)]
        copy = pltpu.make_async_copy(packs[g].at[k], here, pack_self.at[g])
        copy.start()
        return (
            copy,
            remote(packs[g].at[1 - k], here, pack_sems.at[0, g], pack_sems.at[1, g], device(y, 1 - k, seq, half)),
        )

    for copy in fetched[:2]:
        copy.wait()
    for part in range(3):
        columns_in(pack_first, part * hd, w_qkv[part])
    rows_in(pack_first, 3 * hd, w_out)
    loads = [load(0)]
    small = []
    for j, (source, target) in enumerate(((norm_ref, norm_all), (ids_ref, ids_all))):
        slot = (lambda dy: (slice(None), lanes(k * feat + 2 * dy * feat, feat))) if j == 0 else (lambda dy: (2 * y + k,))
        copy = pltpu.make_async_copy(source, target.at[slot(0)], small_self.at[j])
        copy.start()
        small.append(copy)
        for i, (dy, dk, ty, tk) in enumerate(row_peers):
            small.append(
                remote(source, target.at[slot(dy)], small_sems.at[0, j, i], small_sems.at[1, j, i], device(ty, tk, seq, half))
            )
    copy = pltpu.make_async_copy(tab_ref, tab_all.at[0], small_self.at[2])
    copy.start()
    small.append(copy)
    for d in range(1, seqs):
        small.append(remote(tab_ref, tab_all.at[d], tab_sems.at[0, d - 1], tab_sems.at[1, d - 1], others[d - 1]))
    freights = [Freight(full, *take(2), place, seqs) for full in fulls]
    for copy in loads[0]:
        copy.wait()
    for d in freights[0].first():
        freights[0].along(d)
    freights[0].across(0)
    fetched[2].wait()
    columns_in(pack_up, 0, w_up[...])
    loads.append(load(1))
    for copy in x_copies:
        copy.wait()
    x_full[0, half, k] = x_own[0]
    x_spread = Spread(x_full, xh, xc, place, own)
    x_spread.start(0, 0, 0)
    y_copies = [shuffle(str_ref, y_own, n, 1 + n, place, in_send, in_recv, in_local) for n in range(count)]
    y_spread = Spread(y_full, yh, yc, place, own)
    freights[0].pass_along(True)
    for copy in loads[1]:
        copy.wait()
    for d in freights[1].first():
        freights[1].along(d)
    loads.append(load(2))
    for copy in fetched[3:]:
        copy.wait()
    for part in range(2):
        columns_in(pack_last, part * hd, w_kv[part])
    columns_in(pack_last, 2 * hd, w_query[...])
    rows_in(pack_last, 3 * hd, w_co)
    loads.append(load(3))
    x_spread.forward(0, 0, 0)
    freights[0].arrive(True)
    freights[1].across(0)
    for n in range(count):
        for copy in y_copies[n]:
            copy.wait()
        y_full[n, half, k] = y_own[n]
        y_spread.start(n, n, 0)
    freights[1].pass_along(True)
    for g in range(2, groups):
        for copy in loads[g]:
            copy.wait()
    for d in freights[2].first():
        freights[2].along(d)
    freights[1].arrive(True)
    freights[2].pass_along(False)
    for n in range(count):
        y_spread.forward(n, n, 0)
    x_spread.finish(0)
    for n in range(count):
        y_spread.finish(n)
    for copy in leaving:
        copy.start()
    for copy in small:
        copy.wait()
    freights[2].arrive(False)
    for freight in freights:
        freight.finish()
    for copy in leaving:
        copy.wait()


def gather_inputs(seqs, tokens, streams, norm, ids, table, *weights):
    count, own, feat = streams.shape[1], streams.shape[-2], streams.shape[-1]
    depth = 4 * feat
    dma = pltpu.SemaphoreType.DMA
    shape = jax.ShapeDtypeStruct
    vmem = pl.BlockSpec(memory_space=pltpu.VMEM)
    outs = (
        shape((1, own, depth), BF),
        shape((1, 2, 2, own, depth), BF),
        shape((count, own, depth), BF),
        shape((count, 2, 2, own, depth), BF),
        shape((norm.shape[0], depth), F32),
        shape((4,) + ids.shape, jnp.int32),
        shape((seqs,) + table.shape, F32),
    )
    specs = [vmem] * len(outs)
    hd, ff = weights[1].shape[0] // 2, weights[2].shape[1] // 2
    for n in (4 * hd, ff, ff, 4 * hd):
        outs += (shape((seqs, n, depth), BF),)
        specs.append(pl.BlockSpec(memory_space=pl.ANY))
    moves = 1 + count
    scratch = [
        dma((moves, 3)),
        dma((moves, 3)),
        dma((moves,)),
        dma((2, 1)),
        dma((2, 1, 2)),
        dma((2, count)),
        dma((2, count, 2)),
        dma((2, 2, 3)),
        dma((2, seqs - 1)),
        dma((3,)),
        dma((2, 4)),
        dma((4,)),
    ]
    scratch += [pltpu.VMEM((2, n, feat), BF) for n in (4 * hd, ff, 4 * hd)]
    fetched = weights[:3] + weights[4:]
    scratch += [pltpu.VMEM(weight.shape, BF) for weight in fetched] + [dma((len(fetched),))]
    scratch += [pltpu.VMEM(out.shape, out.dtype) for out in outs[1:4]] + [dma((3,))]
    specs[1:4] = [pl.BlockSpec(memory_space=pl.ANY)] * 3
    for _ in range(4):
        scratch += freight_scratch(seqs)
    return pl.pallas_call(
        functools.partial(inputs_kernel, seqs),
        out_shape=outs,
        in_specs=[pl.BlockSpec(memory_space=pl.ANY)] * (5 + len(weights)),
        out_specs=tuple(specs),
        scratch_shapes=scratch,
        compiler_params=pltpu.CompilerParams(collective_id=0, has_side_effects=True, vmem_limit_bytes=60 << 20),
        name="gather_inputs",
    )(tokens, streams, norm, ids, table, *weights)


def outputs_kernel(seqs, count, dqkv, dquery, mix, first_weight, last_weight, x_full, d1_full, d1, d3, small, down, up, tok_out, str_out, small_out, down_out, up_out, first_out, part, first, core_buf, half_send, half_buf, own, land_x, land_y, rc, rh, rs, small_buf, ss, *refs):
    refs = list(refs)
    take = lambda amount: [refs.pop(0) for _ in range(amount)]
    place = spot()
    far = [up, dqkv, first_weight, x_full, mix, d1_full, last_weight, dquery, down, d1, d3]
    near, (sems,) = take(len(far)), take(1)
    lazy = [Lazy(source, target, sems.at[i]) for i, (source, target) in enumerate(zip(far, near))]
    up, dqkv, first_weight, x_full, mix, d1_full, last_weight, dquery, down, d1, d3 = lazy
    y, k, seq, half = place
    rows = part.shape[3]
    feat = part.shape[4] // 4
    bits = [1 << b for b in range((seqs - 1).bit_length())]
    flips = [device(y, k, seq + b - 2 * b * ((seq // b) % 2), half) for b in bits]
    others = [device(y, k, lax.rem(seq + d, seqs), half) for d in range(1, seqs)]
    partners = [device(y, 1 - k, seq, half), device(y, k, seq, 1 - half), device(1 - y, k, seq, half)]
    greet(partners + [device(1 - y, 1 - k, seq, half)] + others)
    partners += flips
    small_out[...] = small[...]

    def start_small(stage):
        return stage, remote(small_out, small_buf.at[stage], ss.at[0, stage], ss.at[1, stage], partners[stage])

    def end_small(started):
        stage, copy = started
        copy.wait()
        small_out[...] += small_buf[stage]

    heads, width = mix.shape[0], mix.shape[1]

    def products(unit):
        for a in range(2):
            for b in range(2):
                start = (2 * a + b) * rows
                if unit == 0:
                    weight = first_weight[:, : 3 * width].reshape(heads * 3 * width, -1)
                    part[unit, a, b] = project(dqkv, weight, start, rows)
                else:
                    weight = last_weight[:, 2 * width : 3 * width].reshape(heads * width, -1)
                    part[unit, a, b] = project(dquery, weight, 4 * (unit - 1) * rows + start, rows)
        reduce.start(unit, unit, 0, True)
        reduce.start(unit, unit, 0, False)

    reduce = Reduce(part, core_buf, half_send, half_buf, rc, rh, place, rows)
    units = range(count + 1)
    down = Collect(down, place, seqs, z_refs=[down_out] + take(5))
    up = Collect(up, place, seqs, y_refs=take(2), z_refs=[up_out] + take(5))
    first_ref = first
    first = Collect(first, place, seqs, y_refs=take(2), z_refs=[first_out] + take(5))
    started = start_small(2)
    for d in up.order:
        up.across(d)
    products(0)
    for d in first.order:
        first_ref[d, : 3 * width] = mm(dqkv[d], x_full[...]).astype(BF)
        first_ref[d, 3 * width :] = mm(mix[d], d1_full[...]).astype(BF)
        first.across(d)
    end_small(started)
    started = start_small(3)
    reduce.pass_on(0, 0, 0)
    products(1)
    for stage in range(4, len(partners)):
        end_small(started)
        started = start_small(stage)
    end_small(started)
    for d in down.order[:2]:
        down.along(d)
    started = start_small(0)
    for unit in units[2:]:
        products(unit)
    end_small(started)
    x_back = Return(own, land_x, rs, place, feat)
    y_back = Return(own, land_y, rs, place, feat)
    x_back.start(0, 0, (d1[0] + reduce.result(0, 0, 0)).astype(BF))
    started = start_small(1)
    for unit in units[1:]:
        reduce.pass_on(unit, unit, 0)
    end_small(started)
    for d in down.order[2:-1]:
        down.along(d)
    for d in up.order[:2]:
        up.along(d)
    for unit in units[1:]:
        y_back.start(unit, unit - 1, (d3[unit - 1] + reduce.result(unit, unit, 0)).astype(BF))
    down.close()
    for d in up.order[2:-1]:
        up.along(d)
    for d in first.order[:2]:
        first.along(d)
    up.close()
    for d in first.order[2:-1]:
        first.along(d)
    for unit in units:
        reduce.finish(unit)
    x_back.finish()
    tok_out[...] = land_x[:, 0].astype(F32)
    first.close()
    y_back.finish()
    str_out[...] = land_y[...].astype(F32)
    for collect in (down, up, first):
        collect.finish()


def scatter_outputs(seqs, collective_id, dqkv, dquery, mix, first_weight, last_weight, x_full, d1_full, d1, d3, small, down, up):
    count, own, depth = d3.shape
    feat, wide = depth // 4, depth // 2
    units = count + 1
    dma = pltpu.SemaphoreType.DMA
    shape = jax.ShapeDtypeStruct
    stages = 3 + (seqs - 1).bit_length()
    outs = (shape((2, 2, own, feat), F32), shape((2, count, 2, own, feat), F32), shape(small.shape, F32))
    outs += tuple(shape((2, group.shape[1], feat), F32) for group in (down, up, first_weight))
    scratch = [
        pltpu.VMEM((units, 2, 2, own, depth), BF),
        pltpu.VMEM(first_weight.shape, BF),
        pltpu.VMEM((units, 2, own, depth), BF),
        pltpu.VMEM((units, own, depth), BF),
        pltpu.VMEM((units, own, depth), BF),
        pltpu.VMEM((units, own, depth), BF),
        pltpu.VMEM((2, 1, 2, own, feat), BF),
        pltpu.VMEM((2, count, 2, own, feat), BF),
        dma((2, units, 2)),
        dma((2, units)),
        dma((2, units, 3)),
        pltpu.VMEM((stages,) + small.shape, F32),
        dma((2, stages)),
    ]
    far = (up, dqkv, first_weight, x_full, mix, d1_full, last_weight, dquery, down, d1, d3)
    scratch += [pltpu.VMEM(array.shape, array.dtype) for array in far] + [dma((len(far),))]
    scratch += along_scratch(seqs, down.shape[1], wide)
    for group in (up, first_weight):
        scratch += across_scratch(seqs, group.shape[1], wide) + along_scratch(seqs, group.shape[1], wide)
    args = (dqkv, dquery, mix, first_weight, last_weight, x_full, d1_full, d1, d3, small, down, up)
    return pl.pallas_call(
        functools.partial(outputs_kernel, seqs, count),
        out_shape=outs,
        in_specs=[pl.BlockSpec(memory_space=pltpu.VMEM if array is small else pl.ANY) for array in args],
        out_specs=tuple(pl.BlockSpec(memory_space=pltpu.VMEM) for _ in outs),
        scratch_shapes=scratch,
        compiler_params=pltpu.CompilerParams(collective_id=collective_id, has_side_effects=True, vmem_limit_bytes=60 << 20),
        name="scatter_outputs",
    )(*args)


def pick(array, index, axis):
    return lax.dynamic_index_in_dim(array, index, axis, keepdims=False)


def dot_f32(spec, left, right):
    return jnp.einsum(spec, left, right, preferred_element_type=F32)


def on_device(
    rows,
    cols,
    tokens,
    streams,
    cotangent,
    block_ids,
    bucket_ids,
    w_qkv,
    enc_table,
    w_out,
    attention_norm_gain,
    attn_bias,
    w_up,
    w_down,
    ffn_gain,
    ffn_bias,
    w_query,
    w_keyval,
    cross_table,
    w_cross_out,
    cross_gain,
    cross_bias,
):
    seqs = cols // 2
    row, col = lax.axis_index(ROW), lax.axis_index(COL)
    y, k, seq, half = row // 2, row % 2, col // 2, col % 2
    low_y = y == 0
    stream_count = streams.shape[1]
    tok = tokens.shape[1]
    own = tok // 2
    feat = tokens.shape[2]
    length = block_ids.shape[2]
    head_dim = w_qkv.shape[2] // 2
    ff = w_up.shape[1] // 2
    table_heads, bucket_count = enc_table.shape

    def columns_back(array, parts):
        return array.reshape(2, parts, -1, feat).transpose(3, 1, 0, 2).reshape(feat, parts, -1)

    hd3, hd2 = 3 * head_dim, 2 * head_dim
    norm_params = jnp.stack([attention_norm_gain, attn_bias, ffn_gain, ffn_bias, cross_gain, cross_bias] + [cross_bias] * 2)
    table_pack = jnp.zeros((8, 128), F32).at[0].set(jnp.stack([enc_table, cross_table]).reshape(-1))
    micro_count = tokens.shape[0]
    x_own, x_full, y_own, y_full, norm_params, all_ids, all_tables, first, up, down, last = gather_inputs(
        seqs,
        tokens.reshape(micro_count, 1, 2, own, feat),
        streams.reshape(micro_count, stream_count, 2, own, feat),
        norm_params,
        block_ids.reshape(8, -1),
        table_pack,
        w_qkv.transpose(1, 0, 2),
        w_out,
        w_up,
        w_down.reshape(2, ff, feat),
        w_keyval.transpose(1, 0, 2),
        w_query,
        w_cross_out,
    )
    x_full, y_full = x_full.reshape(length, D), y_full.reshape(stream_count * length, D)
    segment = pick(pick(all_ids.reshape(rows, micro_count, length), seq, 0), y, 0)
    segq = segment[None]
    own_tables = pick(all_tables[:, 0].reshape(seqs, 2, table_heads, bucket_count), k, 2)
    slot_col = 2 * ((seq - jnp.arange(seqs)) % seqs) + half
    reversed_ids = jnp.concatenate([jnp.full((1,), -1, jnp.int32), bucket_ids[::-1]])
    onehot = bucket_onehot(reversed_ids, bucket_count)
    offsets = jnp.einsum("htb,bo->tho", own_tables, onehot, precision=highest)[:, :, None, :]


    hidden_full, hidden, normed1, inv1, qkv, mix, lse, enc_bias, cross_bias_full, down, last = exchange(
        FORWARD,
        1,
        seqs,
        x_own,
        norm_params,
        0,
        rides=((ACROSS, down), (ALONG, last)),
        attend=(first, x_full, offsets, segq),
    )
    up, down = up.reshape(-1, D), down.reshape(-1, D)
    hidden_full = hidden_full.reshape(length, D)
    enc_full, _, normed2, inv2, act, slope, last = exchange(
        FORWARD,
        2,
        seqs,
        hidden,
        norm_params,
        2,
        rides=((ACROSS, last),),
        feed=(up, down, hidden_full),
    )
    m_kv, m_q, m_co = last[:, :hd2], last[:, hd2:hd3], last[:, hd3:].reshape(-1, D)
    enc_full = enc_full.reshape(length, D)
    kv = dot_f32("snr,tr->snt", m_kv, enc_full).astype(BF)
    query = dot_f32("snr,tr->snt", m_q, y_full).astype(BF)
    cmix, d3_full, output, d3, sums3, dquery, dkv, doff_cross = cross_attention(
        3,
        query,
        kv,
        m_co,
        cross_bias_full,
        y_own,
        norm_params,
        4,
        cotangent.reshape(micro_count, stream_count, 2, own, feat),
    )
    d3_full = d3_full.reshape(stream_count * length, D)

    d2_full, d2, sums2, g_last = exchange(
        BACKWARD,
        4,
        seqs,
        norm_params[None],
        norm_params,
        2,
        normed=normed2,
        inv=inv2,
        cross=(dkv, dquery, last, cmix, enc_full, y_full, d3_full),
    )
    d2_full = d2_full.reshape(length, D)
    d1_full, d1, sums1, dqkv, doff_enc, g_up, g_down, g_last = exchange(
        BACKWARD,
        5,
        seqs,
        d2,
        norm_params,
        0,
        normed=normed1,
        inv=inv1,
        rides=((SUM_ALONG, g_last),),
        attend=(first, qkv, enc_bias, lse),
        feed=(up, down, d2_full, act, slope, hidden_full),
    )
    d1_full = d1_full.reshape(length, D)

    norm_grads = jnp.concatenate([sums1, sums2, sums3])
    norm_grads = jnp.where(low_y, norm_grads, jnp.roll(norm_grads, D // 2, axis=1))
    table_grads = jnp.einsum(
        "tho,bo->thb", jnp.stack([doff_enc[:, 0], doff_cross[:, 0]]), onehot, precision=highest
    )
    heads = 2 * slot_col + k
    spread = (heads[:, None] == jnp.arange(table_heads * cols)[None, :]).astype(F32)
    table_grads = jnp.einsum("thb,hg->tgb", table_grads, spread, precision=highest)
    small = jnp.concatenate([norm_grads.reshape(-1, 128), table_grads.reshape(-1, 128)])
    grad_tokens, grad_streams, small, g_down, g_up, g_first = scatter_outputs(
        seqs, 6, dqkv, dquery, mix, first, last, x_full, d1_full, d1, d3, small, g_down, g_up
    )
    output, grad_streams = output.reshape(streams.shape), grad_streams.reshape(streams.shape)
    grad_tokens = grad_tokens.reshape(tokens.shape)
    count = norm_grads.size // 128
    norm_sums = lax.dynamic_slice_in_dim(small[:count].reshape(6, D), row * feat, feat, axis=1)
    table_sums = small[count:].reshape(2, table_heads * cols, bucket_count)
    table_sums = lax.dynamic_slice_in_dim(table_sums, col * table_heads, table_heads, axis=1)
    return (
        output,
        grad_tokens,
        grad_streams,
        columns_back(g_first[:, :hd3], 3),
        table_sums[0],
        g_first[:, hd3:].reshape(w_out.shape),
        norm_sums[0],
        norm_sums[1],
        columns_back(g_up, 1).reshape(w_up.shape),
        g_down.reshape(w_down.shape),
        norm_sums[2],
        norm_sums[3],
        columns_back(g_last[:, hd2:hd3], 1).reshape(w_query.shape),
        columns_back(g_last[:, :hd2], 2),
        table_sums[1],
        g_last[:, hd3:].reshape(w_cross_out.shape),
        norm_sums[4],
        norm_sums[5],
    )


def solution(mesh):
    whole_row, half_col = mesh.shape[ROW], mesh.shape[COL]
    wide, table, norm = P(ROW, None, COL), P(COL, None), P(ROW)
    up, down = P(ROW, COL), P(COL, ROW)
    weights = (wide, table, down, norm, norm, up, down, norm, norm, up, wide, table, down, norm, norm)

    def run(tokens, *rest):
        micro_count = tokens.shape[0]
        if whole_row == 4 and micro_count == 2 and half_col % 2 == 0:
            device_fn = functools.partial(on_device, whole_row, half_col)
        else:
            device_fn = on_device_general
        return jax.shard_map(
            device_fn,
            mesh=mesh,
            in_specs=(P(None, COL, ROW), P(None, None, COL, ROW), P(None, None, COL, ROW), P(None, ROW, None), P()) + weights,
            out_specs=(P(None, None, COL, ROW), P(None, COL, ROW), P(None, None, COL, ROW)) + weights,
            check_vma=False,
        )(tokens, *rest)

    return run
```

```python
import functools
import math
import types
import jax
import jax.numpy as jnp
from jax import lax
from jax.experimental import pallas as pl
from jax.experimental.pallas import tpu as pltpu
from jax.sharding import PartitionSpec as P

D = 1024
F32 = jnp.float32
BF = jnp.bfloat16
ROW, COL = "row", "col"


epsilon = 1e-05
neg_fill = -1e30
highest = lax.Precision.HIGHEST


def gather_cols(local_rows):
    return lax.all_gather(local_rows, COL, axis=1, tiled=True)


def gather_rows(local_rows):
    return lax.all_gather(local_rows, ROW, axis=1, tiled=True)


def product(matmul_operand, weight_matrix):
    return jnp.einsum(
        "ray,yw->raw", matmul_operand, weight_matrix, preferred_element_type=jnp.float32
    )


def rows_product(operand_full, matrix):
    return lax.psum_scatter(product(operand_full, matrix), ROW, scatter_dimension=1, tiled=True)


def cols_product(operand_full, matrix):
    return lax.psum_scatter(product(operand_full, matrix), COL, scatter_dimension=1, tiled=True)


def weight_grad(matmul_operand, upstream_gradient):
    return jnp.einsum(
        "bpt,bpr->tr", matmul_operand, upstream_gradient, preferred_element_type=jnp.float32
    )


def gelu_exact(argument):
    return jax.nn.gelu(argument, approximate=False)


def norm_forward(residual, gain_vec, bias_vec):
    local_sum = jnp.sum(residual, axis=-1)
    average = lax.psum(local_sum, ROW) / D
    centered = residual - average[..., None]
    spread = lax.psum(jnp.sum(centered * centered, axis=-1), ROW) / D
    inv_std = lax.rsqrt(spread + epsilon)
    normed = centered * inv_std[..., None]
    return (normed * gain_vec + bias_vec, normed, inv_std)


def norm_back(out_grad, normed, inv_std, gain_vec):
    scaled_grad = out_grad * gain_vec
    first_moment, second_moment = lax.psum(
        (jnp.sum(scaled_grad, axis=-1), jnp.sum(scaled_grad * normed, axis=-1)), ROW
    )
    resid_grad = inv_std[..., None] * (
        scaled_grad - first_moment[..., None] / D - normed * (second_moment[..., None] / D)
    )
    return (resid_grad, jnp.sum(out_grad * normed, axis=(0, 1)), jnp.sum(out_grad, axis=(0, 1)))


def bucket_onehot(bucket_ids, bucket_count):
    return (bucket_ids[None, :] == jnp.arange(bucket_count, dtype=jnp.int32)[:, None]).astype(
        jnp.float32
    )


def block_logits(query_blk, key_rows, offsets, segment, first_row):
    row_count = query_blk.shape[2]
    length = key_rows.shape[1]
    score_scale = query_blk.shape[-1] ** (-0.5)
    raw_scores = jnp.einsum(
        "snqhd,nkhd->snhqk", query_blk, key_rows, preferred_element_type=jnp.float32
    )
    places = jnp.arange(length, dtype=jnp.int32)
    query_pos = first_row + jnp.arange(row_count, dtype=jnp.int32)
    offset_index = places[None, :] - query_pos[:, None] + (length - 1)
    pos_bias = jnp.take(offsets, offset_index, axis=1)
    visible = segment[:, first_row : first_row + row_count, None] >= segment[:, None, :]
    return jnp.where(
        visible[None, :, None], raw_scores * score_scale + pos_bias[None, None], neg_fill
    )


def attend(queries, key_rows, value_rows, segment, offsets):
    score_logits = block_logits(queries, key_rows, offsets, segment, 0)
    row_max = jnp.max(score_logits, axis=-1, keepdims=True)
    log_total = row_max + jnp.log(jnp.sum(jnp.exp(score_logits - row_max), axis=-1, keepdims=True))
    weights = jnp.exp(score_logits - log_total).astype(jnp.bfloat16)
    mixed_parts = jnp.einsum(
        "snhqk,nkhd->snqhd", weights, value_rows, preferred_element_type=jnp.float32
    )
    lse_parts = log_total[..., 0]
    return (mixed_parts, lse_parts)


def diagonal_sums(summand):
    head_count, row_count, length = summand.shape
    flipped = summand[:, ::-1, :]
    padded = jnp.concatenate(
        [flipped, jnp.zeros((head_count, row_count, row_count), summand.dtype)], axis=2
    )
    flattened = padded.reshape(head_count, row_count * (length + row_count))[
        :, : row_count * (length + row_count - 1)
    ]
    return jnp.sum(flattened.reshape(head_count, row_count, length + row_count - 1), axis=1)


def attend_back(queries, key_rows, value_rows, segment, offsets, onehot, log_totals, mix_grad):
    length = key_rows.shape[1]
    block_rows = min(512, length)
    score_scale = queries.shape[-1] ** (-0.5)
    offset_grad = jnp.zeros(offsets.shape, jnp.float32)
    score_logits = block_logits(queries, key_rows, offsets, segment, 0)
    probability = jnp.exp(score_logits - log_totals[:, :, :, 0:block_rows, None])
    prob_grad = jnp.einsum(
        "snqhd,nkhd->snhqk", mix_grad, value_rows, preferred_element_type=jnp.float32
    )
    logit_grad = probability * (
        prob_grad - jnp.sum(probability * prob_grad, axis=-1, keepdims=True)
    )
    scaled = (logit_grad * score_scale).astype(jnp.bfloat16)
    query_parts = jnp.einsum(
        "snhqk,nkhd->snqhd", scaled, key_rows, preferred_element_type=jnp.float32
    )
    key_grad = jnp.einsum("snhqk,snqhd->nkhd", scaled, queries, preferred_element_type=jnp.float32)
    value_grad = jnp.einsum(
        "snhqk,snqhd->nkhd",
        probability.astype(jnp.bfloat16),
        mix_grad,
        preferred_element_type=jnp.float32,
    )
    low_end = length - block_rows
    offset_grad = offset_grad.at[:, low_end : low_end + length + block_rows - 1].add(
        diagonal_sums(jnp.sum(logit_grad, axis=(0, 1)))
    )
    table_grad = jnp.dot(offset_grad, onehot.T, precision=highest)
    return (query_parts, key_grad, value_grad, table_grad)


def on_device_general(
    tokens,
    streams,
    cotangent,
    block_ids,
    bucket_ids,
    w_qkv,
    enc_table,
    w_out,
    attention_norm_gain,
    attn_bias,
    w_up,
    w_down,
    ffn_gain,
    ffn_bias,
    w_query,
    w_keyval,
    cross_table,
    w_cross_out,
    cross_gain,
    cross_bias,
):
    micro_count = tokens.shape[0]
    stream_count = streams.shape[1]
    seq_rows = block_ids.shape[1]
    length = block_ids.shape[2]
    head_count = enc_table.shape[0]
    bucket_count = enc_table.shape[1]
    row_width = w_qkv.shape[0]
    col_width = w_qkv.shape[2]
    head_dim = col_width // head_count
    row_tokens = seq_rows * length
    qkv_matrix = w_qkv.reshape(row_width, 3 * col_width)
    keyval_matrix = w_keyval.reshape(row_width, 2 * col_width)
    onehot = bucket_onehot(bucket_ids, bucket_count)
    enc_offsets = jnp.dot(enc_table, onehot, precision=highest)
    cross_offsets = jnp.dot(cross_table, onehot, precision=highest)
    qkv_acc = jnp.zeros((row_width, 3 * col_width), jnp.float32)
    out_acc = jnp.zeros(w_out.shape, jnp.float32)
    up_acc = jnp.zeros(w_up.shape, jnp.float32)
    down_acc = jnp.zeros(w_down.shape, jnp.float32)
    query_acc = jnp.zeros(w_query.shape, jnp.float32)
    keyval_acc = jnp.zeros((row_width, 2 * col_width), jnp.float32)
    cross_out_acc = jnp.zeros(w_cross_out.shape, jnp.float32)
    enc_table_acc = jnp.zeros(enc_table.shape, jnp.float32)
    cross_table_acc = jnp.zeros(cross_table.shape, jnp.float32)
    norm_accs = [jnp.zeros((row_width,), jnp.float32) for place_holder in range(6)]
    outputs = []
    token_grads = []
    stream_grads = []
    for micro in range(micro_count):
        segment = block_ids[micro]
        x_in = tokens[micro][None]
        y_in = streams[micro]
        x_full = gather_cols(x_in)
        qkv = (
            rows_product(x_full, qkv_matrix)
            .astype(jnp.bfloat16)
            .reshape(seq_rows, length, 3, head_count, head_dim)
        )
        enc_query = qkv[:, :, 0][None]
        enc_key = qkv[:, :, 1]
        encoder_value_rows = qkv[:, :, 2]
        enc_mixed, enc_lse = attend(enc_query, enc_key, encoder_value_rows, segment, enc_offsets)
        enc_mix = enc_mixed.reshape(1, row_tokens, col_width).astype(jnp.bfloat16)
        mix_full = gather_rows(enc_mix)
        attn_branch = cols_product(mix_full, w_out)
        hidden, normed_one, inv_one = norm_forward(
            x_in.astype(jnp.float32) + attn_branch, attention_norm_gain, attn_bias
        )
        hidden_low = hidden.astype(jnp.bfloat16)
        hidden_full = gather_cols(hidden_low)
        pre_act = rows_product(hidden_full, w_up)
        act_value, gelu_pull = jax.vjp(gelu_exact, pre_act)
        act_low = act_value.astype(jnp.bfloat16)
        act_full = gather_rows(act_low)
        ffn_branch = cols_product(act_full, w_down)
        encoded, normed_two, inv_two = norm_forward(hidden + ffn_branch, ffn_gain, ffn_bias)
        encoded_low = encoded.astype(jnp.bfloat16)
        enc_full = gather_cols(encoded_low)
        keyval = (
            rows_product(enc_full, keyval_matrix)
            .astype(jnp.bfloat16)
            .reshape(seq_rows, length, 2, head_count, head_dim)
        )
        cross_key = keyval[:, :, 0]
        cross_value = keyval[:, :, 1]
        stream_full = gather_cols(y_in)
        cross_query = (
            rows_product(stream_full, w_query)
            .astype(jnp.bfloat16)
            .reshape(stream_count, seq_rows, length, head_count, head_dim)
        )
        cross_mixed, cross_lse = attend(cross_query, cross_key, cross_value, segment, cross_offsets)
        cross_mix = cross_mixed.reshape(stream_count, row_tokens, col_width).astype(jnp.bfloat16)
        cross_full = gather_rows(cross_mix)
        cross_branch = cols_product(cross_full, w_cross_out)
        result, normed_three, inv_three = norm_forward(
            y_in.astype(jnp.float32) + cross_branch, cross_gain, cross_bias
        )
        outputs.append(result)
        grad_three, gain_part, bias_part = norm_back(
            cotangent[micro].astype(jnp.float32), normed_three, inv_three, cross_gain
        )
        norm_accs[4] = norm_accs[4] + gain_part
        norm_accs[5] = norm_accs[5] + bias_part
        branch_full = gather_cols(grad_three.astype(jnp.bfloat16))
        cross_out_acc = cross_out_acc + weight_grad(cross_full, branch_full)
        cross_mix_grad = (
            rows_product(branch_full, w_cross_out.T)
            .astype(jnp.bfloat16)
            .reshape(stream_count, seq_rows, length, head_count, head_dim)
        )
        query_grad, key_grad, value_grad, table_grad = attend_back(
            cross_query,
            cross_key,
            cross_value,
            segment,
            cross_offsets,
            onehot,
            cross_lse,
            cross_mix_grad,
        )
        cross_table_acc = cross_table_acc + table_grad
        query_low = query_grad.reshape(stream_count, row_tokens, col_width).astype(jnp.bfloat16)
        keyval_low = (
            jnp.stack(
                [
                    key_grad.reshape(row_tokens, col_width),
                    value_grad.reshape(row_tokens, col_width),
                ],
                axis=1,
            )
            .reshape(1, row_tokens, 2 * col_width)
            .astype(jnp.bfloat16)
        )
        query_full = gather_rows(query_low)
        query_acc = query_acc + weight_grad(stream_full, query_full)
        stream_grads.append(grad_three + cols_product(query_full, w_query.T))
        keyval_full = gather_rows(keyval_low)
        keyval_acc = keyval_acc + weight_grad(enc_full, keyval_full)
        encoded_grad = cols_product(keyval_full, keyval_matrix.T)
        grad_two, gain_part, bias_part = norm_back(encoded_grad, normed_two, inv_two, ffn_gain)
        norm_accs[2] = norm_accs[2] + gain_part
        norm_accs[3] = norm_accs[3] + bias_part
        feedforward_full_output = gather_cols(grad_two.astype(jnp.bfloat16))
        down_acc = down_acc + weight_grad(act_full, feedforward_full_output)
        act_grad = rows_product(feedforward_full_output, w_down.T)
        pre_low = gelu_pull(act_grad)[0].astype(jnp.bfloat16)
        pre_full = gather_rows(pre_low)
        up_acc = up_acc + weight_grad(hidden_full, pre_full)
        hidden_grad = grad_two + cols_product(pre_full, w_up.T)
        grad_one, gain_part, bias_part = norm_back(
            hidden_grad, normed_one, inv_one, attention_norm_gain
        )
        norm_accs[0] = norm_accs[0] + gain_part
        norm_accs[1] = norm_accs[1] + bias_part
        attn_full = gather_cols(grad_one.astype(jnp.bfloat16))
        out_acc = out_acc + weight_grad(mix_full, attn_full)
        enc_mix_grad = (
            rows_product(attn_full, w_out.T)
            .astype(jnp.bfloat16)
            .reshape(1, seq_rows, length, head_count, head_dim)
        )
        enc_qgrad, enc_kgrad, enc_vgrad, table_grad = attend_back(
            enc_query,
            enc_key,
            encoder_value_rows,
            segment,
            enc_offsets,
            onehot,
            enc_lse,
            enc_mix_grad,
        )
        enc_table_acc = enc_table_acc + table_grad
        qkv_low = (
            jnp.stack(
                [
                    enc_qgrad.reshape(row_tokens, col_width),
                    enc_kgrad.reshape(row_tokens, col_width),
                    enc_vgrad.reshape(row_tokens, col_width),
                ],
                axis=1,
            )
            .reshape(1, row_tokens, 3 * col_width)
            .astype(jnp.bfloat16)
        )
        qkv_full = gather_rows(qkv_low)
        qkv_acc = qkv_acc + weight_grad(x_full, qkv_full)
        token_grads.append((grad_one + cols_product(qkv_full, qkv_matrix.T))[0])
    norm_stack = jnp.stack(norm_accs)
    table_stack = jnp.stack([enc_table_acc, cross_table_acc])
    norm_sums = lax.psum(norm_stack, COL)
    table_sums = lax.psum(table_stack, ROW)
    return (
        jnp.stack(outputs),
        jnp.stack(token_grads),
        jnp.stack(stream_grads),
        qkv_acc.reshape(row_width, 3, col_width),
        table_sums[0],
        out_acc,
        norm_sums[0],
        norm_sums[1],
        up_acc,
        down_acc,
        norm_sums[2],
        norm_sums[3],
        query_acc,
        keyval_acc.reshape(row_width, 2, col_width),
        table_sums[1],
        cross_out_acc,
        norm_sums[4],
        norm_sums[5],
    )


def mm(a,b):
    return jnp.dot(a,b,preferred_element_type=F32)
def mm_nt(a,b):
    return lax.dot_general(a,b,(((1,),(1,)),((),())),preferred_element_type=F32)

def mm_tn(a, b):
    return lax.dot_general(a, b, (((0,), (0,)), ((), ())), preferred_element_type=F32)


def masked_bias(off_ref, index, segq, segk):
    length = segk.shape[0]
    row = jnp.broadcast_to(off_ref[index], (length, 2 * length))
    rolled = pltpu.roll(row, 0, 1, stride=1, stride_axis=0)
    return jnp.where(segk <= segq, rolled[:, length:], neg_fill)


def head_forward(keys, values, query, bias):
    logits = mm(keys, query) + bias
    top = jnp.max(logits, axis=0, keepdims=True)
    weight = jnp.exp(logits - top)
    total = jnp.sum(weight, axis=0, keepdims=True)
    return (mm(values, weight.astype(BF)) * (1.0 / total)).astype(BF), top + jnp.log(total)


def head_backward(keys, keys_t, values_t, query, grad, lse, bias):
    prob = jnp.exp(mm(keys, query) + (bias - lse))
    dprob = mm(values_t, grad)
    dlogits = prob * (dprob - jnp.sum(prob * dprob, axis=0, keepdims=True))
    low = dlogits.astype(BF)
    return dlogits, mm(keys_t, low).astype(BF), mm_nt(query, low), mm_nt(grad, prob.astype(BF))


def project(mix_ref, weight, start, rows):
    heads, hd = mix_ref.shape[0], mix_ref.shape[1]
    mixed = mix_ref[:, :, start : start + rows].reshape(heads * hd, rows)
    return mm_tn(mixed, weight).astype(BF)


def project_back(weight, rows_value, dmix_ref, start):
    heads, hd = dmix_ref.shape[0], dmix_ref.shape[1]
    rows = rows_value.shape[0]
    dmix_ref[:, :, start : start + rows] = mm_nt(weight, rows_value).astype(BF).reshape(heads, hd, rows)


def scaled(value, scale):
    return (value.astype(F32) * scale).astype(BF)


def offset_sums(g_ref, doff_ref, g_index, out_index, length):
    sub = lax.broadcasted_iota(jnp.int32, (8, 2 * length), 0)
    acc = jnp.zeros((8, 2 * length), F32)
    for i in range(length // 8):
        piece = g_ref[g_index + (pl.ds(8 * i, 8),)]
        padded = jnp.concatenate([jnp.zeros((8, length), F32), piece], axis=1)
        acc = acc + (pltpu.roll(padded, 2 * length - 8 * i, 1) if i else padded)
    for b in (1, 2, 4):
        acc = jnp.where((sub // b) % 2 == 1, pltpu.roll(acc, 2 * length - b, 1), acc)
    doff_ref[out_index] = jnp.sum(acc, axis=0, keepdims=True)


MESH = pl.DeviceIdType.MESH
FORWARD, BACKWARD = range(2)
ACROSS, THROUGH, ALONG, SUM_ALONG = range(4)


def spot():
    row, col = lax.axis_index(ROW), lax.axis_index(COL)
    return row // 2, row % 2, col // 2, col % 2


def device(y, k, seq, half):
    return (2 * y + k, 2 * seq + half)


def greet(devices):
    barrier = pltpu.get_barrier_semaphore()
    for target in devices:
        pl.semaphore_signal(barrier, inc=1, device_id=target, device_id_type=MESH)
    pl.semaphore_wait(barrier, len(devices))


def remote(source, target, send_sem, recv_sem, device_id):
    copy = pltpu.make_async_remote_copy(
        src_ref=source, dst_ref=target, send_sem=send_sem, recv_sem=recv_sem, device_id=device_id, device_id_type=MESH
    )
    copy.start()
    return copy


def lanes(start, size):
    return pl.ds(pl.multiple_of(start, size), size)


def rows_of(place):
    y, k, seq, half = place
    return [(dy, dk, (1 - y if dy else y), (1 - k if dk else k)) for dy, dk in ((0, 1), (1, 0), (1, 1))]


class Spread:
    def __init__(self, full_ref, half_sems, core_sems, place, rows):
        self.full, self.place, self.rows = full_ref, place, rows
        self.half_sems, self.core_sems = half_sems, core_sems
        self.first, self.second = {}, {}

    def block(self, n, piece, half, k):
        return self.full.at[n, half, k, pl.ds(piece * self.rows, self.rows)]

    def start(self, unit, n, piece):
        y, k, seq, half = self.place
        mine = self.block(n, piece, half, k)
        hs, cs = self.half_sems, self.core_sems
        self.first[unit] = (
            remote(mine, mine, hs.at[0, unit], hs.at[1, unit], device(y, k, seq, 1 - half)),
            remote(mine, mine, cs.at[0, unit, 0], cs.at[1, unit, 0], device(y, 1 - k, seq, half)),
        )

    def forward(self, unit, n, piece):
        y, k, seq, half = self.place
        self.first[unit][0].wait_recv()
        theirs = self.block(n, piece, 1 - half, k)
        cs = self.core_sems
        self.second[unit] = remote(theirs, theirs, cs.at[0, unit, 1], cs.at[1, unit, 1], device(y, 1 - k, seq, half))

    def ready(self, unit):
        self.first[unit][1].wait_recv()
        self.second[unit].wait_recv()

    def sent(self, unit):
        for copy in self.first[unit] + (self.second[unit],):
            copy.wait_send()

    def finish(self, unit):
        self.ready(unit)
        self.sent(unit)


class Reduce:
    def __init__(self, partial_ref, core_buf, half_send, half_buf, core_sems, half_sems, place, rows):
        self.partial, self.core_buf, self.half_send, self.half_buf = partial_ref, core_buf, half_send, half_buf
        self.core_sems, self.half_sems, self.place, self.rows = core_sems, half_sems, place, rows
        self.first, self.second = {}, {}

    def part(self, n, piece, half, k):
        return (n, half, k, pl.ds(piece * self.rows, self.rows))

    def start(self, unit, n, piece, away):
        y, k, seq, half = self.place
        side = 1 - half if away else half
        cs = self.core_sems
        lane = 0 if away else 1
        self.first[unit, lane] = remote(
            self.partial.at[self.part(n, piece, side, 1 - k)],
            self.core_buf.at[unit, lane],
            cs.at[0, unit, lane],
            cs.at[1, unit, lane],
            device(y, 1 - k, seq, half),
        )

    def pass_on(self, unit, n, piece):
        y, k, seq, half = self.place
        self.first[unit, 0].wait_recv()
        away = self.partial[self.part(n, piece, 1 - half, k)].astype(F32) + self.core_buf[unit, 0].astype(F32)
        self.half_send[unit] = away.astype(BF)
        hs = self.half_sems
        self.second[unit] = remote(
            self.half_send.at[unit], self.half_buf.at[unit], hs.at[0, unit], hs.at[1, unit], device(y, k, seq, 1 - half)
        )

    def result(self, unit, n, piece):
        y, k, seq, half = self.place
        self.first[unit, 1].wait_recv()
        mine = self.partial[self.part(n, piece, half, k)].astype(F32) + self.core_buf[unit, 1].astype(F32)
        self.second[unit].wait_recv()
        return mine + self.half_buf[unit].astype(F32)

    def finish(self, unit):
        self.first[unit, 0].wait_send()
        self.first[unit, 1].wait_send()
        self.second[unit].wait_send()


class Return:
    def __init__(self, own_ref, landing, sems, place, feat):
        self.own, self.landing, self.sems, self.place, self.feat = own_ref, landing, sems, place, feat
        self.copies = []

    def start(self, unit, n, value):
        y, k, seq, half = self.place
        feat = self.feat
        self.own[unit] = value
        self.landing[y, n, k] = jnp.where(k == 0, value[:, :feat], value[:, feat : 2 * feat])
        for i, (dy, dk, ty, tk) in enumerate(rows_of(self.place)):
            self.copies.append(
                remote(
                    self.own.at[unit, :, lanes(tk * feat + 2 * dy * feat, feat)],
                    self.landing.at[y, n, k],
                    self.sems.at[0, unit, i],
                    self.sems.at[1, unit, i],
                    device(ty, tk, seq, half),
                )
            )

    def finish(self):
        for copy in self.copies:
            copy.wait()


class Freight:
    def __init__(self, full_ref, z_sems, y_sems, place, seqs):
        self.full, self.place, self.seqs = full_ref, place, seqs
        self.z_sems, self.y_sems = z_sems, y_sems
        self.wide = full_ref.shape[2] // 2
        self.z, self.y = {}, {}
        self.turn = seqs // 2

    def along(self, d):
        y, k, seq, half = self.place
        up = d <= self.turn
        source = d - 1 if up else (d + 1) % self.seqs
        if source:
            self.z[source].wait_recv()
        target = lax.rem(seq + (1 if up else self.seqs - 1), self.seqs)
        self.z[d] = remote(
            self.full.at[source, :, : self.wide],
            self.full.at[d, :, : self.wide],
            self.z_sems.at[0, d - 1],
            self.z_sems.at[1, d - 1],
            device(y, k, target, half),
        )

    def first(self):
        return [d for d in (1, self.seqs - 1) if d <= self.turn or d > self.turn][: min(2, self.seqs - 1)]

    def later(self):
        return list(range(2, self.turn + 1)) + list(range(self.seqs - 2, self.turn, -1))

    def last(self):
        return [d for d in range(self.seqs - 1, 0, -1) if d == self.turn or d == self.turn + 1]

    def across(self, d):
        y, k, seq, half = self.place
        self.y[d] = remote(
            self.full.at[d, :, : self.wide],
            self.full.at[d, :, self.wide :],
            self.y_sems.at[0, d],
            self.y_sems.at[1, d],
            device(1 - y, k, seq, half),
        )

    def pass_along(self, cross):
        for d in self.later():
            self.along(d)
            if cross:
                self.across(d - 1 if d <= self.turn else d + 1)

    def arrive(self, cross):
        for d in self.last():
            self.z[d].wait_recv()
            if cross:
                self.across(d)

    def finish(self):
        for copy in self.z.values():
            copy.wait_send()
        for copy in self.y.values():
            copy.wait()


class Collect:
    def __init__(self, source, place, seqs, y_refs=None, z_refs=None):
        self.source, self.place, self.seqs = source, place, seqs
        self.y_refs, self.z_refs = y_refs, z_refs
        self.wide = source.shape[2] // 2 if y_refs else source.shape[2]
        self.turn = seqs // 2
        self.order = list(range(self.turn, seqs)) + list(range(self.turn - 1, -1, -1))
        self.y, self.z, self.core = {}, {}, None

    def across(self, d):
        y, k, seq, half = self.place
        buf, sems = self.y_refs
        self.y[d] = remote(
            self.source.at[d, :, self.wide :], buf.at[d], sems.at[0, d], sems.at[1, d], device(1 - y, k, seq, half)
        )

    def total(self, d):
        if not self.y_refs:
            return self.source[d].astype(F32)
        self.y[d].wait_recv()
        return self.source[d, :, : self.wide].astype(F32) + self.y_refs[0][d].astype(F32)

    def store(self, out):
        for d in self.order:
            out[d] = self.total(d).astype(BF)

    def along(self, d):
        y, k, seq, half = self.place
        out, z_send, z_buf, c_send, z_sems, c_sems = self.z_refs
        left = d <= self.turn
        before = d + 1 if left else d - 1
        value = self.total(d)
        if before in self.z and before not in (self.turn + 1 if left else self.turn,):
            self.z[before].wait_recv()
            value = value + z_buf[before - 1].astype(F32)
        z_send[d - 1] = value.astype(BF)
        target = lax.rem(seq + (self.seqs - 1 if left else 1), self.seqs)
        self.z[d] = remote(
            z_send.at[d - 1], z_buf.at[d - 1], z_sems.at[0, d - 1], z_sems.at[1, d - 1], device(y, k, target, half)
        )

    def close(self):
        y, k, seq, half = self.place
        out, z_send, z_buf, c_send, z_sems, c_sems = self.z_refs
        total = self.total(0)
        for d in sorted({1, self.seqs - 1}):
            self.z[d].wait_recv()
            total = total + z_buf[d - 1].astype(F32)
        low, high = total[:, : self.wide // 2], total[:, self.wide // 2 :]
        out[k] = jnp.where(k == 0, low, high)
        c_send[...] = jnp.where(k == 0, high, low)
        self.core = remote(c_send, out.at[k], c_sems.at[0], c_sems.at[1], device(y, 1 - k, seq, half))

    def finish(self):
        for copy in self.y.values():
            copy.wait_send()
        for copy in self.z.values():
            copy.wait_send()
        if self.core is not None:
            self.core.wait()


def freight_scratch(seqs):
    dma = pltpu.SemaphoreType.DMA
    return [dma((2, seqs - 1)), dma((2, seqs))]


def across_scratch(seqs, n, wide):
    return [pltpu.VMEM((seqs, n, wide), BF), pltpu.SemaphoreType.DMA((2, seqs))]


def along_scratch(seqs, n, wide):
    dma = pltpu.SemaphoreType.DMA
    return [
        pltpu.VMEM((seqs - 1, n, wide), BF),
        pltpu.VMEM((seqs - 1, n, wide), BF),
        pltpu.VMEM((n, wide // 2), F32),
        dma((2, seqs - 1)),
        dma((2,)),
    ]


def along_devices(place, seqs):
    y, k, seq, half = place
    return [device(y, k, lax.rem(seq + d, seqs), half) for d in sorted({1, seqs - 1})]


def shuffle(source, target, n, index, place, sends, receives, local_sems):
    y, k, seq, half = place
    feat = source.shape[-1]
    copies = [pltpu.make_async_copy(source.at[y, n, k], target.at[n, :, lanes(k * feat, feat)], local_sems.at[index])]
    copies[0].start()
    for i, (dy, dk, ty, tk) in enumerate(rows_of(place)):
        copies.append(
            remote(
                source.at[ty, n, tk],
                target.at[n, :, lanes(k * feat + 2 * dy * feat, feat)],
                sends.at[index, i],
                receives.at[index, i],
                device(ty, tk, seq, half),
            )
        )
    return copies


def normalize(residual):
    centered = residual - jnp.mean(residual, axis=-1, keepdims=True)
    inv_std = lax.rsqrt(jnp.mean(centered * centered, axis=-1, keepdims=True) + epsilon)
    return centered * inv_std, inv_std


def normalize_back(out_grad, normed, inv_std, gain):
    scaled = out_grad * gain
    first = jnp.mean(scaled, axis=-1, keepdims=True)
    second = jnp.mean(scaled * normed, axis=-1, keepdims=True)
    return inv_std * (scaled - first - normed * second)


def column_sum(value):
    return jnp.sum(value, axis=0, keepdims=True)


def start_all(reduce, units):
    for unit, n, p in units:
        reduce.start(unit, n, p, True)
    for unit, n, p in units:
        reduce.start(unit, n, p, False)


def bias_of(r, target, table):
    segq = r.seg[...].astype(F32)
    length = segq.shape[1]
    segk = jnp.broadcast_to(segq, (8, length)).T[:, :1]

    def one(h, carry):
        target[h] = masked_bias(r.off, (table, h), segq, segk)
        return carry

    lax.fori_loop(0, r.qkv.shape[0], one, 0)


def out_part(r):
    heads, width, depth = r.weight.shape
    return r.weight[:, 3 * width // 4 :].reshape(heads * (width // 4), depth)


def feed_forward(r):
    block = r.act.shape[0] // 4
    for b in range(4):
        here = slice(b * block, (b + 1) * block)
        pre = mm_nt(r.up[here], r.row[...])
        share = 0.5 + 0.5 * lax.erf(pre * (0.5**0.5))
        r.act[here] = (pre * share).astype(BF)
        r.slope[here] = share + pre * jnp.exp(-0.5 * pre * pre) * ((2.0 * math.pi) ** -0.5)


def attend_all(r):
    heads, hd = r.qkv.shape[0], r.qkv.shape[1] // 3
    bias_of(r, r.masked, 0)
    r.bias_out[0].start()
    weight, row = r.weight.ready(), r.row.ready()

    def one(h, carry):
        r.qkv[h] = mm_nt(weight[h, : 3 * hd], row[...]).astype(BF)
        query = scaled(r.qkv[h, :hd], hd**-0.5)
        keys, values = r.qkv[h, hd : 2 * hd].T, r.qkv[h, 2 * hd :]
        r.mix[h], r.lse[h] = head_forward(keys, values, query, r.masked[h])
        return carry

    lax.fori_loop(0, heads, one, 0)


def cross_slot(r, d):
    span, width = r.dkv.shape[1], r.dquery.shape[1]
    r.g[d, :span] = mm(r.dkv[d], r.row[...]).astype(BF)
    r.g[d, span : span + width] = mm(r.dquery[d], r.stream[...]).astype(BF)
    r.g[d, span + width :] = mm(r.mix[d], r.grad_full[...]).astype(BF)


def attend_all_back(r):
    heads, hd, length = r.qkv.shape[0], r.qkv.shape[1] // 3, r.qkv.shape[2]
    scale = hd**-0.5
    qkv, masked = r.qkv.ready(), r.masked.ready()

    def one(h, carry):
        query, keys, values = (qkv[h, part * hd : (part + 1) * hd] for part in range(3))
        dlogits, dq, dk, dv = head_backward(
            keys.T, scaled(keys, scale), values.T, scaled(query, scale), r.dmix[h], r.lse[h], masked[h]
        )
        r.g_scr[...] = dlogits
        r.dqkv[h, :hd] = dq
        r.dqkv[h, hd : 2 * hd] = dk.astype(BF)
        r.dqkv[h, 2 * hd :] = dv.astype(BF)
        offset_sums(r.g_scr, r.doff, (), (h,), length)
        return carry

    lax.fori_loop(0, heads, one, 0)


def exchange_kernel(kind, norm_row, attend, feed, extra_count, far, count, pieces, seqs, rides, *refs):
    place = spot()
    y, k, seq, half = place
    refs = list(refs)
    take = lambda amount: [refs.pop(0) for _ in range(amount)]
    r = types.SimpleNamespace()
    r.resid, r.norm = take(2)
    if kind == BACKWARD:
        r.normed, r.inv = take(2)
    extras = take(extra_count)
    ride_in = take(len(rides))
    (r.full,) = take(1)
    if kind == FORWARD:
        r.out, r.normed, r.inv = take(3)
    else:
        r.grad, r.sums = take(2)
    if attend:
        if kind == FORWARD:
            r.qkv, r.mix, r.lse, r.masked, r.masked_next = take(5)
        else:
            r.dqkv, r.doff = take(2)
    leave_out = take(2 if kind == FORWARD else 1) if feed else []
    if kind == BACKWARD:
        (r.summed,) = take(1)
    ride_out = take(len(rides))
    if far:
        near, (sems,) = take(len(far)), take(1)
        for i, index in enumerate(far):
            extras[index] = Lazy(extras[index], near[i], sems.at[i])
    if kind == BACKWARD and attend:
        r.up, r.down, r.row, r.act, r.slope, r.hidden, r.weight, r.qkv, r.masked, r.lse = extras
    elif kind == BACKWARD:
        r.dkv, r.dquery, r.weight, r.mix, r.row, r.stream, r.grad_full = extras
    elif attend:
        r.weight, r.row, r.off, r.seg = extras
        biases = [(r.masked, 0), (r.masked_next, 1)]
        r.masked, r.masked_next, bias_sems = take(3)
        r.bias_out = [
            pltpu.make_async_copy(source, target, bias_sems.at[i])
            for i, (source, (target, _)) in enumerate(zip((r.masked, r.masked_next), biases))
        ]
    else:
        r.up, r.down, r.row = extras
    if feed:
        leaving, (sems,) = take(len(leave_out)), take(1)
        if kind == FORWARD:
            r.act, r.slope = leaving
        else:
            (r.g_up,) = leaving
        leaving = [pltpu.make_async_copy(a, b, sems.at[i]) for i, (a, b) in enumerate(zip(leaving, leave_out))]
    (partial,) = take(1)
    if kind == BACKWARD:
        (r.g,) = take(1)
        inner = Collect(r.g, place, seqs, y_refs=take(2))
        if feed:
            (r.dpre,) = take(1)
    if attend:
        if kind == BACKWARD:
            r.g_scr, r.dmix = take(2)
    core_buf, half_send, half_buf, rc, rh, gh, gc = take(7)
    rows = partial.shape[3] // pieces
    peers = [device(y, 1 - k, seq, half), device(y, k, seq, 1 - half)]
    peers.append(device(1 - y, k, seq, half))
    if {ALONG, THROUGH, SUM_ALONG} & set(rides):
        peers += along_devices(place, seqs)
    greet(peers)
    units = [(n * pieces + p, n, p) for n in range(count) for p in range(pieces)]
    reduce = Reduce(partial, core_buf, half_send, half_buf, rc, rh, place, rows)
    spread = Spread(r.full, gh, gc, place, rows)
    moves, sums_along = [], []
    for ride, source, target in zip(rides, ride_in, ride_out):
        if ride == SUM_ALONG:
            sums_along.append(Collect(source, place, seqs, z_refs=[target] + take(5)))
            for d in sums_along[-1].order[:2]:
                sums_along[-1].along(d)
        else:
            moves.append((ride, Freight(target, *take(2), place, seqs)))
            if ride == ACROSS:
                for d in range(seqs):
                    moves[-1][1].across(d)
            else:
                if ride == THROUGH:
                    moves[-1][1].across(0)
                for d in moves[-1][1].first():
                    moves[-1][1].along(d)
    own = partial.shape[3]
    if kind == FORWARD and attend:
        attend_all(r)
        weight = out_part(r)
        product = lambda start: project(r.mix, weight, start, own)
    elif kind == FORWARD:
        feed_forward(r)
        for copy in leaving:
            copy.start()
        product = lambda start: mm_tn(r.act[:, start : start + own], r.down[...]).astype(BF)
    elif feed:
        block = r.g.shape[1]
        for d in range(seqs):
            here = slice(d * block, (d + 1) * block)
            r.dpre[here] = (mm_nt(r.down[here], r.row[...]) * r.slope[here]).astype(BF)
        product = lambda start: mm_tn(r.dpre[:, start : start + own], r.up[...]).astype(BF)
    else:
        span = r.dkv.shape[1]
        weight = r.weight[:, :span].reshape(seqs * span, -1)
        product = lambda start: project(r.dkv, weight, start, own)
    if kind == BACKWARD and not feed:
        grad_slot = lambda d: cross_slot(r, d)
        grad_slot(inner.order[0])
        inner.across(inner.order[0])
    for a in range(2):
        for b in range(2):
            partial[0, a, b] = product((2 * a + b) * own)
    start_all(reduce, units)
    if kind == BACKWARD:
        r.sums[...] = jnp.zeros_like(r.sums)
        for d in inner.order[0 if feed else 1 :]:
            if feed:
                here = slice(d * block, (d + 1) * block)
                r.g[d] = mm(r.act[here], r.row[...]).astype(BF)
            else:
                grad_slot(d)
            inner.across(d)
    gain, bias = r.norm[norm_row : norm_row + 1], r.norm[norm_row + 1 : norm_row + 2]
    for unit, n, p in units:
        reduce.pass_on(unit, n, p)
    for unit, n, p in units:
        here = pl.ds(p * rows, rows)
        branch = reduce.result(unit, n, p)
        if kind == FORWARD:
            normed, inv = normalize(r.resid[n, here].astype(F32) + branch)
            value = normed * gain + bias
            r.out[n, here] = value
            r.normed[n, here] = normed
            r.inv[n, here] = inv
        else:
            upstream = r.resid[n, here] + branch if feed else branch
            normed = r.normed[n, here]
            value = normalize_back(upstream, normed, r.inv[n, here], gain)
            r.grad[n, here] = value
        r.full[n, half, k, here] = value.astype(BF)
        spread.start(unit, n, p)
        if kind != FORWARD:
            r.sums[0:1] += column_sum(upstream * normed)
            r.sums[1:2] += column_sum(upstream)
    for collect in sums_along:
        for d in collect.order[2:-1]:
            collect.along(d)
    for ride, move in moves:
        if ride != ACROSS:
            move.pass_along(ride == THROUGH)
            move.arrive(ride == THROUGH)
    if attend and kind == FORWARD:
        bias_of(r, r.masked_next, 1)
        r.bias_out[1].start()
    elif attend:
        for d in range(seqs):
            here = slice(d * block, (d + 1) * block)
            r.g_up[d] = mm(r.dpre[here], r.hidden[...]).astype(BF)
        for copy in leaving:
            copy.start()
    for unit, n, p in units:
        spread.forward(unit, n, p)
    for collect in sums_along:
        collect.close()
    for unit, n, p in units:
        spread.finish(unit)
        reduce.finish(unit)
    if attend and kind == BACKWARD:
        weight = out_part(r)
        for a in range(2):
            for b in range(2):
                project_back(weight, r.full[0, a, b], r.dmix, (2 * a + b) * own)
        attend_all_back(r)
    if attend and kind == FORWARD:
        for copy in r.bias_out:
            copy.wait()
    if feed:
        for copy in leaving:
            copy.wait()
    for ride, move in moves:
        move.finish()
    if kind == BACKWARD:
        inner.store(r.summed)
        inner.finish()
    for collect in sums_along:
        collect.finish()


def exchange(kind, collective_id, seqs, resid, norm, norm_row, normed=None, inv=None, rides=(), attend=(), feed=(), cross=()):
    count, own, depth = 1, resid.shape[1], norm.shape[1]
    if kind == BACKWARD:
        own = normed.shape[1]
    pieces = 2 if count == 1 else 1
    units, rows = count * pieces, own // pieces
    dma = pltpu.SemaphoreType.DMA
    shape = jax.ShapeDtypeStruct
    vmem = pl.BlockSpec(memory_space=pltpu.VMEM)
    anywhere = pl.BlockSpec(memory_space=pl.ANY)
    full = shape((count, 2, 2, own, depth), BF)
    grad, sums = shape((count, own, depth), F32), shape((2, depth), F32)
    scratch = []
    if kind == FORWARD:
        args = (resid, norm)
        outs = (full, grad, grad, shape((count, own, 1), F32))
    else:
        args = (resid, norm, normed, inv)
        outs = (full, grad, sums)
    extras = tuple(feed) + tuple(attend) + tuple(cross)
    far = tuple(i for i, array in enumerate(extras) if array.size >= 1 << 17)
    base = len(args)
    args += extras
    scratch += [pltpu.VMEM(extras[i].shape, extras[i].dtype) for i in far] + [dma((len(far),))]
    if attend and kind == FORWARD:
        bias = (attend[0].shape[0],) + (attend[1].shape[0],) * 2
        scratch += [pltpu.VMEM(bias, F32), pltpu.VMEM(bias, F32), dma((2,))]
    if feed and kind == FORWARD:
        inner = (feed[0].shape[0], feed[2].shape[0])
        scratch += [pltpu.VMEM(inner, BF), pltpu.VMEM(inner, F32), dma((2,))]
    elif feed:
        scratch += [pltpu.VMEM((seqs, feed[0].shape[0] // seqs, depth), BF), dma((1,))]
    scratch.append(pltpu.VMEM((count, 2, 2, own, depth), BF))
    if kind == BACKWARD:
        n = feed[0].shape[0] // seqs if feed else cross[2].shape[1]
        scratch += [pltpu.VMEM((seqs, n, depth), BF)] + across_scratch(seqs, n, depth // 2)
        if feed:
            scratch.append(pltpu.VMEM(feed[3].shape, BF))
    if attend:
        heads, hd = attend[0].shape[0], attend[0].shape[1] // 4
        length = attend[1].shape[0] if kind == FORWARD else attend[1].shape[2]
        qkv = shape((heads, 3 * hd, length), BF)
        if kind == FORWARD:
            bias = shape((heads, length, length), F32)
            outs += (qkv, shape((heads, hd, length), BF), shape((heads, 1, length), F32), bias, bias)
        else:
            outs += (qkv, shape((heads, 1, 2 * length), F32))
            scratch += [pltpu.VMEM((length, length), F32), pltpu.VMEM((heads, hd, length), BF)]
    if feed and kind == FORWARD:
        inner = (feed[0].shape[0], feed[2].shape[0])
        outs += (shape(inner, BF), shape(inner, F32))
    elif feed:
        outs += (shape((seqs, n, depth), BF),)
    if kind == BACKWARD:
        outs += (shape((seqs, n, depth // 2), BF),)
    scratch += [
        pltpu.VMEM((units, 2, rows, depth), BF),
        pltpu.VMEM((units, rows, depth), BF),
        pltpu.VMEM((units, rows, depth), BF),
        dma((2, units, 2)),
        dma((2, units)),
        dma((2, units)),
        dma((2, units, 2)),
    ]
    in_specs, out_specs = [vmem] * len(args), [vmem] * len(outs)
    for i in far:
        in_specs[base + i] = anywhere
    if kind == FORWARD:
        out_specs[-2:] = [anywhere] * 2
    elif feed:
        out_specs[-2] = anywhere
    aliases = {}
    for ride, array in rides:
        if ride == SUM_ALONG:
            n, wide = array.shape[1], depth // 2
            scratch += along_scratch(seqs, n, wide)
            in_specs.append(vmem)
            out_specs.append(vmem)
            outs += (shape((2, n, wide // 2), F32),)
        else:
            scratch += freight_scratch(seqs)
            aliases[len(args)] = len(outs)
            in_specs.append(anywhere)
            out_specs.append(anywhere)
            outs += (shape(array.shape, array.dtype),)
        args += (array,)
    return pl.pallas_call(
        functools.partial(exchange_kernel, kind, norm_row, bool(attend), bool(feed), len(extras), far, count, pieces, seqs, tuple(ride for ride, _ in rides)),
        out_shape=outs,
        in_specs=in_specs,
        out_specs=tuple(out_specs),
        scratch_shapes=scratch,
        input_output_aliases=aliases,
        compiler_params=pltpu.CompilerParams(collective_id=collective_id, has_side_effects=True, vmem_limit_bytes=60 << 20),
        name="exchange_%d" % collective_id,
    )(*args)


def cross_kernel(count, norm_row, query, kv, out_weight, bias, resid, norm, cot, mix, full_out, output, grad_out, sums, dquery, dkv, doff, full, grad, leave_sems, partial, lse, keys, keys_scaled, values_t, queries, masked, bias_sem, g_scr, dk_scr, dv_scr, dmix, own, landing, return_sems, cot_own, cot_send, cot_recv, cot_local, core_buf, half_send, half_buf, rc, rh, gh, gc):
    place = spot()
    y, k, seq, half = place
    heads, hd, length = query.shape[0], query.shape[1], kv.shape[2]
    depth, rows = partial.shape[4], partial.shape[3]
    scale = hd**-0.5
    bias_copy = pltpu.make_async_copy(bias, masked, bias_sem)
    bias_copy.start()
    greet(
        [device(y, 1 - k, seq, half), device(y, k, seq, 1 - half)]
        + [device(ty, tk, seq, half) for dy, dk, ty, tk in rows_of(place) if dy]
    )
    cots = [shuffle(cot, cot_own, n, n, place, cot_send, cot_recv, cot_local) for n in range(count)]
    reduce = Reduce(partial, core_buf, half_send, half_buf, rc, rh, place, rows)
    spread = Spread(full, gh, gc, place, rows)
    back = Return(own, landing, return_sems, place, depth // 4)
    leaving = []
    sums[...] = jnp.zeros_like(sums)
    g_scr[...] = jnp.zeros_like(g_scr)
    dk_scr[...] = jnp.zeros_like(dk_scr)
    dv_scr[...] = jnp.zeros_like(dv_scr)

    def prepare(h, carry):
        keys[h] = kv[h, :hd].T
        keys_scaled[h] = scaled(kv[h, :hd], scale)
        values_t[h] = kv[h, hd:].T
        queries[h] = scaled(query[h], scale)
        return carry

    lax.fori_loop(0, heads, prepare, 0)
    bias_copy.wait()

    def attend_heads(s, low, high):
        def one(h, carry):
            here = slice(s * length, (s + 1) * length)
            mix[h, :, here], lse[h, :, here] = head_forward(keys[h], kv[h, hd:], queries[h, :, here], masked[h])
            return carry

        lax.fori_loop(low, high, one, 0)

    def send_products(s):
        for a in range(2):
            for b in range(2):
                partial[s, a, b] = project(mix, out_weight[...], s * length + (2 * a + b) * rows, rows)
        reduce.start(s, s, 0, True)
        reduce.start(s, s, 0, False)

    def turn(s):
        normed, inv = normalize(resid[s].astype(F32) + reduce.result(s, s, 0))
        for copy in cots[s]:
            copy.wait()
        upstream = cot_own[s].astype(F32)
        value = normalize_back(upstream, normed, inv, norm[norm_row : norm_row + 1])
        grad[s] = value
        leaving.append(pltpu.make_async_copy(grad.at[s], grad_out.at[s], leave_sems.at[0, s]))
        leaving[-1].start()
        full[s, half, k] = value.astype(BF)
        spread.start(s, s, 0)
        sums[0:1] += column_sum(upstream * normed)
        sums[1:2] += column_sum(upstream)
        back.start(s, s, (normed * norm[norm_row : norm_row + 1] + norm[norm_row + 1 : norm_row + 2]).astype(BF))

    def attend_back(s):
        for a in range(2):
            for b in range(2):
                project_back(out_weight[...], full[s, a, b], dmix, (2 * a + b) * rows)

        def one(h, carry):
            here = slice(s * length, (s + 1) * length)
            dlogits, dq, dk, dv = head_backward(
                keys[h], keys_scaled[h], values_t[h], queries[h, :, here], dmix[h], lse[h, :, here], masked[h]
            )
            g_scr[h] += dlogits
            dquery[h, :, here] = dq
            dk_scr[h] += dk
            dv_scr[h] += dv
            return carry

        lax.fori_loop(0, heads, one, 0)

    for s in range(count):
        attend_heads(s, 0, heads // 2)
        if s >= 1:
            reduce.pass_on(s - 1, s - 1, 0)
        if s >= 2:
            turn(s - 2)
        attend_heads(s, heads // 2, heads)
        send_products(s)
    reduce.pass_on(count - 1, count - 1, 0)
    for s in range(max(count - 2, 0), count):
        turn(s)
    for s in range(count):
        spread.forward(s, s, 0)
        spread.ready(s)
        leaving.append(pltpu.make_async_copy(full.at[s], full_out.at[s], leave_sems.at[1, s]))
        leaving[-1].start()
        attend_back(s)
    for h in range(heads):
        dkv[h, :hd] = dk_scr[h].astype(BF)
        dkv[h, hd:] = dv_scr[h].astype(BF)

    def offsets_of(h, carry):
        offset_sums(g_scr, doff, (h,), (h,), length)
        return carry

    lax.fori_loop(0, heads, offsets_of, 0)
    back.finish()
    output[...] = landing[...].astype(F32)
    for copy in leaving:
        copy.wait()
    for s in range(count):
        spread.sent(s)
        reduce.finish(s)


def cross_attention(collective_id, query, kv, out_weight, masked, resid, norm, norm_row, cot):
    count, own, depth = resid.shape
    heads, hd, total = query.shape
    length = kv.shape[2]
    dma = pltpu.SemaphoreType.DMA
    shape = jax.ShapeDtypeStruct
    outs = (
        shape(query.shape, BF),
        shape((count, 2, 2, own, depth), BF),
        shape((2, count, 2, own, depth // 4), F32),
        shape((count, own, depth), F32),
        shape((2, depth), F32),
        shape(query.shape, BF),
        shape(kv.shape, BF),
        shape((heads, 1, 2 * length), F32),
    )
    whole = pl.BlockSpec(memory_space=pltpu.VMEM)
    anywhere = pl.BlockSpec(memory_space=pl.ANY)
    specs = [whole] * 3 + [anywhere] + [whole] * 2 + [anywhere]
    vmem = pltpu.VMEM
    return pl.pallas_call(
        functools.partial(cross_kernel, count, norm_row),
        out_shape=outs,
        in_specs=specs,
        out_specs=tuple(anywhere if i in (1, 3) else whole for i in range(len(outs))),
        scratch_shapes=[
            vmem((count, 2, 2, own, depth), BF),
            vmem((count, own, depth), F32),
            dma((2, count)),
            vmem((count, 2, 2, own, depth), BF),
            vmem((heads, 1, total), F32),
            vmem((heads, length, hd), BF),
            vmem((heads, hd, length), BF),
            vmem((heads, length, hd), BF),
            vmem(query.shape, BF),
            vmem(masked.shape, F32),
            pltpu.SemaphoreType.DMA,
            vmem((heads, length, length), F32),
            vmem((heads, hd, length), F32),
            vmem((heads, hd, length), F32),
            vmem((heads, hd, length), BF),
            vmem((count, own, depth), BF),
            vmem((2, count, 2, own, depth // 4), BF),
            dma((2, count, 3)),
            vmem((count, own, depth), BF),
            dma((count, 3)),
            dma((count, 3)),
            dma((count,)),
            vmem((count, 2, own, depth), BF),
            vmem((count, own, depth), BF),
            vmem((count, own, depth), BF),
            dma((2, count, 2)),
            dma((2, count)),
            dma((2, count)),
            dma((2, count, 2)),
        ],
        compiler_params=pltpu.CompilerParams(collective_id=collective_id, has_side_effects=True, vmem_limit_bytes=60 << 20),
        name="cross_attention",
    )(query, kv, out_weight, masked, resid, norm, cot)


class Lazy:
    def __init__(self, source, target, sem):
        self.copy, self.ref, self.shape = pltpu.make_async_copy(source, target, sem), target, target.shape
        self.copy.start()

    def ready(self):
        if self.copy is not None:
            self.copy.wait()
            self.copy = None
        return self.ref

    def __getitem__(self, index):
        return self.ready()[index]

    @property
    def at(self):
        return self.ready().at


def fetch(far, near, sems):
    copies = [pltpu.make_async_copy(source, target, sems.at[i]) for i, (source, target) in enumerate(zip(far, near))]
    for copy in copies:
        copy.start()
    return copies


def inputs_kernel(seqs, tok_ref, str_ref, norm_ref, ids_ref, tab_ref, *refs):
    refs = list(refs)
    take = lambda amount: [refs.pop(0) for _ in range(amount)]
    groups = 4
    far = take(7)
    x_own, *leave_out, norm_all, ids_all, tab_all = take(7)
    fulls = take(groups)
    in_send, in_recv, in_local, xh, xc, yh, yc, small_sems, tab_sems, small_self, pack_sems, pack_self = take(12)
    pack_first, pack_up, pack_last = take(3)
    w_qkv, w_out, w_up, w_kv, w_query, w_co = near = take(6)
    (fetch_sems,) = take(1)
    x_full, y_own, y_full = leaving = take(3)
    (leave_sems,) = take(1)
    leaving = [pltpu.make_async_copy(a, b, leave_sems.at[n]) for n, (a, b) in enumerate(zip(leaving, leave_out))]
    w_down = far.pop(3)
    fetched = fetch(far, near, fetch_sems)
    packs = [pack_first, pack_up, w_down, pack_last]
    place = spot()
    y, k, seq, half = place
    feat = tok_ref.shape[-1]
    own = tok_ref.shape[-2]
    row_peers = rows_of(place)
    others = [device(y, k, lax.rem(seq + d, seqs), half) for d in range(1, seqs)]
    greet([device(ty, tk, seq, half) for dy, dk, ty, tk in row_peers] + [device(y, k, seq, 1 - half)] + others)
    count = str_ref.shape[1]
    x_copies = shuffle(tok_ref, x_own, 0, 0, place, in_send, in_recv, in_local)
    hd = w_out.shape[0] // 2

    def columns_in(pack, start, matrix):
        rows = matrix.T
        half_rows = rows.shape[0] // 2
        for core in range(2):
            pack[core, start : start + half_rows] = rows[core * half_rows : (core + 1) * half_rows]

    def rows_in(pack, start, matrix):
        half_rows = matrix.shape[0] // 2
        for core in range(2):
            pack[core, start : start + half_rows] = matrix[core * half_rows : (core + 1) * half_rows]

    def load(g):
        here = fulls[g].at[0, :, lanes(k * feat, feat)]
        copy = pltpu.make_async_copy(packs[g].at[k], here, pack_self.at[g])
        copy.start()
        return (
            copy,
            remote(packs[g].at[1 - k], here, pack_sems.at[0, g], pack_sems.at[1, g], device(y, 1 - k, seq, half)),
        )

    for copy in fetched[:2]:
        copy.wait()
    for part in range(3):
        columns_in(pack_first, part * hd, w_qkv[part])
    rows_in(pack_first, 3 * hd, w_out)
    loads = [load(0)]
    small = []
    for j, (source, target) in enumerate(((norm_ref, norm_all), (ids_ref, ids_all))):
        slot = (lambda dy: (slice(None), lanes(k * feat + 2 * dy * feat, feat))) if j == 0 else (lambda dy: (2 * y + k,))
        copy = pltpu.make_async_copy(source, target.at[slot(0)], small_self.at[j])
        copy.start()
        small.append(copy)
        for i, (dy, dk, ty, tk) in enumerate(row_peers):
            small.append(
                remote(source, target.at[slot(dy)], small_sems.at[0, j, i], small_sems.at[1, j, i], device(ty, tk, seq, half))
            )
    copy = pltpu.make_async_copy(tab_ref, tab_all.at[0], small_self.at[2])
    copy.start()
    small.append(copy)
    for d in range(1, seqs):
        small.append(remote(tab_ref, tab_all.at[d], tab_sems.at[0, d - 1], tab_sems.at[1, d - 1], others[d - 1]))
    freights = [Freight(full, *take(2), place, seqs) for full in fulls]
    for copy in loads[0]:
        copy.wait()
    for d in freights[0].first():
        freights[0].along(d)
    freights[0].across(0)
    fetched[2].wait()
    columns_in(pack_up, 0, w_up[...])
    loads.append(load(1))
    for copy in x_copies:
        copy.wait()
    x_full[0, half, k] = x_own[0]
    x_spread = Spread(x_full, xh, xc, place, own)
    x_spread.start(0, 0, 0)
    y_copies = [shuffle(str_ref, y_own, n, 1 + n, place, in_send, in_recv, in_local) for n in range(count)]
    y_spread = Spread(y_full, yh, yc, place, own)
    freights[0].pass_along(True)
    for copy in loads[1]:
        copy.wait()
    for d in freights[1].first():
        freights[1].along(d)
    loads.append(load(2))
    for copy in fetched[3:]:
        copy.wait()
    for part in range(2):
        columns_in(pack_last, part * hd, w_kv[part])
    columns_in(pack_last, 2 * hd, w_query[...])
    rows_in(pack_last, 3 * hd, w_co)
    loads.append(load(3))
    x_spread.forward(0, 0, 0)
    freights[0].arrive(True)
    freights[1].across(0)
    for n in range(count):
        for copy in y_copies[n]:
            copy.wait()
        y_full[n, half, k] = y_own[n]
        y_spread.start(n, n, 0)
    freights[1].pass_along(True)
    for g in range(2, groups):
        for copy in loads[g]:
            copy.wait()
    for d in freights[2].first():
        freights[2].along(d)
    freights[1].arrive(True)
    freights[2].pass_along(False)
    for n in range(count):
        y_spread.forward(n, n, 0)
    x_spread.finish(0)
    for n in range(count):
        y_spread.finish(n)
    for copy in leaving:
        copy.start()
    for copy in small:
        copy.wait()
    freights[2].arrive(False)
    for freight in freights:
        freight.finish()
    for copy in leaving:
        copy.wait()


def gather_inputs(seqs, tokens, streams, norm, ids, table, *weights):
    count, own, feat = streams.shape[1], streams.shape[-2], streams.shape[-1]
    depth = 4 * feat
    dma = pltpu.SemaphoreType.DMA
    shape = jax.ShapeDtypeStruct
    vmem = pl.BlockSpec(memory_space=pltpu.VMEM)
    outs = (
        shape((1, own, depth), BF),
        shape((1, 2, 2, own, depth), BF),
        shape((count, own, depth), BF),
        shape((count, 2, 2, own, depth), BF),
        shape((norm.shape[0], depth), F32),
        shape((4,) + ids.shape, jnp.int32),
        shape((seqs,) + table.shape, F32),
    )
    specs = [vmem] * len(outs)
    hd, ff = weights[1].shape[0] // 2, weights[2].shape[1] // 2
    for n in (4 * hd, ff, ff, 4 * hd):
        outs += (shape((seqs, n, depth), BF),)
        specs.append(pl.BlockSpec(memory_space=pl.ANY))
    moves = 1 + count
    scratch = [
        dma((moves, 3)),
        dma((moves, 3)),
        dma((moves,)),
        dma((2, 1)),
        dma((2, 1, 2)),
        dma((2, count)),
        dma((2, count, 2)),
        dma((2, 2, 3)),
        dma((2, seqs - 1)),
        dma((3,)),
        dma((2, 4)),
        dma((4,)),
    ]
    scratch += [pltpu.VMEM((2, n, feat), BF) for n in (4 * hd, ff, 4 * hd)]
    fetched = weights[:3] + weights[4:]
    scratch += [pltpu.VMEM(weight.shape, BF) for weight in fetched] + [dma((len(fetched),))]
    scratch += [pltpu.VMEM(out.shape, out.dtype) for out in outs[1:4]] + [dma((3,))]
    specs[1:4] = [pl.BlockSpec(memory_space=pl.ANY)] * 3
    for _ in range(4):
        scratch += freight_scratch(seqs)
    return pl.pallas_call(
        functools.partial(inputs_kernel, seqs),
        out_shape=outs,
        in_specs=[pl.BlockSpec(memory_space=pl.ANY)] * (5 + len(weights)),
        out_specs=tuple(specs),
        scratch_shapes=scratch,
        compiler_params=pltpu.CompilerParams(collective_id=0, has_side_effects=True, vmem_limit_bytes=60 << 20),
        name="gather_inputs",
    )(tokens, streams, norm, ids, table, *weights)


def outputs_kernel(seqs, count, dqkv, dquery, mix, first_weight, last_weight, x_full, d1_full, d1, d3, small, down, up, tok_out, str_out, small_out, down_out, up_out, first_out, part, first, core_buf, half_send, half_buf, own, land_x, land_y, rc, rh, rs, small_buf, ss, *refs):
    refs = list(refs)
    take = lambda amount: [refs.pop(0) for _ in range(amount)]
    place = spot()
    far = [up, dqkv, first_weight, x_full, mix, d1_full, last_weight, dquery, down, d1, d3]
    near, (sems,) = take(len(far)), take(1)
    lazy = [Lazy(source, target, sems.at[i]) for i, (source, target) in enumerate(zip(far, near))]
    up, dqkv, first_weight, x_full, mix, d1_full, last_weight, dquery, down, d1, d3 = lazy
    y, k, seq, half = place
    rows = part.shape[3]
    feat = part.shape[4] // 4
    bits = [1 << b for b in range((seqs - 1).bit_length())]
    flips = [device(y, k, seq + b - 2 * b * ((seq // b) % 2), half) for b in bits]
    others = [device(y, k, lax.rem(seq + d, seqs), half) for d in range(1, seqs)]
    partners = [device(y, 1 - k, seq, half), device(y, k, seq, 1 - half), device(1 - y, k, seq, half)]
    greet(partners + [device(1 - y, 1 - k, seq, half)] + others)
    partners += flips
    small_out[...] = small[...]

    def start_small(stage):
        return stage, remote(small_out, small_buf.at[stage], ss.at[0, stage], ss.at[1, stage], partners[stage])

    def end_small(started):
        stage, copy = started
        copy.wait()
        small_out[...] += small_buf[stage]

    heads, width = mix.shape[0], mix.shape[1]

    def products(unit):
        for a in range(2):
            for b in range(2):
                start = (2 * a + b) * rows
                if unit == 0:
                    weight = first_weight[:, : 3 * width].reshape(heads * 3 * width, -1)
                    part[unit, a, b] = project(dqkv, weight, start, rows)
                else:
                    weight = last_weight[:, 2 * width : 3 * width].reshape(heads * width, -1)
                    part[unit, a, b] = project(dquery, weight, 4 * (unit - 1) * rows + start, rows)
        reduce.start(unit, unit, 0, True)
        reduce.start(unit, unit, 0, False)

    reduce = Reduce(part, core_buf, half_send, half_buf, rc, rh, place, rows)
    units = range(count + 1)
    down = Collect(down, place, seqs, z_refs=[down_out] + take(5))
    up = Collect(up, place, seqs, y_refs=take(2), z_refs=[up_out] + take(5))
    first_ref = first
    first = Collect(first, place, seqs, y_refs=take(2), z_refs=[first_out] + take(5))
    started = start_small(2)
    for d in up.order:
        up.across(d)
    products(0)
    for d in first.order:
        first_ref[d, : 3 * width] = mm(dqkv[d], x_full[...]).astype(BF)
        first_ref[d, 3 * width :] = mm(mix[d], d1_full[...]).astype(BF)
        first.across(d)
    end_small(started)
    started = start_small(3)
    reduce.pass_on(0, 0, 0)
    products(1)
    for stage in range(4, len(partners)):
        end_small(started)
        started = start_small(stage)
    end_small(started)
    for d in down.order[:2]:
        down.along(d)
    started = start_small(0)
    for unit in units[2:]:
        products(unit)
    end_small(started)
    x_back = Return(own, land_x, rs, place, feat)
    y_back = Return(own, land_y, rs, place, feat)
    x_back.start(0, 0, (d1[0] + reduce.result(0, 0, 0)).astype(BF))
    started = start_small(1)
    for unit in units[1:]:
        reduce.pass_on(unit, unit, 0)
    end_small(started)
    for d in down.order[2:-1]:
        down.along(d)
    for d in up.order[:2]:
        up.along(d)
    for unit in units[1:]:
        y_back.start(unit, unit - 1, (d3[unit - 1] + reduce.result(unit, unit, 0)).astype(BF))
    down.close()
    for d in up.order[2:-1]:
        up.along(d)
    for d in first.order[:2]:
        first.along(d)
    up.close()
    for d in first.order[2:-1]:
        first.along(d)
    for unit in units:
        reduce.finish(unit)
    x_back.finish()
    tok_out[...] = land_x[:, 0].astype(F32)
    first.close()
    y_back.finish()
    str_out[...] = land_y[...].astype(F32)
    for collect in (down, up, first):
        collect.finish()


def scatter_outputs(seqs, collective_id, dqkv, dquery, mix, first_weight, last_weight, x_full, d1_full, d1, d3, small, down, up):
    count, own, depth = d3.shape
    feat, wide = depth // 4, depth // 2
    units = count + 1
    dma = pltpu.SemaphoreType.DMA
    shape = jax.ShapeDtypeStruct
    stages = 3 + (seqs - 1).bit_length()
    outs = (shape((2, 2, own, feat), F32), shape((2, count, 2, own, feat), F32), shape(small.shape, F32))
    outs += tuple(shape((2, group.shape[1], feat), F32) for group in (down, up, first_weight))
    scratch = [
        pltpu.VMEM((units, 2, 2, own, depth), BF),
        pltpu.VMEM(first_weight.shape, BF),
        pltpu.VMEM((units, 2, own, depth), BF),
        pltpu.VMEM((units, own, depth), BF),
        pltpu.VMEM((units, own, depth), BF),
        pltpu.VMEM((units, own, depth), BF),
        pltpu.VMEM((2, 1, 2, own, feat), BF),
        pltpu.VMEM((2, count, 2, own, feat), BF),
        dma((2, units, 2)),
        dma((2, units)),
        dma((2, units, 3)),
        pltpu.VMEM((stages,) + small.shape, F32),
        dma((2, stages)),
    ]
    far = (up, dqkv, first_weight, x_full, mix, d1_full, last_weight, dquery, down, d1, d3)
    scratch += [pltpu.VMEM(array.shape, array.dtype) for array in far] + [dma((len(far),))]
    scratch += along_scratch(seqs, down.shape[1], wide)
    for group in (up, first_weight):
        scratch += across_scratch(seqs, group.shape[1], wide) + along_scratch(seqs, group.shape[1], wide)
    args = (dqkv, dquery, mix, first_weight, last_weight, x_full, d1_full, d1, d3, small, down, up)
    return pl.pallas_call(
        functools.partial(outputs_kernel, seqs, count),
        out_shape=outs,
        in_specs=[pl.BlockSpec(memory_space=pltpu.VMEM if array is small else pl.ANY) for array in args],
        out_specs=tuple(pl.BlockSpec(memory_space=pltpu.VMEM) for _ in outs),
        scratch_shapes=scratch,
        compiler_params=pltpu.CompilerParams(collective_id=collective_id, has_side_effects=True, vmem_limit_bytes=60 << 20),
        name="scatter_outputs",
    )(*args)


def pick(array, index, axis):
    return lax.dynamic_index_in_dim(array, index, axis, keepdims=False)


def dot_f32(spec, left, right):
    return jnp.einsum(spec, left, right, preferred_element_type=F32)


def on_device(
    rows,
    cols,
    tokens,
    streams,
    cotangent,
    block_ids,
    bucket_ids,
    w_qkv,
    enc_table,
    w_out,
    attention_norm_gain,
    attn_bias,
    w_up,
    w_down,
    ffn_gain,
    ffn_bias,
    w_query,
    w_keyval,
    cross_table,
    w_cross_out,
    cross_gain,
    cross_bias,
):
    seqs = cols // 2
    row, col = lax.axis_index(ROW), lax.axis_index(COL)
    y, k, seq, half = row // 2, row % 2, col // 2, col % 2
    low_y = y == 0
    stream_count = streams.shape[1]
    tok = tokens.shape[1]
    own = tok // 2
    feat = tokens.shape[2]
    length = block_ids.shape[2]
    head_dim = w_qkv.shape[2] // 2
    ff = w_up.shape[1] // 2
    table_heads, bucket_count = enc_table.shape

    def columns_back(array, parts):
        return array.reshape(2, parts, -1, feat).transpose(3, 1, 0, 2).reshape(feat, parts, -1)

    hd3, hd2 = 3 * head_dim, 2 * head_dim
    norm_params = jnp.stack([attention_norm_gain, attn_bias, ffn_gain, ffn_bias, cross_gain, cross_bias] + [cross_bias] * 2)
    table_pack = jnp.broadcast_to(jnp.stack([enc_table, cross_table]).reshape(1, -1), (8, 128))
    micro_count = tokens.shape[0]
    x_own, x_full, y_own, y_full, norm_params, all_ids, all_tables, first, up, down, last = gather_inputs(
        seqs,
        tokens.reshape(micro_count, 1, 2, own, feat),
        streams.reshape(micro_count, stream_count, 2, own, feat),
        norm_params,
        block_ids.reshape(8, -1),
        table_pack,
        w_qkv.transpose(1, 0, 2),
        w_out,
        w_up,
        w_down.reshape(2, ff, feat),
        w_keyval.transpose(1, 0, 2),
        w_query,
        w_cross_out,
    )
    x_full, y_full = x_full.reshape(length, D), y_full.reshape(stream_count * length, D)
    segment = pick(pick(all_ids.reshape(rows, micro_count, length), seq, 0), y, 0)
    segq = segment[None]
    own_tables = pick(all_tables[:, 0].reshape(seqs, 2, table_heads, bucket_count), k, 2)
    slot_col = 2 * ((seq - jnp.arange(seqs)) % seqs) + half
    reversed_ids = jnp.concatenate([jnp.full((1,), -1, jnp.int32), bucket_ids[::-1]])
    onehot = bucket_onehot(reversed_ids, bucket_count)
    offsets = jnp.einsum("htb,bo->tho", own_tables, onehot, precision=highest)[:, :, None, :]


    hidden_full, hidden, normed1, inv1, qkv, mix, lse, enc_bias, cross_bias_full, down, last = exchange(
        FORWARD,
        1,
        seqs,
        x_own,
        norm_params,
        0,
        rides=((ACROSS, down), (ALONG, last)),
        attend=(first, x_full, offsets, segq),
    )
    up, down = up.reshape(-1, D), down.reshape(-1, D)
    hidden_full = hidden_full.reshape(length, D)
    enc_full, _, normed2, inv2, act, slope, last = exchange(
        FORWARD,
        2,
        seqs,
        hidden,
        norm_params,
        2,
        rides=((ACROSS, last),),
        feed=(up, down, hidden_full),
    )
    m_kv, m_q, m_co = last[:, :hd2], last[:, hd2:hd3], last[:, hd3:].reshape(-1, D)
    enc_full = enc_full.reshape(length, D)
    kv = dot_f32("snr,tr->snt", m_kv, enc_full).astype(BF)
    query = dot_f32("snr,tr->snt", m_q, y_full).astype(BF)
    cmix, d3_full, output, d3, sums3, dquery, dkv, doff_cross = cross_attention(
        3,
        query,
        kv,
        m_co,
        cross_bias_full,
        y_own,
        norm_params,
        4,
        cotangent.reshape(micro_count, stream_count, 2, own, feat),
    )
    d3_full = d3_full.reshape(stream_count * length, D)

    d2_full, d2, sums2, g_last = exchange(
        BACKWARD,
        4,
        seqs,
        norm_params[None],
        norm_params,
        2,
        normed=normed2,
        inv=inv2,
        cross=(dkv, dquery, last, cmix, enc_full, y_full, d3_full),
    )
    d2_full = d2_full.reshape(length, D)
    d1_full, d1, sums1, dqkv, doff_enc, g_up, g_down, g_last = exchange(
        BACKWARD,
        5,
        seqs,
        d2,
        norm_params,
        0,
        normed=normed1,
        inv=inv1,
        rides=((SUM_ALONG, g_last),),
        attend=(first, qkv, enc_bias, lse),
        feed=(up, down, d2_full, act, slope, hidden_full),
    )
    d1_full = d1_full.reshape(length, D)

    norm_grads = jnp.concatenate([sums1, sums2, sums3])
    norm_grads = jnp.where(low_y, norm_grads, jnp.roll(norm_grads, D // 2, axis=1))
    table_grads = jnp.einsum(
        "tho,bo->thb", jnp.stack([doff_enc[:, 0], doff_cross[:, 0]]), onehot, precision=highest
    )
    heads = 2 * slot_col + k
    spread = (heads[:, None] == jnp.arange(table_heads * cols)[None, :]).astype(F32)
    table_grads = jnp.einsum("thb,hg->tgb", table_grads, spread, precision=highest)
    small = jnp.concatenate([norm_grads.reshape(-1, 128), table_grads.reshape(-1, 128)])
    grad_tokens, grad_streams, small, g_down, g_up, g_first = scatter_outputs(
        seqs, 6, dqkv, dquery, mix, first, last, x_full, d1_full, d1, d3, small, g_down, g_up
    )
    output, grad_streams = output.reshape(streams.shape), grad_streams.reshape(streams.shape)
    grad_tokens = grad_tokens.reshape(tokens.shape)
    count = norm_grads.size // 128
    norm_sums = lax.dynamic_slice_in_dim(small[:count].reshape(6, D), row * feat, feat, axis=1)
    table_sums = small[count:].reshape(2, table_heads * cols, bucket_count)
    table_sums = lax.dynamic_slice_in_dim(table_sums, col * table_heads, table_heads, axis=1)
    return (
        output,
        grad_tokens,
        grad_streams,
        columns_back(g_first[:, :hd3], 3),
        table_sums[0],
        g_first[:, hd3:].reshape(w_out.shape),
        norm_sums[0],
        norm_sums[1],
        columns_back(g_up, 1).reshape(w_up.shape),
        g_down.reshape(w_down.shape),
        norm_sums[2],
        norm_sums[3],
        columns_back(g_last[:, hd2:hd3], 1).reshape(w_query.shape),
        columns_back(g_last[:, :hd2], 2),
        table_sums[1],
        g_last[:, hd3:].reshape(w_cross_out.shape),
        norm_sums[4],
        norm_sums[5],
    )


def solution(mesh):
    whole_row, half_col = mesh.shape[ROW], mesh.shape[COL]
    wide, table, norm = P(ROW, None, COL), P(COL, None), P(ROW)
    up, down = P(ROW, COL), P(COL, ROW)
    weights = (wide, table, down, norm, norm, up, down, norm, norm, up, wide, table, down, norm, norm)

    def run(tokens, *rest):
        micro_count = tokens.shape[0]
        if whole_row == 4 and micro_count == 2 and half_col % 2 == 0:
            device_fn = functools.partial(on_device, whole_row, half_col)
        else:
            device_fn = on_device_general
        return jax.shard_map(
            device_fn,
            mesh=mesh,
            in_specs=(P(None, COL, ROW), P(None, None, COL, ROW), P(None, None, COL, ROW), P(None, ROW, None), P()) + weights,
            out_specs=(P(None, None, COL, ROW), P(None, COL, ROW), P(None, None, COL, ROW)) + weights,
            check_vma=False,
        )(tokens, *rest)

    return run
```
